128 devices in a mesh: pts: 64 (over x, y, z), grp: 2 (over core).
Axes of the slice: x: 4, y: 4, z: 4, core: 2. Of those that a mesh axis runs over, the one named last changes fastest.
Arguments:
- points: bfloat16 [65536, 256], P(('pts', 'grp')), may hold values from -56 to 56
- rotated_place: int32 [65536], P(('pts', 'grp')), may hold values from 0 to 65535, as said below
- rotated_source: int32 [65536], P(('pts', 'grp')), may hold values from 0 to 65535, as said below
- ball_counts: int32 [256], replicated, may hold values from 64 to 256
- fine_projection: bfloat16 [256, 768], replicated, may hold values from -12 to 12
- fine_output: bfloat16 [256, 256], replicated, may hold values from -0.375 to 0.375
- pool_weight: bfloat16 [512, 512], replicated, may hold values from -0.25 to 0.25
- coarse_projection: bfloat16 [512, 1536], replicated, may hold values from -12 to 12
- coarse_output: bfloat16 [512, 512], replicated, may hold values from -0.25 to 0.25
- coarse_cotangent: bfloat16 [32768, 512], P(('pts', 'grp')), may hold values from -6 to 6
Outputs:
- coarse_result: bfloat16 [32768, 512], P(('pts', 'grp'))
- points_gradient: bfloat16 [65536, 256], P(('pts', 'grp'))
- fine_projection_gradient: float32 [256, 768], replicated
- fine_output_gradient: float32 [256, 256], replicated
- pool_gradient: float32 [512, 512], replicated
- coarse_projection_gradient: float32 [512, 1536], replicated
- coarse_output_gradient: float32 [512, 512], replicated
The draws below stay inside these ranges and needn't reach their ends.
Inputs may be any that keep to these rules, and one draw needn't show every extreme that they name: `rotated_place`: A permutation. Reading rows in blocks of 512, the tokens of one block that go to one block number at most 8, and every block sends exactly 8 to some block. `rotated_source`: the inverse permutation of rotated_place.
All inputs are finite; a program needn't handle non-finite values.
Results may differ from the reference program's by a relative error of at most 0.034.
The reference program's roundings to bfloat16 on the way count: a program that leaves them out, or rounds other values in their place, can miss the bound.
Values may be sent and summed in bfloat16 or wider, within the bound.
No kernel may reach another device: no remote copies, remote signals or barrier semaphores. Data moves between devices by JAX's collectives and lax.ppermute only.
A program may use at most 64 MiB of HBM per device.

```python
import jax
import jax.numpy as jnp
from jax import lax

C = 256
CB = 512
HD = 64
BALL = 256
TOK_DEV = 512
TOKENS = 65536
BALLS = 256
COARSE = 32768
CAP = 8
N_PTS = 64
N_GRP = 2


def rotation(key):
    device_count = N_PTS * N_GRP
    half_cap = CAP // 2
    subkeys = jax.random.split(key, 5)
    spread = jax.random.randint(subkeys[0], (device_count // 2,), -half_cap, half_cap + 1)
    spread = spread.at[0].set(half_cap)
    run_loads = jnp.stack([half_cap + spread, half_cap - spread], axis=1).reshape(device_count)
    labels = jax.random.permutation(subkeys[1], device_count)
    senders = jax.random.permutation(subkeys[2], device_count)
    device_ids = jnp.arange(device_count, dtype=jnp.int32)
    pair_counts = run_loads[labels[jnp.bitwise_xor(senders[:, None], device_ids[None, :])]]
    row_end = jnp.cumsum(pair_counts, axis=1)
    row_start = row_end - pair_counts
    column_start = jnp.cumsum(pair_counts, axis=0) - pair_counts
    sender_order = jax.vmap(lambda sub: jax.random.permutation(sub, TOK_DEV))(jax.random.split(subkeys[3], device_count))
    receiver_order = jax.vmap(lambda sub: jax.random.permutation(sub, TOK_DEV))(jax.random.split(subkeys[4], device_count))
    owner_ids = jax.vmap(lambda ends, ranks: jnp.searchsorted(ends, ranks, side='right'))(row_end, sender_order).astype(jnp.int32)
    offset = sender_order - jnp.take_along_axis(row_start, owner_ids, axis=1) + jnp.take_along_axis(column_start, owner_ids, axis=1)
    position = receiver_order[owner_ids, offset]
    return (owner_ids * TOK_DEV + position).reshape(device_count * TOK_DEV).astype(jnp.int32)


def draw_rotated_place(key, part):
    return rotation(key)


def draw_rotated_source(key, part):
    placed = rotation(key)
    return jnp.zeros_like(placed).at[placed].set(jnp.arange(placed.shape[0], dtype=jnp.int32))


def draw_points(key, part):
    key = jax.random.fold_in(key, 5)
    subkeys = jax.random.split(key, 3)
    row_scale = jnp.exp(jax.random.uniform(subkeys[1], (TOKENS, 1), minval=-1.2, maxval=1.2))
    column_scale = jnp.exp(jax.random.uniform(subkeys[2], (1, C), minval=-1.2, maxval=1.2))
    noise_part = jax.random.normal(subkeys[0], (TOKENS, C))
    return (jnp.clip(noise_part, -5.0, 5.0) * row_scale * column_scale).astype(jnp.bfloat16)


def projection_matrix(key, features):
    subkeys = jax.random.split(key, 1)
    matrix = jnp.clip(jax.random.normal(subkeys[0], (features, 3 * features)), -5.0, 5.0) * features ** (-0.5)
    keys_part = matrix[:, features:2 * features]
    return jnp.concatenate([matrix[:, :features], keys_part, matrix[:, 2 * features:]], axis=1).astype(jnp.bfloat16)


def draw_fine_projection(key, part):
    key = jax.random.fold_in(key, 7)
    return projection_matrix(key, C)


def draw_coarse_projection(key, part):
    key = jax.random.fold_in(key, 9)
    return projection_matrix(key, CB)


def place_ends(values, stream_key, low, top_value):
    place = [jax.random.randint(jax.random.fold_in(stream_key, axis), (), 0, length) for axis, length in enumerate(values.shape)]
    widest = values.shape.index(max(values.shape))
    next_to = place[:widest] + [(place[widest] + 1) % values.shape[widest]] + place[widest + 1:]
    return values.at[tuple(place)].set(low).at[tuple(next_to)].set(top_value)


def block_scale(own_key, extent, cuts, smallest, largest):
    level = 1.0
    for axis_at, blocks in cuts:
        heights = jax.random.uniform(jax.random.fold_in(jax.random.fold_in(own_key, 6), axis_at), (blocks,), jnp.float32, smallest / len(cuts), largest / len(cuts))
        level = level * jnp.repeat(jnp.exp(heights), extent[axis_at] // blocks).reshape((-1,) + (1,) * (len(extent) - 1 - axis_at))
    return level


def scatter_about(key, extent, width, most, shards=(), held_as=jnp.bfloat16):
    factor_of = block_scale(key, extent, shards, -0.22, 0.18) if shards else 1.0
    array = jax.random.normal(key, extent, jnp.float32) * width * factor_of
    return jnp.minimum(jnp.maximum(array, -most), most).astype(held_as)


def setup_inputs(seed: int = 0) -> dict:
    streams_of = jax.random.split(jax.random.key(seed), 11)
    points = draw_points(jax.random.fold_in(streams_of[10], 71), 0)
    rotated_place = draw_rotated_place(jax.random.fold_in(streams_of[10], 71), 0)
    rotated_source = draw_rotated_source(jax.random.fold_in(streams_of[10], 71), 0)
    ball_counts = place_ends(jax.random.randint(streams_of[3], (BALLS,), BALL // 4, BALL + 1), jax.random.fold_in(streams_of[3], 1), BALL // 4, BALL).astype(jnp.int32)
    fine_projection = draw_fine_projection(jax.random.fold_in(streams_of[10], 71), 0)
    fine_output = scatter_about(streams_of[5], (C, C), C ** -0.5, 0.375)
    pool_weight = scatter_about(streams_of[6], (2 * C, CB), (2 * C) ** -0.5, 0.25)
    coarse_projection = draw_coarse_projection(jax.random.fold_in(streams_of[10], 71), 0)
    coarse_output = scatter_about(streams_of[8], (CB, CB), CB ** -0.5, 0.25)
    coarse_cotangent = scatter_about(streams_of[9], (COARSE, CB), 1.0, 6.0, ((0, 128),))
    return {"points": points, "rotated_place": rotated_place, "rotated_source": rotated_source, "ball_counts": ball_counts, "fine_projection": fine_projection, "fine_output": fine_output, "pool_weight": pool_weight, "coarse_projection": coarse_projection, "coarse_output": coarse_output, "coarse_cotangent": coarse_cotangent}


epsilon = 1e-05

def normalize(values):
    floats = values.astype(jnp.float32)
    center = floats - lax.optimization_barrier(jnp.mean(floats, axis=-1, keepdims=True))
    inverse = lax.rsqrt(lax.optimization_barrier(jnp.mean(center * center, axis=-1, keepdims=True)) + epsilon)
    return (center * inverse, inverse)

def norm_backward(incoming, normed, inverse):
    first_mean = lax.optimization_barrier(jnp.mean(incoming, axis=-1, keepdims=True))
    second_mean = lax.optimization_barrier(jnp.mean(incoming * normed, axis=-1, keepdims=True))
    return inverse * (incoming - first_mean - normed * second_mean)

def split_heads(blocked):
    row_count, features = blocked.shape
    return jnp.transpose(blocked.reshape(row_count, features // HD, HD), (1, 0, 2))

def merge_heads(blocked):
    head_count, row_count, head_size = blocked.shape
    return jnp.transpose(blocked, (1, 0, 2)).reshape(row_count, head_count * head_size)

def head_forward(query_rows, key_rows, value_rows, key_live):
    scores = jnp.dot(query_rows, key_rows.T, preferred_element_type=jnp.float32) * HD ** (-0.5)
    scores = jnp.where(key_live[None, :], scores, -1e+30)
    highest = lax.optimization_barrier(jnp.max(scores, axis=-1, keepdims=True))
    raised = jnp.exp(scores - highest)
    weights = (raised / lax.optimization_barrier(jnp.sum(raised, axis=-1, keepdims=True))).astype(jnp.bfloat16)
    mixture = jnp.dot(weights, value_rows, preferred_element_type=jnp.float32).astype(jnp.bfloat16)
    return (mixture, weights)

def head_backward(query_rows, key_rows, value_rows, weights, incoming):
    against = jnp.dot(incoming, value_rows.T, preferred_element_type=jnp.float32)
    wide_weights = weights.astype(jnp.float32)
    diagonal = lax.optimization_barrier(jnp.sum(wide_weights * against, axis=-1, keepdims=True))
    slopes = (wide_weights * (against - diagonal) * HD ** (-0.5)).astype(jnp.bfloat16)
    query_grad = jnp.dot(slopes, key_rows, preferred_element_type=jnp.float32)
    key_grad = jnp.dot(slopes.T, query_rows, preferred_element_type=jnp.float32)
    value_grad = jnp.dot(weights.T, incoming, preferred_element_type=jnp.float32)
    return (query_grad, key_grad, value_grad)

def attention(query_rows, key_rows, value_rows, key_live):

    def one_head(pieces):
        return head_forward(pieces[0], pieces[1], pieces[2], key_live)
    mixture, weights = lax.map(one_head, (split_heads(query_rows), split_heads(key_rows), split_heads(value_rows)))
    return (merge_heads(mixture), weights)

def attention_backward(query_rows, key_rows, value_rows, weights, incoming):

    def one_head(pieces):
        return head_backward(pieces[0], pieces[1], pieces[2], pieces[3], pieces[4])
    query_grad, key_grad, value_grad = lax.map(one_head, (split_heads(query_rows), split_heads(key_rows), split_heads(value_rows), weights, split_heads(incoming)))
    return (merge_heads(query_grad), merge_heads(key_grad), merge_heads(value_grad))

def fine_forward(rotated_balls, live_balls, projection, output):
    ball_total, ball_size, features = rotated_balls.shape
    normed, inverse = normalize(rotated_balls)
    unit_rows = normed.astype(jnp.bfloat16)
    projected = jnp.dot(unit_rows.reshape(ball_total * ball_size, features), projection, preferred_element_type=jnp.float32)
    projected = projected.astype(jnp.bfloat16).reshape(ball_total, ball_size, 3 * features)

    def one_ball(pieces):
        rows_in = pieces[0]
        return attention(rows_in[:, :features], rows_in[:, features:2 * features], rows_in[:, 2 * features:], pieces[1])
    mixture, weights = lax.map(one_ball, (projected, live_balls))
    update = jnp.dot(mixture.reshape(ball_total * ball_size, features), output, preferred_element_type=jnp.float32)
    result = (rotated_balls.astype(jnp.float32) + update.reshape(ball_total, ball_size, features)).astype(jnp.bfloat16)
    return (result, (unit_rows, normed, inverse, projected, mixture, weights))

def fine_backward(stored, incoming, projection, output):
    unit_rows, normed, inverse, projected, mixture, weights = stored
    ball_total, ball_size, features = incoming.shape
    incoming_flat = incoming.reshape(ball_total * ball_size, features)
    output_term = jnp.dot(mixture.reshape(ball_total * ball_size, features).T, incoming_flat, preferred_element_type=jnp.float32)
    mixed_grad = jnp.dot(incoming_flat, output.T, preferred_element_type=jnp.float32).astype(jnp.bfloat16)
    mixed_grad = mixed_grad.reshape(ball_total, ball_size, features)

    def one_ball(pieces):
        rows_in = pieces[0]
        query_grad, key_grad, value_grad = attention_backward(rows_in[:, :features], rows_in[:, features:2 * features], rows_in[:, 2 * features:], pieces[1], pieces[2])
        return jnp.concatenate([query_grad, key_grad, value_grad], axis=1).astype(jnp.bfloat16)
    grad_projected = lax.map(one_ball, (projected, weights, mixed_grad))
    grad_flat = grad_projected.reshape(ball_total * ball_size, 3 * features)
    projection_term = jnp.dot(unit_rows.reshape(ball_total * ball_size, features).T, grad_flat, preferred_element_type=jnp.float32)
    spread_back = jnp.dot(grad_flat, projection.T, preferred_element_type=jnp.float32).reshape(ball_total, ball_size, features)
    grad_input = (incoming.astype(jnp.float32) + norm_backward(spread_back, normed, inverse)).astype(jnp.bfloat16)
    return (grad_input, projection_term, output_term)

def pair_step(coarse_pair, cotangent_pair, projection, output):
    features = coarse_pair.shape[1]
    normed, inverse = normalize(coarse_pair)
    unit_rows = normed.astype(jnp.bfloat16)
    projected = jnp.dot(unit_rows, projection, preferred_element_type=jnp.float32).astype(jnp.bfloat16)
    query_rows = projected[:, :features]
    key_rows = projected[:, features:2 * features]
    value_rows = projected[:, 2 * features:]
    everyone = jnp.arange(coarse_pair.shape[0]) >= 0
    mixture, weights = attention(query_rows, key_rows, value_rows, everyone)
    result = (coarse_pair.astype(jnp.float32) + jnp.dot(mixture, output, preferred_element_type=jnp.float32)).astype(jnp.bfloat16)
    incoming = jnp.dot(cotangent_pair, output.T, preferred_element_type=jnp.float32).astype(jnp.bfloat16)
    query_grad, key_grad, value_grad = attention_backward(query_rows, key_rows, value_rows, weights, incoming)
    grad_projected = jnp.concatenate([query_grad, key_grad, value_grad], axis=1).astype(jnp.bfloat16)
    spread_back = jnp.dot(grad_projected, projection.T, preferred_element_type=jnp.float32)
    coarse_grad = (cotangent_pair.astype(jnp.float32) + norm_backward(spread_back, normed, inverse)).astype(jnp.bfloat16)
    return (result, coarse_grad, unit_rows, grad_projected, mixture)

def reference(points, rotated_place, rotated_source, ball_counts, fine_projection, fine_output, pool_weight, coarse_projection, coarse_output, coarse_cotangent):
    features = points.shape[1]
    live_tree = (jnp.arange(BALL, dtype=jnp.int32)[None, :] < ball_counts[:, None]).reshape(TOKENS)
    rotated = points[rotated_source].reshape(BALLS, BALL, features)
    live_rows = live_tree[rotated_source].reshape(BALLS, BALL)
    fine_rotated, stored = fine_forward(rotated, live_rows, fine_projection, fine_output)
    fine_tree = fine_rotated.reshape(TOKENS, features)[rotated_place]
    joined = fine_tree.reshape(COARSE, 2 * features)
    coarse = jnp.dot(joined, pool_weight, preferred_element_type=jnp.float32).astype(jnp.bfloat16)
    wide = coarse.shape[1]

    def one_pair(pieces):
        return pair_step(pieces[0], pieces[1], coarse_projection, coarse_output)
    outcome = lax.map(one_pair, (coarse.reshape(COARSE // TOK_DEV, TOK_DEV, wide), coarse_cotangent.reshape(COARSE // TOK_DEV, TOK_DEV, wide)))
    coarse_result = outcome[0].reshape(COARSE, wide)
    coarse_grad = outcome[1].reshape(COARSE, wide)
    coarse_unit = outcome[2].reshape(COARSE, wide)
    coarse_grad_projected = outcome[3].reshape(COARSE, 3 * wide)
    coarse_mixture = outcome[4].reshape(COARSE, wide)
    factor = 1.0 / TOKENS ** 0.5
    coarse_projection_term = jnp.dot(coarse_unit.T, coarse_grad_projected, preferred_element_type=jnp.float32)
    coarse_output_term = jnp.dot(coarse_mixture.T, coarse_cotangent, preferred_element_type=jnp.float32)
    pool_term = jnp.dot(joined.T, coarse_grad, preferred_element_type=jnp.float32)
    fine_grad = jnp.dot(coarse_grad, pool_weight.T, preferred_element_type=jnp.float32).astype(jnp.bfloat16).reshape(TOKENS, features)
    grad_rotated = fine_grad[rotated_source].reshape(BALLS, BALL, features)
    grad_back, fine_projection_term, fine_output_term = fine_backward(stored, grad_rotated, fine_projection, fine_output)
    points_gradient = grad_back.reshape(TOKENS, features)[rotated_place]
    return (coarse_result, points_gradient, fine_projection_term * factor, fine_output_term * factor, pool_term * factor, coarse_projection_term * factor, coarse_output_term * factor)
```

```python
import math

import jax
import jax.numpy as jnp
from jax import lax
from jax.experimental import pallas as pl
from jax.experimental.pallas import tpu as pltpu
from jax.sharding import PartitionSpec as P

HD = 64
BALL = 256
PAIR = 2 * HD
EPSILON = 1e-05
BF = jnp.bfloat16
F32 = jnp.float32


def mm(a, b, contract=(1, 0)):
    return lax.dot_general(
        a, b, (((contract[0],), (contract[1],)), ((), ())), preferred_element_type=F32
    )


def normalize(values):
    floats = values.astype(F32)
    center = floats - jnp.mean(floats, axis=-1, keepdims=True)
    inverse = lax.rsqrt(jnp.mean(center * center, axis=-1, keepdims=True) + EPSILON)
    return center * inverse, inverse


def norm_backward(incoming, normed, inverse):
    first_mean = jnp.mean(incoming, axis=-1, keepdims=True)
    second_mean = jnp.mean(incoming * normed, axis=-1, keepdims=True)
    return inverse * (incoming - first_mean - normed * second_mean)


def one_hot(slots, total):
    shape = (total, slots.shape[1])
    return (lax.broadcasted_iota(jnp.int32, shape, 0) == slots).astype(BF)


def head_half(shape, half):
    lanes = lax.broadcasted_iota(jnp.int32, shape, 1)
    return (lanes < HD) if half == 0 else (lanes >= HD)


def keep_half(rows, half):
    return jnp.where(head_half(rows.shape, half), rows, jnp.zeros_like(rows))


def softmax_rows(scores):
    raised = jnp.exp(scores - jnp.max(scores, axis=-1, keepdims=True))
    return (raised / jnp.sum(raised, axis=-1, keepdims=True)).astype(BF)


def slopes_of(weights, against):
    wide = weights.astype(F32)
    diagonal = jnp.sum(wide * against, axis=-1, keepdims=True)
    return (wide * (against - diagonal) * HD ** (-0.5)).astype(BF)


def column_of(row):
    count = row.shape[1]
    turned = jnp.broadcast_to(row.astype(F32), (128, count)).T
    return jnp.concatenate([turned] * (count // 128), axis=1)


def route_kernel(place, source, counts, points, send, send_slot, receive_slot, live):
    count = place.shape[1]
    shift = count.bit_length() - 1
    capacity = send.shape[0] * count // (counts.shape[1] * BALL)
    to_row = place[...] >> shift
    rows = lax.broadcasted_iota(jnp.int32, (count, count), 0)
    columns = lax.broadcasted_iota(jnp.int32, (count, count), 1)
    earlier = (column_of(to_row) == to_row.astype(F32)) & (rows < columns)
    rank = jnp.sum(jnp.where(earlier, 1.0, 0.0), axis=0, keepdims=True)
    slot = to_row * capacity + rank.astype(jnp.int32)
    send_slot[...] = slot
    source_row = source[...]
    from_row = source_row >> shift
    earlier = (column_of(from_row) == from_row.astype(F32)) & (
        column_of(source_row) < source_row.astype(F32)
    )
    rank = jnp.sum(jnp.where(earlier, 1.0, 0.0), axis=0, keepdims=True)
    receive_slot[...] = from_row * capacity + rank.astype(jnp.int32)
    balls = counts.shape[1]
    own_ball = one_hot(source_row >> (BALL.bit_length() - 1), balls)
    filled = mm(jnp.broadcast_to(counts[...].astype(F32), (8, balls)).astype(BF), own_ball)
    inside = (source_row & (BALL - 1)).astype(F32)
    live[...] = jnp.where(inside < filled[:1], 1.0, 0.0)
    send[...] = mm(one_hot(slot, send.shape[0]), points[...]).astype(BF)


def fine_forward_kernel(
    arrived, receive_slot, live, projection, output, send, rotated, projected, mixture, weights
):
    place = one_hot(receive_slot[...], arrived.shape[0])
    rows_in = mm(place, arrived[...], (0, 0))
    rotated[...] = rows_in.astype(BF)
    features = rows_in.shape[1]
    normed, _ = normalize(rows_in)
    projected[...] = mm(normed.astype(BF), projection[...]).astype(BF)
    balls = rows_in.shape[0] // BALL
    pairs = features // PAIR
    for ball in range(balls):
        rows = slice(ball * BALL, (ball + 1) * BALL)
        alive = live[:, rows] > 0.5
        for pair in range(pairs):
            lanes = slice(pair * PAIR, (pair + 1) * PAIR)
            query = projected[rows, lanes]
            key = projected[rows, features + pair * PAIR : features + (pair + 1) * PAIR]
            value = projected[rows, 2 * features + pair * PAIR : 2 * features + (pair + 1) * PAIR]
            halves = []
            for half in range(2):
                scores = mm(keep_half(query, half), key, (1, 1)) * HD ** (-0.5)
                head_weights = softmax_rows(jnp.where(alive, scores, -1e30))
                weights[(ball * pairs + pair) * 2 + half] = head_weights
                halves.append(mm(head_weights, value))
            mixed = jnp.where(head_half(halves[0].shape, 0), halves[0], halves[1])
            mixture[rows, lanes] = mixed.astype(BF)
    result = (rows_in + mm(mixture[...], output[...])).astype(BF)
    send[...] = mm(place, result).astype(BF)


def join_kernel(arrived, slots, joined):
    half = joined.shape[1] // 2
    for side in range(2):
        place = one_hot(slots[side : side + 1, :], arrived.shape[0])
        joined[:, side * half : (side + 1) * half] = mm(place, arrived[...], (0, 0)).astype(BF)


def coarse_kernel(
    group,
    own_joined,
    other_joined,
    own_cotangent,
    other_cotangent,
    pool,
    projection,
    output,
    coarse,
    unit,
    keep,
    give,
):
    half_rows, wide = own_joined.shape
    part = wide // 2
    first = pl.multiple_of(group[0] * part, part)
    joined = jnp.concatenate([own_joined[...], other_joined[...]], axis=0)
    cotangent = jnp.concatenate([own_cotangent[...], other_cotangent[...]], axis=0)
    tokens = mm(joined, pool[...]).astype(BF)
    coarse[...] = tokens[:half_rows]
    normed, _ = normalize(tokens)
    unit_rows = normed.astype(BF)
    unit[...] = unit_rows
    queries = mm(unit_rows, projection[:, pl.ds(first, part)]).astype(BF)
    keys = mm(unit_rows, projection[:, pl.ds(wide + first, part)]).astype(BF)
    values = mm(unit_rows, projection[:, pl.ds(2 * wide + first, part)]).astype(BF)
    incoming = mm(cotangent, output[pl.ds(first, part), :], (1, 1)).astype(BF)
    for pair in range(part // PAIR):
        lanes = slice(pair * PAIR, (pair + 1) * PAIR)
        query, key, value = queries[:, lanes], keys[:, lanes], values[:, lanes]
        entering = incoming[:, lanes]
        parts = ([], [], [], [])
        for half in range(2):
            scores = mm(keep_half(query, half), key, (1, 1)) * HD ** (-0.5)
            head_weights = softmax_rows(scores)
            parts[0].append(mm(head_weights, value))
            against = mm(keep_half(entering, half), value, (1, 1))
            slopes = slopes_of(head_weights, against)
            parts[1].append(mm(slopes, key))
            parts[2].append(mm(slopes, query, (0, 0)))
            parts[3].append(mm(head_weights, entering, (0, 0)))
        for at, (low, high) in enumerate(parts):
            both = jnp.where(head_half(low.shape, 0), low, high).astype(BF)
            target = slice(at * part + pair * PAIR, at * part + (pair + 1) * PAIR)
            keep[:, target] = both[:half_rows]
            give[:, target] = both[half_rows:]


def coarse_finish_kernel(
    group,
    coarse,
    keep,
    got,
    cotangent,
    pool,
    projection,
    output,
    slots,
    result,
    gradient,
    send,
):
    half_rows, wide = coarse.shape
    part = wide // 2
    mixed = coarse[...].astype(F32)
    back = jnp.zeros((half_rows, wide), F32)
    for source, index in ((keep, group[0]), (got, 1 - group[0])):
        first = pl.multiple_of(index * part, part)
        mixed = mixed + mm(source[:, :part], output[pl.ds(first, part), :])
        for at in range(3):
            back = back + mm(
                source[:, (at + 1) * part : (at + 2) * part],
                projection[:, pl.ds(at * wide + first, part)],
                (1, 1),
            )
    result[...] = mixed.astype(BF)
    normed, inverse = normalize(coarse[...])
    gradient_rows = (
        cotangent[...].astype(F32) + norm_backward(back, normed, inverse)
    ).astype(BF)
    gradient[...] = gradient_rows
    fine = mm(gradient_rows, pool[...], (1, 1)).astype(BF)
    features = send.shape[1]
    total = mm(one_hot(slots[0:1, :], send.shape[0]), fine[:, :features])
    total = total + mm(one_hot(slots[1:2, :], send.shape[0]), fine[:, features:])
    send[...] = total.astype(BF)


def coarse_weights_kernel(
    unit, keep, give, own_cotangent, other_cotangent, projection_term, output_term
):
    part = keep.shape[1] // 4
    stacked = jnp.concatenate([keep[...], give[...]], axis=0)
    cotangent = jnp.concatenate([own_cotangent[...], other_cotangent[...]], axis=0)
    projection_term[...] = mm(unit[...], stacked[:, part:], (0, 0))
    output_term[...] = mm(stacked[:, :part], cotangent, (0, 0))


def pool_weights_kernel(group, own_joined, other_joined, own_gradient, other_gradient, term):
    part = term.shape[0]
    first = pl.multiple_of(group[0] * part, part)
    term[...] = mm(own_joined[:, pl.ds(first, part)], own_gradient[...], (0, 0)) + mm(
        other_joined[:, pl.ds(first, part)], other_gradient[...], (0, 0)
    )


def fine_backward_kernel(
    arrived,
    receive_slot,
    rotated,
    projected,
    mixture,
    weights,
    projection,
    output,
    send,
    projection_term,
    output_term,
    grad_projected,
):
    place = one_hot(receive_slot[...], arrived.shape[0])
    gradient_in = mm(place, arrived[...], (0, 0))
    gradient_rows = gradient_in.astype(BF)
    features = rotated.shape[1]
    entering = mm(gradient_rows, output[...], (1, 1)).astype(BF)
    output_term[...] = mm(mixture[...], gradient_rows, (0, 0))
    balls = rotated.shape[0] // BALL
    pairs = features // PAIR
    for ball in range(balls):
        rows = slice(ball * BALL, (ball + 1) * BALL)
        for pair in range(pairs):
            lanes = slice(pair * PAIR, (pair + 1) * PAIR)
            query = projected[rows, lanes]
            key = projected[rows, features + pair * PAIR : features + (pair + 1) * PAIR]
            value = projected[rows, 2 * features + pair * PAIR : 2 * features + (pair + 1) * PAIR]
            enters = entering[rows, lanes]
            parts = ([], [], [])
            for half in range(2):
                head_weights = weights[(ball * pairs + pair) * 2 + half]
                against = mm(keep_half(enters, half), value, (1, 1))
                slopes = slopes_of(head_weights, against)
                parts[0].append(mm(slopes, key))
                parts[1].append(mm(slopes, query, (0, 0)))
                parts[2].append(mm(head_weights, enters, (0, 0)))
            for at, (low, high) in enumerate(parts):
                both = jnp.where(head_half(low.shape, 0), low, high).astype(BF)
                target = at * features + pair * PAIR
                grad_projected[rows, target : target + PAIR] = both
    normed, inverse = normalize(rotated[...])
    projection_term[...] = mm(normed.astype(BF), grad_projected[...], (0, 0))
    back = mm(grad_projected[...], projection[...], (1, 1))
    result = (gradient_in + norm_backward(back, normed, inverse)).astype(BF)
    send[...] = mm(place, result).astype(BF)


def take_kernel(arrived, slots, rows_out):
    place = one_hot(slots[...], arrived.shape[0])
    rows_out[...] = mm(place, arrived[...], (0, 0)).astype(BF)


VMEM = pl.BlockSpec(memory_space=pltpu.VMEM)
SMEM = pl.BlockSpec(memory_space=pltpu.SMEM)


def call(kernel, inputs, outputs, scalar=False, scratch=()):
    in_specs = [VMEM] * len(inputs)
    if scalar:
        in_specs[0] = SMEM
    shapes = [jax.ShapeDtypeStruct(shape, dtype) for shape, dtype in outputs]
    return pl.pallas_call(
        kernel,
        out_shape=shapes,
        in_specs=in_specs,
        out_specs=[VMEM] * len(shapes),
        scratch_shapes=list(scratch),
        compiler_params=pltpu.CompilerParams(vmem_limit_bytes=56 * 1024 * 1024),
    )(*inputs)


def exchange(values):
    return lax.ppermute(values, "grp", [(0, 1), (1, 0)])


def route(values, devices):
    rows, features = values.shape
    arrived = lax.all_to_all(
        values.reshape(devices, rows // devices, features),
        ("pts", "grp"),
        split_axis=0,
        concat_axis=0,
        tiled=True,
    )
    return arrived.reshape(rows, features)


def on_device(
    points,
    rotated_place,
    rotated_source,
    ball_counts,
    fine_projection,
    fine_output,
    pool_weight,
    coarse_projection,
    coarse_output,
    coarse_cotangent,
):
    count, features = points.shape
    devices = lax.axis_size(("pts", "grp"))
    slots = 2 * count
    scaling = 1.0 / math.sqrt(count * devices)
    group = lax.axis_index("grp").astype(jnp.int32).reshape(1)
    wide = 2 * features
    half_rows = count // 2

    send, send_slot, receive_slot, live = call(
        route_kernel,
        (
            rotated_place.reshape(1, count),
            rotated_source.reshape(1, count),
            ball_counts.reshape(1, -1),
            points,
        ),
        (
            ((slots, features), BF),
            ((1, count), jnp.int32),
            ((1, count), jnp.int32),
            ((1, count), F32),
        ),
    )
    other_cotangent = exchange(coarse_cotangent)
    arrived = route(send, devices)
    pair_slots = send_slot.reshape(half_rows, 2).T
    heads = features // HD * (count // BALL)
    send, rotated, projected, mixture, weights = call(
        fine_forward_kernel,
        (arrived, receive_slot, live, fine_projection, fine_output),
        (
            ((slots, features), BF),
            ((count, features), BF),
            ((count, 3 * features), BF),
            ((count, features), BF),
            ((heads, BALL, BALL), BF),
        ),
    )
    arrived = route(send, devices)
    (own_joined,) = call(join_kernel, (arrived, pair_slots), (((half_rows, wide), BF),))
    other_joined = exchange(own_joined)
    coarse, unit, keep, give = call(
        coarse_kernel,
        (
            group,
            own_joined,
            other_joined,
            coarse_cotangent,
            other_cotangent,
            pool_weight,
            coarse_projection,
            coarse_output,
        ),
        (
            ((half_rows, wide), BF),
            ((count, wide), BF),
            ((half_rows, 2 * wide), BF),
            ((half_rows, 2 * wide), BF),
        ),
        scalar=True,
    )
    got = exchange(give)
    coarse_result, coarse_gradient, send = call(
        coarse_finish_kernel,
        (
            group,
            coarse,
            keep,
            got,
            coarse_cotangent,
            pool_weight,
            coarse_projection,
            coarse_output,
            pair_slots,
        ),
        (((half_rows, wide), BF), ((half_rows, wide), BF), ((slots, features), BF)),
        scalar=True,
    )
    arrived = route(send, devices)
    projection_term, output_term = call(
        coarse_weights_kernel,
        (unit, keep, give, coarse_cotangent, other_cotangent),
        (((wide, 3 * wide // 2), F32), ((wide // 2, wide), F32)),
    )
    other_gradient = exchange(coarse_gradient)
    (pool_term,) = call(
        pool_weights_kernel,
        (group, own_joined, other_joined, coarse_gradient, other_gradient),
        (((wide // 2, wide), F32),),
        scalar=True,
    )
    send, fine_projection_term, fine_output_term = call(
        fine_backward_kernel,
        (
            arrived,
            receive_slot,
            rotated,
            projected,
            mixture,
            weights,
            fine_projection,
            fine_output,
        ),
        (
            ((slots, features), BF),
            ((features, 3 * features), F32),
            ((features, features), F32),
        ),
        scratch=(pltpu.VMEM((count, 3 * features), BF),),
    )
    arrived = route(send, devices)
    (points_gradient,) = call(take_kernel, (arrived, send_slot), (((count, features), BF),))

    sums = lax.psum(
        (fine_projection_term, fine_output_term, pool_term, projection_term, output_term), "pts"
    )
    fine_projection_sum, fine_output_sum = lax.psum(sums[:2], "grp")
    pool_sum, projection_sum, output_sum = lax.all_gather(sums[2:], "grp", axis=0, tiled=False)
    projection_sum = projection_sum.reshape(2, wide, 3, wide // 2).transpose(1, 2, 0, 3)
    return (
        coarse_result,
        points_gradient,
        fine_projection_sum * scaling,
        fine_output_sum * scaling,
        pool_sum.reshape(wide, wide) * scaling,
        projection_sum.reshape(wide, 3 * wide) * scaling,
        output_sum.reshape(wide, wide) * scaling,
    )


def solution(mesh):
    tokens = P(("pts", "grp"), None)
    in_specs = (
        tokens,
        P(("pts", "grp")),
        P(("pts", "grp")),
        P(),
        P(),
        P(),
        P(),
        P(),
        P(),
        tokens,
    )
    out_specs = (tokens, tokens, P(), P(), P(), P(), P())
    return jax.shard_map(
        on_device, mesh=mesh, in_specs=in_specs, out_specs=out_specs, check_vma=False
    )
```

```python
import functools
import math

import jax
import jax.numpy as jnp
from jax import lax
from jax.experimental import pallas as pl
from jax.experimental.pallas import tpu as pltpu
from jax.sharding import PartitionSpec as P

HD = 64
BALL = 256
PAIR = 2 * HD
EPSILON = 1e-05
BF = jnp.bfloat16
F32 = jnp.float32


def mm(a, b, contract=(1, 0)):
    return lax.dot_general(
        a, b, (((contract[0],), (contract[1],)), ((), ())), preferred_element_type=F32
    )


def normalize(values):
    floats = values.astype(F32)
    center = floats - jnp.mean(floats, axis=-1, keepdims=True)
    inverse = lax.rsqrt(jnp.mean(center * center, axis=-1, keepdims=True) + EPSILON)
    return center * inverse, inverse


def norm_backward(incoming, normed, inverse):
    first_mean = jnp.mean(incoming, axis=-1, keepdims=True)
    second_mean = jnp.mean(incoming * normed, axis=-1, keepdims=True)
    return inverse * (incoming - first_mean - normed * second_mean)


def one_hot(slots, total):
    shape = (total, slots.shape[1])
    return (lax.broadcasted_iota(jnp.int32, shape, 0) == slots).astype(BF)


def head_half(shape, half):
    lanes = lax.broadcasted_iota(jnp.int32, shape, 1)
    return (lanes < HD) if half == 0 else (lanes >= HD)


def keep_half(rows, half):
    return jnp.where(head_half(rows.shape, half), rows, jnp.zeros_like(rows))


def softmax_rows(scores):
    raised = jnp.exp(scores - jnp.max(scores, axis=-1, keepdims=True))
    return (raised / jnp.sum(raised, axis=-1, keepdims=True)).astype(BF)


def slopes_of(weights, against):
    wide = weights.astype(F32)
    diagonal = jnp.sum(wide * against, axis=-1, keepdims=True)
    return (wide * (against - diagonal) * HD ** (-0.5)).astype(BF)


def column_of(row):
    count = row.shape[1]
    turned = jnp.broadcast_to(row.astype(F32), (128, count)).T
    return jnp.concatenate([turned] * (count // 128), axis=1)


def route_kernel(place, source, counts, points, send, send_slot, receive_slot, live):
    count = place.shape[1]
    shift = count.bit_length() - 1
    capacity = send.shape[0] * count // (counts.shape[1] * BALL)
    to_row = place[...] >> shift
    rows = lax.broadcasted_iota(jnp.int32, (count, count), 0)
    columns = lax.broadcasted_iota(jnp.int32, (count, count), 1)
    earlier = (column_of(to_row) == to_row.astype(F32)) & (rows < columns)
    rank = jnp.sum(jnp.where(earlier, 1.0, 0.0), axis=0, keepdims=True)
    slot = to_row * capacity + rank.astype(jnp.int32)
    send_slot[...] = slot
    source_row = source[...]
    from_row = source_row >> shift
    earlier = (column_of(from_row) == from_row.astype(F32)) & (
        column_of(source_row) < source_row.astype(F32)
    )
    rank = jnp.sum(jnp.where(earlier, 1.0, 0.0), axis=0, keepdims=True)
    receive_slot[...] = from_row * capacity + rank.astype(jnp.int32)
    balls = counts.shape[1]
    own_ball = one_hot(source_row >> (BALL.bit_length() - 1), balls)
    filled = mm(jnp.broadcast_to(counts[...].astype(F32), (8, balls)).astype(BF), own_ball)
    inside = (source_row & (BALL - 1)).astype(F32)
    live[...] = jnp.where(inside < filled[:1], 1.0, 0.0)
    send[...] = mm(one_hot(slot, send.shape[0]), points[...]).astype(BF)


def fine_forward_kernel(
    arrived, receive_slot, live, projection, output, send, rotated, projected, mixture, weights
):
    place = one_hot(receive_slot[...], arrived.shape[0])
    rows_in = mm(place, arrived[...], (0, 0))
    rotated[...] = rows_in.astype(BF)
    features = rows_in.shape[1]
    normed, _ = normalize(rows_in)
    projected[...] = mm(normed.astype(BF), projection[...]).astype(BF)
    balls = rows_in.shape[0] // BALL
    pairs = features // PAIR
    for ball in range(balls):
        rows = slice(ball * BALL, (ball + 1) * BALL)
        alive = live[:, rows] > 0.5
        for pair in range(pairs):
            lanes = slice(pair * PAIR, (pair + 1) * PAIR)
            query = projected[rows, lanes]
            key = projected[rows, features + pair * PAIR : features + (pair + 1) * PAIR]
            value = projected[rows, 2 * features + pair * PAIR : 2 * features + (pair + 1) * PAIR]
            halves = []
            for half in range(2):
                scores = mm(keep_half(query, half), key, (1, 1)) * HD ** (-0.5)
                head_weights = softmax_rows(jnp.where(alive, scores, -1e30))
                weights[(ball * pairs + pair) * 2 + half] = head_weights
                halves.append(mm(head_weights, value))
            mixed = jnp.where(head_half(halves[0].shape, 0), halves[0], halves[1])
            mixture[rows, lanes] = mixed.astype(BF)
    result = (rows_in + mm(mixture[...], output[...])).astype(BF)
    send[...] = mm(place, result).astype(BF)


def join_kernel(arrived, slots, joined):
    half = joined.shape[1] // 2
    for side in range(2):
        place = one_hot(slots[side : side + 1, :], arrived.shape[0])
        joined[:, side * half : (side + 1) * half] = mm(place, arrived[...], (0, 0)).astype(BF)


def coarse_kernel(
    group,
    own_joined,
    other_joined,
    own_cotangent,
    other_cotangent,
    pool,
    projection,
    output,
    coarse,
    unit,
    keep,
    give,
):
    half_rows, wide = own_joined.shape
    part = wide // 2
    first = pl.multiple_of(group[0] * part, part)
    joined = jnp.concatenate([own_joined[...], other_joined[...]], axis=0)
    cotangent = jnp.concatenate([own_cotangent[...], other_cotangent[...]], axis=0)
    tokens = mm(joined, pool[...]).astype(BF)
    coarse[...] = tokens[:half_rows]
    normed, _ = normalize(tokens)
    unit_rows = normed.astype(BF)
    unit[...] = unit_rows
    queries = mm(unit_rows, projection[:, pl.ds(first, part)]).astype(BF)
    keys = mm(unit_rows, projection[:, pl.ds(wide + first, part)]).astype(BF)
    values = mm(unit_rows, projection[:, pl.ds(2 * wide + first, part)]).astype(BF)
    incoming = mm(cotangent, output[pl.ds(first, part), :], (1, 1)).astype(BF)
    for pair in range(part // PAIR):
        lanes = slice(pair * PAIR, (pair + 1) * PAIR)
        query, key, value = queries[:, lanes], keys[:, lanes], values[:, lanes]
        entering = incoming[:, lanes]
        parts = ([], [], [], [])
        for half in range(2):
            scores = mm(keep_half(query, half), key, (1, 1)) * HD ** (-0.5)
            head_weights = softmax_rows(scores)
            parts[0].append(mm(head_weights, value))
            against = mm(keep_half(entering, half), value, (1, 1))
            slopes = slopes_of(head_weights, against)
            parts[1].append(mm(slopes, key))
            parts[2].append(mm(slopes, query, (0, 0)))
            parts[3].append(mm(head_weights, entering, (0, 0)))
        for at, (low, high) in enumerate(parts):
            both = jnp.where(head_half(low.shape, 0), low, high).astype(BF)
            target = slice(at * part + pair * PAIR, at * part + (pair + 1) * PAIR)
            keep[:, target] = both[:half_rows]
            give[:, target] = both[half_rows:]


def coarse_finish_kernel(
    group,
    coarse,
    keep,
    got,
    cotangent,
    pool,
    projection,
    output,
    slots,
    result,
    gradient,
    send,
):
    half_rows, wide = coarse.shape
    part = wide // 2
    mixed = coarse[...].astype(F32)
    back = jnp.zeros((half_rows, wide), F32)
    for source, index in ((keep, group[0]), (got, 1 - group[0])):
        first = pl.multiple_of(index * part, part)
        mixed = mixed + mm(source[:, :part], output[pl.ds(first, part), :])
        for at in range(3):
            back = back + mm(
                source[:, (at + 1) * part : (at + 2) * part],
                projection[:, pl.ds(at * wide + first, part)],
                (1, 1),
            )
    result[...] = mixed.astype(BF)
    normed, inverse = normalize(coarse[...])
    gradient_rows = (
        cotangent[...].astype(F32) + norm_backward(back, normed, inverse)
    ).astype(BF)
    gradient[...] = gradient_rows
    fine = mm(gradient_rows, pool[...], (1, 1)).astype(BF)
    features = send.shape[1]
    total = mm(one_hot(slots[0:1, :], send.shape[0]), fine[:, :features])
    total = total + mm(one_hot(slots[1:2, :], send.shape[0]), fine[:, features:])
    send[...] = total.astype(BF)


def coarse_weights_kernel(
    group,
    unit,
    keep,
    give,
    own_cotangent,
    other_cotangent,
    own_joined,
    other_joined,
    own_gradient,
    other_gradient,
    terms,
):
    part = keep.shape[1] // 4
    first = pl.multiple_of(group[0] * part, part)
    stacked = jnp.concatenate([keep[...], give[...]], axis=0)
    cotangent = jnp.concatenate([own_cotangent[...], other_cotangent[...]], axis=0)
    terms[:, : 3 * part] = mm(unit[...], stacked[:, part:], (0, 0)).astype(BF)
    output_term = mm(stacked[:, :part], cotangent, (0, 0)).astype(BF)
    pool_term = mm(own_joined[:, pl.ds(first, part)], own_gradient[...], (0, 0)) + mm(
        other_joined[:, pl.ds(first, part)], other_gradient[...], (0, 0)
    )
    pool_term = pool_term.astype(BF)
    for side in range(2):
        rows, columns = slice(side * part, (side + 1) * part), slice(side * part, (side + 1) * part)
        terms[rows, 3 * part : 4 * part] = output_term[:, columns]
        terms[rows, 4 * part :] = pool_term[:, columns]


def sum_kernel(arrived, spread):
    total = jnp.sum(arrived[...].astype(F32), axis=0, keepdims=True).astype(BF)
    spread[...] = jnp.broadcast_to(total, spread.shape)


def coarse_sums_kernel(group, own, other, pool, projection, output, *, scaling):
    wide = pool.shape[1]
    part = wide // 2
    for terms, index in ((own, group[0]), (other, 1 - group[0])):
        first = pl.multiple_of(index * part, part)
        for at in range(3):
            projection[:, pl.ds(at * wide + first, part)] = (
                terms[:, at * part : (at + 1) * part].astype(F32) * scaling
            )
        for side in range(2):
            rows, columns = slice(side * part, (side + 1) * part), slice(side * part, (side + 1) * part)
            output[pl.ds(first, part), columns] = (
                terms[rows, 3 * part : 4 * part].astype(F32) * scaling
            )
            pool[pl.ds(first, part), columns] = terms[rows, 4 * part :].astype(F32) * scaling


def fine_sums_kernel(terms, projection, output, *, scaling):
    features = output.shape[0]
    for at in range(3):
        projection[:, at * features : (at + 1) * features] = (
            terms[at * features : (at + 1) * features, :].astype(F32) * scaling
        )
    output[...] = terms[3 * features :, :].astype(F32) * scaling


def fine_backward_kernel(
    arrived,
    receive_slot,
    rotated,
    projected,
    mixture,
    weights,
    projection,
    output,
    send,
    terms,
    grad_projected,
):
    place = one_hot(receive_slot[...], arrived.shape[0])
    gradient_in = mm(place, arrived[...], (0, 0))
    gradient_rows = gradient_in.astype(BF)
    features = rotated.shape[1]
    entering = mm(gradient_rows, output[...], (1, 1)).astype(BF)
    terms[3 * features :, :] = mm(mixture[...], gradient_rows, (0, 0)).astype(BF)
    balls = rotated.shape[0] // BALL
    pairs = features // PAIR
    for ball in range(balls):
        rows = slice(ball * BALL, (ball + 1) * BALL)
        for pair in range(pairs):
            lanes = slice(pair * PAIR, (pair + 1) * PAIR)
            query = projected[rows, lanes]
            key = projected[rows, features + pair * PAIR : features + (pair + 1) * PAIR]
            value = projected[rows, 2 * features + pair * PAIR : 2 * features + (pair + 1) * PAIR]
            enters = entering[rows, lanes]
            parts = ([], [], [])
            for half in range(2):
                head_weights = weights[(ball * pairs + pair) * 2 + half]
                against = mm(keep_half(enters, half), value, (1, 1))
                slopes = slopes_of(head_weights, against)
                parts[0].append(mm(slopes, key))
                parts[1].append(mm(slopes, query, (0, 0)))
                parts[2].append(mm(head_weights, enters, (0, 0)))
            for at, (low, high) in enumerate(parts):
                both = jnp.where(head_half(low.shape, 0), low, high).astype(BF)
                target = at * features + pair * PAIR
                grad_projected[rows, target : target + PAIR] = both
    normed, inverse = normalize(rotated[...])
    unit_rows = normed.astype(BF)
    for at in range(3):
        columns = slice(at * features, (at + 1) * features)
        terms[columns, :] = mm(unit_rows, grad_projected[:, columns], (0, 0)).astype(BF)
    back = mm(grad_projected[...], projection[...], (1, 1))
    result = (gradient_in + norm_backward(back, normed, inverse)).astype(BF)
    send[...] = mm(place, result).astype(BF)


def take_kernel(arrived, slots, rows_out):
    place = one_hot(slots[...], arrived.shape[0])
    rows_out[...] = mm(place, arrived[...], (0, 0)).astype(BF)


VMEM = pl.BlockSpec(memory_space=pltpu.VMEM)
SMEM = pl.BlockSpec(memory_space=pltpu.SMEM)


def call(kernel, inputs, outputs, scalar=False, scratch=()):
    in_specs = [VMEM] * len(inputs)
    if scalar:
        in_specs[0] = SMEM
    shapes = [jax.ShapeDtypeStruct(shape, dtype) for shape, dtype in outputs]
    return pl.pallas_call(
        kernel,
        out_shape=shapes,
        in_specs=in_specs,
        out_specs=[VMEM] * len(shapes),
        scratch_shapes=list(scratch),
        compiler_params=pltpu.CompilerParams(vmem_limit_bytes=56 * 1024 * 1024),
    )(*inputs)


def exchange(values):
    return lax.ppermute(values, "grp", [(0, 1), (1, 0)])


def spread_blocks(values, axes):
    return lax.all_to_all(values, axes, split_axis=0, concat_axis=0, tiled=True)


def route(values, devices):
    rows, features = values.shape
    blocks = values.reshape(devices, rows // devices, features)
    return spread_blocks(blocks, ("pts", "grp")).reshape(rows, features)


def sum_over(terms, axes):
    rows, columns = terms.shape
    owners = lax.axis_size(axes)
    blocks = (owners, rows // owners, columns)
    arrived = spread_blocks(terms.reshape(blocks), axes)
    (spread,) = call(sum_kernel, (arrived,), ((blocks, BF),))
    return spread_blocks(spread, axes).reshape(rows, columns)


def on_device(
    points,
    rotated_place,
    rotated_source,
    ball_counts,
    fine_projection,
    fine_output,
    pool_weight,
    coarse_projection,
    coarse_output,
    coarse_cotangent,
):
    count, features = points.shape
    devices = lax.axis_size(("pts", "grp"))
    slots = 2 * count
    scaling = 1.0 / math.sqrt(count * devices)
    group = lax.axis_index("grp").astype(jnp.int32).reshape(1)
    wide = 2 * features
    half_rows = count // 2

    send, send_slot, receive_slot, live = call(
        route_kernel,
        (
            rotated_place.reshape(1, count),
            rotated_source.reshape(1, count),
            ball_counts.reshape(1, -1),
            points,
        ),
        (
            ((slots, features), BF),
            ((1, count), jnp.int32),
            ((1, count), jnp.int32),
            ((1, count), F32),
        ),
    )
    other_cotangent = exchange(coarse_cotangent)
    arrived = route(send, devices)
    pair_slots = send_slot.reshape(half_rows, 2).T
    heads = features // HD * (count // BALL)
    send, rotated, projected, mixture, weights = call(
        fine_forward_kernel,
        (arrived, receive_slot, live, fine_projection, fine_output),
        (
            ((slots, features), BF),
            ((count, features), BF),
            ((count, 3 * features), BF),
            ((count, features), BF),
            ((heads, BALL, BALL), BF),
        ),
    )
    arrived = route(send, devices)
    (own_joined,) = call(join_kernel, (arrived, pair_slots), (((half_rows, wide), BF),))
    other_joined = exchange(own_joined)
    coarse, unit, keep, give = call(
        coarse_kernel,
        (
            group,
            own_joined,
            other_joined,
            coarse_cotangent,
            other_cotangent,
            pool_weight,
            coarse_projection,
            coarse_output,
        ),
        (
            ((half_rows, wide), BF),
            ((count, wide), BF),
            ((half_rows, 2 * wide), BF),
            ((half_rows, 2 * wide), BF),
        ),
        scalar=True,
    )
    got = exchange(give)
    coarse_result, coarse_gradient, send = call(
        coarse_finish_kernel,
        (
            group,
            coarse,
            keep,
            got,
            coarse_cotangent,
            pool_weight,
            coarse_projection,
            coarse_output,
            pair_slots,
        ),
        (((half_rows, wide), BF), ((half_rows, wide), BF), ((slots, features), BF)),
        scalar=True,
    )
    arrived = route(send, devices)
    other_gradient = exchange(coarse_gradient)
    (coarse_terms,) = call(
        coarse_weights_kernel,
        (
            group,
            unit,
            keep,
            give,
            coarse_cotangent,
            other_cotangent,
            own_joined,
            other_joined,
            coarse_gradient,
            other_gradient,
        ),
        (((wide, 5 * wide // 2), BF),),
        scalar=True,
    )
    own_sums = sum_over(coarse_terms, "pts")
    other_sums = exchange(own_sums)
    send, fine_terms = call(
        fine_backward_kernel,
        (
            arrived,
            receive_slot,
            rotated,
            projected,
            mixture,
            weights,
            fine_projection,
            fine_output,
        ),
        (((slots, features), BF), ((4 * features, features), BF)),
        scratch=(pltpu.VMEM((count, 3 * features), BF),),
    )
    fine_sums = sum_over(fine_terms, ("pts", "grp"))
    arrived = route(send, devices)
    (points_gradient,) = call(take_kernel, (arrived, send_slot), (((count, features), BF),))
    pool_sum, projection_sum, output_sum = call(
        functools.partial(coarse_sums_kernel, scaling=scaling),
        (group, own_sums, other_sums),
        (((wide, wide), F32), ((wide, 3 * wide), F32), ((wide, wide), F32)),
        scalar=True,
    )
    fine_projection_sum, fine_output_sum = call(
        functools.partial(fine_sums_kernel, scaling=scaling),
        (fine_sums,),
        (((features, 3 * features), F32), ((features, features), F32)),
    )
    return (
        coarse_result,
        points_gradient,
        fine_projection_sum,
        fine_output_sum,
        pool_sum,
        projection_sum,
        output_sum,
    )


def solution(mesh):
    tokens = P(("pts", "grp"), None)
    in_specs = (
        tokens,
        P(("pts", "grp")),
        P(("pts", "grp")),
        P(),
        P(),
        P(),
        P(),
        P(),
        P(),
        tokens,
    )
    out_specs = (tokens, tokens, P(), P(), P(), P(), P())
    return jax.shard_map(
        on_device, mesh=mesh, in_specs=in_specs, out_specs=out_specs, check_vma=False
    )
```

```python
import functools
import math

import jax
import jax.numpy as jnp
from jax import lax
from jax.experimental import pallas as pl
from jax.experimental.pallas import tpu as pltpu
from jax.sharding import PartitionSpec as P

HD = 64
BALL = 256
PAIR = 2 * HD
EPSILON = 1e-05
BF = jnp.bfloat16
F32 = jnp.float32


def mm(a, b, contract=(1, 0)):
    return lax.dot_general(
        a, b, (((contract[0],), (contract[1],)), ((), ())), preferred_element_type=F32
    )


def normalize(values):
    floats = values.astype(F32)
    center = floats - jnp.mean(floats, axis=-1, keepdims=True)
    inverse = lax.rsqrt(jnp.mean(center * center, axis=-1, keepdims=True) + EPSILON)
    return center * inverse, inverse


def norm_backward(incoming, normed, inverse):
    first_mean = jnp.mean(incoming, axis=-1, keepdims=True)
    second_mean = jnp.mean(incoming * normed, axis=-1, keepdims=True)
    return inverse * (incoming - first_mean - normed * second_mean)


def one_hot(slots, total):
    shape = (total, slots.shape[1])
    return (lax.broadcasted_iota(jnp.int32, shape, 0) == slots).astype(BF)


def head_half(shape, half):
    lanes = lax.broadcasted_iota(jnp.int32, shape, 1)
    return (lanes < HD) if half == 0 else (lanes >= HD)


def keep_half(rows, half):
    return jnp.where(head_half(rows.shape, half), rows, jnp.zeros_like(rows))


def softmax_rows(scores):
    raised = jnp.exp(scores - jnp.max(scores, axis=-1, keepdims=True))
    return (raised / jnp.sum(raised, axis=-1, keepdims=True)).astype(BF)


def slopes_of(weights, against):
    wide = weights.astype(F32)
    diagonal = jnp.sum(wide * against, axis=-1, keepdims=True)
    return (wide * (against - diagonal) * HD ** (-0.5)).astype(BF)


def column_of(row):
    count = row.shape[1]
    turned = jnp.broadcast_to(row.astype(F32), (128, count)).T
    return jnp.concatenate([turned] * (count // 128), axis=1)


def route_kernel(place, source, counts, points, send, send_slot, receive_slot, live):
    count = place.shape[1]
    shift = count.bit_length() - 1
    capacity = send.shape[0] * count // (counts.shape[1] * BALL)
    to_row = place[...] >> shift
    rows = lax.broadcasted_iota(jnp.int32, (count, count), 0)
    columns = lax.broadcasted_iota(jnp.int32, (count, count), 1)
    earlier = (column_of(to_row) == to_row.astype(F32)) & (rows < columns)
    rank = jnp.sum(jnp.where(earlier, 1.0, 0.0), axis=0, keepdims=True)
    slot = to_row * capacity + rank.astype(jnp.int32)
    send_slot[...] = slot
    source_row = source[...]
    from_row = source_row >> shift
    earlier = (column_of(from_row) == from_row.astype(F32)) & (
        column_of(source_row) < source_row.astype(F32)
    )
    rank = jnp.sum(jnp.where(earlier, 1.0, 0.0), axis=0, keepdims=True)
    receive_slot[...] = from_row * capacity + rank.astype(jnp.int32)
    balls = counts.shape[1]
    own_ball = one_hot(source_row >> (BALL.bit_length() - 1), balls)
    filled = mm(jnp.broadcast_to(counts[...].astype(F32), (8, balls)).astype(BF), own_ball)
    inside = (source_row & (BALL - 1)).astype(F32)
    live[...] = jnp.where(inside < filled[:1], 1.0, 0.0)
    send[...] = mm(one_hot(slot, send.shape[0]), points[...]).astype(BF)


def fine_forward_kernel(
    arrived, receive_slot, live, projection, output, send, rotated, projected, mixture, weights
):
    place = one_hot(receive_slot[...], arrived.shape[0])
    rows_in = mm(place, arrived[...], (0, 0))
    rotated[...] = rows_in.astype(BF)
    features = rows_in.shape[1]
    normed, _ = normalize(rows_in)
    projected[...] = mm(normed.astype(BF), projection[...]).astype(BF)
    balls = rows_in.shape[0] // BALL
    pairs = features // PAIR
    for ball in range(balls):
        rows = slice(ball * BALL, (ball + 1) * BALL)
        alive = live[:, rows] > 0.5
        for pair in range(pairs):
            lanes = slice(pair * PAIR, (pair + 1) * PAIR)
            query = projected[rows, lanes]
            key = projected[rows, features + pair * PAIR : features + (pair + 1) * PAIR]
            value = projected[rows, 2 * features + pair * PAIR : 2 * features + (pair + 1) * PAIR]
            halves = []
            for half in range(2):
                scores = mm(keep_half(query, half), key, (1, 1)) * HD ** (-0.5)
                head_weights = softmax_rows(jnp.where(alive, scores, -1e30))
                weights[(ball * pairs + pair) * 2 + half] = head_weights
                halves.append(mm(head_weights, value))
            mixed = jnp.where(head_half(halves[0].shape, 0), halves[0], halves[1])
            mixture[rows, lanes] = mixed.astype(BF)
    result = (rows_in + mm(mixture[...], output[...])).astype(BF)
    send[...] = mm(place, result).astype(BF)


def join_kernel(arrived, slots, joined):
    half = joined.shape[1] // 2
    for side in range(2):
        place = one_hot(slots[side : side + 1, :], arrived.shape[0])
        joined[:, side * half : (side + 1) * half] = mm(place, arrived[...], (0, 0)).astype(BF)


def coarse_kernel(
    group,
    own_joined,
    other_joined,
    own_cotangent,
    other_cotangent,
    pool,
    projection,
    output,
    coarse,
    unit,
    keep,
    give,
):
    half_rows, wide = own_joined.shape
    part = wide // 2
    first = pl.multiple_of(group[0] * part, part)
    joined = jnp.concatenate([own_joined[...], other_joined[...]], axis=0)
    cotangent = jnp.concatenate([own_cotangent[...], other_cotangent[...]], axis=0)
    tokens = mm(joined, pool[...]).astype(BF)
    coarse[...] = tokens[:half_rows]
    normed, _ = normalize(tokens)
    unit_rows = normed.astype(BF)
    unit[...] = unit_rows
    queries = mm(unit_rows, projection[:, pl.ds(first, part)]).astype(BF)
    keys = mm(unit_rows, projection[:, pl.ds(wide + first, part)]).astype(BF)
    values = mm(unit_rows, projection[:, pl.ds(2 * wide + first, part)]).astype(BF)
    incoming = mm(cotangent, output[pl.ds(first, part), :], (1, 1)).astype(BF)
    for pair in range(part // PAIR):
        lanes = slice(pair * PAIR, (pair + 1) * PAIR)
        query, key, value = queries[:, lanes], keys[:, lanes], values[:, lanes]
        entering = incoming[:, lanes]
        parts = ([], [], [], [])
        for half in range(2):
            scores = mm(keep_half(query, half), key, (1, 1)) * HD ** (-0.5)
            head_weights = softmax_rows(scores)
            parts[0].append(mm(head_weights, value))
            against = mm(keep_half(entering, half), value, (1, 1))
            slopes = slopes_of(head_weights, against)
            parts[1].append(mm(slopes, key))
            parts[2].append(mm(slopes, query, (0, 0)))
            parts[3].append(mm(head_weights, entering, (0, 0)))
        for at, (low, high) in enumerate(parts):
            both = jnp.where(head_half(low.shape, 0), low, high).astype(BF)
            target = slice(at * part + pair * PAIR, at * part + (pair + 1) * PAIR)
            keep[:, target] = both[:half_rows]
            give[:, target] = both[half_rows:]


def coarse_finish_kernel(
    group,
    coarse,
    keep,
    got,
    cotangent,
    pool,
    projection,
    output,
    slots,
    result,
    gradient,
    send,
):
    half_rows, wide = coarse.shape
    part = wide // 2
    mixed = coarse[...].astype(F32)
    back = jnp.zeros((half_rows, wide), F32)
    for source, index in ((keep, group[0]), (got, 1 - group[0])):
        first = pl.multiple_of(index * part, part)
        mixed = mixed + mm(source[:, :part], output[pl.ds(first, part), :])
        for at in range(3):
            back = back + mm(
                source[:, (at + 1) * part : (at + 2) * part],
                projection[:, pl.ds(at * wide + first, part)],
                (1, 1),
            )
    result[...] = mixed.astype(BF)
    normed, inverse = normalize(coarse[...])
    gradient_rows = (
        cotangent[...].astype(F32) + norm_backward(back, normed, inverse)
    ).astype(BF)
    gradient[...] = gradient_rows
    fine = mm(gradient_rows, pool[...], (1, 1)).astype(BF)
    features = send.shape[1]
    total = mm(one_hot(slots[0:1, :], send.shape[0]), fine[:, :features])
    total = total + mm(one_hot(slots[1:2, :], send.shape[0]), fine[:, features:])
    send[...] = total.astype(BF)


def coarse_weights_kernel(
    group,
    unit,
    keep,
    give,
    own_cotangent,
    other_cotangent,
    own_joined,
    other_joined,
    own_gradient,
    other_gradient,
    terms,
):
    part = keep.shape[1] // 4
    first = pl.multiple_of(group[0] * part, part)
    stacked = jnp.concatenate([keep[...], give[...]], axis=0)
    cotangent = jnp.concatenate([own_cotangent[...], other_cotangent[...]], axis=0)
    projection_term = mm(unit[...], stacked[:, part:], (0, 0))
    output_term = mm(stacked[:, :part], cotangent, (0, 0))
    pool_term = mm(own_joined[:, pl.ds(first, part)], own_gradient[...], (0, 0)) + mm(
        other_joined[:, pl.ds(first, part)], other_gradient[...], (0, 0)
    )
    across = projection_term.shape[1] // 2
    for side in range(2):
        columns = projection_term[:, side * across : (side + 1) * across]
        put_blocks(terms, side, 0, columns)
        for at, term in enumerate((output_term, pool_term)):
            width = term.shape[1] // 4
            stack = [term[:, (2 * side + k) * width : (2 * side + k + 1) * width] for k in range(2)]
            put_blocks(terms, side, across + at * width, jnp.concatenate(stack, axis=0))


def put_blocks(blocks, side, lane, rows):
    owners, width = blocks.shape[0], rows.shape[1]
    pieces = rows.reshape(owners, rows.shape[0] // owners, width)
    blocks[:, side, :, lane : lane + width] = pieces.astype(BF)


def sum_kernel(arrived, spread, *, tokens, fine):
    fine_part = jnp.sum(arrived[:, :, :, tokens : tokens + fine].astype(F32), axis=0)
    coarse_part = jnp.sum(arrived[:, :, :, tokens + fine :].astype(F32), axis=0)
    total = [fine_part[0] + fine_part[1], coarse_part[0], coarse_part[1]]
    total = jnp.concatenate(total, axis=1).astype(BF)
    spread[...] = jnp.broadcast_to(total[None], spread.shape)


def sums_kernel(
    group, own, other, fine_projection, fine_output, pool, projection, output, *, scaling
):
    features = fine_output.shape[0]
    wide = pool.shape[0]
    part = wide // 2
    width = wide // 4
    across = 3 * part // 2

    def write(low, high):
        for side, terms in enumerate((low, high)):
            rows = terms.shape[0] * terms.shape[1]

            def lanes(start, count):
                values = terms[:, :, start : start + count].astype(F32) * scaling
                return values.reshape(rows, count)

            fine = lanes(0, features)
            for k in range(2):
                at = 2 * side + k
                block = fine[k * features : (k + 1) * features]
                if at < 3:
                    fine_projection[:, at * features : (at + 1) * features] = block
                else:
                    fine_output[...] = block
            for heads in range(2):
                start = features + heads * (across + 2 * width)
                place = heads * part
                for k in range(3):
                    column = side * across + k * width
                    at, inner = column // part, column % part
                    target = at * wide + place + inner
                    projection[:, target : target + width] = lanes(start + k * width, width)
                for at, ref in enumerate((output, pool)):
                    block = lanes(start + across + at * width, width)
                    for k in range(2):
                        column = (2 * side + k) * width
                        ref[place : place + part, column : column + width] = block[
                            k * part : (k + 1) * part
                        ]

    @pl.when(group[0] == 0)
    def _():
        write(own, other)

    @pl.when(group[0] != 0)
    def _():
        write(other, own)


def fine_backward_kernel(
    arrived,
    receive_slot,
    rotated,
    projected,
    mixture,
    weights,
    projection,
    output,
    coarse_terms,
    send,
    grad_projected,
):
    place = one_hot(receive_slot[...], arrived.shape[0])
    gradient_in = mm(place, arrived[...], (0, 0))
    gradient_rows = gradient_in.astype(BF)
    features = rotated.shape[1]
    entering = mm(gradient_rows, output[...], (1, 1)).astype(BF)
    terms = [mm(mixture[...], gradient_rows, (0, 0))]
    balls = rotated.shape[0] // BALL
    pairs = features // PAIR
    for ball in range(balls):
        rows = slice(ball * BALL, (ball + 1) * BALL)
        for pair in range(pairs):
            lanes = slice(pair * PAIR, (pair + 1) * PAIR)
            query = projected[rows, lanes]
            key = projected[rows, features + pair * PAIR : features + (pair + 1) * PAIR]
            value = projected[rows, 2 * features + pair * PAIR : 2 * features + (pair + 1) * PAIR]
            enters = entering[rows, lanes]
            parts = ([], [], [])
            for half in range(2):
                head_weights = weights[(ball * pairs + pair) * 2 + half]
                against = mm(keep_half(enters, half), value, (1, 1))
                slopes = slopes_of(head_weights, against)
                parts[0].append(mm(slopes, key))
                parts[1].append(mm(slopes, query, (0, 0)))
                parts[2].append(mm(head_weights, enters, (0, 0)))
            for at, (low, high) in enumerate(parts):
                both = jnp.where(head_half(low.shape, 0), low, high).astype(BF)
                target = at * features + pair * PAIR
                grad_projected[rows, target : target + PAIR] = both
    normed, inverse = normalize(rotated[...])
    unit_rows = normed.astype(BF)
    for at in range(3):
        columns = slice(at * features, (at + 1) * features)
        terms.insert(at, mm(unit_rows, grad_projected[:, columns], (0, 0)))
    back = mm(grad_projected[...], projection[...], (1, 1))
    result = (gradient_in + norm_backward(back, normed, inverse)).astype(BF)
    tokens = mm(place, result)
    send[:, :, :, :features] = tokens.reshape(send.shape[:3] + (features,)).astype(BF)
    for side in range(2):
        put_blocks(send, side, features, jnp.concatenate(terms[2 * side : 2 * side + 2], axis=0))
    send[:, :, :, 2 * features :] = coarse_terms[...]


def take_kernel(arrived, slots, rows_out):
    place = one_hot(slots[...], slots.shape[1] * 2)
    rows = arrived[...].reshape(place.shape[0], arrived.shape[-1])
    rows_out[...] = mm(place, rows, (0, 0)).astype(BF)


VMEM = pl.BlockSpec(memory_space=pltpu.VMEM)
SMEM = pl.BlockSpec(memory_space=pltpu.SMEM)


def call(kernel, inputs, outputs, scalar=False, scratch=()):
    in_specs = [VMEM] * len(inputs)
    if scalar:
        in_specs[0] = SMEM
    shapes = [jax.ShapeDtypeStruct(shape, dtype) for shape, dtype in outputs]
    return pl.pallas_call(
        kernel,
        out_shape=shapes,
        in_specs=in_specs,
        out_specs=[VMEM] * len(shapes),
        scratch_shapes=list(scratch),
        compiler_params=pltpu.CompilerParams(vmem_limit_bytes=16 * 1024 * 1024),
    )(*inputs)


def exchange(values):
    return lax.ppermute(values, "grp", [(0, 1), (1, 0)])


def spread_blocks(values, axes):
    return lax.all_to_all(values, axes, split_axis=0, concat_axis=0, tiled=True)


def route(values, devices):
    rows, features = values.shape
    blocks = values.reshape(devices, rows // devices, features)
    return spread_blocks(blocks, ("pts", "grp")).reshape(rows, features)


def on_device(
    points,
    rotated_place,
    rotated_source,
    ball_counts,
    fine_projection,
    fine_output,
    pool_weight,
    coarse_projection,
    coarse_output,
    coarse_cotangent,
):
    count, features = points.shape
    devices = lax.axis_size(("pts", "grp"))
    slots = 2 * count
    scaling = 1.0 / math.sqrt(count * devices)
    group = lax.axis_index("grp").astype(jnp.int32).reshape(1)
    wide = 2 * features
    half_rows = count // 2

    send, send_slot, receive_slot, live = call(
        route_kernel,
        (
            rotated_place.reshape(1, count),
            rotated_source.reshape(1, count),
            ball_counts.reshape(1, -1),
            points,
        ),
        (
            ((slots, features), BF),
            ((1, count), jnp.int32),
            ((1, count), jnp.int32),
            ((1, count), F32),
        ),
    )
    other_cotangent = exchange(coarse_cotangent)
    arrived = route(send, devices)
    pair_slots = send_slot.reshape(half_rows, 2).T
    heads = features // HD * (count // BALL)
    send, rotated, projected, mixture, weights = call(
        fine_forward_kernel,
        (arrived, receive_slot, live, fine_projection, fine_output),
        (
            ((slots, features), BF),
            ((count, features), BF),
            ((count, 3 * features), BF),
            ((count, features), BF),
            ((heads, BALL, BALL), BF),
        ),
    )
    arrived = route(send, devices)
    (own_joined,) = call(join_kernel, (arrived, pair_slots), (((half_rows, wide), BF),))
    other_joined = exchange(own_joined)
    coarse, unit, keep, give = call(
        coarse_kernel,
        (
            group,
            own_joined,
            other_joined,
            coarse_cotangent,
            other_cotangent,
            pool_weight,
            coarse_projection,
            coarse_output,
        ),
        (
            ((half_rows, wide), BF),
            ((count, wide), BF),
            ((half_rows, 2 * wide), BF),
            ((half_rows, 2 * wide), BF),
        ),
        scalar=True,
    )
    got = exchange(give)
    coarse_result, coarse_gradient, send = call(
        coarse_finish_kernel,
        (
            group,
            coarse,
            keep,
            got,
            coarse_cotangent,
            pool_weight,
            coarse_projection,
            coarse_output,
            pair_slots,
        ),
        (((half_rows, wide), BF), ((half_rows, wide), BF), ((slots, features), BF)),
        scalar=True,
    )
    arrived = route(send, devices)
    other_gradient = exchange(coarse_gradient)
    owners = lax.axis_size("pts")
    (coarse_terms,) = call(
        coarse_weights_kernel,
        (
            group,
            unit,
            keep,
            give,
            coarse_cotangent,
            other_cotangent,
            own_joined,
            other_joined,
            coarse_gradient,
            other_gradient,
        ),
        (((owners, 2, slots // devices, 5 * wide // 4), BF),),
        scalar=True,
    )
    across = 2 * features + 5 * wide // 4
    (send,) = call(
        fine_backward_kernel,
        (
            arrived,
            receive_slot,
            rotated,
            projected,
            mixture,
            weights,
            fine_projection,
            fine_output,
            coarse_terms,
        ),
        (((owners, 2, slots // devices, across), BF),),
        scratch=(pltpu.VMEM((count, 3 * features), BF),),
    )
    arrived = spread_blocks(send.reshape(devices, slots // devices, across), ("pts", "grp"))
    (spread,) = call(
        functools.partial(sum_kernel, tokens=features, fine=features),
        (arrived.reshape(send.shape),),
        (((owners, slots // devices, features + 5 * wide // 2), BF),),
    )
    own_sums = spread_blocks(spread, "pts")
    (points_gradient,) = call(
        take_kernel, (arrived[:, :, :features], send_slot), (((count, features), BF),)
    )
    other_sums = exchange(own_sums)
    sums = call(
        functools.partial(sums_kernel, scaling=scaling),
        (group, own_sums, other_sums),
        (
            ((features, 3 * features), F32),
            ((features, features), F32),
            ((wide, wide), F32),
            ((wide, 3 * wide), F32),
            ((wide, wide), F32),
        ),
        scalar=True,
    )
    return (coarse_result, points_gradient, *sums)


def solution(mesh):
    tokens = P(("pts", "grp"), None)
    in_specs = (
        tokens,
        P(("pts", "grp")),
        P(("pts", "grp")),
        P(),
        P(),
        P(),
        P(),
        P(),
        P(),
        tokens,
    )
    out_specs = (tokens, tokens, P(), P(), P(), P(), P())
    return jax.shard_map(
        on_device, mesh=mesh, in_specs=in_specs, out_specs=out_specs, check_vma=False
    )
```

```python
import functools
import math
from typing import NamedTuple

import jax
import jax.numpy as jnp
from jax import lax
from jax.experimental import pallas as pl
from jax.experimental.pallas import tpu as pltpu
from jax.sharding import PartitionSpec as P

HD = 64
BALL = 256
PAIR = 2 * HD
EPSILON = 1e-05
BF = jnp.bfloat16
F32 = jnp.float32


def mm(a, b, contract=(1, 0)):
    return lax.dot_general(
        a, b, (((contract[0],), (contract[1],)), ((), ())), preferred_element_type=F32
    )


def normalize(values):
    floats = values.astype(F32)
    center = floats - jnp.mean(floats, axis=-1, keepdims=True)
    inverse = lax.rsqrt(jnp.mean(center * center, axis=-1, keepdims=True) + EPSILON)
    return center * inverse, inverse


def norm_backward(incoming, normed, inverse):
    first_mean = jnp.mean(incoming, axis=-1, keepdims=True)
    second_mean = jnp.mean(incoming * normed, axis=-1, keepdims=True)
    return inverse * (incoming - first_mean - normed * second_mean)


def one_hot(slots, total):
    shape = (total, slots.shape[1])
    return (lax.broadcasted_iota(jnp.int32, shape, 0) == slots).astype(BF)


def head_half(shape, half):
    lanes = lax.broadcasted_iota(jnp.int32, shape, 1)
    return (lanes < HD) if half == 0 else (lanes >= HD)


def keep_half(rows, half):
    return jnp.where(head_half(rows.shape, half), rows, jnp.zeros_like(rows))


def softmax_rows(scores):
    raised = jnp.exp(scores - jnp.max(scores, axis=-1, keepdims=True))
    return (raised / jnp.sum(raised, axis=-1, keepdims=True)).astype(BF)


def slopes_of(weights, against):
    wide = weights.astype(F32)
    diagonal = jnp.sum(wide * against, axis=-1, keepdims=True)
    return (wide * (against - diagonal) * HD ** (-0.5)).astype(BF)


def column_of(row):
    count = row.shape[1]
    turned = jnp.broadcast_to(row.astype(F32), (128, count)).T
    return jnp.concatenate([turned] * (count // 128), axis=1)


def route_kernel(place, source, counts, points, send, send_slot, receive_slot, live):
    count = place.shape[1]
    shift = count.bit_length() - 1
    capacity = send.shape[0] * count // (counts.shape[1] * BALL)
    to_row = place[...] >> shift
    rows = lax.broadcasted_iota(jnp.int32, (count, count), 0)
    columns = lax.broadcasted_iota(jnp.int32, (count, count), 1)
    earlier = (column_of(to_row) == to_row.astype(F32)) & (rows < columns)
    rank = jnp.sum(jnp.where(earlier, 1.0, 0.0), axis=0, keepdims=True)
    slot = to_row * capacity + rank.astype(jnp.int32)
    send_slot[...] = slot
    source_row = source[...]
    from_row = source_row >> shift
    earlier = (column_of(from_row) == from_row.astype(F32)) & (
        column_of(source_row) < source_row.astype(F32)
    )
    rank = jnp.sum(jnp.where(earlier, 1.0, 0.0), axis=0, keepdims=True)
    receive_slot[...] = from_row * capacity + rank.astype(jnp.int32)
    balls = counts.shape[1]
    own_ball = one_hot(source_row >> (BALL.bit_length() - 1), balls)
    filled = mm(jnp.broadcast_to(counts[...].astype(F32), (8, balls)).astype(BF), own_ball)
    inside = (source_row & (BALL - 1)).astype(F32)
    live[...] = jnp.where(inside < filled[:1], 1.0, 0.0)
    send[...] = mm(one_hot(slot, send.shape[0]), points[...]).astype(BF)


def fine_forward_kernel(
    arrived, receive_slot, live, projection, output, send, rotated, projected, mixture, weights
):
    place = one_hot(receive_slot[...], arrived.shape[0])
    rows_in = mm(place, arrived[...], (0, 0))
    rotated[...] = rows_in.astype(BF)
    rotated.flush()
    features = rows_in.shape[1]
    normed, _ = normalize(rows_in)
    projected[...] = mm(normed.astype(BF), projection[...]).astype(BF)
    projected.flush()
    balls = rows_in.shape[0] // BALL
    pairs = features // PAIR
    for ball in range(balls):
        rows = slice(ball * BALL, (ball + 1) * BALL)
        alive = live[:, rows] > 0.5
        for pair in range(pairs):
            lanes = slice(pair * PAIR, (pair + 1) * PAIR)
            query = projected[rows, lanes]
            key = projected[rows, features + pair * PAIR : features + (pair + 1) * PAIR]
            value = projected[rows, 2 * features + pair * PAIR : 2 * features + (pair + 1) * PAIR]
            halves = []
            for half in range(2):
                scores = mm(keep_half(query, half), key, (1, 1)) * HD ** (-0.5)
                head_weights = softmax_rows(jnp.where(alive, scores, -1e30))
                weights[(ball * pairs + pair) * 2 + half] = head_weights
                halves.append(mm(head_weights, value))
            mixed = jnp.where(head_half(halves[0].shape, 0), halves[0], halves[1])
            mixture[rows, lanes] = mixed.astype(BF)
    weights.flush()
    mixture.flush()
    result = (rows_in + mm(mixture[...], output[...])).astype(BF)
    send[...] = mm(place, result).astype(BF)


def join_kernel(arrived, slots, joined):
    half = joined.shape[1] // 2
    for side in range(2):
        place = one_hot(slots[side : side + 1, :], arrived.shape[0])
        joined[:, side * half : (side + 1) * half] = mm(place, arrived[...], (0, 0)).astype(BF)


def coarse_kernel(
    group,
    own_joined,
    other_joined,
    own_cotangent,
    other_cotangent,
    pool,
    projection,
    output,
    coarse,
    keep,
    give,
    both_joined,
    unit,
    stacked,
):
    half_rows, wide = own_joined.shape
    part = wide // 2
    first = pl.multiple_of(group[0] * part, part)
    joined = jnp.concatenate([own_joined[...], other_joined[...]], axis=0)
    both_joined[...] = joined
    both_joined.flush()
    tokens = mm(joined, pool[...]).astype(BF)
    coarse[...] = tokens[:half_rows]
    normed, _ = normalize(tokens)
    unit_rows = normed.astype(BF)
    unit[...] = unit_rows
    unit.flush()
    queries = mm(unit_rows, projection[:, pl.ds(first, part)]).astype(BF)
    keys = mm(unit_rows, projection[:, pl.ds(wide + first, part)]).astype(BF)
    values = mm(unit_rows, projection[:, pl.ds(2 * wide + first, part)]).astype(BF)
    cotangent = jnp.concatenate([own_cotangent[...], other_cotangent[...]], axis=0)
    incoming = mm(cotangent, output[pl.ds(first, part), :], (1, 1)).astype(BF)
    for pair in range(part // PAIR):
        lanes = slice(pair * PAIR, (pair + 1) * PAIR)
        query, key, value = queries[:, lanes], keys[:, lanes], values[:, lanes]
        entering = incoming[:, lanes]
        parts = ([], [], [], [])
        for half in range(2):
            scores = mm(keep_half(query, half), key, (1, 1)) * HD ** (-0.5)
            head_weights = softmax_rows(scores)
            parts[0].append(mm(head_weights, value))
            against = mm(keep_half(entering, half), value, (1, 1))
            slopes = slopes_of(head_weights, against)
            parts[1].append(mm(slopes, key))
            parts[2].append(mm(slopes, query, (0, 0)))
            parts[3].append(mm(head_weights, entering, (0, 0)))
        for at, (low, high) in enumerate(parts):
            both = jnp.where(head_half(low.shape, 0), low, high).astype(BF)
            target = slice(at * part + pair * PAIR, at * part + (pair + 1) * PAIR)
            keep[:, target] = both[:half_rows]
            give[:, target] = both[half_rows:]
            stacked[:, target] = both


def coarse_finish_kernel(
    group,
    coarse,
    keep,
    got,
    cotangent,
    pool,
    projection,
    output,
    slots,
    result,
    gradient,
    send,
):
    half_rows, wide = coarse.shape
    part = wide // 2
    mixed = coarse[...].astype(F32)
    back = jnp.zeros((half_rows, wide), F32)
    for source, index in ((keep, group[0]), (got, 1 - group[0])):
        first = pl.multiple_of(index * part, part)
        mixed = mixed + mm(source[:, :part], output[pl.ds(first, part), :])
        for at in range(3):
            back = back + mm(
                source[:, (at + 1) * part : (at + 2) * part],
                projection[:, pl.ds(at * wide + first, part)],
                (1, 1),
            )
    result[...] = mixed.astype(BF)
    result.flush()
    normed, inverse = normalize(coarse[...])
    gradient_rows = (
        cotangent[...].astype(F32) + norm_backward(back, normed, inverse)
    ).astype(BF)
    gradient[...] = gradient_rows
    fine = mm(gradient_rows, pool[...], (1, 1)).astype(BF)
    features = send.shape[1]
    total = mm(one_hot(slots[0:1, :], send.shape[0]), fine[:, :features])
    total = total + mm(one_hot(slots[1:2, :], send.shape[0]), fine[:, features:])
    send[...] = total.astype(BF)


def coarse_weights_kernel(
    group,
    unit,
    stacked,
    own_cotangent,
    other_cotangent,
    joined,
    own_gradient,
    other_gradient,
    terms,
):
    part = stacked.shape[1] // 4
    first = pl.multiple_of(group[0] * part, part)
    projection_term = mm(unit[...], stacked[:, part:], (0, 0))
    cotangent = jnp.concatenate([own_cotangent[...], other_cotangent[...]], axis=0)
    output_term = mm(stacked[:, :part], cotangent, (0, 0))
    gradient = jnp.concatenate([own_gradient[...], other_gradient[...]], axis=0)
    pool_term = mm(joined[:, pl.ds(first, part)], gradient, (0, 0))
    across = projection_term.shape[1] // 2
    for side in range(2):
        columns = projection_term[:, side * across : (side + 1) * across]
        put_blocks(terms, side, 0, columns)
        for at, term in enumerate((output_term, pool_term)):
            width = term.shape[1] // 4
            stack = [term[:, (2 * side + k) * width : (2 * side + k + 1) * width] for k in range(2)]
            put_blocks(terms, side, across + at * width, jnp.concatenate(stack, axis=0))


def put_blocks(blocks, side, lane, rows):
    owners, width = blocks.shape[0], rows.shape[1]
    pieces = rows.reshape(owners, rows.shape[0] // owners, width)
    blocks[:, side, :, lane : lane + width] = pieces.astype(BF)


def sum_kernel(arrived, spread, *, tokens, fine):
    fine_part = jnp.sum(arrived[:, :, :, tokens : tokens + fine].astype(F32), axis=0)
    coarse_part = jnp.sum(arrived[:, :, :, tokens + fine :].astype(F32), axis=0)
    total = [fine_part[0] + fine_part[1], coarse_part[0], coarse_part[1]]
    total = jnp.concatenate(total, axis=1).astype(BF)
    spread[...] = jnp.broadcast_to(total[None], spread.shape)


def sums_kernel(
    group, own, other, fine_projection, fine_output, pool, projection, output, *, scaling
):
    features = fine_output.shape[0]
    wide = pool.shape[0]
    part = wide // 2
    width = wide // 4
    across = 3 * part // 2

    owns_low = group[0] == 0

    def lanes(side, start, count):
        here, there = own[:, :, start : start + count], other[:, :, start : start + count]
        low = owns_low if side == 0 else jnp.logical_not(owns_low)
        values = jnp.where(low, here, there).astype(F32) * scaling
        return values.reshape(own.shape[0] * own.shape[1], count)

    def start_of(heads):
        return features + heads * (across + 2 * width)

    for side in range(2):
        for heads in range(2):
            for k in range(3):
                column = side * across + k * width
                at, inner = column // part, column % part
                target = at * wide + heads * part + inner
                projection[:, target : target + width] = lanes(
                    side, start_of(heads) + k * width, width
                )
    projection.flush()
    for at, ref in enumerate((output, pool)):
        for side in range(2):
            for heads in range(2):
                block = lanes(side, start_of(heads) + across + at * width, width)
                for k in range(2):
                    column = (2 * side + k) * width
                    ref[heads * part : (heads + 1) * part, column : column + width] = block[
                        k * part : (k + 1) * part
                    ]
        ref.flush()
    for side in range(2):
        fine = lanes(side, 0, features)
        for k in range(2):
            at = 2 * side + k
            block = fine[k * features : (k + 1) * features]
            if at < 3:
                fine_projection[:, at * features : (at + 1) * features] = block
            else:
                fine_output[...] = block


def fine_backward_kernel(
    arrived,
    receive_slot,
    rotated,
    projected,
    mixture,
    weights,
    projection,
    output,
    coarse_terms,
    send,
    grad_projected,
    arriving,
):
    filling = pltpu.make_async_copy(
        coarse_terms, send.at[:, :, :, 2 * rotated.shape[1] :], arriving
    )
    filling.start()
    place = one_hot(receive_slot[...], arrived.shape[0])
    gradient_in = mm(place, arrived[...], (0, 0))
    gradient_rows = gradient_in.astype(BF)
    features = rotated.shape[1]
    entering = mm(gradient_rows, output[...], (1, 1)).astype(BF)
    terms = [mm(mixture[...], gradient_rows, (0, 0))]
    balls = rotated.shape[0] // BALL
    pairs = features // PAIR
    for ball in range(balls):
        rows = slice(ball * BALL, (ball + 1) * BALL)
        for pair in range(pairs):
            lanes = slice(pair * PAIR, (pair + 1) * PAIR)
            query = projected[rows, lanes]
            key = projected[rows, features + pair * PAIR : features + (pair + 1) * PAIR]
            value = projected[rows, 2 * features + pair * PAIR : 2 * features + (pair + 1) * PAIR]
            enters = entering[rows, lanes]
            parts = ([], [], [])
            for half in range(2):
                head_weights = weights[(ball * pairs + pair) * 2 + half]
                against = mm(keep_half(enters, half), value, (1, 1))
                slopes = slopes_of(head_weights, against)
                parts[0].append(mm(slopes, key))
                parts[1].append(mm(slopes, query, (0, 0)))
                parts[2].append(mm(head_weights, enters, (0, 0)))
            for at, (low, high) in enumerate(parts):
                both = jnp.where(head_half(low.shape, 0), low, high).astype(BF)
                target = at * features + pair * PAIR
                grad_projected[rows, target : target + PAIR] = both
    normed, inverse = normalize(rotated[...])
    unit_rows = normed.astype(BF)
    for at in range(3):
        columns = slice(at * features, (at + 1) * features)
        terms.insert(at, mm(unit_rows, grad_projected[:, columns], (0, 0)))
    back = mm(grad_projected[...], projection[...], (1, 1))
    result = (gradient_in + norm_backward(back, normed, inverse)).astype(BF)
    tokens = mm(place, result)
    send[:, :, :, :features] = tokens.reshape(send.shape[:3] + (features,)).astype(BF)
    for side in range(2):
        put_blocks(send, side, features, jnp.concatenate(terms[2 * side : 2 * side + 2], axis=0))
    filling.wait()


def take_kernel(arrived, slots, rows_out):
    place = one_hot(slots[...], slots.shape[1] * 2)
    rows = arrived[...].reshape(place.shape[0], arrived.shape[-1])
    rows_out[...] = mm(place, rows, (0, 0)).astype(BF)


VMEM = pl.BlockSpec(memory_space=pltpu.VMEM)
SMEM = pl.BlockSpec(memory_space=pltpu.SMEM)
HBM = pl.BlockSpec(memory_space=pltpu.HBM)


class Far(NamedTuple):
    value: jax.Array


class Direct(NamedTuple):
    value: jax.Array


class Near(NamedTuple):
    shape: tuple
    dtype: jnp.dtype = BF
    far: bool = False


class Fetched:
    def __init__(self, source, buffer, semaphore):
        self.buffer, self.shape, self.waited = buffer, buffer.shape, False
        self.copy = pltpu.make_async_copy(source, buffer, semaphore)
        self.copy.start()

    def wait(self):
        if not self.waited:
            self.copy.wait()
            self.waited = True

    def __getitem__(self, index):
        self.wait()
        return self.buffer[index]


class Stored:
    def __init__(self, target, buffer, semaphore):
        self.buffer, self.shape, self.dtype, self.started = buffer, buffer.shape, buffer.dtype, False
        self.copy = pltpu.make_async_copy(buffer, target, semaphore)

    def __setitem__(self, index, values):
        self.buffer[index] = values

    def __getitem__(self, index):
        return self.buffer[index]

    def flush(self):
        if not self.started:
            self.copy.start()
            self.started = True


def call(kernel, inputs, outputs, scalar=False, scratch=()):
    in_specs, arrays, buffers = [], [], []
    for at, value in enumerate(inputs):
        far, direct = isinstance(value, Far), isinstance(value, Direct)
        in_specs.append(SMEM if scalar and at == 0 else HBM if far or direct else VMEM)
        arrays.append(value.value if far or direct else value)
        if far:
            buffers.append(pltpu.VMEM(value.value.shape, value.value.dtype))
    buffers.extend(pltpu.VMEM(out.shape, out.dtype) for out in outputs if out.far)
    flags = [isinstance(value, Far) for value in inputs] + [out.far for out in outputs]
    sizes = len(inputs), len(flags), len(flags) + len(buffers)

    def body(*refs):
        semaphores = refs[sizes[2]] if buffers else None
        given, views = 0, []
        for at, far in enumerate(flags):
            if far:
                kind = Fetched if at < sizes[0] else Stored
                views.append(kind(refs[at], refs[sizes[1] + given], semaphores.at[given]))
                given += 1
            else:
                views.append(refs[at])
        kernel(*views, *refs[sizes[2] + (1 if buffers else 0) :])
        for view in views:
            if isinstance(view, Stored):
                view.flush()
        for view in views:
            if isinstance(view, Fetched):
                view.wait()
            if isinstance(view, Stored):
                view.copy.wait()

    own = [pltpu.SemaphoreType.DMA((len(buffers),))] if buffers else []
    return pl.pallas_call(
        body,
        out_shape=[jax.ShapeDtypeStruct(out.shape, out.dtype) for out in outputs],
        in_specs=in_specs,
        out_specs=[HBM if out.far else VMEM for out in outputs],
        scratch_shapes=buffers + own + list(scratch),
        compiler_params=pltpu.CompilerParams(vmem_limit_bytes=20 * 1024 * 1024),
    )(*arrays)


def exchange(values):
    return lax.ppermute(values, "grp", [(0, 1), (1, 0)])


def spread_blocks(values, axes):
    return lax.all_to_all(values, axes, split_axis=0, concat_axis=0, tiled=True)


def route(values, devices):
    rows, features = values.shape
    blocks = values.reshape(devices, rows // devices, features)
    return spread_blocks(blocks, ("pts", "grp")).reshape(rows, features)


def on_device(
    points,
    rotated_place,
    rotated_source,
    ball_counts,
    fine_projection,
    fine_output,
    pool_weight,
    coarse_projection,
    coarse_output,
    coarse_cotangent,
):
    count, features = points.shape
    devices = lax.axis_size(("pts", "grp"))
    slots = 2 * count
    scaling = 1.0 / math.sqrt(count * devices)
    group = lax.axis_index("grp").astype(jnp.int32).reshape(1)
    wide = 2 * features
    half_rows = count // 2

    send, send_slot, receive_slot, live = call(
        route_kernel,
        (
            Far(rotated_place.reshape(1, count)),
            Far(rotated_source.reshape(1, count)),
            Far(ball_counts.reshape(1, -1)),
            Far(points),
        ),
        (
            Near((slots, features)),
            Near((1, count), jnp.int32),
            Near((1, count), jnp.int32),
            Near((1, count), F32),
        ),
    )
    other_cotangent = exchange(coarse_cotangent)
    arrived = route(send, devices)
    pair_slots = send_slot.reshape(half_rows, 2).T
    heads = features // HD * (count // BALL)
    send, rotated, projected, mixture, weights = call(
        fine_forward_kernel,
        (arrived, receive_slot, live, Far(fine_projection), Far(fine_output)),
        (
            Near((slots, features)),
            Near((count, features), far=True),
            Near((count, 3 * features), far=True),
            Near((count, features), far=True),
            Near((heads, BALL, BALL), far=True),
        ),
    )
    arrived = route(send, devices)
    (own_joined,) = call(join_kernel, (arrived, pair_slots), (Near((half_rows, wide)),))
    other_joined = exchange(own_joined)
    coarse, keep, give, joined, unit, stacked = call(
        coarse_kernel,
        (
            group,
            own_joined,
            other_joined,
            Far(coarse_cotangent),
            Far(other_cotangent),
            Far(pool_weight),
            Far(coarse_projection),
            Far(coarse_output),
        ),
        (
            Near((half_rows, wide)),
            Near((half_rows, 2 * wide)),
            Near((half_rows, 2 * wide)),
            Near((count, wide), far=True),
            Near((count, wide), far=True),
            Near((count, 2 * wide), far=True),
        ),
        scalar=True,
    )
    got = exchange(give)
    coarse_result, coarse_gradient, send = call(
        coarse_finish_kernel,
        (
            group,
            coarse,
            keep,
            got,
            Far(coarse_cotangent),
            Far(pool_weight),
            Far(coarse_projection),
            Far(coarse_output),
            pair_slots,
        ),
        (
            Near((half_rows, wide), far=True),
            Near((half_rows, wide)),
            Near((slots, features)),
        ),
        scalar=True,
    )
    arrived = route(send, devices)
    other_gradient = exchange(coarse_gradient)
    owners = lax.axis_size("pts")
    (coarse_terms,) = call(
        coarse_weights_kernel,
        (
            group,
            Far(unit),
            Far(stacked),
            Far(coarse_cotangent),
            Far(other_cotangent),
            Far(joined),
            coarse_gradient,
            other_gradient,
        ),
        (Near((owners, 2, slots // devices, 5 * wide // 4), far=True),),
        scalar=True,
    )
    across = 2 * features + 5 * wide // 4
    (send,) = call(
        fine_backward_kernel,
        (
            arrived,
            receive_slot,
            Far(rotated),
            Far(projected),
            Far(mixture),
            Far(weights),
            Far(fine_projection),
            Far(fine_output),
            Direct(coarse_terms),
        ),
        (Near((owners, 2, slots // devices, across)),),
        scratch=(pltpu.VMEM((count, 3 * features), BF), pltpu.SemaphoreType.DMA),
    )
    arrived = spread_blocks(send.reshape(devices, slots // devices, across), ("pts", "grp"))
    (spread,) = call(
        functools.partial(sum_kernel, tokens=features, fine=features),
        (arrived.reshape(send.shape),),
        (Near((owners, slots // devices, features + 5 * wide // 2)),),
    )
    own_sums = spread_blocks(spread, "pts")
    (points_gradient,) = call(
        take_kernel, (arrived[:, :, :features], send_slot), (Near((count, features)),)
    )
    other_sums = exchange(own_sums)
    sums = call(
        functools.partial(sums_kernel, scaling=scaling),
        (group, own_sums, other_sums),
        (
            Near((features, 3 * features), F32, far=True),
            Near((features, features), F32, far=True),
            Near((wide, wide), F32, far=True),
            Near((wide, 3 * wide), F32, far=True),
            Near((wide, wide), F32, far=True),
        ),
        scalar=True,
    )
    return (coarse_result, points_gradient, *sums)


def solution(mesh):
    tokens = P(("pts", "grp"), None)
    in_specs = (
        tokens,
        P(("pts", "grp")),
        P(("pts", "grp")),
        P(),
        P(),
        P(),
        P(),
        P(),
        P(),
        tokens,
    )
    out_specs = (tokens, tokens, P(), P(), P(), P(), P())
    return jax.shard_map(
        on_device, mesh=mesh, in_specs=in_specs, out_specs=out_specs, check_vma=False
    )
```

```python
import functools
import math
from typing import NamedTuple

import jax
import jax.numpy as jnp
from jax import lax
from jax.experimental import pallas as pl
from jax.experimental.pallas import tpu as pltpu
from jax.sharding import PartitionSpec as P

HD = 64
BALL = 256
PAIR = 2 * HD
EPSILON = 1e-05
BF = jnp.bfloat16
F32 = jnp.float32


def mm(a, b, contract=(1, 0)):
    return lax.dot_general(
        a, b, (((contract[0],), (contract[1],)), ((), ())), preferred_element_type=F32
    )


def normalize(values):
    floats = values.astype(F32)
    center = floats - jnp.mean(floats, axis=-1, keepdims=True)
    inverse = lax.rsqrt(jnp.mean(center * center, axis=-1, keepdims=True) + EPSILON)
    return center * inverse, inverse


def norm_backward(incoming, normed, inverse):
    first_mean = jnp.mean(incoming, axis=-1, keepdims=True)
    second_mean = jnp.mean(incoming * normed, axis=-1, keepdims=True)
    return inverse * (incoming - first_mean - normed * second_mean)


def one_hot(slots, total):
    shape = (total, slots.shape[1])
    return (lax.broadcasted_iota(jnp.int32, shape, 0) == slots).astype(BF)


def head_half(shape, half):
    lanes = lax.broadcasted_iota(jnp.int32, shape, 1)
    return (lanes < HD) if half == 0 else (lanes >= HD)


def keep_half(rows, half):
    return jnp.where(head_half(rows.shape, half), rows, jnp.zeros_like(rows))


def softmax_rows(scores):
    raised = jnp.exp(scores - jnp.max(scores, axis=-1, keepdims=True))
    return (raised / jnp.sum(raised, axis=-1, keepdims=True)).astype(BF)


def slopes_of(weights, against):
    wide = weights.astype(F32)
    diagonal = jnp.sum(wide * against, axis=-1, keepdims=True)
    return (wide * (against - diagonal) * HD ** (-0.5)).astype(BF)


def column_of(row):
    count = row.shape[1]
    turned = jnp.broadcast_to(row.astype(F32), (128, count)).T
    return jnp.concatenate([turned] * (count // 128), axis=1)


def route_kernel(
    place, source, counts, points, send, send_slot, pair_slot, receive_slot, live
):
    count = place.shape[1]
    shift = count.bit_length() - 1
    capacity = send.shape[0] * count // (counts.shape[1] * BALL)
    to_row = place[...] >> shift
    rows = lax.broadcasted_iota(jnp.int32, (count, count), 0)
    columns = lax.broadcasted_iota(jnp.int32, (count, count), 1)
    earlier = (column_of(to_row) == to_row.astype(F32)) & (rows < columns)
    rank = jnp.sum(jnp.where(earlier, 1.0, 0.0), axis=0, keepdims=True)
    slot = to_row * capacity + rank.astype(jnp.int32)
    send_slot[...] = slot
    even_first = jnp.where(columns < count // 2, 2 * columns, 2 * columns + 1 - count)
    digits = jnp.concatenate([slot >> 5, slot & 31] + [jnp.zeros_like(slot)] * 6, axis=0)
    moved = mm(digits.astype(F32).astype(BF), (rows == even_first).astype(BF)).astype(jnp.int32)
    pair_slot[...] = moved[0:1] * 32 + moved[1:2]
    source_row = source[...]
    from_row = source_row >> shift
    earlier = (column_of(from_row) == from_row.astype(F32)) & (
        column_of(source_row) < source_row.astype(F32)
    )
    rank = jnp.sum(jnp.where(earlier, 1.0, 0.0), axis=0, keepdims=True)
    receive_slot[...] = from_row * capacity + rank.astype(jnp.int32)
    balls = counts.shape[1]
    own_ball = one_hot(source_row >> (BALL.bit_length() - 1), balls)
    filled = mm(jnp.broadcast_to(counts[...].astype(F32), (8, balls)).astype(BF), own_ball)
    inside = (source_row & (BALL - 1)).astype(F32)
    live[...] = jnp.where(inside < filled[:1], 1.0, 0.0)
    send[...] = mm(one_hot(slot, send.shape[0]), points[...]).astype(BF)


def fine_forward_kernel(
    arrived, receive_slot, live, projection, output, send, rotated, projected, mixture, weights
):
    place = one_hot(receive_slot[...], arrived.shape[0])
    rows_in = mm(place, arrived[...], (0, 0))
    rotated[...] = rows_in.astype(BF)
    features = rows_in.shape[1]
    normed, _ = normalize(rows_in)
    projected[...] = mm(normed.astype(BF), projection[...]).astype(BF)
    balls = rows_in.shape[0] // BALL
    pairs = features // PAIR
    for ball in range(balls):
        rows = slice(ball * BALL, (ball + 1) * BALL)
        alive = live[:, rows] > 0.5
        for pair in range(pairs):
            lanes = slice(pair * PAIR, (pair + 1) * PAIR)
            query = projected[rows, lanes]
            key = projected[rows, features + pair * PAIR : features + (pair + 1) * PAIR]
            value = projected[rows, 2 * features + pair * PAIR : 2 * features + (pair + 1) * PAIR]
            halves = []
            for half in range(2):
                scores = mm(keep_half(query, half), key, (1, 1)) * HD ** (-0.5)
                head_weights = softmax_rows(jnp.where(alive, scores, -1e30))
                weights[(ball * pairs + pair) * 2 + half] = head_weights
                halves.append(mm(head_weights, value))
            mixed = jnp.where(head_half(halves[0].shape, 0), halves[0], halves[1])
            mixture[rows, lanes] = mixed.astype(BF)
    result = (rows_in + mm(mixture[...], output[...])).astype(BF)
    send[...] = mm(place, result).astype(BF)


def join_kernel(arrived, pair_slot, cotangent, pack):
    half_rows, wide = cotangent.shape
    place = one_hot(pair_slot[...], arrived.shape[0])
    rows = mm(place, arrived[...], (0, 0)).astype(BF)
    pack[:, : wide // 2] = rows[:half_rows]
    pack[:, wide // 2 : wide] = rows[half_rows:]
    pack[:, wide:] = cotangent[...]


def coarse_kernel(
    group, own_pack, other_pack, pool, projection, output, coarse, keep, give, unit
):
    half_rows, wide = coarse.shape
    part = wide // 2
    first = pl.multiple_of(group[0] * part, part)
    joined = jnp.concatenate([own_pack[:, :wide], other_pack[:, :wide]], axis=0)
    tokens = mm(joined, pool[...]).astype(BF)
    coarse[...] = tokens[:half_rows]
    normed, _ = normalize(tokens)
    unit_rows = normed.astype(BF)
    unit[...] = unit_rows
    queries = mm(unit_rows, projection[:, pl.ds(first, part)]).astype(BF)
    keys = mm(unit_rows, projection[:, pl.ds(wide + first, part)]).astype(BF)
    values = mm(unit_rows, projection[:, pl.ds(2 * wide + first, part)]).astype(BF)
    cotangent = jnp.concatenate([own_pack[:, wide:], other_pack[:, wide:]], axis=0)
    incoming = mm(cotangent, output[pl.ds(first, part), :], (1, 1)).astype(BF)
    for pair in range(part // PAIR):
        lanes = slice(pair * PAIR, (pair + 1) * PAIR)
        query, key, value = queries[:, lanes], keys[:, lanes], values[:, lanes]
        entering = incoming[:, lanes]
        parts = ([], [], [], [])
        for half in range(2):
            scores = mm(keep_half(query, half), key, (1, 1)) * HD ** (-0.5)
            head_weights = softmax_rows(scores)
            parts[0].append(mm(head_weights, value))
            against = mm(keep_half(entering, half), value, (1, 1))
            slopes = slopes_of(head_weights, against)
            parts[1].append(mm(slopes, key))
            parts[2].append(mm(slopes, query, (0, 0)))
            parts[3].append(mm(head_weights, entering, (0, 0)))
        for at, (low, high) in enumerate(parts):
            both = jnp.where(head_half(low.shape, 0), low, high).astype(BF)
            target = slice(at * part + pair * PAIR, at * part + (pair + 1) * PAIR)
            keep[:, target] = both[:half_rows]
            give[:, target] = both[half_rows:]


def coarse_finish_kernel(
    group,
    coarse,
    keep,
    got,
    cotangent,
    pool,
    projection,
    output,
    pair_slot,
    result,
    gradient,
    send,
):
    half_rows, wide = coarse.shape
    part = wide // 2
    mixed = coarse[...].astype(F32)
    back = jnp.zeros((half_rows, wide), F32)
    for source, index in ((keep, group[0]), (got, 1 - group[0])):
        first = pl.multiple_of(index * part, part)
        mixed = mixed + mm(source[:, :part], output[pl.ds(first, part), :])
        for at in range(3):
            back = back + mm(
                source[:, (at + 1) * part : (at + 2) * part],
                projection[:, pl.ds(at * wide + first, part)],
                (1, 1),
            )
    result[...] = mixed.astype(BF)
    result.flush()
    normed, inverse = normalize(coarse[...])
    gradient_rows = (
        cotangent[...].astype(F32) + norm_backward(back, normed, inverse)
    ).astype(BF)
    gradient[...] = gradient_rows
    fine = mm(gradient_rows, pool[...], (1, 1)).astype(BF)
    features = send.shape[1]
    stacked = jnp.concatenate([fine[:, :features], fine[:, features:]], axis=0)
    send[...] = mm(one_hot(pair_slot[...], send.shape[0]), stacked).astype(BF)


def coarse_weights_kernel(
    arrived, unit, keep, give, own_pack, other_pack, gradient, terms, gradient_out
):
    gradient_out[...] = gradient[...]
    wide = unit.shape[1]
    part = wide // 2
    stacked = jnp.concatenate([keep[...], give[...]], axis=0)
    cotangent = jnp.concatenate([own_pack[:, wide:], other_pack[:, wide:]], axis=0)
    projection_term = mm(unit[...], stacked[:, part:], (0, 0))
    across = projection_term.shape[1] // 2
    for side in range(2):
        columns = projection_term[:, side * across : (side + 1) * across]
        put_blocks(terms, side, 0, columns)
    put_quarters(terms, across, mm(stacked[:, :part], cotangent, (0, 0)))


def put_quarters(blocks, lane, term):
    width = term.shape[1] // 4
    for side in range(2):
        stack = [term[:, (2 * side + k) * width : (2 * side + k + 1) * width] for k in range(2)]
        put_blocks(blocks, side, lane, jnp.concatenate(stack, axis=0))


def put_blocks(blocks, side, lane, rows):
    owners, width = blocks.shape[0], rows.shape[1]
    pieces = rows.reshape(owners, rows.shape[0] // owners, width)
    blocks[:, side, :, lane : lane + width] = pieces.astype(BF)


def sum_kernel(arrived, spread, *, tokens, fine):
    fine_part = jnp.sum(arrived[:, :, :, tokens : tokens + fine].astype(F32), axis=0)
    coarse_part = jnp.sum(arrived[:, :, :, tokens + fine :].astype(F32), axis=0)
    total = [fine_part[0] + fine_part[1], coarse_part[0], coarse_part[1]]
    total = jnp.concatenate(total, axis=1).astype(BF)
    spread[...] = jnp.broadcast_to(total[None], spread.shape)


def sums_kernel(
    group, own, other, fine_projection, fine_output, pool, projection, output, *, scaling
):
    features = fine_output.shape[0]
    wide = pool.shape[0]
    part = wide // 2
    width = wide // 4
    across = 3 * part // 2

    owns_low = group[0] == 0

    def lanes(side, start, count):
        here, there = own[:, :, start : start + count], other[:, :, start : start + count]
        low = owns_low if side == 0 else jnp.logical_not(owns_low)
        values = jnp.where(low, here, there).astype(F32) * scaling
        return values.reshape(own.shape[0] * own.shape[1], count)

    def start_of(heads):
        return features + heads * (across + 2 * width)

    for side in range(2):
        for heads in range(2):
            for k in range(3):
                column = side * across + k * width
                at, inner = column // part, column % part
                target = at * wide + heads * part + inner
                projection[:, target : target + width] = lanes(
                    side, start_of(heads) + k * width, width
                )
    projection.flush()
    for at, ref in enumerate((output, pool)):
        for side in range(2):
            for heads in range(2):
                block = lanes(side, start_of(heads) + across + at * width, width)
                for k in range(2):
                    column = (2 * side + k) * width
                    ref[heads * part : (heads + 1) * part, column : column + width] = block[
                        k * part : (k + 1) * part
                    ]
        ref.flush()
    for side in range(2):
        fine = lanes(side, 0, features)
        for k in range(2):
            at = 2 * side + k
            block = fine[k * features : (k + 1) * features]
            if at < 3:
                fine_projection[:, at * features : (at + 1) * features] = block
            else:
                fine_output[...] = block


def fine_backward_kernel(
    group,
    arrived,
    receive_slot,
    rotated,
    projected,
    mixture,
    weights,
    projection,
    output,
    coarse_terms,
    own_pack,
    other_pack,
    own_gradient,
    other_gradient,
    send,
    grad_projected,
):
    place = one_hot(receive_slot[...], arrived.shape[0])
    gradient_in = mm(place, arrived[...], (0, 0))
    gradient_rows = gradient_in.astype(BF)
    features = rotated.shape[1]
    entering = mm(gradient_rows, output[...], (1, 1)).astype(BF)
    terms = [mm(mixture[...], gradient_rows, (0, 0))]
    balls = rotated.shape[0] // BALL
    pairs = features // PAIR
    for ball in range(balls):
        rows = slice(ball * BALL, (ball + 1) * BALL)
        for pair in range(pairs):
            lanes = slice(pair * PAIR, (pair + 1) * PAIR)
            query = projected[rows, lanes]
            key = projected[rows, features + pair * PAIR : features + (pair + 1) * PAIR]
            value = projected[rows, 2 * features + pair * PAIR : 2 * features + (pair + 1) * PAIR]
            enters = entering[rows, lanes]
            parts = ([], [], [])
            for half in range(2):
                head_weights = weights[(ball * pairs + pair) * 2 + half]
                against = mm(keep_half(enters, half), value, (1, 1))
                slopes = slopes_of(head_weights, against)
                parts[0].append(mm(slopes, key))
                parts[1].append(mm(slopes, query, (0, 0)))
                parts[2].append(mm(head_weights, enters, (0, 0)))
            for at, (low, high) in enumerate(parts):
                both = jnp.where(head_half(low.shape, 0), low, high).astype(BF)
                target = at * features + pair * PAIR
                grad_projected[rows, target : target + PAIR] = both
    normed, inverse = normalize(rotated[...])
    unit_rows = normed.astype(BF)
    for at in range(3):
        columns = slice(at * features, (at + 1) * features)
        terms.insert(at, mm(unit_rows, grad_projected[:, columns], (0, 0)))
    back = mm(grad_projected[...], projection[...], (1, 1))
    result = (gradient_in + norm_backward(back, normed, inverse)).astype(BF)
    tokens = mm(place, result)
    send[:, :, :, :features] = tokens.reshape(send.shape[:3] + (features,)).astype(BF)
    for side in range(2):
        put_blocks(send, side, features, jnp.concatenate(terms[2 * side : 2 * side + 2], axis=0))
    settled = 2 * features + coarse_terms.shape[3]
    send[:, :, :, 2 * features : settled] = coarse_terms[...]
    part = own_gradient.shape[1] // 2
    first = pl.multiple_of(group[0] * part, part)
    pool_term = mm(own_pack[:, pl.ds(first, part)], own_gradient[...], (0, 0))
    pool_term = pool_term + mm(other_pack[:, pl.ds(first, part)], other_gradient[...], (0, 0))
    put_quarters(send, settled, pool_term)


def take_kernel(arrived, slots, rows_out):
    place = one_hot(slots[...], slots.shape[1] * 2)
    rows = arrived[...].reshape(place.shape[0], arrived.shape[-1])
    rows_out[...] = mm(place, rows, (0, 0)).astype(BF)


VMEM = pl.BlockSpec(memory_space=pltpu.VMEM)
SMEM = pl.BlockSpec(memory_space=pltpu.SMEM)
HBM = pl.BlockSpec(memory_space=pltpu.HBM)


class Far(NamedTuple):
    value: jax.Array


class Near(NamedTuple):
    shape: tuple
    dtype: jnp.dtype = BF
    far: bool = False


class Fetched:
    def __init__(self, source, buffer, semaphore):
        self.buffer, self.shape, self.waited = buffer, buffer.shape, False
        self.copy = pltpu.make_async_copy(source, buffer, semaphore)
        self.copy.start()

    def wait(self):
        if not self.waited:
            self.copy.wait()
            self.waited = True

    def __getitem__(self, index):
        self.wait()
        return self.buffer[index]


class Stored:
    def __init__(self, target, buffer, semaphore):
        self.buffer, self.shape, self.dtype, self.started = buffer, buffer.shape, buffer.dtype, False
        self.copy = pltpu.make_async_copy(buffer, target, semaphore)

    def __setitem__(self, index, values):
        self.buffer[index] = values

    def __getitem__(self, index):
        return self.buffer[index]

    def flush(self):
        if not self.started:
            self.copy.start()
            self.started = True


def call(kernel, inputs, outputs, scalar=False, scratch=(), mebibytes=16):
    in_specs, arrays, buffers = [], [], []
    for at, value in enumerate(inputs):
        far = isinstance(value, Far)
        in_specs.append(SMEM if scalar and at == 0 else HBM if far else VMEM)
        arrays.append(value.value if far else value)
        if far:
            buffers.append(pltpu.VMEM(value.value.shape, value.value.dtype))
    buffers.extend(pltpu.VMEM(out.shape, out.dtype) for out in outputs if out.far)
    flags = [isinstance(value, Far) for value in inputs] + [out.far for out in outputs]
    sizes = len(inputs), len(flags), len(flags) + len(buffers)

    def body(*refs):
        semaphores = refs[sizes[2]] if buffers else None
        given, views = 0, []
        for at, far in enumerate(flags):
            if far:
                kind = Fetched if at < sizes[0] else Stored
                views.append(kind(refs[at], refs[sizes[1] + given], semaphores.at[given]))
                given += 1
            else:
                views.append(refs[at])
        kernel(*views, *refs[sizes[2] + (1 if buffers else 0) :])
        for view in views:
            if isinstance(view, Stored):
                view.flush()
        for view in views:
            if isinstance(view, Fetched):
                view.wait()
            if isinstance(view, Stored):
                view.copy.wait()

    own = [pltpu.SemaphoreType.DMA((len(buffers),))] if buffers else []
    return pl.pallas_call(
        body,
        out_shape=[jax.ShapeDtypeStruct(out.shape, out.dtype) for out in outputs],
        in_specs=in_specs,
        out_specs=[HBM if out.far else VMEM for out in outputs],
        scratch_shapes=buffers + own + list(scratch),
        compiler_params=pltpu.CompilerParams(vmem_limit_bytes=mebibytes * 1024 * 1024),
    )(*arrays)


def exchange(values):
    return lax.ppermute(values, "grp", [(0, 1), (1, 0)])


def spread_blocks(values, axes):
    return lax.all_to_all(values, axes, split_axis=0, concat_axis=0, tiled=True)


def route(values, devices):
    rows, features = values.shape
    blocks = values.reshape(devices, rows // devices, features)
    return spread_blocks(blocks, ("pts", "grp")).reshape(rows, features)


def on_device(
    points,
    rotated_place,
    rotated_source,
    ball_counts,
    fine_projection,
    fine_output,
    pool_weight,
    coarse_projection,
    coarse_output,
    coarse_cotangent,
):
    count, features = points.shape
    devices = lax.axis_size(("pts", "grp"))
    slots = 2 * count
    scaling = 1.0 / math.sqrt(count * devices)
    group = lax.axis_index("grp").astype(jnp.int32).reshape(1)
    wide = 2 * features
    half_rows = count // 2

    send, send_slot, pair_slot, receive_slot, live = call(
        route_kernel,
        (
            Far(rotated_place.reshape(1, count)),
            Far(rotated_source.reshape(1, count)),
            Far(ball_counts.reshape(1, -1)),
            Far(points),
        ),
        (
            Near((slots, features)),
            Near((1, count), jnp.int32),
            Near((1, count), jnp.int32),
            Near((1, count), jnp.int32),
            Near((1, count), F32),
        ),
        mebibytes=56,
    )
    arrived = route(send, devices)
    heads = features // HD * (count // BALL)
    send, rotated, projected, mixture, weights = call(
        fine_forward_kernel,
        (arrived, receive_slot, live, fine_projection, fine_output),
        (
            Near((slots, features)),
            Near((count, features)),
            Near((count, 3 * features)),
            Near((count, features)),
            Near((heads, BALL, BALL)),
        ),
    )
    arrived = route(send, devices)
    (own_pack,) = call(
        join_kernel, (arrived, pair_slot, coarse_cotangent), (Near((half_rows, 2 * wide)),)
    )
    other_pack = exchange(own_pack)
    coarse, keep, give, unit = call(
        coarse_kernel,
        (group, own_pack, other_pack, pool_weight, coarse_projection, coarse_output),
        (
            Near((half_rows, wide)),
            Near((half_rows, 2 * wide)),
            Near((half_rows, 2 * wide)),
            Near((count, wide)),
        ),
        scalar=True,
    )
    got = exchange(give)
    coarse_result, coarse_gradient, send = call(
        coarse_finish_kernel,
        (
            group,
            coarse,
            keep,
            got,
            coarse_cotangent,
            pool_weight,
            coarse_projection,
            coarse_output,
            pair_slot,
        ),
        (
            Near((half_rows, wide), far=True),
            Near((half_rows, wide)),
            Near((slots, features)),
        ),
        scalar=True,
    )
    arrived = route(send, devices)
    owners = lax.axis_size("pts")
    coarse_terms, own_gradient = call(
        coarse_weights_kernel,
        (arrived, unit, keep, give, own_pack, other_pack, coarse_gradient),
        (Near((owners, 2, slots // devices, wide)), Near((half_rows, wide))),
    )
    other_gradient = exchange(own_gradient)
    across = 2 * features + 5 * wide // 4
    (send,) = call(
        fine_backward_kernel,
        (
            group,
            arrived,
            receive_slot,
            rotated,
            projected,
            mixture,
            weights,
            fine_projection,
            fine_output,
            coarse_terms,
            own_pack,
            other_pack,
            own_gradient,
            other_gradient,
        ),
        (Near((owners, 2, slots // devices, across)),),
        scalar=True,
        scratch=(pltpu.VMEM((count, 3 * features), BF),),
    )
    arrived = spread_blocks(send.reshape(devices, slots // devices, across), ("pts", "grp"))
    (spread,) = call(
        functools.partial(sum_kernel, tokens=features, fine=features),
        (arrived.reshape(send.shape),),
        (Near((owners, slots // devices, features + 5 * wide // 2)),),
    )
    own_sums = spread_blocks(spread, "pts")
    (points_gradient,) = call(
        take_kernel, (arrived[:, :, :features], send_slot), (Near((count, features)),)
    )
    other_sums = exchange(own_sums)
    sums = call(
        functools.partial(sums_kernel, scaling=scaling),
        (group, own_sums, other_sums),
        (
            Near((features, 3 * features), F32, far=True),
            Near((features, features), F32, far=True),
            Near((wide, wide), F32, far=True),
            Near((wide, 3 * wide), F32, far=True),
            Near((wide, wide), F32, far=True),
        ),
        scalar=True,
    )
    return (coarse_result, points_gradient, *sums)


def solution(mesh):
    tokens = P(("pts", "grp"), None)
    in_specs = (
        tokens,
        P(("pts", "grp")),
        P(("pts", "grp")),
        P(),
        P(),
        P(),
        P(),
        P(),
        P(),
        tokens,
    )
    out_specs = (tokens, tokens, P(), P(), P(), P(), P())
    return jax.shard_map(
        on_device, mesh=mesh, in_specs=in_specs, out_specs=out_specs, check_vma=False
    )
```

```python
import functools
import math
from typing import NamedTuple

import jax
import jax.numpy as jnp
from jax import lax
from jax.experimental import pallas as pl
from jax.experimental.pallas import tpu as pltpu
from jax.sharding import PartitionSpec as P

HD = 64
BALL = 256
PAIR = 2 * HD
EPSILON = 1e-05
BF = jnp.bfloat16
F32 = jnp.float32


def mm(a, b, contract=(1, 0)):
    return lax.dot_general(
        a, b, (((contract[0],), (contract[1],)), ((), ())), preferred_element_type=F32
    )


def normalize(values):
    floats = values.astype(F32)
    center = floats - jnp.mean(floats, axis=-1, keepdims=True)
    inverse = lax.rsqrt(jnp.mean(center * center, axis=-1, keepdims=True) + EPSILON)
    return center * inverse, inverse


def norm_backward(incoming, normed, inverse):
    first_mean = jnp.mean(incoming, axis=-1, keepdims=True)
    second_mean = jnp.mean(incoming * normed, axis=-1, keepdims=True)
    return inverse * (incoming - first_mean - normed * second_mean)


def one_hot(slots, total):
    shape = (total, slots.shape[1])
    return (lax.broadcasted_iota(jnp.int32, shape, 0) == slots).astype(BF)


def head_half(shape, half):
    lanes = lax.broadcasted_iota(jnp.int32, shape, 1)
    return (lanes < HD) if half == 0 else (lanes >= HD)


def keep_half(rows, half):
    return jnp.where(head_half(rows.shape, half), rows, jnp.zeros_like(rows))


def softmax_rows(scores):
    raised = jnp.exp(scores - jnp.max(scores, axis=-1, keepdims=True))
    return (raised / jnp.sum(raised, axis=-1, keepdims=True)).astype(BF)


def slopes_of(weights, against):
    wide = weights.astype(F32)
    diagonal = jnp.sum(wide * against, axis=-1, keepdims=True)
    return (wide * (against - diagonal) * HD ** (-0.5)).astype(BF)


def column_of(row):
    count = row.shape[1]
    turned = jnp.broadcast_to(row.astype(F32), (128, count)).T
    return jnp.concatenate([turned] * (count // 128), axis=1)


def route_kernel(
    place, source, counts, points, send, send_slot, pair_slot, receive_slot, live
):
    count = place.shape[1]
    shift = count.bit_length() - 1
    capacity = send.shape[0] * count // (counts.shape[1] * BALL)
    to_row = place[...] >> shift
    rows = lax.broadcasted_iota(jnp.int32, (count, count), 0)
    columns = lax.broadcasted_iota(jnp.int32, (count, count), 1)
    earlier = (column_of(to_row) == to_row.astype(F32)) & (rows < columns)
    rank = jnp.sum(jnp.where(earlier, 1.0, 0.0), axis=0, keepdims=True)
    slot = to_row * capacity + rank.astype(jnp.int32)
    send_slot[...] = slot
    even_first = jnp.where(columns < count // 2, 2 * columns, 2 * columns + 1 - count)
    digits = jnp.concatenate([slot >> 5, slot & 31] + [jnp.zeros_like(slot)] * 6, axis=0)
    moved = mm(digits.astype(F32).astype(BF), (rows == even_first).astype(BF)).astype(jnp.int32)
    pair_slot[...] = moved[0:1] * 32 + moved[1:2]
    source_row = source[...]
    from_row = source_row >> shift
    earlier = (column_of(from_row) == from_row.astype(F32)) & (
        column_of(source_row) < source_row.astype(F32)
    )
    rank = jnp.sum(jnp.where(earlier, 1.0, 0.0), axis=0, keepdims=True)
    receive_slot[...] = from_row * capacity + rank.astype(jnp.int32)
    balls = counts.shape[1]
    own_ball = one_hot(source_row >> (BALL.bit_length() - 1), balls)
    filled = mm(jnp.broadcast_to(counts[...].astype(F32), (8, balls)).astype(BF), own_ball)
    inside = (source_row & (BALL - 1)).astype(F32)
    live[...] = jnp.where(inside < filled[:1], 1.0, 0.0)
    send[...] = mm(one_hot(slot, send.shape[0]), points[...]).astype(BF)


def fine_forward_kernel(
    arrived, receive_slot, live, projection, output, send, rotated, projected, mixture, weights
):
    place = one_hot(receive_slot[...], arrived.shape[0])
    rows_in = mm(place, arrived[...], (0, 0))
    rotated[...] = rows_in.astype(BF)
    features = rows_in.shape[1]
    normed, _ = normalize(rows_in)
    projected[...] = mm(normed.astype(BF), projection[...]).astype(BF)
    balls = rows_in.shape[0] // BALL
    pairs = features // PAIR
    for ball in range(balls):
        rows = slice(ball * BALL, (ball + 1) * BALL)
        alive = live[:, rows] > 0.5
        for pair in range(pairs):
            lanes = slice(pair * PAIR, (pair + 1) * PAIR)
            query = projected[rows, lanes]
            key = projected[rows, features + pair * PAIR : features + (pair + 1) * PAIR]
            value = projected[rows, 2 * features + pair * PAIR : 2 * features + (pair + 1) * PAIR]
            halves = []
            for half in range(2):
                scores = mm(keep_half(query, half), key, (1, 1)) * HD ** (-0.5)
                head_weights = softmax_rows(jnp.where(alive, scores, -1e30))
                weights[(ball * pairs + pair) * 2 + half] = head_weights
                halves.append(mm(head_weights, value))
            mixed = jnp.where(head_half(halves[0].shape, 0), halves[0], halves[1])
            mixture[rows, lanes] = mixed.astype(BF)
    result = (rows_in + mm(mixture[...], output[...])).astype(BF)
    send[...] = mm(place, result).astype(BF)


def join_kernel(arrived, pair_slot, cotangent, pack):
    half_rows, wide = cotangent.shape
    place = one_hot(pair_slot[...], arrived.shape[0])
    rows = mm(place, arrived[...], (0, 0)).astype(BF)
    pack[:, : wide // 2] = rows[:half_rows]
    pack[:, wide // 2 : wide] = rows[half_rows:]
    pack[:, wide:] = cotangent[...]


def coarse_kernel(
    group, own_pack, other_pack, pool, projection, output, coarse, keep, give, unit, both_joined
):
    half_rows, wide = coarse.shape
    part = wide // 2
    first = pl.multiple_of(group[0] * part, part)
    joined = jnp.concatenate([own_pack[:, :wide], other_pack[:, :wide]], axis=0)
    both_joined[...] = joined
    both_joined.flush()
    tokens = mm(joined, pool[...]).astype(BF)
    coarse[...] = tokens[:half_rows]
    normed, _ = normalize(tokens)
    unit_rows = normed.astype(BF)
    unit[...] = unit_rows
    queries = mm(unit_rows, projection[:, pl.ds(first, part)]).astype(BF)
    keys = mm(unit_rows, projection[:, pl.ds(wide + first, part)]).astype(BF)
    values = mm(unit_rows, projection[:, pl.ds(2 * wide + first, part)]).astype(BF)
    cotangent = jnp.concatenate([own_pack[:, wide:], other_pack[:, wide:]], axis=0)
    incoming = mm(cotangent, output[pl.ds(first, part), :], (1, 1)).astype(BF)
    for pair in range(part // PAIR):
        lanes = slice(pair * PAIR, (pair + 1) * PAIR)
        query, key, value = queries[:, lanes], keys[:, lanes], values[:, lanes]
        entering = incoming[:, lanes]
        parts = ([], [], [], [])
        for half in range(2):
            scores = mm(keep_half(query, half), key, (1, 1)) * HD ** (-0.5)
            head_weights = softmax_rows(scores)
            parts[0].append(mm(head_weights, value))
            against = mm(keep_half(entering, half), value, (1, 1))
            slopes = slopes_of(head_weights, against)
            parts[1].append(mm(slopes, key))
            parts[2].append(mm(slopes, query, (0, 0)))
            parts[3].append(mm(head_weights, entering, (0, 0)))
        for at, (low, high) in enumerate(parts):
            both = jnp.where(head_half(low.shape, 0), low, high).astype(BF)
            target = slice(at * part + pair * PAIR, at * part + (pair + 1) * PAIR)
            keep[:, target] = both[:half_rows]
            give[:, target] = both[half_rows:]


def coarse_finish_kernel(
    group,
    coarse,
    keep,
    got,
    cotangent,
    pool,
    projection,
    output,
    pair_slot,
    mark,
    result,
    gradient,
    send,
):
    half_rows, wide = coarse.shape
    part = wide // 2
    mixed = coarse[...].astype(F32)
    back = jnp.zeros((half_rows, wide), F32)
    for source, index in ((keep, group[0]), (got, 1 - group[0])):
        first = pl.multiple_of(index * part, part)
        mixed = mixed + mm(source[:, :part], output[pl.ds(first, part), :])
        for at in range(3):
            back = back + mm(
                source[:, (at + 1) * part : (at + 2) * part],
                projection[:, pl.ds(at * wide + first, part)],
                (1, 1),
            )
    result[...] = mixed.astype(BF)
    result.flush()
    normed, inverse = normalize(coarse[...])
    gradient_rows = (
        cotangent[...].astype(F32) + norm_backward(back, normed, inverse)
    ).astype(BF)
    gradient[...] = gradient_rows
    fine = mm(gradient_rows, pool[...], (1, 1)).astype(BF)
    features = send.shape[1]
    stacked = jnp.concatenate([fine[:, :features], fine[:, features:]], axis=0)
    send[...] = mm(one_hot(pair_slot[...], send.shape[0]), stacked).astype(BF)


def coarse_weights_kernel(
    parity, unit, keep, give, own_pack, other_pack, kept, first_half, second_half, mark
):
    wide = unit.shape[1]
    part = wide // 2
    stacked = jnp.concatenate([keep[...], give[...]], axis=0)
    cotangent = jnp.concatenate([own_pack[:, wide:], other_pack[:, wide:]], axis=0)
    projection_term = mm(unit[...], stacked[:, part:], (0, 0))
    output_term = mm(stacked[:, :part], cotangent, (0, 0))
    across = projection_term.shape[1] // 2
    width = wide // 4
    for side in range(2):
        stack = [output_term[:, (2 * side + k) * width : (2 * side + k + 1) * width] for k in range(2)]
        columns = projection_term[:, side * across : (side + 1) * across]
        terms = jnp.concatenate([columns, jnp.concatenate(stack, axis=0)], axis=1)
        for at, passed in enumerate((first_half, second_half)):
            low = terms[:, 2 * at * width : (2 * at + 1) * width]
            high = terms[:, (2 * at + 1) * width : (2 * at + 2) * width]
            upper = parity[at] == 1
            put_blocks(kept, side, at * width, jnp.where(upper, high, low))
            put_blocks(passed, side, 0, jnp.where(upper, low, high))
    mark[...] = jnp.zeros_like(mark)


def put_quarters(blocks, lane, term):
    width = term.shape[1] // 4
    for side in range(2):
        stack = [term[:, (2 * side + k) * width : (2 * side + k + 1) * width] for k in range(2)]
        put_blocks(blocks, side, lane, jnp.concatenate(stack, axis=0))


def put_blocks(blocks, side, lane, rows):
    owners, width = blocks.shape[0], rows.shape[1]
    pieces = rows.reshape(owners, rows.shape[0] // owners, width)
    blocks[:, side, :, lane : lane + width] = pieces.astype(BF)


def sum_kernel(arrived, spread, *, tokens, fine, run, step):
    senders, _, rows, across = arrived.shape
    start = tokens + fine
    width = (across - start) // 3
    fine_part = jnp.sum(arrived[:, :, :, tokens:start].astype(F32), axis=0)
    total = [fine_part[0] + fine_part[1]]
    for side in range(2):
        for at, block in enumerate((run, step)):
            values = arrived[:, side, :, start + at * width : start + (at + 1) * width]
            split = values.astype(F32).reshape(senders // (2 * block), 2, block, rows, width)
            halves = jnp.sum(jnp.sum(split, axis=2), axis=0)
            total.extend([halves[0], halves[1]])
        total.append(jnp.sum(arrived[:, side, :, start + 2 * width :].astype(F32), axis=0))
    total = jnp.concatenate(total, axis=1).astype(BF)
    spread[...] = jnp.broadcast_to(total[None], spread.shape)


def sums_kernel(
    group, own, other, fine_projection, fine_output, pool, projection, output, *, scaling
):
    features = fine_output.shape[0]
    wide = pool.shape[0]
    part = wide // 2
    width = wide // 4
    across = 3 * part // 2

    owns_low = group[0] == 0

    def lanes(side, start, count):
        here, there = own[:, :, start : start + count], other[:, :, start : start + count]
        low = owns_low if side == 0 else jnp.logical_not(owns_low)
        values = jnp.where(low, here, there).astype(F32) * scaling
        return values.reshape(own.shape[0] * own.shape[1], count)

    def start_of(heads):
        return features + heads * (across + 2 * width)

    for side in range(2):
        for heads in range(2):
            for k in range(3):
                column = side * across + k * width
                at, inner = column // part, column % part
                target = at * wide + heads * part + inner
                projection[:, target : target + width] = lanes(
                    side, start_of(heads) + k * width, width
                )
    projection.flush()
    for at, ref in enumerate((output, pool)):
        for side in range(2):
            for heads in range(2):
                block = lanes(side, start_of(heads) + across + at * width, width)
                for k in range(2):
                    column = (2 * side + k) * width
                    ref[heads * part : (heads + 1) * part, column : column + width] = block[
                        k * part : (k + 1) * part
                    ]
        ref.flush()
    for side in range(2):
        fine = lanes(side, 0, features)
        for k in range(2):
            at = 2 * side + k
            block = fine[k * features : (k + 1) * features]
            if at < 3:
                fine_projection[:, at * features : (at + 1) * features] = block
            else:
                fine_output[...] = block


def fine_backward_kernel(
    group,
    arrived,
    receive_slot,
    rotated,
    projected,
    mixture,
    weights,
    projection,
    output,
    kept,
    got_first,
    got_second,
    joined,
    own_gradient,
    other_gradient,
    send,
    grad_projected,
):
    place = one_hot(receive_slot[...], arrived.shape[0])
    gradient_in = mm(place, arrived[...], (0, 0))
    gradient_rows = gradient_in.astype(BF)
    features = rotated.shape[1]
    entering = mm(gradient_rows, output[...], (1, 1)).astype(BF)
    terms = [mm(mixture[...], gradient_rows, (0, 0))]
    balls = rotated.shape[0] // BALL
    pairs = features // PAIR
    for ball in range(balls):
        rows = slice(ball * BALL, (ball + 1) * BALL)
        for pair in range(pairs):
            lanes = slice(pair * PAIR, (pair + 1) * PAIR)
            query = projected[rows, lanes]
            key = projected[rows, features + pair * PAIR : features + (pair + 1) * PAIR]
            value = projected[rows, 2 * features + pair * PAIR : 2 * features + (pair + 1) * PAIR]
            enters = entering[rows, lanes]
            parts = ([], [], [])
            for half in range(2):
                head_weights = weights[(ball * pairs + pair) * 2 + half]
                against = mm(keep_half(enters, half), value, (1, 1))
                slopes = slopes_of(head_weights, against)
                parts[0].append(mm(slopes, key))
                parts[1].append(mm(slopes, query, (0, 0)))
                parts[2].append(mm(head_weights, enters, (0, 0)))
            for at, (low, high) in enumerate(parts):
                both = jnp.where(head_half(low.shape, 0), low, high).astype(BF)
                target = at * features + pair * PAIR
                grad_projected[rows, target : target + PAIR] = both
    normed, inverse = normalize(rotated[...])
    unit_rows = normed.astype(BF)
    for at in range(3):
        columns = slice(at * features, (at + 1) * features)
        terms.insert(at, mm(unit_rows, grad_projected[:, columns], (0, 0)))
    back = mm(grad_projected[...], projection[...], (1, 1))
    result = (gradient_in + norm_backward(back, normed, inverse)).astype(BF)
    tokens = mm(place, result)
    send[:, :, :, :features] = tokens.reshape(send.shape[:3] + (features,)).astype(BF)
    for side in range(2):
        put_blocks(send, side, features, jnp.concatenate(terms[2 * side : 2 * side + 2], axis=0))
    width = got_first.shape[3]
    for at, got in enumerate((got_first, got_second)):
        mine = kept[:, :, :, at * width : (at + 1) * width].astype(F32)
        start = 2 * features + at * width
        send[:, :, :, start : start + width] = (mine + got[...].astype(F32)).astype(BF)
    part = own_gradient.shape[1] // 2
    first = pl.multiple_of(group[0] * part, part)
    gradient = jnp.concatenate([own_gradient[...], other_gradient[...]], axis=0)
    pool_term = mm(joined[:, pl.ds(first, part)], gradient, (0, 0))
    put_quarters(send, 2 * features + 2 * width, pool_term)


def take_kernel(arrived, slots, rows_out):
    place = one_hot(slots[...], slots.shape[1] * 2)
    rows = arrived[...].reshape(place.shape[0], arrived.shape[-1])
    rows_out[...] = mm(place, rows, (0, 0)).astype(BF)


VMEM = pl.BlockSpec(memory_space=pltpu.VMEM)
SMEM = pl.BlockSpec(memory_space=pltpu.SMEM)
HBM = pl.BlockSpec(memory_space=pltpu.HBM)


class Far(NamedTuple):
    value: jax.Array


class Near(NamedTuple):
    shape: tuple
    dtype: jnp.dtype = BF
    far: bool = False


class Fetched:
    def __init__(self, source, buffer, semaphore):
        self.buffer, self.shape, self.waited = buffer, buffer.shape, False
        self.copy = pltpu.make_async_copy(source, buffer, semaphore)
        self.copy.start()

    def wait(self):
        if not self.waited:
            self.copy.wait()
            self.waited = True

    def __getitem__(self, index):
        self.wait()
        return self.buffer[index]


class Stored:
    def __init__(self, target, buffer, semaphore):
        self.buffer, self.shape, self.dtype, self.started = buffer, buffer.shape, buffer.dtype, False
        self.copy = pltpu.make_async_copy(buffer, target, semaphore)

    def __setitem__(self, index, values):
        self.buffer[index] = values

    def __getitem__(self, index):
        return self.buffer[index]

    def flush(self):
        if not self.started:
            self.copy.start()
            self.started = True


def call(kernel, inputs, outputs, scalar=False, scratch=(), mebibytes=16):
    in_specs, arrays, buffers = [], [], []
    for at, value in enumerate(inputs):
        far = isinstance(value, Far)
        in_specs.append(SMEM if scalar and at == 0 else HBM if far else VMEM)
        arrays.append(
            pltpu.with_memory_space_constraint(value.value, pltpu.HBM) if far else value
        )
        if far:
            buffers.append(pltpu.VMEM(value.value.shape, value.value.dtype))
    buffers.extend(pltpu.VMEM(out.shape, out.dtype) for out in outputs if out.far)
    flags = [isinstance(value, Far) for value in inputs] + [out.far for out in outputs]
    sizes = len(inputs), len(flags), len(flags) + len(buffers)

    def body(*refs):
        semaphores = refs[sizes[2]] if buffers else None
        given, views = 0, []
        for at, far in enumerate(flags):
            if far:
                kind = Fetched if at < sizes[0] else Stored
                views.append(kind(refs[at], refs[sizes[1] + given], semaphores.at[given]))
                given += 1
            else:
                views.append(refs[at])
        kernel(*views, *refs[sizes[2] + (1 if buffers else 0) :])
        for view in views:
            if isinstance(view, Stored):
                view.flush()
        for view in views:
            if isinstance(view, Fetched):
                view.wait()
            if isinstance(view, Stored):
                view.copy.wait()

    own = [pltpu.SemaphoreType.DMA((len(buffers),))] if buffers else []
    return pl.pallas_call(
        body,
        out_shape=[
            (pltpu.HBM if out.far else jax.ShapeDtypeStruct)(out.shape, out.dtype)
            for out in outputs
        ],
        in_specs=in_specs,
        out_specs=[HBM if out.far else VMEM for out in outputs],
        scratch_shapes=buffers + own + list(scratch),
        compiler_params=pltpu.CompilerParams(vmem_limit_bytes=mebibytes * 1024 * 1024),
    )(*arrays)


def exchange(values):
    return lax.ppermute(values, "grp", [(0, 1), (1, 0)])


def spread_blocks(values, axes):
    return lax.all_to_all(values, axes, split_axis=0, concat_axis=0, tiled=True)


def route(values, devices):
    rows, features = values.shape
    blocks = values.reshape(devices, rows // devices, features)
    return spread_blocks(blocks, ("pts", "grp")).reshape(rows, features)


def on_device(
    points,
    rotated_place,
    rotated_source,
    ball_counts,
    fine_projection,
    fine_output,
    pool_weight,
    coarse_projection,
    coarse_output,
    coarse_cotangent,
):
    count, features = points.shape
    devices = lax.axis_size(("pts", "grp"))
    slots = 2 * count
    scaling = 1.0 / math.sqrt(count * devices)
    group = lax.axis_index("grp").astype(jnp.int32).reshape(1)
    wide = 2 * features
    half_rows = count // 2

    send, send_slot, pair_slot, receive_slot, live = call(
        route_kernel,
        (
            Far(rotated_place.reshape(1, count)),
            Far(rotated_source.reshape(1, count)),
            Far(ball_counts.reshape(1, -1)),
            Far(points),
        ),
        (
            Near((slots, features)),
            Near((1, count), jnp.int32),
            Near((1, count), jnp.int32),
            Near((1, count), jnp.int32),
            Near((1, count), F32),
        ),
    )
    arrived = route(send, devices)
    heads = features // HD * (count // BALL)
    send, rotated, projected, mixture, weights = call(
        fine_forward_kernel,
        (arrived, receive_slot, live, Far(fine_projection), Far(fine_output)),
        (
            Near((slots, features)),
            Near((count, features)),
            Near((count, 3 * features)),
            Near((count, features)),
            Near((heads, BALL, BALL)),
        ),
    )
    arrived = route(send, devices)
    (own_pack,) = call(
        join_kernel, (arrived, pair_slot, coarse_cotangent), (Near((half_rows, 2 * wide)),)
    )
    other_pack = exchange(own_pack)
    coarse, keep, give, unit, joined = call(
        coarse_kernel,
        (group, own_pack, other_pack, pool_weight, coarse_projection, Far(coarse_output)),
        (
            Near((half_rows, wide)),
            Near((half_rows, 2 * wide)),
            Near((half_rows, 2 * wide)),
            Near((count, wide)),
            Near((count, wide), far=True),
        ),
        scalar=True,
    )
    got = exchange(give)
    owners = lax.axis_size("pts")
    run, step = owners // 4, owners // 16
    place = lax.axis_index("pts").astype(jnp.int32)
    parity = jnp.stack([place // run % 2, place // step % 2])
    blocks = (owners, 2, slots // devices)
    kept, first_half, second_half, mark = call(
        coarse_weights_kernel,
        (parity, unit, keep, give, own_pack, other_pack),
        (
            Near((*blocks, wide // 2), far=True),
            Near((*blocks, wide // 4), far=True),
            Near((*blocks, wide // 4), far=True),
            Near((8, 128), F32),
        ),
        scalar=True,
    )
    got_first = lax.ppermute(first_half, "pts", [(i, i ^ run) for i in range(owners)])
    got_second = lax.ppermute(second_half, "pts", [(i, i ^ step) for i in range(owners)])
    coarse_result, coarse_gradient, send = call(
        coarse_finish_kernel,
        (
            group,
            coarse,
            keep,
            got,
            coarse_cotangent,
            pool_weight,
            coarse_projection,
            coarse_output,
            pair_slot,
            mark,
        ),
        (
            Near((half_rows, wide), far=True),
            Near((half_rows, wide)),
            Near((slots, features)),
        ),
        scalar=True,
    )
    arrived = route(send, devices)
    other_gradient = exchange(coarse_gradient)
    across = 2 * features + 3 * wide // 4
    (send,) = call(
        fine_backward_kernel,
        (
            group,
            arrived,
            receive_slot,
            rotated,
            projected,
            mixture,
            weights,
            fine_projection,
            fine_output,
            Far(kept),
            got_first,
            got_second,
            Far(joined),
            coarse_gradient,
            other_gradient,
        ),
        (Near((*blocks, across)),),
        scalar=True,
        scratch=(pltpu.VMEM((count, 3 * features), BF),),
    )
    arrived = spread_blocks(send.reshape(devices, slots // devices, across), ("pts", "grp"))
    (spread,) = call(
        functools.partial(sum_kernel, tokens=features, fine=features, run=run, step=step),
        (arrived.reshape(send.shape),),
        (Near((owners, slots // devices, features + 5 * wide // 2)),),
    )
    own_sums = spread_blocks(spread, "pts")
    (points_gradient,) = call(
        take_kernel, (arrived[:, :, :features], send_slot), (Near((count, features)),)
    )
    other_sums = exchange(own_sums)
    sums = call(
        functools.partial(sums_kernel, scaling=scaling),
        (group, own_sums, other_sums),
        (
            Near((features, 3 * features), F32, far=True),
            Near((features, features), F32, far=True),
            Near((wide, wide), F32, far=True),
            Near((wide, 3 * wide), F32, far=True),
            Near((wide, wide), F32, far=True),
        ),
        scalar=True,
    )
    return (coarse_result, points_gradient, *sums)


def solution(mesh):
    tokens = P(("pts", "grp"), None)
    in_specs = (
        tokens,
        P(("pts", "grp")),
        P(("pts", "grp")),
        P(),
        P(),
        P(),
        P(),
        P(),
        P(),
        tokens,
    )
    out_specs = (tokens, tokens, P(), P(), P(), P(), P())
    return jax.shard_map(
        on_device, mesh=mesh, in_specs=in_specs, out_specs=out_specs, check_vma=False
    )
```

```python
import functools
import math
from typing import NamedTuple

import jax
import jax.numpy as jnp
from jax import lax
from jax.experimental import pallas as pl
from jax.experimental.pallas import tpu as pltpu
from jax.sharding import PartitionSpec as P

HD = 64
BALL = 256
PAIR = 2 * HD
EPSILON = 1e-05
BF = jnp.bfloat16
F32 = jnp.float32


def mm(a, b, contract=(1, 0)):
    return lax.dot_general(
        a, b, (((contract[0],), (contract[1],)), ((), ())), preferred_element_type=F32
    )


def normalize(values):
    floats = values.astype(F32)
    center = floats - jnp.mean(floats, axis=-1, keepdims=True)
    inverse = lax.rsqrt(jnp.mean(center * center, axis=-1, keepdims=True) + EPSILON)
    return center * inverse, inverse


def norm_backward(incoming, normed, inverse):
    first_mean = jnp.mean(incoming, axis=-1, keepdims=True)
    second_mean = jnp.mean(incoming * normed, axis=-1, keepdims=True)
    return inverse * (incoming - first_mean - normed * second_mean)


def one_hot(slots, total):
    shape = (total, slots.shape[1])
    return (lax.broadcasted_iota(jnp.int32, shape, 0) == slots).astype(BF)


def head_half(shape, half):
    lanes = lax.broadcasted_iota(jnp.int32, shape, 1)
    return (lanes < HD) if half == 0 else (lanes >= HD)


def keep_half(rows, half):
    return jnp.where(head_half(rows.shape, half), rows, jnp.zeros_like(rows))


def softmax_rows(scores):
    raised = jnp.exp(scores - jnp.max(scores, axis=-1, keepdims=True))
    return (raised * (1.0 / jnp.sum(raised, axis=-1, keepdims=True))).astype(BF)


def slopes_of(weights, against):
    wide = weights.astype(F32)
    diagonal = jnp.sum(wide * against, axis=-1, keepdims=True)
    return (wide * (against - diagonal)).astype(BF)


def scaled_half(rows, half):
    return keep_half(rows * jnp.asarray(HD ** (-0.5), BF), half)


def column_of(row):
    count = row.shape[1]
    turned = jnp.broadcast_to(row.astype(F32), (128, count)).T
    return jnp.concatenate([turned] * (count // 128), axis=1)


def route_kernel(
    place, source, counts, points, send, send_slot, pair_slot, receive_slot, live
):
    count = place.shape[1]
    shift = count.bit_length() - 1
    capacity = send.shape[0] * count // (counts.shape[1] * BALL)
    to_row = place[...] >> shift
    rows = lax.broadcasted_iota(jnp.int32, (count, count), 0)
    columns = lax.broadcasted_iota(jnp.int32, (count, count), 1)
    earlier = (column_of(to_row) == to_row.astype(F32)) & (rows < columns)
    rank = jnp.sum(jnp.where(earlier, 1.0, 0.0), axis=0, keepdims=True)
    slot = to_row * capacity + rank.astype(jnp.int32)
    send_slot[...] = slot
    even_first = jnp.where(columns < count // 2, 2 * columns, 2 * columns + 1 - count)
    digits = jnp.concatenate([slot >> 5, slot & 31] + [jnp.zeros_like(slot)] * 6, axis=0)
    moved = mm(digits.astype(F32).astype(BF), (rows == even_first).astype(BF)).astype(jnp.int32)
    pair_slot[...] = moved[0:1] * 32 + moved[1:2]
    source_row = source[...]
    from_row = source_row >> shift
    earlier = (column_of(from_row) == from_row.astype(F32)) & (
        column_of(source_row) < source_row.astype(F32)
    )
    rank = jnp.sum(jnp.where(earlier, 1.0, 0.0), axis=0, keepdims=True)
    receive_slot[...] = from_row * capacity + rank.astype(jnp.int32)
    balls = counts.shape[1]
    own_ball = one_hot(source_row >> (BALL.bit_length() - 1), balls)
    filled = mm(jnp.broadcast_to(counts[...].astype(F32), (8, balls)).astype(BF), own_ball)
    inside = (source_row & (BALL - 1)).astype(F32)
    live[...] = jnp.where(inside < filled[:1], 1.0, 0.0)
    send[...] = mm(one_hot(slot, send.shape[0]), points[...]).astype(BF)


def fine_forward_kernel(
    arrived, receive_slot, live, projection, output, send, rotated, projected, mixture, weights
):
    place = one_hot(receive_slot[...], arrived.shape[0])
    rows_in = mm(place, arrived[...], (0, 0))
    rotated[...] = rows_in.astype(BF)
    features = rows_in.shape[1]
    normed, _ = normalize(rows_in)
    projected[...] = mm(normed.astype(BF), projection[...]).astype(BF)
    balls = rows_in.shape[0] // BALL
    pairs = features // PAIR
    for ball in range(balls):
        rows = slice(ball * BALL, (ball + 1) * BALL)
        alive = live[:, rows] > 0.5
        for pair in range(pairs):
            lanes = slice(pair * PAIR, (pair + 1) * PAIR)
            query = projected[rows, lanes]
            key = projected[rows, features + pair * PAIR : features + (pair + 1) * PAIR]
            value = projected[rows, 2 * features + pair * PAIR : 2 * features + (pair + 1) * PAIR]
            halves = []
            for half in range(2):
                scores = mm(scaled_half(query, half), key, (1, 1))
                head_weights = softmax_rows(jnp.where(alive, scores, -1e30))
                weights[(ball * pairs + pair) * 2 + half] = head_weights
                halves.append(mm(head_weights, value))
            mixed = jnp.where(head_half(halves[0].shape, 0), halves[0], halves[1])
            mixture[rows, lanes] = mixed.astype(BF)
    result = (rows_in + mm(mixture[...], output[...])).astype(BF)
    send[...] = mm(place, result).astype(BF)


def join_kernel(arrived, pair_slot, cotangent, pack):
    half_rows, wide = cotangent.shape
    place = one_hot(pair_slot[...], arrived.shape[0])
    rows = mm(place, arrived[...], (0, 0)).astype(BF)
    pack[:, : wide // 2] = rows[:half_rows]
    pack[:, wide // 2 : wide] = rows[half_rows:]
    pack[:, wide:] = cotangent[...]


def coarse_kernel(
    group, own_pack, other_pack, pool, projection, output, coarse, keep, give, unit
):
    half_rows, wide = coarse.shape
    part = wide // 2
    first = pl.multiple_of(group[0] * part, part)
    joined = jnp.concatenate([own_pack[:, :wide], other_pack[:, :wide]], axis=0)
    tokens = mm(joined, pool[...]).astype(BF)
    coarse[...] = tokens[:half_rows]
    normed, _ = normalize(tokens)
    unit_rows = normed.astype(BF)
    unit[...] = unit_rows
    queries = mm(unit_rows, projection[:, pl.ds(first, part)]).astype(BF)
    keys = mm(unit_rows, projection[:, pl.ds(wide + first, part)]).astype(BF)
    values = mm(unit_rows, projection[:, pl.ds(2 * wide + first, part)]).astype(BF)
    cotangent = jnp.concatenate([own_pack[:, wide:], other_pack[:, wide:]], axis=0)
    incoming = mm(cotangent, output[pl.ds(first, part), :], (1, 1)).astype(BF)
    for pair in range(part // PAIR):
        lanes = slice(pair * PAIR, (pair + 1) * PAIR)
        query, key, value = queries[:, lanes], keys[:, lanes], values[:, lanes]
        entering = incoming[:, lanes]
        parts = ([], [], [], [])
        for half in range(2):
            scores = mm(scaled_half(query, half), key, (1, 1))
            head_weights = softmax_rows(scores)
            parts[0].append(mm(head_weights, value))
            against = mm(keep_half(entering, half), value, (1, 1))
            slopes = slopes_of(head_weights, against)
            parts[1].append(mm(slopes, key) * HD ** (-0.5))
            parts[2].append(mm(slopes, query, (0, 0)) * HD ** (-0.5))
            parts[3].append(mm(head_weights, entering, (0, 0)))
        for at, (low, high) in enumerate(parts):
            both = jnp.where(head_half(low.shape, 0), low, high).astype(BF)
            target = slice(at * part + pair * PAIR, at * part + (pair + 1) * PAIR)
            keep[:, target] = both[:half_rows]
            give[:, target] = both[half_rows:]


def coarse_finish_kernel(
    group,
    coarse,
    keep,
    got,
    cotangent,
    pool,
    projection,
    output,
    pair_slot,
    result,
    gradient,
    send,
):
    half_rows, wide = coarse.shape
    part = wide // 2
    mixed = coarse[...].astype(F32)
    back = jnp.zeros((half_rows, wide), F32)
    for source, index in ((keep, group[0]), (got, 1 - group[0])):
        first = pl.multiple_of(index * part, part)
        mixed = mixed + mm(source[:, :part], output[pl.ds(first, part), :])
        for at in range(3):
            back = back + mm(
                source[:, (at + 1) * part : (at + 2) * part],
                projection[:, pl.ds(at * wide + first, part)],
                (1, 1),
            )
    result[...] = mixed.astype(BF)
    result.flush()
    normed, inverse = normalize(coarse[...])
    gradient_rows = (
        cotangent[...].astype(F32) + norm_backward(back, normed, inverse)
    ).astype(BF)
    gradient[...] = gradient_rows
    fine = mm(gradient_rows, pool[...], (1, 1)).astype(BF)
    features = send.shape[1]
    stacked = jnp.concatenate([fine[:, :features], fine[:, features:]], axis=0)
    send[...] = mm(one_hot(pair_slot[...], send.shape[0]), stacked).astype(BF)


def coarse_weights_kernel(
    parity,
    arrived,
    unit,
    keep,
    give,
    own_pack,
    other_pack,
    gradient,
    kept,
    first_half,
    second_half,
    gradient_out,
):
    wide = unit.shape[1]
    part = wide // 2
    stacked = jnp.concatenate([keep[...], give[...]], axis=0)
    cotangent = jnp.concatenate([own_pack[:, wide:], other_pack[:, wide:]], axis=0)
    projection_term = mm(unit[...], stacked[:, part:], (0, 0))
    output_term = mm(stacked[:, :part], cotangent, (0, 0))
    across = projection_term.shape[1] // 2
    width = wide // 4
    for side in range(2):
        stack = [output_term[:, (2 * side + k) * width : (2 * side + k + 1) * width] for k in range(2)]
        columns = projection_term[:, side * across : (side + 1) * across]
        terms = jnp.concatenate([columns, jnp.concatenate(stack, axis=0)], axis=1)
        for at, passed in enumerate((first_half, second_half)):
            low = terms[:, 2 * at * width : (2 * at + 1) * width]
            high = terms[:, (2 * at + 1) * width : (2 * at + 2) * width]
            upper = parity[at] == 1
            put_blocks(kept, side, at * width, jnp.where(upper, high, low))
            put_blocks(passed, side, 0, jnp.where(upper, low, high))
    gradient_out[...] = gradient[...]


def put_quarters(blocks, lane, term):
    width = term.shape[1] // 4
    for side in range(2):
        stack = [term[:, (2 * side + k) * width : (2 * side + k + 1) * width] for k in range(2)]
        put_blocks(blocks, side, lane, jnp.concatenate(stack, axis=0))


def put_blocks(blocks, side, lane, rows):
    owners, width = blocks.shape[0], rows.shape[1]
    pieces = rows.reshape(owners, rows.shape[0] // owners, width)
    blocks[:, side, :, lane : lane + width] = pieces.astype(BF)


def sum_kernel(arrived, spread, *, tokens, fine, run, step):
    senders, _, rows, across = arrived.shape
    start = tokens + fine
    width = (across - start) // 3
    fine_part = jnp.sum(arrived[:, :, :, tokens:start].astype(F32), axis=0)
    total = [fine_part[0] + fine_part[1]]
    for side in range(2):
        for at, block in enumerate((run, step)):
            values = arrived[:, side, :, start + at * width : start + (at + 1) * width]
            split = values.astype(F32).reshape(senders // (2 * block), 2, block, rows, width)
            halves = jnp.sum(jnp.sum(split, axis=2), axis=0)
            total.extend([halves[0], halves[1]])
        total.append(jnp.sum(arrived[:, side, :, start + 2 * width :].astype(F32), axis=0))
    total = jnp.concatenate(total, axis=1).astype(BF)
    spread[...] = jnp.broadcast_to(total[None], spread.shape)


def sums_kernel(
    group, own, other, fine_projection, fine_output, pool, projection, output, *, scaling
):
    features = fine_output.shape[0]
    wide = pool.shape[0]
    part = wide // 2
    width = wide // 4
    across = 3 * part // 2

    owns_low = group[0] == 0

    def lanes(side, start, count):
        here, there = own[:, :, start : start + count], other[:, :, start : start + count]
        low = owns_low if side == 0 else jnp.logical_not(owns_low)
        values = jnp.where(low, here, there).astype(F32) * scaling
        return values.reshape(own.shape[0] * own.shape[1], count)

    def start_of(heads):
        return features + heads * (across + 2 * width)

    for side in range(2):
        for heads in range(2):
            for k in range(3):
                column = side * across + k * width
                at, inner = column // part, column % part
                target = at * wide + heads * part + inner
                projection[:, target : target + width] = lanes(
                    side, start_of(heads) + k * width, width
                )
    projection.flush()
    for at, ref in enumerate((output, pool)):
        for side in range(2):
            for heads in range(2):
                block = lanes(side, start_of(heads) + across + at * width, width)
                for k in range(2):
                    column = (2 * side + k) * width
                    ref[heads * part : (heads + 1) * part, column : column + width] = block[
                        k * part : (k + 1) * part
                    ]
        ref.flush()
    for side in range(2):
        fine = lanes(side, 0, features)
        for k in range(2):
            at = 2 * side + k
            block = fine[k * features : (k + 1) * features]
            if at < 3:
                fine_projection[:, at * features : (at + 1) * features] = block
            else:
                fine_output[...] = block


def fine_backward_kernel(
    arrived,
    receive_slot,
    rotated,
    projected,
    mixture,
    weights,
    projection,
    output,
    send,
    grad_projected,
):
    place = one_hot(receive_slot[...], arrived.shape[0])
    gradient_in = mm(place, arrived[...], (0, 0))
    gradient_rows = gradient_in.astype(BF)
    features = rotated.shape[1]
    entering = mm(gradient_rows, output[...], (1, 1)).astype(BF)
    terms = [mm(mixture[...], gradient_rows, (0, 0))]
    balls = rotated.shape[0] // BALL
    pairs = features // PAIR
    for ball in range(balls):
        rows = slice(ball * BALL, (ball + 1) * BALL)
        for pair in range(pairs):
            lanes = slice(pair * PAIR, (pair + 1) * PAIR)
            query = projected[rows, lanes]
            key = projected[rows, features + pair * PAIR : features + (pair + 1) * PAIR]
            value = projected[rows, 2 * features + pair * PAIR : 2 * features + (pair + 1) * PAIR]
            enters = entering[rows, lanes]
            parts = ([], [], [])
            for half in range(2):
                head_weights = weights[(ball * pairs + pair) * 2 + half]
                against = mm(keep_half(enters, half), value, (1, 1))
                slopes = slopes_of(head_weights, against)
                parts[0].append(mm(slopes, key) * HD ** (-0.5))
                parts[1].append(mm(slopes, query, (0, 0)) * HD ** (-0.5))
                parts[2].append(mm(head_weights, enters, (0, 0)))
            for at, (low, high) in enumerate(parts):
                both = jnp.where(head_half(low.shape, 0), low, high).astype(BF)
                target = at * features + pair * PAIR
                grad_projected[rows, target : target + PAIR] = both
    normed, inverse = normalize(rotated[...])
    unit_rows = normed.astype(BF)
    for at in range(3):
        columns = slice(at * features, (at + 1) * features)
        terms.insert(at, mm(unit_rows, grad_projected[:, columns], (0, 0)))
    back = mm(grad_projected[...], projection[...], (1, 1))
    result = (gradient_in + norm_backward(back, normed, inverse)).astype(BF)
    tokens = mm(place, result)
    send[:, :, :, :features] = tokens.reshape(send.shape[:3] + (features,)).astype(BF)
    for side in range(2):
        put_blocks(send, side, features, jnp.concatenate(terms[2 * side : 2 * side + 2], axis=0))

def assemble_kernel(
    group, fine, kept, got_first, got_second, own_pack, other_pack, own_gradient, other_gradient, send
):
    start, width = fine.shape[3], got_first.shape[3]
    send[:, :, :, :start] = fine[...]
    for at, got in enumerate((got_first, got_second)):
        mine = kept[:, :, :, at * width : (at + 1) * width].astype(F32)
        send[:, :, :, start : start + width] = (mine + got[...].astype(F32)).astype(BF)
        start += width
    part = own_gradient.shape[1] // 2
    first = pl.multiple_of(group[0] * part, part)
    pool_term = mm(own_pack[:, pl.ds(first, part)], own_gradient[...], (0, 0))
    pool_term = pool_term + mm(other_pack[:, pl.ds(first, part)], other_gradient[...], (0, 0))
    put_quarters(send, start, pool_term)


def take_kernel(arrived, slots, rows_out):
    place = one_hot(slots[...], slots.shape[1] * 2)
    rows = arrived[...].reshape(place.shape[0], arrived.shape[-1])
    rows_out[...] = mm(place, rows, (0, 0)).astype(BF)


VMEM = pl.BlockSpec(memory_space=pltpu.VMEM)
SMEM = pl.BlockSpec(memory_space=pltpu.SMEM)
HBM = pl.BlockSpec(memory_space=pltpu.HBM)


class Far(NamedTuple):
    value: jax.Array


class Near(NamedTuple):
    shape: tuple
    dtype: jnp.dtype = BF
    far: bool = False


class Fetched:
    def __init__(self, source, buffer, semaphore):
        self.buffer, self.shape, self.waited = buffer, buffer.shape, False
        self.copy = pltpu.make_async_copy(source, buffer, semaphore)
        self.copy.start()

    def wait(self):
        if not self.waited:
            self.copy.wait()
            self.waited = True

    def __getitem__(self, index):
        self.wait()
        return self.buffer[index]


class Stored:
    def __init__(self, target, buffer, semaphore):
        self.buffer, self.shape, self.dtype, self.started = buffer, buffer.shape, buffer.dtype, False
        self.copy = pltpu.make_async_copy(buffer, target, semaphore)

    def __setitem__(self, index, values):
        self.buffer[index] = values

    def __getitem__(self, index):
        return self.buffer[index]

    def flush(self):
        if not self.started:
            self.copy.start()
            self.started = True


def call(kernel, inputs, outputs, scalar=False, scratch=(), mebibytes=16):
    in_specs, arrays, buffers = [], [], []
    for at, value in enumerate(inputs):
        far = isinstance(value, Far)
        in_specs.append(SMEM if scalar and at == 0 else HBM if far else VMEM)
        arrays.append(
            pltpu.with_memory_space_constraint(value.value, pltpu.HBM) if far else value
        )
        if far:
            buffers.append(pltpu.VMEM(value.value.shape, value.value.dtype))
    buffers.extend(pltpu.VMEM(out.shape, out.dtype) for out in outputs if out.far)
    flags = [isinstance(value, Far) for value in inputs] + [out.far for out in outputs]
    sizes = len(inputs), len(flags), len(flags) + len(buffers)

    def body(*refs):
        semaphores = refs[sizes[2]] if buffers else None
        given, views = 0, []
        for at, far in enumerate(flags):
            if far:
                kind = Fetched if at < sizes[0] else Stored
                views.append(kind(refs[at], refs[sizes[1] + given], semaphores.at[given]))
                given += 1
            else:
                views.append(refs[at])
        kernel(*views, *refs[sizes[2] + (1 if buffers else 0) :])
        for view in views:
            if isinstance(view, Stored):
                view.flush()
        for view in views:
            if isinstance(view, Fetched):
                view.wait()
            if isinstance(view, Stored):
                view.copy.wait()

    own = [pltpu.SemaphoreType.DMA((len(buffers),))] if buffers else []
    return pl.pallas_call(
        body,
        out_shape=[
            (pltpu.HBM if out.far else jax.ShapeDtypeStruct)(out.shape, out.dtype)
            for out in outputs
        ],
        in_specs=in_specs,
        out_specs=[HBM if out.far else VMEM for out in outputs],
        scratch_shapes=buffers + own + list(scratch),
        compiler_params=pltpu.CompilerParams(vmem_limit_bytes=mebibytes * 1024 * 1024),
    )(*arrays)


def exchange(values):
    return lax.ppermute(values, "grp", [(0, 1), (1, 0)])


def spread_blocks(values, axes):
    return lax.all_to_all(values, axes, split_axis=0, concat_axis=0, tiled=True)


def route(values, devices):
    rows, features = values.shape
    blocks = values.reshape(devices, rows // devices, features)
    return spread_blocks(blocks, ("pts", "grp")).reshape(rows, features)


def on_device(
    points,
    rotated_place,
    rotated_source,
    ball_counts,
    fine_projection,
    fine_output,
    pool_weight,
    coarse_projection,
    coarse_output,
    coarse_cotangent,
):
    count, features = points.shape
    devices = lax.axis_size(("pts", "grp"))
    slots = 2 * count
    scaling = 1.0 / math.sqrt(count * devices)
    group = lax.axis_index("grp").astype(jnp.int32).reshape(1)
    wide = 2 * features
    half_rows = count // 2

    send, send_slot, pair_slot, receive_slot, live = call(
        route_kernel,
        (
            Far(rotated_place.reshape(1, count)),
            Far(rotated_source.reshape(1, count)),
            Far(ball_counts.reshape(1, -1)),
            Far(points),
        ),
        (
            Near((slots, features)),
            Near((1, count), jnp.int32),
            Near((1, count), jnp.int32),
            Near((1, count), jnp.int32),
            Near((1, count), F32),
        ),
    )
    arrived = route(send, devices)
    heads = features // HD * (count // BALL)
    send, rotated, projected, mixture, weights = call(
        fine_forward_kernel,
        (arrived, receive_slot, live, Far(fine_projection), Far(fine_output)),
        (
            Near((slots, features)),
            Near((count, features)),
            Near((count, 3 * features)),
            Near((count, features)),
            Near((heads, BALL, BALL)),
        ),
    )
    arrived = route(send, devices)
    (own_pack,) = call(
        join_kernel, (arrived, pair_slot, coarse_cotangent), (Near((half_rows, 2 * wide)),)
    )
    other_pack = exchange(own_pack)
    coarse, keep, give, unit = call(
        coarse_kernel,
        (group, own_pack, other_pack, pool_weight, coarse_projection, coarse_output),
        (
            Near((half_rows, wide)),
            Near((half_rows, 2 * wide)),
            Near((half_rows, 2 * wide)),
            Near((count, wide)),
        ),
        scalar=True,
    )
    got = exchange(give)
    coarse_result, coarse_gradient, send = call(
        coarse_finish_kernel,
        (
            group,
            coarse,
            keep,
            got,
            coarse_cotangent,
            pool_weight,
            coarse_projection,
            coarse_output,
            pair_slot,
        ),
        (
            Near((half_rows, wide), far=True),
            Near((half_rows, wide)),
            Near((slots, features)),
        ),
        scalar=True,
    )
    arrived = route(send, devices)
    owners = lax.axis_size("pts")
    run, step = owners // 4, owners // 16
    place = lax.axis_index("pts").astype(jnp.int32)
    parity = jnp.stack([place // run % 2, place // step % 2])
    blocks = (owners, 2, slots // devices)
    kept, first_half, second_half, own_gradient = call(
        coarse_weights_kernel,
        (parity, arrived, unit, keep, give, own_pack, other_pack, coarse_gradient),
        (
            Near((*blocks, wide // 2)),
            Near((*blocks, wide // 4)),
            Near((*blocks, wide // 4)),
            Near((half_rows, wide)),
        ),
        scalar=True,
    )
    got_first = lax.ppermute(first_half, "pts", [(i, i ^ run) for i in range(owners)])
    got_second = lax.ppermute(second_half, "pts", [(i, i ^ step) for i in range(owners)])
    other_gradient = exchange(own_gradient)
    (fine,) = call(
        fine_backward_kernel,
        (
            arrived,
            receive_slot,
            rotated,
            projected,
            mixture,
            weights,
            fine_projection,
            fine_output,
        ),
        (Near((*blocks, 2 * features)),),
        scratch=(pltpu.VMEM((count, 3 * features), BF),),
    )
    across = 2 * features + 3 * wide // 4
    (send,) = call(
        assemble_kernel,
        (
            group,
            fine,
            kept,
            got_first,
            got_second,
            own_pack,
            other_pack,
            own_gradient,
            other_gradient,
        ),
        (Near((*blocks, across)),),
        scalar=True,
    )
    arrived = spread_blocks(send.reshape(devices, slots // devices, across), ("pts", "grp"))
    (spread,) = call(
        functools.partial(sum_kernel, tokens=features, fine=features, run=run, step=step),
        (arrived.reshape(send.shape),),
        (Near((owners, slots // devices, features + 5 * wide // 2)),),
    )
    own_sums = spread_blocks(spread, "pts")
    (points_gradient,) = call(
        take_kernel, (arrived[:, :, :features], send_slot), (Near((count, features)),)
    )
    other_sums = exchange(own_sums)
    sums = call(
        functools.partial(sums_kernel, scaling=scaling),
        (group, own_sums, other_sums),
        (
            Near((features, 3 * features), F32, far=True),
            Near((features, features), F32, far=True),
            Near((wide, wide), F32, far=True),
            Near((wide, 3 * wide), F32, far=True),
            Near((wide, wide), F32, far=True),
        ),
        scalar=True,
    )
    return (coarse_result, points_gradient, *sums)


def solution(mesh):
    tokens = P(("pts", "grp"), None)
    in_specs = (
        tokens,
        P(("pts", "grp")),
        P(("pts", "grp")),
        P(),
        P(),
        P(),
        P(),
        P(),
        P(),
        tokens,
    )
    out_specs = (tokens, tokens, P(), P(), P(), P(), P())
    return jax.shard_map(
        on_device, mesh=mesh, in_specs=in_specs, out_specs=out_specs, check_vma=False
    )
```

```python
import functools
import math
from typing import NamedTuple

import jax
import jax.numpy as jnp
from jax import lax
from jax.experimental import pallas as pl
from jax.experimental.pallas import tpu as pltpu
from jax.sharding import PartitionSpec as P

HD = 64
BALL = 256
PAIR = 2 * HD
EPSILON = 1e-05
BF = jnp.bfloat16
F32 = jnp.float32


def mm(a, b, contract=(1, 0)):
    return lax.dot_general(
        a, b, (((contract[0],), (contract[1],)), ((), ())), preferred_element_type=F32
    )


def normalize(values):
    floats = values.astype(F32)
    center = floats - jnp.mean(floats, axis=-1, keepdims=True)
    inverse = lax.rsqrt(jnp.mean(center * center, axis=-1, keepdims=True) + EPSILON)
    return center * inverse, inverse


def norm_backward(incoming, normed, inverse):
    first_mean = jnp.mean(incoming, axis=-1, keepdims=True)
    second_mean = jnp.mean(incoming * normed, axis=-1, keepdims=True)
    return inverse * (incoming - first_mean - normed * second_mean)


def one_hot(slots, total):
    shape = (total, slots.shape[1])
    return (lax.broadcasted_iota(jnp.int32, shape, 0) == slots).astype(BF)


def head_half(shape, half):
    lanes = lax.broadcasted_iota(jnp.int32, shape, 1)
    return (lanes < HD) if half == 0 else (lanes >= HD)


def keep_half(rows, half):
    return jnp.where(head_half(rows.shape, half), rows, jnp.zeros_like(rows))


def softmax_columns(scores):
    raised = jnp.exp(scores - jnp.max(scores, axis=0, keepdims=True))
    return (raised * (1.0 / jnp.sum(raised, axis=0, keepdims=True))).astype(BF)


def slopes_of(weights, against):
    wide = weights.astype(F32)
    diagonal = jnp.sum(wide * against, axis=0, keepdims=True)
    return (wide * (against - diagonal)).astype(BF)


def attend(query, key, value_turned, half, alive=None):
    scores = mm(key, scaled_half(query, half), (1, 1))
    if alive is not None:
        scores = jnp.where(alive, scores, -1e30)
    weights = softmax_columns(scores)
    return weights, mm(value_turned[half * HD : (half + 1) * HD], weights)


def attend_backward(query, key_turned, value, entering, weights, half):
    slopes = slopes_of(weights, mm(value, keep_half(entering, half), (1, 1)))
    query_part = mm(key_turned[half * HD : (half + 1) * HD], slopes) * HD ** (-0.5)
    key_part = mm(slopes, query) * HD ** (-0.5)
    return query_part, key_part, mm(weights, entering)


def pick_halves(low, high):
    return jnp.where(head_half(low.shape, 0), low, high).astype(BF)


def turned(rows):
    return rows.astype(F32).T.astype(BF)


def scaled_half(rows, half):
    return keep_half(rows * jnp.asarray(HD ** (-0.5), BF), half)


def column_of(row):
    count = row.shape[1]
    turned = jnp.broadcast_to(row.astype(F32), (128, count)).T
    return jnp.concatenate([turned] * (count // 128), axis=1)


def route_kernel(
    where, place, source, counts, points, send, send_slot, pair_slot, receive_slot, live
):
    count = place.shape[1]
    shift = count.bit_length() - 1
    capacity = send.shape[0] * count // (counts.shape[1] * BALL)
    to_row = place[...] >> shift
    rows = lax.broadcasted_iota(jnp.int32, (count, count), 0)
    columns = lax.broadcasted_iota(jnp.int32, (count, count), 1)
    earlier = (column_of(to_row) == to_row.astype(F32)) & (rows < columns)
    rank = jnp.sum(jnp.where(earlier, 1.0, 0.0), axis=0, keepdims=True)
    slot = to_row * capacity + rank.astype(jnp.int32)
    send_slot[...] = slot
    even_first = jnp.where(columns < count // 2, 2 * columns, 2 * columns + 1 - count)
    digits = jnp.concatenate([slot >> 5, slot & 31] + [jnp.zeros_like(slot)] * 6, axis=0)
    moved = mm(digits.astype(F32).astype(BF), (rows == even_first).astype(BF)).astype(jnp.int32)
    pair_slot[...] = moved[0:1] * 32 + moved[1:2]
    source_row = source[...]
    from_row = source_row >> shift
    earlier = (column_of(from_row) == from_row.astype(F32)) & (
        column_of(source_row) < source_row.astype(F32)
    )
    rank = jnp.sum(jnp.where(earlier, 1.0, 0.0), axis=0, keepdims=True)
    receive_slot[...] = from_row * capacity + rank.astype(jnp.int32)
    balls = counts.shape[1]
    own_ball = one_hot(source_row >> (BALL.bit_length() - 1), balls)
    filled = mm(jnp.broadcast_to(counts[...].astype(F32), (8, balls)).astype(BF), own_ball)
    inside = (source_row & (BALL - 1)).astype(F32)
    live[...] = jnp.where(inside < filled[:1], 1.0, 0.0)
    send[...] = mm(one_hot(slot, send.shape[0]), points[...]).astype(BF)


def fine_forward_kernel(
    arrived, receive_slot, live, projection, output, send, rotated, projected, mixture, weights
):
    place = one_hot(receive_slot[...], arrived.shape[0])
    rows_in = mm(place, arrived[...], (0, 0))
    rotated[...] = rows_in.astype(BF)
    features = rows_in.shape[1]
    normed, _ = normalize(rows_in)
    projected[...] = mm(normed.astype(BF), projection[...]).astype(BF)
    balls = rows_in.shape[0] // BALL
    pairs = features // PAIR
    alive = jnp.broadcast_to(live[...], (128, rows_in.shape[0])).T
    alive = jnp.concatenate([alive] * (BALL // 128), axis=1) > 0.5
    value_turned = turned(projected[:, 2 * features :])
    mixed = []
    for ball in range(balls):
        rows = slice(ball * BALL, (ball + 1) * BALL)
        pieces = []
        for pair in range(pairs):
            lanes = slice(pair * PAIR, (pair + 1) * PAIR)
            query = projected[rows, lanes]
            key = projected[rows, features + pair * PAIR : features + (pair + 1) * PAIR]
            for half in range(2):
                head_weights, piece = attend(
                    query, key, value_turned[lanes, rows], half, alive[rows]
                )
                weights[(ball * pairs + pair) * 2 + half] = head_weights
                pieces.append(piece)
        mixed.append(jnp.concatenate(pieces, axis=0))
    mixture[...] = jnp.concatenate(mixed, axis=1).T.astype(BF)
    result = (rows_in + mm(mixture[...], output[...])).astype(BF)
    send[...] = mm(place, result).astype(BF)


def join_kernel(arrived, pair_slot, cotangent, pack):
    half_rows, wide = cotangent.shape
    place = one_hot(pair_slot[...], arrived.shape[0])
    rows = mm(place, arrived[...], (0, 0)).astype(BF)
    pack[:, : wide // 2] = rows[:half_rows]
    pack[:, wide // 2 : wide] = rows[half_rows:]
    pack[:, wide:] = cotangent[...]


def coarse_kernel(
    group, own_pack, other_pack, pool, projection, output, coarse, keep, give, unit
):
    half_rows, wide = coarse.shape
    part = wide // 2
    first = pl.multiple_of(group[0] * part, part)
    joined = jnp.concatenate([own_pack[:, :wide], other_pack[:, :wide]], axis=0)
    tokens = mm(joined, pool[...]).astype(BF)
    coarse[...] = tokens[:half_rows]
    normed, _ = normalize(tokens)
    unit_rows = normed.astype(BF)
    unit[...] = unit_rows
    queries = mm(unit_rows, projection[:, pl.ds(first, part)]).astype(BF)
    keys = mm(unit_rows, projection[:, pl.ds(wide + first, part)]).astype(BF)
    values = mm(unit_rows, projection[:, pl.ds(2 * wide + first, part)]).astype(BF)
    cotangent = jnp.concatenate([own_pack[:, wide:], other_pack[:, wide:]], axis=0)
    incoming = mm(cotangent, output[pl.ds(first, part), :], (1, 1)).astype(BF)
    keys_turned, values_turned = turned(keys), turned(values)
    mixed, query_grads = [], []

    def put(at, rows):
        target = slice(at, at + rows.shape[1])
        keep[:, target] = rows[:half_rows]
        give[:, target] = rows[half_rows:]

    for pair in range(part // PAIR):
        lanes = slice(pair * PAIR, (pair + 1) * PAIR)
        query, key, value = queries[:, lanes], keys[:, lanes], values[:, lanes]
        entering = incoming[:, lanes]
        key_parts, value_parts = [], []
        for half in range(2):
            head_weights, piece = attend(query, key, values_turned[lanes], half)
            mixed.append(piece)
            query_part, key_part, value_part = attend_backward(
                query, keys_turned[lanes], value, entering, head_weights, half
            )
            query_grads.append(query_part)
            key_parts.append(key_part)
            value_parts.append(value_part)
        put(2 * part + pair * PAIR, pick_halves(*key_parts))
        put(3 * part + pair * PAIR, pick_halves(*value_parts))
    put(0, jnp.concatenate(mixed, axis=0).T.astype(BF))
    put(part, jnp.concatenate(query_grads, axis=0).T.astype(BF))


def coarse_finish_kernel(
    group,
    coarse,
    keep,
    got,
    cotangent,
    pool,
    projection,
    output,
    pair_slot,
    result,
    gradient,
    send,
):
    half_rows, wide = coarse.shape
    part = wide // 2
    mixed = coarse[...].astype(F32)
    back = jnp.zeros((half_rows, wide), F32)
    for source, index in ((keep, group[0]), (got, 1 - group[0])):
        first = pl.multiple_of(index * part, part)
        mixed = mixed + mm(source[:, :part], output[pl.ds(first, part), :])
        for at in range(3):
            back = back + mm(
                source[:, (at + 1) * part : (at + 2) * part],
                projection[:, pl.ds(at * wide + first, part)],
                (1, 1),
            )
    result[...] = mixed.astype(BF)
    result.flush()
    normed, inverse = normalize(coarse[...])
    gradient_rows = (
        cotangent[...].astype(F32) + norm_backward(back, normed, inverse)
    ).astype(BF)
    gradient[...] = gradient_rows
    fine = mm(gradient_rows, pool[...], (1, 1)).astype(BF)
    features = send.shape[1]
    stacked = jnp.concatenate([fine[:, :features], fine[:, features:]], axis=0)
    send[...] = mm(one_hot(pair_slot[...], send.shape[0]), stacked).astype(BF)


def coarse_weights_kernel(
    where,
    arrived,
    unit,
    keep,
    give,
    own_pack,
    other_pack,
    gradient,
    kept,
    first_half,
    second_half,
    gradient_out,
):
    wide = unit.shape[1]
    part = wide // 2
    stacked = jnp.concatenate([keep[...], give[...]], axis=0)
    cotangent = jnp.concatenate([own_pack[:, wide:], other_pack[:, wide:]], axis=0)
    projection_term = mm(unit[...], stacked[:, part:], (0, 0))
    output_term = mm(stacked[:, :part], cotangent, (0, 0))
    across = projection_term.shape[1] // 2
    width = wide // 4
    for side in range(2):
        stack = [output_term[:, (2 * side + k) * width : (2 * side + k + 1) * width] for k in range(2)]
        columns = projection_term[:, side * across : (side + 1) * across]
        terms = jnp.concatenate([columns, jnp.concatenate(stack, axis=0)], axis=1)
        for at, passed in enumerate((first_half, second_half)):
            low = terms[:, 2 * at * width : (2 * at + 1) * width]
            high = terms[:, (2 * at + 1) * width : (2 * at + 2) * width]
            upper = where[1 + at] == 1
            put_blocks(kept, side, at * width, jnp.where(upper, high, low))
            put_blocks(passed, side, 0, jnp.where(upper, low, high))
    gradient_out[...] = gradient[...]


def put_quarters(blocks, lane, term):
    width = term.shape[1] // 4
    for side in range(2):
        stack = [term[:, (2 * side + k) * width : (2 * side + k + 1) * width] for k in range(2)]
        put_blocks(blocks, side, lane, jnp.concatenate(stack, axis=0))


def put_blocks(blocks, side, lane, rows):
    owners, width = blocks.shape[0], rows.shape[1]
    pieces = rows.reshape(owners, rows.shape[0] // owners, width)
    blocks[:, side, :, lane : lane + width] = pieces.astype(BF)


def sum_kernel(arrived, spread, *, tokens, fine, run, step):
    senders, _, rows, across = arrived.shape
    start = tokens + fine
    width = (across - start) // 3
    fine_part = jnp.sum(arrived[:, :, :, tokens:start].astype(F32), axis=0)
    total = [fine_part[0] + fine_part[1]]
    for side in range(2):
        for at, block in enumerate((run, step)):
            values = arrived[:, side, :, start + at * width : start + (at + 1) * width]
            split = values.astype(F32).reshape(senders // (2 * block), 2, block, rows, width)
            halves = jnp.sum(jnp.sum(split, axis=2), axis=0)
            total.extend([halves[0], halves[1]])
        total.append(jnp.sum(arrived[:, side, :, start + 2 * width :].astype(F32), axis=0))
    total = jnp.concatenate(total, axis=1).astype(BF)
    spread[...] = jnp.broadcast_to(total[None], spread.shape)


def sums_kernel(
    group, own, other, fine_projection, fine_output, pool, projection, output, *, scaling
):
    features = fine_output.shape[0]
    wide = pool.shape[0]
    part = wide // 2
    width = wide // 4
    across = 3 * part // 2

    owns_low = group[0] == 0

    def lanes(side, start, count):
        here, there = own[:, :, start : start + count], other[:, :, start : start + count]
        low = owns_low if side == 0 else jnp.logical_not(owns_low)
        values = jnp.where(low, here, there).astype(F32) * scaling
        return values.reshape(own.shape[0] * own.shape[1], count)

    def start_of(heads):
        return features + heads * (across + 2 * width)

    for side in range(2):
        for heads in range(2):
            for k in range(3):
                column = side * across + k * width
                at, inner = column // part, column % part
                target = at * wide + heads * part + inner
                projection[:, target : target + width] = lanes(
                    side, start_of(heads) + k * width, width
                )
    projection.flush()
    for at, ref in enumerate((output, pool)):
        for side in range(2):
            for heads in range(2):
                block = lanes(side, start_of(heads) + across + at * width, width)
                for k in range(2):
                    column = (2 * side + k) * width
                    ref[heads * part : (heads + 1) * part, column : column + width] = block[
                        k * part : (k + 1) * part
                    ]
        ref.flush()
    for side in range(2):
        fine = lanes(side, 0, features)
        for k in range(2):
            at = 2 * side + k
            block = fine[k * features : (k + 1) * features]
            if at < 3:
                fine_projection[:, at * features : (at + 1) * features] = block
            else:
                fine_output[...] = block


def fine_backward_kernel(
    arrived,
    receive_slot,
    rotated,
    projected,
    mixture,
    weights,
    projection,
    output,
    send,
    grad_projected,
):
    place = one_hot(receive_slot[...], arrived.shape[0])
    gradient_in = mm(place, arrived[...], (0, 0))
    gradient_rows = gradient_in.astype(BF)
    features = rotated.shape[1]
    entering = mm(gradient_rows, output[...], (1, 1)).astype(BF)
    terms = [mm(mixture[...], gradient_rows, (0, 0))]
    balls = rotated.shape[0] // BALL
    pairs = features // PAIR
    key_turned = turned(projected[:, features : 2 * features])
    query_grads = []
    for ball in range(balls):
        rows = slice(ball * BALL, (ball + 1) * BALL)
        pieces = []
        for pair in range(pairs):
            lanes = slice(pair * PAIR, (pair + 1) * PAIR)
            query = projected[rows, lanes]
            value = projected[rows, 2 * features + pair * PAIR : 2 * features + (pair + 1) * PAIR]
            key_parts, value_parts = [], []
            for half in range(2):
                query_part, key_part, value_part = attend_backward(
                    query,
                    key_turned[lanes, rows],
                    value,
                    entering[rows, lanes],
                    weights[(ball * pairs + pair) * 2 + half],
                    half,
                )
                pieces.append(query_part)
                key_parts.append(key_part)
                value_parts.append(value_part)
            for at, halves in ((1, key_parts), (2, value_parts)):
                target = at * features + pair * PAIR
                grad_projected[rows, target : target + PAIR] = pick_halves(*halves)
        query_grads.append(jnp.concatenate(pieces, axis=0))
    grad_projected[:, :features] = jnp.concatenate(query_grads, axis=1).T.astype(BF)
    normed, inverse = normalize(rotated[...])
    unit_rows = normed.astype(BF)
    for at in range(3):
        columns = slice(at * features, (at + 1) * features)
        terms.insert(at, mm(unit_rows, grad_projected[:, columns], (0, 0)))
    back = mm(grad_projected[...], projection[...], (1, 1))
    result = (gradient_in + norm_backward(back, normed, inverse)).astype(BF)
    tokens = mm(place, result)
    send[:, :, :, :features] = tokens.reshape(send.shape[:3] + (features,)).astype(BF)
    for side in range(2):
        put_blocks(send, side, features, jnp.concatenate(terms[2 * side : 2 * side + 2], axis=0))

def assemble_kernel(
    group, fine, kept, got_first, got_second, own_pack, other_pack, own_gradient, other_gradient, send
):
    start, width = fine.shape[3], got_first.shape[3]
    send[:, :, :, :start] = fine[...]
    for at, got in enumerate((got_first, got_second)):
        mine = kept[:, :, :, at * width : (at + 1) * width].astype(F32)
        send[:, :, :, start : start + width] = (mine + got[...].astype(F32)).astype(BF)
        start += width
    part = own_gradient.shape[1] // 2
    first = pl.multiple_of(group[0] * part, part)
    pool_term = mm(own_pack[:, pl.ds(first, part)], own_gradient[...], (0, 0))
    pool_term = pool_term + mm(other_pack[:, pl.ds(first, part)], other_gradient[...], (0, 0))
    put_quarters(send, start, pool_term)


def take_kernel(arrived, slots, rows_out):
    place = one_hot(slots[...], slots.shape[1] * 2)
    rows = arrived[...].reshape(place.shape[0], arrived.shape[-1])
    rows_out[...] = mm(place, rows, (0, 0)).astype(BF)


VMEM = pl.BlockSpec(memory_space=pltpu.VMEM)
SMEM = pl.BlockSpec(memory_space=pltpu.SMEM)
HBM = pl.BlockSpec(memory_space=pltpu.HBM)


class Far(NamedTuple):
    value: jax.Array


class Near(NamedTuple):
    shape: tuple
    dtype: jnp.dtype = BF
    far: bool = False


class Fetched:
    def __init__(self, source, buffer, semaphore):
        self.buffer, self.shape, self.waited = buffer, buffer.shape, False
        self.copy = pltpu.make_async_copy(source, buffer, semaphore)
        self.copy.start()

    def wait(self):
        if not self.waited:
            self.copy.wait()
            self.waited = True

    def __getitem__(self, index):
        self.wait()
        return self.buffer[index]


class Stored:
    def __init__(self, target, buffer, semaphore):
        self.buffer, self.shape, self.dtype, self.started = buffer, buffer.shape, buffer.dtype, False
        self.copy = pltpu.make_async_copy(buffer, target, semaphore)

    def __setitem__(self, index, values):
        self.buffer[index] = values

    def __getitem__(self, index):
        return self.buffer[index]

    def flush(self):
        if not self.started:
            self.copy.start()
            self.started = True


def call(kernel, inputs, outputs, scalar=False, scratch=(), mebibytes=16):
    in_specs, arrays, buffers = [], [], []
    for at, value in enumerate(inputs):
        far = isinstance(value, Far)
        in_specs.append(SMEM if scalar and at == 0 else HBM if far else VMEM)
        arrays.append(
            pltpu.with_memory_space_constraint(value.value, pltpu.HBM) if far else value
        )
        if far:
            buffers.append(pltpu.VMEM(value.value.shape, value.value.dtype))
    buffers.extend(pltpu.VMEM(out.shape, out.dtype) for out in outputs if out.far)
    flags = [isinstance(value, Far) for value in inputs] + [out.far for out in outputs]
    sizes = len(inputs), len(flags), len(flags) + len(buffers)

    def body(*refs):
        semaphores = refs[sizes[2]] if buffers else None
        given, views = 0, []
        for at, far in enumerate(flags):
            if far:
                kind = Fetched if at < sizes[0] else Stored
                views.append(kind(refs[at], refs[sizes[1] + given], semaphores.at[given]))
                given += 1
            else:
                views.append(refs[at])
        kernel(*views, *refs[sizes[2] + (1 if buffers else 0) :])
        for view in views:
            if isinstance(view, Stored):
                view.flush()
        for view in views:
            if isinstance(view, Fetched):
                view.wait()
            if isinstance(view, Stored):
                view.copy.wait()

    own = [pltpu.SemaphoreType.DMA((len(buffers),))] if buffers else []
    return pl.pallas_call(
        body,
        out_shape=[
            (pltpu.HBM if out.far else jax.ShapeDtypeStruct)(out.shape, out.dtype)
            for out in outputs
        ],
        in_specs=in_specs,
        out_specs=[HBM if out.far else VMEM for out in outputs],
        scratch_shapes=buffers + own + list(scratch),
        compiler_params=pltpu.CompilerParams(vmem_limit_bytes=mebibytes * 1024 * 1024),
    )(*arrays)


def exchange(values):
    return lax.ppermute(values, "grp", [(0, 1), (1, 0)])


def spread_blocks(values, axes):
    return lax.all_to_all(values, axes, split_axis=0, concat_axis=0, tiled=True)


def route(values, devices):
    rows, features = values.shape
    blocks = values.reshape(devices, rows // devices, features)
    return spread_blocks(blocks, ("pts", "grp")).reshape(rows, features)


def on_device(
    points,
    rotated_place,
    rotated_source,
    ball_counts,
    fine_projection,
    fine_output,
    pool_weight,
    coarse_projection,
    coarse_output,
    coarse_cotangent,
):
    count, features = points.shape
    devices = lax.axis_size(("pts", "grp"))
    slots = 2 * count
    scaling = 1.0 / math.sqrt(count * devices)
    owners = lax.axis_size("pts")
    run, step = owners // 4, owners // 16
    chip = lax.axis_index("pts")
    group = jnp.stack([lax.axis_index("grp"), chip // run % 2, chip // step % 2]).astype(jnp.int32)
    wide = 2 * features
    half_rows = count // 2

    send, send_slot, pair_slot, receive_slot, live = call(
        route_kernel,
        (
            group,
            Far(rotated_place.reshape(1, count)),
            Far(rotated_source.reshape(1, count)),
            Far(ball_counts.reshape(1, -1)),
            Far(points),
        ),
        (
            Near((slots, features)),
            Near((1, count), jnp.int32),
            Near((1, count), jnp.int32),
            Near((1, count), jnp.int32),
            Near((1, count), F32),
        ),
        scalar=True,
    )
    arrived = route(send, devices)
    heads = features // HD * (count // BALL)
    send, rotated, projected, mixture, weights = call(
        fine_forward_kernel,
        (arrived, receive_slot, live, fine_projection, Far(fine_output)),
        (
            Near((slots, features)),
            Near((count, features)),
            Near((count, 3 * features)),
            Near((count, features)),
            Near((heads, BALL, BALL)),
        ),
    )
    arrived = route(send, devices)
    (own_pack,) = call(
        join_kernel, (arrived, pair_slot, coarse_cotangent), (Near((half_rows, 2 * wide)),)
    )
    other_pack = exchange(own_pack)
    coarse, keep, give, unit = call(
        coarse_kernel,
        (group, own_pack, other_pack, pool_weight, coarse_projection, Far(coarse_output)),
        (
            Near((half_rows, wide)),
            Near((half_rows, 2 * wide)),
            Near((half_rows, 2 * wide)),
            Near((count, wide)),
        ),
        scalar=True,
    )
    got = exchange(give)
    coarse_result, coarse_gradient, send = call(
        coarse_finish_kernel,
        (
            group,
            coarse,
            keep,
            got,
            coarse_cotangent,
            pool_weight,
            coarse_projection,
            coarse_output,
            pair_slot,
        ),
        (
            Near((half_rows, wide), far=True),
            Near((half_rows, wide)),
            Near((slots, features)),
        ),
        scalar=True,
    )
    arrived = route(send, devices)
    blocks = (owners, 2, slots // devices)
    kept, first_half, second_half, own_gradient = call(
        coarse_weights_kernel,
        (group, arrived, unit, keep, give, own_pack, other_pack, coarse_gradient),
        (
            Near((*blocks, wide // 2)),
            Near((*blocks, wide // 4)),
            Near((*blocks, wide // 4)),
            Near((half_rows, wide)),
        ),
        scalar=True,
    )
    got_first = lax.ppermute(first_half, "pts", [(i, i ^ run) for i in range(owners)])
    got_second = lax.ppermute(second_half, "pts", [(i, i ^ step) for i in range(owners)])
    other_gradient = exchange(own_gradient)
    (fine,) = call(
        fine_backward_kernel,
        (
            arrived,
            receive_slot,
            rotated,
            projected,
            mixture,
            weights,
            fine_projection,
            fine_output,
        ),
        (Near((*blocks, 2 * features)),),
        scratch=(pltpu.VMEM((count, 3 * features), BF),),
    )
    across = 2 * features + 3 * wide // 4
    (send,) = call(
        assemble_kernel,
        (
            group,
            fine,
            kept,
            got_first,
            got_second,
            own_pack,
            other_pack,
            own_gradient,
            other_gradient,
        ),
        (Near((*blocks, across)),),
        scalar=True,
    )
    arrived = spread_blocks(send.reshape(devices, slots // devices, across), ("pts", "grp"))
    (spread,) = call(
        functools.partial(sum_kernel, tokens=features, fine=features, run=run, step=step),
        (arrived.reshape(send.shape),),
        (Near((owners, slots // devices, features + 5 * wide // 2)),),
    )
    own_sums = spread_blocks(spread, "pts")
    (points_gradient,) = call(
        take_kernel, (arrived[:, :, :features], send_slot), (Near((count, features)),)
    )
    other_sums = exchange(own_sums)
    sums = call(
        functools.partial(sums_kernel, scaling=scaling),
        (group, own_sums, other_sums),
        (
            Near((features, 3 * features), F32, far=True),
            Near((features, features), F32, far=True),
            Near((wide, wide), F32, far=True),
            Near((wide, 3 * wide), F32, far=True),
            Near((wide, wide), F32, far=True),
        ),
        scalar=True,
    )
    return (coarse_result, points_gradient, *sums)


def solution(mesh):
    tokens = P(("pts", "grp"), None)
    in_specs = (
        tokens,
        P(("pts", "grp")),
        P(("pts", "grp")),
        P(),
        P(),
        P(),
        P(),
        P(),
        P(),
        tokens,
    )
    out_specs = (tokens, tokens, P(), P(), P(), P(), P())
    return jax.shard_map(
        on_device, mesh=mesh, in_specs=in_specs, out_specs=out_specs, check_vma=False
    )
```

```python
import functools
import math
from typing import NamedTuple

import jax
import jax.numpy as jnp
from jax import lax
from jax.experimental import pallas as pl
from jax.experimental.pallas import tpu as pltpu
from jax.sharding import PartitionSpec as P

HD = 64
BALL = 256
PAIR = 2 * HD
EPSILON = 1e-05
BF = jnp.bfloat16
F32 = jnp.float32


def mm(a, b, contract=(1, 0)):
    return lax.dot_general(
        a, b, (((contract[0],), (contract[1],)), ((), ())), preferred_element_type=F32
    )


def normalize(values):
    floats = values.astype(F32)
    center = floats - jnp.mean(floats, axis=-1, keepdims=True)
    inverse = lax.rsqrt(jnp.mean(center * center, axis=-1, keepdims=True) + EPSILON)
    return center * inverse, inverse


def norm_backward(incoming, normed, inverse):
    first_mean = jnp.mean(incoming, axis=-1, keepdims=True)
    second_mean = jnp.mean(incoming * normed, axis=-1, keepdims=True)
    return inverse * (incoming - first_mean - normed * second_mean)


def one_hot(slots, total):
    shape = (total, slots.shape[1])
    return (lax.broadcasted_iota(jnp.int32, shape, 0) == slots).astype(BF)


def head_half(shape, half):
    lanes = lax.broadcasted_iota(jnp.int32, shape, 1)
    return (lanes < HD) if half == 0 else (lanes >= HD)


def keep_half(rows, half):
    return jnp.where(head_half(rows.shape, half), rows, jnp.zeros_like(rows))


def softmax_rows(scores):
    raised = jnp.exp(scores - jnp.max(scores, axis=-1, keepdims=True))
    return (raised * (1.0 / jnp.sum(raised, axis=-1, keepdims=True))).astype(BF)


def slopes_of(weights, against):
    wide = weights.astype(F32)
    diagonal = jnp.sum(wide * against, axis=-1, keepdims=True)
    return (wide * (against - diagonal)).astype(BF)


def scaled_half(rows, half):
    return keep_half(rows * jnp.asarray(HD ** (-0.5), BF), half)


def column_of(row):
    count = row.shape[1]
    turned = jnp.broadcast_to(row.astype(F32), (128, count)).T
    return jnp.concatenate([turned] * (count // 128), axis=1)


def route_kernel(
    place, source, counts, points, send, send_slot, pair_slot, receive_slot, live
):
    count = place.shape[1]
    shift = count.bit_length() - 1
    capacity = send.shape[0] * count // (counts.shape[1] * BALL)
    to_row = place[...] >> shift
    rows = lax.broadcasted_iota(jnp.int32, (count, count), 0)
    columns = lax.broadcasted_iota(jnp.int32, (count, count), 1)
    earlier = (column_of(to_row) == to_row.astype(F32)) & (rows < columns)
    rank = jnp.sum(jnp.where(earlier, 1.0, 0.0), axis=0, keepdims=True)
    slot = to_row * capacity + rank.astype(jnp.int32)
    send_slot[...] = slot
    even_first = jnp.where(columns < count // 2, 2 * columns, 2 * columns + 1 - count)
    digits = jnp.concatenate([slot >> 5, slot & 31] + [jnp.zeros_like(slot)] * 6, axis=0)
    moved = mm(digits.astype(F32).astype(BF), (rows == even_first).astype(BF)).astype(jnp.int32)
    pair_slot[...] = moved[0:1] * 32 + moved[1:2]
    source_row = source[...]
    from_row = source_row >> shift
    earlier = (column_of(from_row) == from_row.astype(F32)) & (
        column_of(source_row) < source_row.astype(F32)
    )
    rank = jnp.sum(jnp.where(earlier, 1.0, 0.0), axis=0, keepdims=True)
    receive_slot[...] = from_row * capacity + rank.astype(jnp.int32)
    balls = counts.shape[1]
    own_ball = one_hot(source_row >> (BALL.bit_length() - 1), balls)
    filled = mm(jnp.broadcast_to(counts[...].astype(F32), (8, balls)).astype(BF), own_ball)
    inside = (source_row & (BALL - 1)).astype(F32)
    live[...] = jnp.where(inside < filled[:1], 1.0, 0.0)
    send[...] = mm(one_hot(slot, send.shape[0]), points[...]).astype(BF)


def fine_forward_kernel(
    arrived, receive_slot, live, projection, output, send, rotated, projected, mixture, weights
):
    place = one_hot(receive_slot[...], arrived.shape[0])
    rows_in = mm(place, arrived[...], (0, 0))
    rotated[...] = rows_in.astype(BF)
    features = rows_in.shape[1]
    normed, _ = normalize(rows_in)
    projected[...] = mm(normed.astype(BF), projection[...]).astype(BF)
    balls = rows_in.shape[0] // BALL
    pairs = features // PAIR
    for ball in range(balls):
        rows = slice(ball * BALL, (ball + 1) * BALL)
        alive = live[:, rows] > 0.5
        for pair in range(pairs):
            lanes = slice(pair * PAIR, (pair + 1) * PAIR)
            query = projected[rows, lanes]
            key = projected[rows, features + pair * PAIR : features + (pair + 1) * PAIR]
            value = projected[rows, 2 * features + pair * PAIR : 2 * features + (pair + 1) * PAIR]
            halves = []
            for half in range(2):
                scores = mm(scaled_half(query, half), key, (1, 1))
                head_weights = softmax_rows(jnp.where(alive, scores, -1e30))
                weights[(ball * pairs + pair) * 2 + half] = head_weights
                halves.append(mm(head_weights, value))
            mixed = jnp.where(head_half(halves[0].shape, 0), halves[0], halves[1])
            mixture[rows, lanes] = mixed.astype(BF)
    result = (rows_in + mm(mixture[...], output[...])).astype(BF)
    send[...] = mm(place, result).astype(BF)


def join_kernel(arrived, pair_slot, cotangent, pack):
    half_rows, wide = cotangent.shape
    place = one_hot(pair_slot[...], arrived.shape[0])
    rows = mm(place, arrived[...], (0, 0)).astype(BF)
    pack[:, : wide // 2] = rows[:half_rows]
    pack[:, wide // 2 : wide] = rows[half_rows:]
    pack[:, wide:] = cotangent[...]


def coarse_kernel(
    own_pack, other_pack, pool, projection, output, coarse, keep, give, unit
):
    half_rows, wide = coarse.shape
    part = wide // 2
    first = pl.multiple_of(lax.axis_index("grp") * part, part)
    joined = jnp.concatenate([own_pack[:, :wide], other_pack[:, :wide]], axis=0)
    tokens = mm(joined, pool[...]).astype(BF)
    coarse[...] = tokens[:half_rows]
    normed, _ = normalize(tokens)
    unit_rows = normed.astype(BF)
    unit[...] = unit_rows
    queries = mm(unit_rows, projection[:, pl.ds(first, part)]).astype(BF)
    keys = mm(unit_rows, projection[:, pl.ds(wide + first, part)]).astype(BF)
    values = mm(unit_rows, projection[:, pl.ds(2 * wide + first, part)]).astype(BF)
    cotangent = jnp.concatenate([own_pack[:, wide:], other_pack[:, wide:]], axis=0)
    incoming = mm(cotangent, output[pl.ds(first, part), :], (1, 1)).astype(BF)
    for pair in range(part // PAIR):
        lanes = slice(pair * PAIR, (pair + 1) * PAIR)
        query, key, value = queries[:, lanes], keys[:, lanes], values[:, lanes]
        entering = incoming[:, lanes]
        parts = ([], [], [], [])
        for half in range(2):
            scores = mm(scaled_half(query, half), key, (1, 1))
            head_weights = softmax_rows(scores)
            parts[0].append(mm(head_weights, value))
            against = mm(keep_half(entering, half), value, (1, 1))
            slopes = slopes_of(head_weights, against)
            parts[1].append(mm(slopes, key) * HD ** (-0.5))
            parts[2].append(mm(slopes, query, (0, 0)) * HD ** (-0.5))
            parts[3].append(mm(head_weights, entering, (0, 0)))
        for at, (low, high) in enumerate(parts):
            both = jnp.where(head_half(low.shape, 0), low, high).astype(BF)
            target = slice(at * part + pair * PAIR, at * part + (pair + 1) * PAIR)
            keep[:, target] = both[:half_rows]
            give[:, target] = both[half_rows:]


def coarse_finish_kernel(
    coarse,
    keep,
    got,
    cotangent,
    pool,
    projection,
    output,
    pair_slot,
    result,
    gradient,
    send,
):
    half_rows, wide = coarse.shape
    part = wide // 2
    mixed = coarse[...].astype(F32)
    back = jnp.zeros((half_rows, wide), F32)
    for source, index in ((keep, lax.axis_index("grp")), (got, 1 - lax.axis_index("grp"))):
        first = pl.multiple_of(index * part, part)
        mixed = mixed + mm(source[:, :part], output[pl.ds(first, part), :])
        for at in range(3):
            back = back + mm(
                source[:, (at + 1) * part : (at + 2) * part],
                projection[:, pl.ds(at * wide + first, part)],
                (1, 1),
            )
    result[...] = mixed.astype(BF)
    result.flush()
    normed, inverse = normalize(coarse[...])
    gradient_rows = (
        cotangent[...].astype(F32) + norm_backward(back, normed, inverse)
    ).astype(BF)
    gradient[...] = gradient_rows
    fine = mm(gradient_rows, pool[...], (1, 1)).astype(BF)
    features = send.shape[1]
    stacked = jnp.concatenate([fine[:, :features], fine[:, features:]], axis=0)
    send[...] = mm(one_hot(pair_slot[...], send.shape[0]), stacked).astype(BF)


def coarse_weights_kernel(
    arrived,
    unit,
    keep,
    give,
    own_pack,
    other_pack,
    gradient,
    kept,
    first_half,
    second_half,
    gradient_out,
    *,
    strides,
):
    chip = lax.axis_index("pts")
    wide = unit.shape[1]
    part = wide // 2
    stacked = jnp.concatenate([keep[...], give[...]], axis=0)
    cotangent = jnp.concatenate([own_pack[:, wide:], other_pack[:, wide:]], axis=0)
    projection_term = mm(unit[...], stacked[:, part:], (0, 0))
    output_term = mm(stacked[:, :part], cotangent, (0, 0))
    across = projection_term.shape[1] // 2
    width = wide // 4
    for side in range(2):
        stack = [output_term[:, (2 * side + k) * width : (2 * side + k + 1) * width] for k in range(2)]
        columns = projection_term[:, side * across : (side + 1) * across]
        terms = jnp.concatenate([columns, jnp.concatenate(stack, axis=0)], axis=1)
        for at, passed in enumerate((first_half, second_half)):
            low = terms[:, 2 * at * width : (2 * at + 1) * width]
            high = terms[:, (2 * at + 1) * width : (2 * at + 2) * width]
            upper = chip // strides[at] % 2 == 1
            put_blocks(kept, side, at * width, jnp.where(upper, high, low))
            put_blocks(passed, side, 0, jnp.where(upper, low, high))
    gradient_out[...] = gradient[...]


def put_quarters(blocks, lane, term):
    width = term.shape[1] // 4
    for side in range(2):
        stack = [term[:, (2 * side + k) * width : (2 * side + k + 1) * width] for k in range(2)]
        put_blocks(blocks, side, lane, jnp.concatenate(stack, axis=0))


def put_blocks(blocks, side, lane, rows):
    owners, width = blocks.shape[0], rows.shape[1]
    pieces = rows.reshape(owners, rows.shape[0] // owners, width)
    blocks[:, side, :, lane : lane + width] = pieces.astype(BF)


def sum_kernel(arrived, spread, *, tokens, fine, run, step):
    senders, _, rows, across = arrived.shape
    start = tokens + fine
    width = (across - start) // 3
    fine_part = jnp.sum(arrived[:, :, :, tokens:start].astype(F32), axis=0)
    total = [fine_part[0] + fine_part[1]]
    for side in range(2):
        for at, block in enumerate((run, step)):
            values = arrived[:, side, :, start + at * width : start + (at + 1) * width]
            split = values.astype(F32).reshape(senders // (2 * block), 2, block, rows, width)
            halves = jnp.sum(jnp.sum(split, axis=2), axis=0)
            total.extend([halves[0], halves[1]])
        total.append(jnp.sum(arrived[:, side, :, start + 2 * width :].astype(F32), axis=0))
    total = jnp.concatenate(total, axis=1).astype(BF)
    spread[...] = jnp.broadcast_to(total[None], spread.shape)


def sums_kernel(
    own, other, fine_projection, fine_output, pool, projection, output, *, scaling
):
    features = fine_output.shape[0]
    wide = pool.shape[0]
    part = wide // 2
    width = wide // 4
    across = 3 * part // 2

    owns_low = lax.axis_index("grp") == 0

    def lanes(side, start, count):
        here, there = own[:, :, start : start + count], other[:, :, start : start + count]
        low = owns_low if side == 0 else jnp.logical_not(owns_low)
        values = jnp.where(low, here, there).astype(F32) * scaling
        return values.reshape(own.shape[0] * own.shape[1], count)

    def start_of(heads):
        return features + heads * (across + 2 * width)

    for side in range(2):
        for heads in range(2):
            for k in range(3):
                column = side * across + k * width
                at, inner = column // part, column % part
                target = at * wide + heads * part + inner
                projection[:, target : target + width] = lanes(
                    side, start_of(heads) + k * width, width
                )
    projection.flush()
    for at, ref in enumerate((output, pool)):
        for side in range(2):
            for heads in range(2):
                block = lanes(side, start_of(heads) + across + at * width, width)
                for k in range(2):
                    column = (2 * side + k) * width
                    ref[heads * part : (heads + 1) * part, column : column + width] = block[
                        k * part : (k + 1) * part
                    ]
        ref.flush()
    for side in range(2):
        fine = lanes(side, 0, features)
        for k in range(2):
            at = 2 * side + k
            block = fine[k * features : (k + 1) * features]
            if at < 3:
                fine_projection[:, at * features : (at + 1) * features] = block
            else:
                fine_output[...] = block


def fine_backward_kernel(
    arrived,
    receive_slot,
    rotated,
    projected,
    mixture,
    weights,
    projection,
    output,
    send,
    grad_projected,
):
    place = one_hot(receive_slot[...], arrived.shape[0])
    gradient_in = mm(place, arrived[...], (0, 0))
    gradient_rows = gradient_in.astype(BF)
    features = rotated.shape[1]
    entering = mm(gradient_rows, output[...], (1, 1)).astype(BF)
    terms = [mm(mixture[...], gradient_rows, (0, 0))]
    balls = rotated.shape[0] // BALL
    pairs = features // PAIR
    for ball in range(balls):
        rows = slice(ball * BALL, (ball + 1) * BALL)
        for pair in range(pairs):
            lanes = slice(pair * PAIR, (pair + 1) * PAIR)
            query = projected[rows, lanes]
            key = projected[rows, features + pair * PAIR : features + (pair + 1) * PAIR]
            value = projected[rows, 2 * features + pair * PAIR : 2 * features + (pair + 1) * PAIR]
            enters = entering[rows, lanes]
            parts = ([], [], [])
            for half in range(2):
                head_weights = weights[(ball * pairs + pair) * 2 + half]
                against = mm(keep_half(enters, half), value, (1, 1))
                slopes = slopes_of(head_weights, against)
                parts[0].append(mm(slopes, key) * HD ** (-0.5))
                parts[1].append(mm(slopes, query, (0, 0)) * HD ** (-0.5))
                parts[2].append(mm(head_weights, enters, (0, 0)))
            for at, (low, high) in enumerate(parts):
                both = jnp.where(head_half(low.shape, 0), low, high).astype(BF)
                target = at * features + pair * PAIR
                grad_projected[rows, target : target + PAIR] = both
    normed, inverse = normalize(rotated[...])
    unit_rows = normed.astype(BF)
    for at in range(3):
        columns = slice(at * features, (at + 1) * features)
        terms.insert(at, mm(unit_rows, grad_projected[:, columns], (0, 0)))
    back = mm(grad_projected[...], projection[...], (1, 1))
    result = (gradient_in + norm_backward(back, normed, inverse)).astype(BF)
    tokens = mm(place, result)
    send[:, :, :, :features] = tokens.reshape(send.shape[:3] + (features,)).astype(BF)
    for side in range(2):
        put_blocks(send, side, features, jnp.concatenate(terms[2 * side : 2 * side + 2], axis=0))

def assemble_kernel(
    fine, kept, got_first, got_second, own_pack, other_pack, own_gradient, other_gradient, send
):
    start, width = fine.shape[3], got_first.shape[3]
    send[:, :, :, :start] = fine[...]
    for at, got in enumerate((got_first, got_second)):
        mine = kept[:, :, :, at * width : (at + 1) * width].astype(F32)
        send[:, :, :, start : start + width] = (mine + got[...].astype(F32)).astype(BF)
        start += width
    part = own_gradient.shape[1] // 2
    first = pl.multiple_of(lax.axis_index("grp") * part, part)
    pool_term = mm(own_pack[:, pl.ds(first, part)], own_gradient[...], (0, 0))
    pool_term = pool_term + mm(other_pack[:, pl.ds(first, part)], other_gradient[...], (0, 0))
    put_quarters(send, start, pool_term)


def take_kernel(arrived, slots, rows_out):
    place = one_hot(slots[...], slots.shape[1] * 2)
    rows = arrived[...].reshape(place.shape[0], arrived.shape[-1])
    rows_out[...] = mm(place, rows, (0, 0)).astype(BF)


VMEM = pl.BlockSpec(memory_space=pltpu.VMEM)
HBM = pl.BlockSpec(memory_space=pltpu.HBM)


class Far(NamedTuple):
    value: jax.Array


class Near(NamedTuple):
    shape: tuple
    dtype: jnp.dtype = BF
    far: bool = False


class Fetched:
    def __init__(self, source, buffer, semaphore):
        self.buffer, self.shape, self.waited = buffer, buffer.shape, False
        self.copy = pltpu.make_async_copy(source, buffer, semaphore)
        self.copy.start()

    def wait(self):
        if not self.waited:
            self.copy.wait()
            self.waited = True

    def __getitem__(self, index):
        self.wait()
        return self.buffer[index]


class Stored:
    def __init__(self, target, buffer, semaphore):
        self.buffer, self.shape, self.dtype, self.started = buffer, buffer.shape, buffer.dtype, False
        self.copy = pltpu.make_async_copy(buffer, target, semaphore)

    def __setitem__(self, index, values):
        self.buffer[index] = values

    def __getitem__(self, index):
        return self.buffer[index]

    def flush(self):
        if not self.started:
            self.copy.start()
            self.started = True


def call(kernel, inputs, outputs, scratch=(), mebibytes=16):
    in_specs, arrays, buffers = [], [], []
    for value in inputs:
        far = isinstance(value, Far)
        in_specs.append(HBM if far else VMEM)
        arrays.append(
            pltpu.with_memory_space_constraint(value.value, pltpu.HBM) if far else value
        )
        if far:
            buffers.append(pltpu.VMEM(value.value.shape, value.value.dtype))
    buffers.extend(pltpu.VMEM(out.shape, out.dtype) for out in outputs if out.far)
    flags = [isinstance(value, Far) for value in inputs] + [out.far for out in outputs]
    sizes = len(inputs), len(flags), len(flags) + len(buffers)

    def body(*refs):
        semaphores = refs[sizes[2]] if buffers else None
        given, views = 0, []
        for at, far in enumerate(flags):
            if far:
                kind = Fetched if at < sizes[0] else Stored
                views.append(kind(refs[at], refs[sizes[1] + given], semaphores.at[given]))
                given += 1
            else:
                views.append(refs[at])
        kernel(*views, *refs[sizes[2] + (1 if buffers else 0) :])
        for view in views:
            if isinstance(view, Stored):
                view.flush()
        for view in views:
            if isinstance(view, Fetched):
                view.wait()
            if isinstance(view, Stored):
                view.copy.wait()

    own = [pltpu.SemaphoreType.DMA((len(buffers),))] if buffers else []
    return pl.pallas_call(
        body,
        out_shape=[
            (pltpu.HBM if out.far else jax.ShapeDtypeStruct)(out.shape, out.dtype)
            for out in outputs
        ],
        in_specs=in_specs,
        out_specs=[HBM if out.far else VMEM for out in outputs],
        scratch_shapes=buffers + own + list(scratch),
        compiler_params=pltpu.CompilerParams(vmem_limit_bytes=mebibytes * 1024 * 1024),
    )(*arrays)


def exchange(values):
    return lax.ppermute(values, "grp", [(0, 1), (1, 0)])


def spread_blocks(values, axes):
    return lax.all_to_all(values, axes, split_axis=0, concat_axis=0, tiled=True)


def route(values, devices):
    rows, features = values.shape
    blocks = values.reshape(devices, rows // devices, features)
    return spread_blocks(blocks, ("pts", "grp")).reshape(rows, features)


def on_device(
    points,
    rotated_place,
    rotated_source,
    ball_counts,
    fine_projection,
    fine_output,
    pool_weight,
    coarse_projection,
    coarse_output,
    coarse_cotangent,
):
    count, features = points.shape
    devices = lax.axis_size(("pts", "grp"))
    slots = 2 * count
    scaling = 1.0 / math.sqrt(count * devices)
    owners = lax.axis_size("pts")
    run, step = owners // 4, owners // 16
    wide = 2 * features
    half_rows = count // 2

    send, send_slot, pair_slot, receive_slot, live = call(
        route_kernel,
        (
            Far(rotated_place.reshape(1, count)),
            Far(rotated_source.reshape(1, count)),
            Far(ball_counts.reshape(1, -1)),
            Far(points),
        ),
        (
            Near((slots, features)),
            Near((1, count), jnp.int32),
            Near((1, count), jnp.int32),
            Near((1, count), jnp.int32),
            Near((1, count), F32),
        ),
    )
    arrived = route(send, devices)
    heads = features // HD * (count // BALL)
    send, rotated, projected, mixture, weights = call(
        fine_forward_kernel,
        (arrived, receive_slot, live, fine_projection, Far(fine_output)),
        (
            Near((slots, features)),
            Near((count, features)),
            Near((count, 3 * features)),
            Near((count, features)),
            Near((heads, BALL, BALL)),
        ),
    )
    arrived = route(send, devices)
    (own_pack,) = call(
        join_kernel, (arrived, pair_slot, coarse_cotangent), (Near((half_rows, 2 * wide)),)
    )
    other_pack = exchange(own_pack)
    coarse, keep, give, unit = call(
        coarse_kernel,
        (own_pack, other_pack, pool_weight, coarse_projection, Far(coarse_output)),
        (
            Near((half_rows, wide)),
            Near((half_rows, 2 * wide)),
            Near((half_rows, 2 * wide)),
            Near((count, wide)),
        ),
    )
    got = exchange(give)
    coarse_result, coarse_gradient, send = call(
        coarse_finish_kernel,
        (
            coarse,
            keep,
            got,
            coarse_cotangent,
            pool_weight,
            coarse_projection,
            coarse_output,
            pair_slot,
        ),
        (
            Near((half_rows, wide), far=True),
            Near((half_rows, wide)),
            Near((slots, features)),
        ),
    )
    arrived = route(send, devices)
    blocks = (owners, 2, slots // devices)
    kept, first_half, second_half, own_gradient = call(
        functools.partial(coarse_weights_kernel, strides=(run, step)),
        (arrived, unit, keep, give, own_pack, other_pack, coarse_gradient),
        (
            Near((*blocks, wide // 2)),
            Near((*blocks, wide // 4)),
            Near((*blocks, wide // 4)),
            Near((half_rows, wide)),
        ),
    )
    got_first = lax.ppermute(first_half, "pts", [(i, i ^ run) for i in range(owners)])
    got_second = lax.ppermute(second_half, "pts", [(i, i ^ step) for i in range(owners)])
    other_gradient = exchange(own_gradient)
    (fine,) = call(
        fine_backward_kernel,
        (
            arrived,
            receive_slot,
            rotated,
            projected,
            mixture,
            weights,
            fine_projection,
            fine_output,
        ),
        (Near((*blocks, 2 * features)),),
        scratch=(pltpu.VMEM((count, 3 * features), BF),),
    )
    across = 2 * features + 3 * wide // 4
    (send,) = call(
        assemble_kernel,
        (
            fine,
            kept,
            got_first,
            got_second,
            own_pack,
            other_pack,
            own_gradient,
            other_gradient,
        ),
        (Near((*blocks, across)),),
    )
    arrived = spread_blocks(send.reshape(devices, slots // devices, across), ("pts", "grp"))
    (spread,) = call(
        functools.partial(sum_kernel, tokens=features, fine=features, run=run, step=step),
        (arrived.reshape(send.shape),),
        (Near((owners, slots // devices, features + 5 * wide // 2)),),
    )
    own_sums = spread_blocks(spread, "pts")
    (points_gradient,) = call(
        take_kernel, (arrived[:, :, :features], send_slot), (Near((count, features)),)
    )
    other_sums = exchange(own_sums)
    sums = call(
        functools.partial(sums_kernel, scaling=scaling),
        (own_sums, other_sums),
        (
            Near((features, 3 * features), F32, far=True),
            Near((features, features), F32, far=True),
            Near((wide, wide), F32, far=True),
            Near((wide, 3 * wide), F32, far=True),
            Near((wide, wide), F32, far=True),
        ),
    )
    return (coarse_result, points_gradient, *sums)


def solution(mesh):
    tokens = P(("pts", "grp"), None)
    in_specs = (
        tokens,
        P(("pts", "grp")),
        P(("pts", "grp")),
        P(),
        P(),
        P(),
        P(),
        P(),
        P(),
        tokens,
    )
    out_specs = (tokens, tokens, P(), P(), P(), P(), P())
    return jax.shard_map(
        on_device, mesh=mesh, in_specs=in_specs, out_specs=out_specs, check_vma=False
    )
```

```python
import functools
import math
from typing import NamedTuple

import jax
import jax.numpy as jnp
from jax import lax
from jax.experimental import pallas as pl
from jax.experimental.pallas import tpu as pltpu
from jax.sharding import PartitionSpec as P

HD = 64
BALL = 256
PAIR = 2 * HD
EPSILON = 1e-05
BF = jnp.bfloat16
F32 = jnp.float32


def mm(a, b, contract=(1, 0)):
    return lax.dot_general(
        a, b, (((contract[0],), (contract[1],)), ((), ())), preferred_element_type=F32
    )


def normalize(values):
    floats = values.astype(F32)
    center = floats - jnp.mean(floats, axis=-1, keepdims=True)
    inverse = lax.rsqrt(jnp.mean(center * center, axis=-1, keepdims=True) + EPSILON)
    return center * inverse, inverse


def norm_backward(incoming, normed, inverse):
    first_mean = jnp.mean(incoming, axis=-1, keepdims=True)
    second_mean = jnp.mean(incoming * normed, axis=-1, keepdims=True)
    return inverse * (incoming - first_mean - normed * second_mean)


def one_hot(slots, total):
    shape = (total, slots.shape[1])
    return (lax.broadcasted_iota(jnp.int32, shape, 0) == slots).astype(BF)


def head_half(shape, half):
    lanes = lax.broadcasted_iota(jnp.int32, shape, 1)
    return (lanes < HD) if half == 0 else (lanes >= HD)


def keep_half(rows, half):
    return jnp.where(head_half(rows.shape, half), rows, jnp.zeros_like(rows))


def softmax_rows(scores):
    raised = jnp.exp(scores - jnp.max(scores, axis=-1, keepdims=True))
    return (raised * (1.0 / jnp.sum(raised, axis=-1, keepdims=True))).astype(BF)


def slopes_of(weights, against):
    wide = weights.astype(F32)
    diagonal = jnp.sum(wide * against, axis=-1, keepdims=True)
    return (wide * (against - diagonal)).astype(BF)


def scaled_half(rows, half):
    return keep_half(rows * jnp.asarray(HD ** (-0.5), BF), half)


def turned(rows):
    return rows.astype(F32).T.astype(BF)


def column_of(row):
    count = row.shape[1]
    turned = jnp.broadcast_to(row.astype(F32), (128, count)).T
    return jnp.concatenate([turned] * (count // 128), axis=1)


def route_kernel(
    place, source, counts, points, send, send_slot, pair_slot, receive_slot, live
):
    count = place.shape[1]
    shift = count.bit_length() - 1
    capacity = send.shape[0] * count // (counts.shape[1] * BALL)
    to_row = place[...] >> shift
    rows = lax.broadcasted_iota(jnp.int32, (count, count), 0)
    columns = lax.broadcasted_iota(jnp.int32, (count, count), 1)
    earlier = (column_of(to_row) == to_row.astype(F32)) & (rows < columns)
    rank = jnp.sum(jnp.where(earlier, 1.0, 0.0), axis=0, keepdims=True)
    slot = to_row * capacity + rank.astype(jnp.int32)
    send_slot[...] = slot
    even_first = jnp.where(columns < count // 2, 2 * columns, 2 * columns + 1 - count)
    digits = jnp.concatenate([slot >> 5, slot & 31] + [jnp.zeros_like(slot)] * 6, axis=0)
    moved = mm(digits.astype(F32).astype(BF), (rows == even_first).astype(BF)).astype(jnp.int32)
    pair_slot[...] = moved[0:1] * 32 + moved[1:2]
    source_row = source[...]
    from_row = source_row >> shift
    earlier = (column_of(from_row) == from_row.astype(F32)) & (
        column_of(source_row) < source_row.astype(F32)
    )
    rank = jnp.sum(jnp.where(earlier, 1.0, 0.0), axis=0, keepdims=True)
    receive_slot[...] = from_row * capacity + rank.astype(jnp.int32)
    balls = counts.shape[1]
    own_ball = one_hot(source_row >> (BALL.bit_length() - 1), balls)
    filled = mm(jnp.broadcast_to(counts[...].astype(F32), (8, balls)).astype(BF), own_ball)
    inside = (source_row & (BALL - 1)).astype(F32)
    live[...] = jnp.where(inside < filled[:1], 1.0, 0.0)
    send[...] = mm(one_hot(slot, send.shape[0]), points[...]).astype(BF)


def fine_forward_kernel(
    arrived, receive_slot, live, projection, output, send, rotated, projected, mixture, weights
):
    place = one_hot(receive_slot[...], arrived.shape[0])
    rows_in = mm(place, arrived[...], (0, 0))
    rotated[...] = rows_in.astype(BF)
    features = rows_in.shape[1]
    normed, _ = normalize(rows_in)
    projected[...] = mm(normed.astype(BF), projection[...]).astype(BF)
    balls = rows_in.shape[0] // BALL
    pairs = features // PAIR
    for ball in range(balls):
        rows = slice(ball * BALL, (ball + 1) * BALL)
        alive = live[:, rows] > 0.5
        for pair in range(pairs):
            lanes = slice(pair * PAIR, (pair + 1) * PAIR)
            query = projected[rows, lanes]
            key = projected[rows, features + pair * PAIR : features + (pair + 1) * PAIR]
            value = projected[rows, 2 * features + pair * PAIR : 2 * features + (pair + 1) * PAIR]
            halves = []
            for half in range(2):
                scores = mm(scaled_half(query, half), key, (1, 1))
                head_weights = softmax_rows(jnp.where(alive, scores, -1e30))
                weights[(ball * pairs + pair) * 2 + half] = head_weights
                halves.append(mm(head_weights, value))
            mixed = jnp.where(head_half(halves[0].shape, 0), halves[0], halves[1])
            mixture[rows, lanes] = mixed.astype(BF)
    result = (rows_in + mm(mixture[...], output[...])).astype(BF)
    send[...] = mm(place, result).astype(BF)


def join_kernel(arrived, pair_slot, cotangent, pack):
    half_rows, wide = cotangent.shape
    place = one_hot(pair_slot[...], arrived.shape[0])
    rows = mm(place, arrived[...], (0, 0)).astype(BF)
    pack[:, : wide // 2] = rows[:half_rows]
    pack[:, wide // 2 : wide] = rows[half_rows:]
    pack[:, wide:] = cotangent[...]


def coarse_kernel(
    own_pack, other_pack, pool, projection, output, coarse, keep, give, unit
):
    half_rows, wide = coarse.shape
    part = wide // 2
    first = pl.multiple_of(lax.axis_index("grp") * part, part)
    joined = jnp.concatenate([own_pack[:, :wide], other_pack[:, :wide]], axis=0)
    tokens = mm(joined, pool[...]).astype(BF)
    coarse[...] = tokens[:half_rows]
    normed, _ = normalize(tokens)
    unit_rows = normed.astype(BF)
    unit[...] = unit_rows
    queries = mm(unit_rows, projection[:, pl.ds(first, part)]).astype(BF)
    keys = mm(unit_rows, projection[:, pl.ds(wide + first, part)]).astype(BF)
    values = mm(unit_rows, projection[:, pl.ds(2 * wide + first, part)]).astype(BF)
    cotangent = jnp.concatenate([own_pack[:, wide:], other_pack[:, wide:]], axis=0)
    incoming = mm(cotangent, output[pl.ds(first, part), :], (1, 1)).astype(BF)
    queries_turned, incoming_turned = turned(queries), turned(incoming)
    key_parts, value_parts = [], []

    def put(at, rows):
        target = slice(at, at + rows.shape[1])
        keep[:, target] = rows[:half_rows]
        give[:, target] = rows[half_rows:]

    for pair in range(part // PAIR):
        lanes = slice(pair * PAIR, (pair + 1) * PAIR)
        query, key, value = queries[:, lanes], keys[:, lanes], values[:, lanes]
        entering = incoming[:, lanes]
        parts = ([], [])
        for half in range(2):
            band = slice(pair * PAIR + half * HD, pair * PAIR + (half + 1) * HD)
            scores = mm(scaled_half(query, half), key, (1, 1))
            head_weights = softmax_rows(scores)
            parts[0].append(mm(head_weights, value))
            against = mm(keep_half(entering, half), value, (1, 1))
            slopes = slopes_of(head_weights, against)
            parts[1].append(mm(slopes, key) * HD ** (-0.5))
            key_parts.append(mm(queries_turned[band], slopes) * HD ** (-0.5))
            value_parts.append(mm(incoming_turned[band], head_weights))
        for at, (low, high) in enumerate(parts):
            both = jnp.where(head_half(low.shape, 0), low, high).astype(BF)
            put(at * part + pair * PAIR, both)
    put(2 * part, jnp.concatenate(key_parts, axis=0).T.astype(BF))
    put(3 * part, jnp.concatenate(value_parts, axis=0).T.astype(BF))


def coarse_finish_kernel(
    coarse,
    keep,
    got,
    cotangent,
    pool,
    projection,
    output,
    pair_slot,
    result,
    gradient,
    send,
):
    half_rows, wide = coarse.shape
    part = wide // 2
    mixed = coarse[...].astype(F32)
    back = jnp.zeros((half_rows, wide), F32)
    for source, index in ((keep, lax.axis_index("grp")), (got, 1 - lax.axis_index("grp"))):
        first = pl.multiple_of(index * part, part)
        mixed = mixed + mm(source[:, :part], output[pl.ds(first, part), :])
        for at in range(3):
            back = back + mm(
                source[:, (at + 1) * part : (at + 2) * part],
                projection[:, pl.ds(at * wide + first, part)],
                (1, 1),
            )
    result[...] = mixed.astype(BF)
    result.flush()
    normed, inverse = normalize(coarse[...])
    gradient_rows = (
        cotangent[...].astype(F32) + norm_backward(back, normed, inverse)
    ).astype(BF)
    gradient[...] = gradient_rows
    fine = mm(gradient_rows, pool[...], (1, 1)).astype(BF)
    features = send.shape[1]
    stacked = jnp.concatenate([fine[:, :features], fine[:, features:]], axis=0)
    send[...] = mm(one_hot(pair_slot[...], send.shape[0]), stacked).astype(BF)


def coarse_weights_kernel(
    unit, keep, give, own_pack, other_pack, kept, first_half, second_half, *, strides
):
    chip = lax.axis_index("pts")
    wide = unit.shape[1]
    part = wide // 2
    stacked = jnp.concatenate([keep[...], give[...]], axis=0)
    cotangent = jnp.concatenate([own_pack[:, wide:], other_pack[:, wide:]], axis=0)
    projection_term = mm(unit[...], stacked[:, part:], (0, 0))
    output_term = mm(stacked[:, :part], cotangent, (0, 0))
    across = projection_term.shape[1] // 2
    width = wide // 4
    for side in range(2):
        stack = [output_term[:, (2 * side + k) * width : (2 * side + k + 1) * width] for k in range(2)]
        columns = projection_term[:, side * across : (side + 1) * across]
        terms = jnp.concatenate([columns, jnp.concatenate(stack, axis=0)], axis=1)
        for at, passed in enumerate((first_half, second_half)):
            low = terms[:, 2 * at * width : (2 * at + 1) * width]
            high = terms[:, (2 * at + 1) * width : (2 * at + 2) * width]
            upper = chip // strides[at] % 2 == 1
            put_blocks(kept, side, at * width, jnp.where(upper, high, low))
            put_blocks(passed, side, 0, jnp.where(upper, low, high))


def put_quarters(blocks, lane, term):
    width = term.shape[1] // 4
    for side in range(2):
        stack = [term[:, (2 * side + k) * width : (2 * side + k + 1) * width] for k in range(2)]
        put_blocks(blocks, side, lane, jnp.concatenate(stack, axis=0))


def put_blocks(blocks, side, lane, rows):
    owners, width = blocks.shape[0], rows.shape[1]
    pieces = rows.reshape(owners, rows.shape[0] // owners, width)
    blocks[:, side, :, lane : lane + width] = pieces.astype(BF)


def sum_kernel(arrived, spread, *, tokens, run, step):
    senders, _, rows, across = arrived.shape
    width = (across - tokens) // 4

    def pieces(side, at):
        start = tokens + at * width
        return arrived[:, side, :, start : start + width].astype(F32)

    total = [jnp.sum(pieces(side, 0), axis=0) for side in range(2)]
    for side in range(2):
        for at, block in enumerate((run, step)):
            split = pieces(side, 1 + at).reshape(senders // (2 * block), 2, block, rows, width)
            halves = jnp.sum(jnp.sum(split, axis=2), axis=0)
            total.extend([halves[0], halves[1]])
        total.append(jnp.sum(pieces(side, 3), axis=0))
    total = jnp.concatenate(total, axis=1).astype(BF)
    spread[...] = jnp.broadcast_to(total[None], spread.shape)


def sums_kernel(
    own, other, fine_projection, fine_output, pool, projection, output, *, scaling
):
    features = fine_output.shape[0]
    wide = pool.shape[0]
    part = wide // 2
    width = wide // 4
    across = 3 * part // 2

    owns_low = lax.axis_index("grp") == 0

    def lanes(side, start, count):
        here, there = own[:, :, start : start + count], other[:, :, start : start + count]
        low = owns_low if side == 0 else jnp.logical_not(owns_low)
        values = jnp.where(low, here, there).astype(F32) * scaling
        return values.reshape(own.shape[0] * own.shape[1], count)

    def start_of(heads):
        return features + heads * (across + 2 * width)

    for side in range(2):
        for heads in range(2):
            for k in range(3):
                column = side * across + k * width
                at, inner = column // part, column % part
                target = at * wide + heads * part + inner
                projection[:, target : target + width] = lanes(
                    side, start_of(heads) + k * width, width
                )
    projection.flush()
    for at, ref in enumerate((output, pool)):
        for side in range(2):
            for heads in range(2):
                block = lanes(side, start_of(heads) + across + at * width, width)
                for k in range(2):
                    column = (2 * side + k) * width
                    ref[heads * part : (heads + 1) * part, column : column + width] = block[
                        k * part : (k + 1) * part
                    ]
        ref.flush()
    for side in range(2):
        for heads in range(2):
            block = lanes(side, heads * width, width)
            for k in range(2):
                column = (2 * heads + side) * features + k * width
                piece = block[k * features : (k + 1) * features]
                if column < 3 * features:
                    fine_projection[:, column : column + width] = piece
                else:
                    fine_output[:, column - 3 * features : column - 3 * features + width] = piece


def fine_backward_kernel(
    arrived,
    receive_slot,
    rotated,
    projected,
    mixture,
    weights,
    projection,
    output,
    tokens,
    kept,
    passed,
    grad_projected,
):
    place = one_hot(receive_slot[...], arrived.shape[0])
    gradient_rows = mm(place, arrived[...], (0, 0)).astype(BF)
    features = rotated.shape[1]
    entering = mm(gradient_rows, output[...], (1, 1)).astype(BF)
    terms = [mm(mixture[...], gradient_rows, (0, 0))]
    balls = rotated.shape[0] // BALL
    pairs = features // PAIR
    query_turned, entering_turned = turned(projected[:, :features]), turned(entering)
    turned_parts = ([], [])
    for ball in range(balls):
        rows = slice(ball * BALL, (ball + 1) * BALL)
        pieces = ([], [])
        for pair in range(pairs):
            lanes = slice(pair * PAIR, (pair + 1) * PAIR)
            key = projected[rows, features + pair * PAIR : features + (pair + 1) * PAIR]
            value = projected[rows, 2 * features + pair * PAIR : 2 * features + (pair + 1) * PAIR]
            query_parts = []
            for half in range(2):
                band = slice(pair * PAIR + half * HD, pair * PAIR + (half + 1) * HD)
                head_weights = weights[(ball * pairs + pair) * 2 + half]
                against = mm(keep_half(entering[rows, lanes], half), value, (1, 1))
                slopes = slopes_of(head_weights, against)
                query_parts.append(mm(slopes, key) * HD ** (-0.5))
                pieces[0].append(mm(query_turned[band, rows], slopes) * HD ** (-0.5))
                pieces[1].append(mm(entering_turned[band, rows], head_weights))
            low, high = query_parts
            both = jnp.where(head_half(low.shape, 0), low, high).astype(BF)
            grad_projected[rows, lanes] = both
        for at in range(2):
            turned_parts[at].append(jnp.concatenate(pieces[at], axis=0))
    for at in range(2):
        whole = jnp.concatenate(turned_parts[at], axis=1).T.astype(BF)
        grad_projected[:, (at + 1) * features : (at + 2) * features] = whole
    normed, inverse = normalize(rotated[...])
    unit_rows = normed.astype(BF)
    for at in range(3):
        columns = slice(at * features, (at + 1) * features)
        terms.insert(at, mm(unit_rows, grad_projected[:, columns], (0, 0)))
    low = jnp.concatenate(terms[:2], axis=1)
    high = jnp.concatenate(terms[2:], axis=1)
    upper = lax.axis_index("grp") == 1
    kept[...] = jnp.where(upper, high, low)
    passed[...] = jnp.where(upper, low, high).astype(BF)
    back = mm(grad_projected[...], projection[...], (1, 1))
    result = gradient_rows.astype(F32) + norm_backward(back, normed, inverse)
    tokens[...] = mm(place, result.astype(BF)).reshape(tokens.shape).astype(BF)


def coarse_part_kernel(
    kept, got_first, got_second, own_pack, other_pack, own_gradient, other_gradient, coarse
):
    width = got_first.shape[3]
    for at, got in enumerate((got_first, got_second)):
        lanes = slice(at * width, (at + 1) * width)
        mine = kept[:, :, :, lanes].astype(F32)
        coarse[:, :, :, lanes] = (mine + got[...].astype(F32)).astype(BF)
    part = own_gradient.shape[1] // 2
    first = pl.multiple_of(lax.axis_index("grp") * part, part)
    pool_term = mm(own_pack[:, pl.ds(first, part)], own_gradient[...], (0, 0))
    pool_term = pool_term + mm(other_pack[:, pl.ds(first, part)], other_gradient[...], (0, 0))
    put_quarters(coarse, 2 * width, pool_term)


def assemble_kernel(tokens, fine_kept, fine_got, coarse, send):
    start = tokens.shape[3]
    send[:, :, :, :start] = tokens[...]
    put_quarters(send, start, fine_kept[...] + fine_got[...].astype(F32))
    send[:, :, :, send.shape[3] - coarse.shape[3] :] = coarse[...]


def take_kernel(arrived, slots, rows_out):
    place = one_hot(slots[...], slots.shape[1] * 2)
    rows = arrived[...].reshape(place.shape[0], arrived.shape[-1])
    rows_out[...] = mm(place, rows, (0, 0)).astype(BF)


VMEM = pl.BlockSpec(memory_space=pltpu.VMEM)
HBM = pl.BlockSpec(memory_space=pltpu.HBM)


class Far(NamedTuple):
    value: jax.Array


class Near(NamedTuple):
    shape: tuple
    dtype: jnp.dtype = BF
    far: bool = False


class Fetched:
    def __init__(self, source, buffer, semaphore):
        self.buffer, self.shape, self.waited = buffer, buffer.shape, False
        self.copy = pltpu.make_async_copy(source, buffer, semaphore)
        self.copy.start()

    def wait(self):
        if not self.waited:
            self.copy.wait()
            self.waited = True

    def __getitem__(self, index):
        self.wait()
        return self.buffer[index]


class Stored:
    def __init__(self, target, buffer, semaphore):
        self.buffer, self.shape, self.dtype, self.started = buffer, buffer.shape, buffer.dtype, False
        self.copy = pltpu.make_async_copy(buffer, target, semaphore)

    def __setitem__(self, index, values):
        self.buffer[index] = values

    def __getitem__(self, index):
        return self.buffer[index]

    def flush(self):
        if not self.started:
            self.copy.start()
            self.started = True


def call(kernel, inputs, outputs, scratch=(), mebibytes=16):
    in_specs, arrays, buffers = [], [], []
    for value in inputs:
        far = isinstance(value, Far)
        in_specs.append(HBM if far else VMEM)
        arrays.append(
            pltpu.with_memory_space_constraint(value.value, pltpu.HBM) if far else value
        )
        if far:
            buffers.append(pltpu.VMEM(value.value.shape, value.value.dtype))
    buffers.extend(pltpu.VMEM(out.shape, out.dtype) for out in outputs if out.far)
    flags = [isinstance(value, Far) for value in inputs] + [out.far for out in outputs]
    sizes = len(inputs), len(flags), len(flags) + len(buffers)

    def body(*refs):
        semaphores = refs[sizes[2]] if buffers else None
        given, views = 0, []
        for at, far in enumerate(flags):
            if far:
                kind = Fetched if at < sizes[0] else Stored
                views.append(kind(refs[at], refs[sizes[1] + given], semaphores.at[given]))
                given += 1
            else:
                views.append(refs[at])
        kernel(*views, *refs[sizes[2] + (1 if buffers else 0) :])
        for view in views:
            if isinstance(view, Stored):
                view.flush()
        for view in views:
            if isinstance(view, Fetched):
                view.wait()
            if isinstance(view, Stored):
                view.copy.wait()

    own = [pltpu.SemaphoreType.DMA((len(buffers),))] if buffers else []
    return pl.pallas_call(
        body,
        out_shape=[
            (pltpu.HBM if out.far else jax.ShapeDtypeStruct)(out.shape, out.dtype)
            for out in outputs
        ],
        in_specs=in_specs,
        out_specs=[HBM if out.far else VMEM for out in outputs],
        scratch_shapes=buffers + own + list(scratch),
        compiler_params=pltpu.CompilerParams(vmem_limit_bytes=mebibytes * 1024 * 1024),
    )(*arrays)


def exchange(values):
    return lax.ppermute(values, "grp", [(0, 1), (1, 0)])


def spread_blocks(values, axes):
    return lax.all_to_all(values, axes, split_axis=0, concat_axis=0, tiled=True)


def route(values, devices):
    rows, features = values.shape
    blocks = values.reshape(devices, rows // devices, features)
    return spread_blocks(blocks, ("pts", "grp")).reshape(rows, features)


def on_device(
    points,
    rotated_place,
    rotated_source,
    ball_counts,
    fine_projection,
    fine_output,
    pool_weight,
    coarse_projection,
    coarse_output,
    coarse_cotangent,
):
    count, features = points.shape
    devices = lax.axis_size(("pts", "grp"))
    slots = 2 * count
    scaling = 1.0 / math.sqrt(count * devices)
    owners = lax.axis_size("pts")
    run, step = owners // 4, owners // 16
    wide = 2 * features
    half_rows = count // 2

    send, send_slot, pair_slot, receive_slot, live = call(
        route_kernel,
        (
            Far(rotated_place.reshape(1, count)),
            Far(rotated_source.reshape(1, count)),
            Far(ball_counts.reshape(1, -1)),
            Far(points),
        ),
        (
            Near((slots, features)),
            Near((1, count), jnp.int32),
            Near((1, count), jnp.int32),
            Near((1, count), jnp.int32),
            Near((1, count), F32),
        ),
    )
    arrived = route(send, devices)
    heads = features // HD * (count // BALL)
    send, rotated, projected, mixture, weights = call(
        fine_forward_kernel,
        (arrived, receive_slot, live, fine_projection, Far(fine_output)),
        (
            Near((slots, features)),
            Near((count, features)),
            Near((count, 3 * features)),
            Near((count, features)),
            Near((heads, BALL, BALL)),
        ),
    )
    arrived = route(send, devices)
    (own_pack,) = call(
        join_kernel, (arrived, pair_slot, coarse_cotangent), (Near((half_rows, 2 * wide)),)
    )
    other_pack = exchange(own_pack)
    coarse, keep, give, unit = call(
        coarse_kernel,
        (own_pack, other_pack, pool_weight, coarse_projection, Far(coarse_output)),
        (
            Near((half_rows, wide)),
            Near((half_rows, 2 * wide)),
            Near((half_rows, 2 * wide)),
            Near((count, wide)),
        ),
    )
    got = exchange(give)
    blocks = (owners, 2, slots // devices)
    kept, first_half, second_half = call(
        functools.partial(coarse_weights_kernel, strides=(run, step)),
        (unit, keep, give, own_pack, other_pack),
        (
            Near((*blocks, wide // 2)),
            Near((*blocks, wide // 4)),
            Near((*blocks, wide // 4)),
        ),
    )
    got, kept, first_half, second_half = lax.optimization_barrier(
        (got, kept, first_half, second_half)
    )
    coarse_result, coarse_gradient, send = call(
        coarse_finish_kernel,
        (
            coarse,
            keep,
            got,
            coarse_cotangent,
            pool_weight,
            coarse_projection,
            coarse_output,
            pair_slot,
        ),
        (
            Near((half_rows, wide), far=True),
            Near((half_rows, wide)),
            Near((slots, features)),
        ),
    )
    arrived = route(send, devices)
    arrived, first_half, second_half, coarse_gradient = lax.optimization_barrier(
        (arrived, first_half, second_half, coarse_gradient)
    )
    got_first = lax.ppermute(first_half, "pts", [(i, i ^ run) for i in range(owners)])
    got_second = lax.ppermute(second_half, "pts", [(i, i ^ step) for i in range(owners)])
    other_gradient = exchange(coarse_gradient)
    tokens, fine_kept, fine_passed = call(
        fine_backward_kernel,
        (
            arrived,
            receive_slot,
            rotated,
            projected,
            mixture,
            weights,
            fine_projection,
            fine_output,
        ),
        (
            Near((*blocks, features)),
            Near((features, 2 * features), F32),
            Near((features, 2 * features)),
        ),
        scratch=(pltpu.VMEM((count, 3 * features), BF),),
    )
    fine_got = exchange(fine_passed)
    (coarse_part,) = call(
        coarse_part_kernel,
        (
            kept,
            got_first,
            got_second,
            own_pack,
            other_pack,
            coarse_gradient,
            other_gradient,
        ),
        (Near((*blocks, 3 * wide // 4)),),
    )
    across = features + wide
    (send,) = call(
        assemble_kernel,
        (tokens, fine_kept, fine_got, coarse_part),
        (Near((*blocks, across)),),
    )
    arrived = spread_blocks(send.reshape(devices, slots // devices, across), ("pts", "grp"))
    (spread,) = call(
        functools.partial(sum_kernel, tokens=features, run=run, step=step),
        (arrived.reshape(send.shape),),
        (Near((owners, slots // devices, features + 5 * wide // 2)),),
    )
    own_sums = spread_blocks(spread, "pts")
    (points_gradient,) = call(
        take_kernel, (arrived[:, :, :features], send_slot), (Near((count, features)),)
    )
    other_sums = exchange(own_sums)
    sums = call(
        functools.partial(sums_kernel, scaling=scaling),
        (own_sums, other_sums),
        (
            Near((features, 3 * features), F32, far=True),
            Near((features, features), F32, far=True),
            Near((wide, wide), F32, far=True),
            Near((wide, 3 * wide), F32, far=True),
            Near((wide, wide), F32, far=True),
        ),
    )
    return (coarse_result, points_gradient, *sums)


def solution(mesh):
    tokens = P(("pts", "grp"), None)
    in_specs = (
        tokens,
        P(("pts", "grp")),
        P(("pts", "grp")),
        P(),
        P(),
        P(),
        P(),
        P(),
        P(),
        tokens,
    )
    out_specs = (tokens, tokens, P(), P(), P(), P(), P())
    return jax.shard_map(
        on_device, mesh=mesh, in_specs=in_specs, out_specs=out_specs, check_vma=False
    )
```

```python
import functools
import math
from typing import NamedTuple

import jax
import jax.numpy as jnp
from jax import lax
from jax.experimental import pallas as pl
from jax.experimental.pallas import tpu as pltpu
from jax.sharding import PartitionSpec as P

HD = 64
BALL = 256
PAIR = 2 * HD
EPSILON = 1e-05
BF = jnp.bfloat16
F32 = jnp.float32


def mm(a, b, contract=(1, 0)):
    return lax.dot_general(
        a, b, (((contract[0],), (contract[1],)), ((), ())), preferred_element_type=F32
    )


def normalize(values):
    floats = values.astype(F32)
    center = floats - jnp.mean(floats, axis=-1, keepdims=True)
    inverse = lax.rsqrt(jnp.mean(center * center, axis=-1, keepdims=True) + EPSILON)
    return center * inverse, inverse


def norm_backward(incoming, normed, inverse):
    first_mean = jnp.mean(incoming, axis=-1, keepdims=True)
    second_mean = jnp.mean(incoming * normed, axis=-1, keepdims=True)
    return inverse * (incoming - first_mean - normed * second_mean)


def one_hot(slots, total):
    shape = (total, slots.shape[1])
    return (lax.broadcasted_iota(jnp.int32, shape, 0) == slots).astype(BF)


def head_half(shape, half):
    lanes = lax.broadcasted_iota(jnp.int32, shape, 1)
    return (lanes < HD) if half == 0 else (lanes >= HD)


def keep_half(rows, half):
    return jnp.where(head_half(rows.shape, half), rows, jnp.zeros_like(rows))


def softmax_rows(scores):
    raised = jnp.exp(scores - jnp.max(scores, axis=-1, keepdims=True))
    return (raised * (1.0 / jnp.sum(raised, axis=-1, keepdims=True))).astype(BF)


def slopes_of(weights, against):
    wide = weights.astype(F32)
    diagonal = jnp.sum(wide * against, axis=-1, keepdims=True)
    return (wide * (against - diagonal)).astype(BF)


def scaled_half(rows, half):
    return keep_half(rows * jnp.asarray(HD ** (-0.5), BF), half)


def stack_heads(rows, heads):
    lanes = lax.broadcasted_iota(jnp.int32, rows.shape, 1) // HD
    none = jnp.zeros_like(rows)
    return jnp.concatenate([jnp.where(lanes == at, rows, none) for at in range(heads)], axis=0)


def unstack_heads(rows, heads):
    count = rows.shape[0] // heads
    merged = rows[:count]
    lanes = lax.broadcasted_iota(jnp.int32, merged.shape, 1) // HD
    for at in range(1, heads):
        merged = jnp.where(lanes == at, rows[at * count : (at + 1) * count], merged)
    return merged


def turned(rows):
    return rows.astype(F32).T.astype(BF)


def column_of(row):
    count = row.shape[1]
    turned = jnp.broadcast_to(row.astype(F32), (128, count)).T
    return jnp.concatenate([turned] * (count // 128), axis=1)


def route_kernel(
    place, source, counts, points, send, send_slot, pair_slot, receive_slot, live
):
    count = place.shape[1]
    shift = count.bit_length() - 1
    capacity = send.shape[0] * count // (counts.shape[1] * BALL)
    to_row = place[...] >> shift
    rows = lax.broadcasted_iota(jnp.int32, (count, count), 0)
    columns = lax.broadcasted_iota(jnp.int32, (count, count), 1)
    earlier = (column_of(to_row) == to_row.astype(F32)) & (rows < columns)
    rank = jnp.sum(jnp.where(earlier, 1.0, 0.0), axis=0, keepdims=True)
    slot = to_row * capacity + rank.astype(jnp.int32)
    send_slot[...] = slot
    even_first = jnp.where(columns < count // 2, 2 * columns, 2 * columns + 1 - count)
    digits = jnp.concatenate([slot >> 5, slot & 31] + [jnp.zeros_like(slot)] * 6, axis=0)
    moved = mm(digits.astype(F32).astype(BF), (rows == even_first).astype(BF)).astype(jnp.int32)
    pair_slot[...] = moved[0:1] * 32 + moved[1:2]
    source_row = source[...]
    from_row = source_row >> shift
    earlier = (column_of(from_row) == from_row.astype(F32)) & (
        column_of(source_row) < source_row.astype(F32)
    )
    rank = jnp.sum(jnp.where(earlier, 1.0, 0.0), axis=0, keepdims=True)
    receive_slot[...] = from_row * capacity + rank.astype(jnp.int32)
    balls = counts.shape[1]
    own_ball = one_hot(source_row >> (BALL.bit_length() - 1), balls)
    filled = mm(jnp.broadcast_to(counts[...].astype(F32), (8, balls)).astype(BF), own_ball)
    inside = (source_row & (BALL - 1)).astype(F32)
    live[...] = jnp.where(inside < filled[:1], 1.0, 0.0)
    send[...] = mm(one_hot(slot, send.shape[0]), points[...]).astype(BF)


def fine_forward_kernel(
    arrived, receive_slot, live, projection, output, send, rotated, projected, mixture, weights
):
    place = one_hot(receive_slot[...], arrived.shape[0])
    rows_in = mm(place, arrived[...], (0, 0))
    rotated[...] = rows_in.astype(BF)
    features = rows_in.shape[1]
    normed, _ = normalize(rows_in)
    projected[...] = mm(normed.astype(BF), projection[...]).astype(BF)
    balls = rows_in.shape[0] // BALL
    for ball in range(balls):
        rows = slice(ball * BALL, (ball + 1) * BALL)
        alive = live[:, rows] > 0.5
        for pair in range(features // PAIR):
            lanes = slice(pair * PAIR, (pair + 1) * PAIR)
            query = projected[rows, lanes] * jnp.asarray(HD ** (-0.5), BF)
            key = projected[rows, features + pair * PAIR : features + (pair + 1) * PAIR]
            value = projected[rows, 2 * features + pair * PAIR : 2 * features + (pair + 1) * PAIR]
            scores = mm(stack_heads(query, 2), key, (1, 1))
            both = softmax_rows(jnp.where(alive, scores, -1e30))
            first = (ball * features + pair * PAIR) // HD
            weights[first : first + 2] = both.reshape(2, BALL, BALL)
            mixture[rows, lanes] = unstack_heads(mm(both, value), 2).astype(BF)
    result = (rows_in + mm(mixture[...], output[...])).astype(BF)
    send[...] = mm(place, result).astype(BF)


def join_kernel(arrived, pair_slot, cotangent, pack):
    half_rows, wide = cotangent.shape
    place = one_hot(pair_slot[...], arrived.shape[0])
    rows = mm(place, arrived[...], (0, 0)).astype(BF)
    pack[:, : wide // 2] = rows[:half_rows]
    pack[:, wide // 2 : wide] = rows[half_rows:]
    pack[:, wide:] = cotangent[...]


def coarse_kernel(
    own_pack, other_pack, pool, projection, output, coarse, keep, give, unit
):
    half_rows, wide = coarse.shape
    part = wide // 2
    first = pl.multiple_of(lax.axis_index("grp") * part, part)
    joined = jnp.concatenate([own_pack[:, :wide], other_pack[:, :wide]], axis=0)
    tokens = mm(joined, pool[...]).astype(BF)
    coarse[...] = tokens[:half_rows]
    normed, _ = normalize(tokens)
    unit_rows = normed.astype(BF)
    unit[...] = unit_rows
    queries = mm(unit_rows, projection[:, pl.ds(first, part)]).astype(BF)
    keys = mm(unit_rows, projection[:, pl.ds(wide + first, part)]).astype(BF)
    values = mm(unit_rows, projection[:, pl.ds(2 * wide + first, part)]).astype(BF)
    cotangent = jnp.concatenate([own_pack[:, wide:], other_pack[:, wide:]], axis=0)
    incoming = mm(cotangent, output[pl.ds(first, part), :], (1, 1)).astype(BF)
    queries_turned, incoming_turned = turned(queries), turned(incoming)
    key_parts, value_parts = [], []

    def put(at, rows):
        target = slice(at, at + rows.shape[1])
        keep[:, target] = rows[:half_rows]
        give[:, target] = rows[half_rows:]

    for pair in range(part // PAIR):
        lanes = slice(pair * PAIR, (pair + 1) * PAIR)
        query, key, value = queries[:, lanes], keys[:, lanes], values[:, lanes]
        entering = incoming[:, lanes]
        parts = ([], [])
        for half in range(2):
            band = slice(pair * PAIR + half * HD, pair * PAIR + (half + 1) * HD)
            scores = mm(scaled_half(query, half), key, (1, 1))
            head_weights = softmax_rows(scores)
            parts[0].append(mm(head_weights, value))
            against = mm(keep_half(entering, half), value, (1, 1))
            slopes = slopes_of(head_weights, against)
            parts[1].append(mm(slopes, key) * HD ** (-0.5))
            key_parts.append(mm(queries_turned[band], slopes) * HD ** (-0.5))
            value_parts.append(mm(incoming_turned[band], head_weights))
        for at, (low, high) in enumerate(parts):
            both = jnp.where(head_half(low.shape, 0), low, high).astype(BF)
            put(at * part + pair * PAIR, both)
    put(2 * part, jnp.concatenate(key_parts, axis=0).T.astype(BF))
    put(3 * part, jnp.concatenate(value_parts, axis=0).T.astype(BF))


def coarse_finish_kernel(
    coarse,
    keep,
    got,
    cotangent,
    pool,
    projection,
    output,
    pair_slot,
    result,
    gradient,
    send,
):
    half_rows, wide = coarse.shape
    part = wide // 2
    mixed = coarse[...].astype(F32)
    back = jnp.zeros((half_rows, wide), F32)
    for source, index in ((keep, lax.axis_index("grp")), (got, 1 - lax.axis_index("grp"))):
        first = pl.multiple_of(index * part, part)
        mixed = mixed + mm(source[:, :part], output[pl.ds(first, part), :])
        for at in range(3):
            back = back + mm(
                source[:, (at + 1) * part : (at + 2) * part],
                projection[:, pl.ds(at * wide + first, part)],
                (1, 1),
            )
    result[...] = mixed.astype(BF)
    result.flush()
    normed, inverse = normalize(coarse[...])
    gradient_rows = (
        cotangent[...].astype(F32) + norm_backward(back, normed, inverse)
    ).astype(BF)
    gradient[...] = gradient_rows
    fine = mm(gradient_rows, pool[...], (1, 1)).astype(BF)
    features = send.shape[1]
    stacked = jnp.concatenate([fine[:, :features], fine[:, features:]], axis=0)
    send[...] = mm(one_hot(pair_slot[...], send.shape[0]), stacked).astype(BF)


def coarse_weights_kernel(
    unit, keep, give, own_pack, other_pack, kept, first_half, second_half, *, strides
):
    chip, core = lax.axis_index("pts"), lax.axis_index("grp")
    wide = unit.shape[1]
    part = wide // 2
    stacked = jnp.concatenate([keep[...], give[...]], axis=0)
    cotangent = jnp.concatenate([own_pack[:, wide:], other_pack[:, wide:]], axis=0)
    projection_term = mm(unit[...], stacked[:, part:], (0, 0))
    output_term = mm(stacked[:, :part], cotangent, (0, 0))
    across = projection_term.shape[1] // 2
    width = wide // 4
    for side in range(2):
        stack = [output_term[:, (2 * side + k) * width : (2 * side + k + 1) * width] for k in range(2)]
        columns = projection_term[:, side * across : (side + 1) * across]
        terms = jnp.concatenate([columns, jnp.concatenate(stack, axis=0)], axis=1)
        for at, passed in enumerate((first_half, second_half)):
            low = terms[:, 2 * at * width : (2 * at + 1) * width]
            high = terms[:, (2 * at + 1) * width : (2 * at + 2) * width]
            upper = (chip // strides[at] + core) % 2 == 1
            put_blocks(kept, side, at * width, jnp.where(upper, high, low))
            put_blocks(passed, side, 0, jnp.where(upper, low, high))


def put_quarters(blocks, lane, term):
    width = term.shape[1] // 4
    for side in range(2):
        stack = [term[:, (2 * side + k) * width : (2 * side + k + 1) * width] for k in range(2)]
        put_blocks(blocks, side, lane, jnp.concatenate(stack, axis=0))


def put_blocks(blocks, side, lane, rows):
    owners, width = blocks.shape[0], rows.shape[1]
    pieces = rows.reshape(owners, rows.shape[0] // owners, width)
    blocks[:, side, :, lane : lane + width] = pieces.astype(BF)


def sum_kernel(arrived, spread, *, tokens, run, step):
    senders, _, rows, across = arrived.shape
    width = (across - tokens) // 4

    def pieces(side, at):
        start = tokens + at * width
        return arrived[:, side, :, start : start + width].astype(F32)

    total = [jnp.sum(pieces(side, 0), axis=0) for side in range(2)]
    for side in range(2):
        for at, block in enumerate((run, step)):
            split = pieces(side, 1 + at).reshape(senders // (2 * block), 2, block, rows, width)
            halves = jnp.sum(jnp.sum(split, axis=2), axis=0)
            total.extend([halves[side], halves[1 - side]])
        total.append(jnp.sum(pieces(side, 3), axis=0))
    total = jnp.concatenate(total, axis=1).astype(BF)
    spread[...] = jnp.broadcast_to(total[None], spread.shape)


def write_half(terms, side, refs, stages, semaphores, scaling):
    projection, output, pool = refs
    tall, square = stages
    wide = pool.shape[0]
    part, width = wide // 2, wide // 4
    across = 3 * part // 2
    copies = []

    def lanes(start, count):
        values = terms[:, :, start : start + count].astype(F32) * scaling
        return values.reshape(terms.shape[0] * terms.shape[1], count)

    def send(stage, target):
        copies.append(pltpu.make_async_copy(stage, target, semaphores.at[len(copies)]))
        copies[-1].start()

    for heads in range(2):
        start = 2 * width + heads * (across + 2 * width)
        for k in range(3):
            columns = [half * across + k * width for half in range(2)]
            places = [column // part * wide + heads * part + column % part for column in columns]
            target = pl.multiple_of(jnp.where(side == 0, places[0], places[1]), width)
            stage = tall.at[3 * heads + k]
            stage[...] = lanes(start + k * width, width)
            send(stage, projection.at[:, pl.ds(target, width)])
        for at, ref in enumerate((output, pool)):
            block = lanes(start + across + at * width, width)
            stage = square.at[2 * heads + at]
            stage[:, :width] = block[:part]
            stage[:, width:] = block[part:]
            target = pl.multiple_of(side * part, part)
            send(stage, ref.at[heads * part : (heads + 1) * part, pl.ds(target, part)])
    return copies


def own_sums_kernel(own, projection, output, pool, tall, square, semaphores, *, scaling):
    side = lax.axis_index("grp")
    refs = (projection, output, pool)
    for copy in write_half(own, side, refs, (tall, square), semaphores, scaling):
        copy.wait()


def other_sums_kernel(
    own,
    other,
    projection_in,
    output_in,
    pool_in,
    projection,
    output,
    pool,
    fine_projection,
    fine_output,
    tall,
    square,
    semaphores,
    fine,
    fine_square,
    fine_semaphores,
    *,
    scaling,
):
    side = 1 - lax.axis_index("grp")
    refs = (projection, output, pool)
    copies = write_half(other, side, refs, (tall, square), semaphores, scaling)
    features = fine_output.shape[0]
    width = features // 2
    for heads in range(2):
        start = heads * width
        here, there = own[:, :, start : start + width], other[:, :, start : start + width]
        for half in range(2):
            values = jnp.where(side == half, there, here).astype(F32) * scaling
            block = values.reshape(own.shape[0] * own.shape[1], width)
            column = (2 * heads + half) * features
            for k in range(2):
                piece = block[k * features : (k + 1) * features]
                if column < 3 * features:
                    fine[:, column + k * width : column + (k + 1) * width] = piece
                else:
                    fine_square[:, k * width : (k + 1) * width] = piece
    copies.append(pltpu.make_async_copy(fine, fine_projection, fine_semaphores.at[0]))
    copies.append(pltpu.make_async_copy(fine_square, fine_output, fine_semaphores.at[1]))
    for copy in copies[-2:]:
        copy.start()
    for copy in copies:
        copy.wait()


def write_sums(own, other, features, wide, scaling):
    part, width = wide // 2, wide // 4
    shapes = [(wide, 3 * wide), (wide, wide), (wide, wide)]
    stages = [
        pltpu.VMEM((6, wide, width), F32),
        pltpu.VMEM((4, part, part), F32),
        pltpu.SemaphoreType.DMA((10,)),
    ]
    limits = pltpu.CompilerParams(vmem_limit_bytes=16 * 1024 * 1024)
    firsts = pl.pallas_call(
        functools.partial(own_sums_kernel, scaling=scaling),
        out_shape=[pltpu.HBM(shape, F32) for shape in shapes],
        in_specs=[VMEM],
        out_specs=[HBM] * 3,
        scratch_shapes=stages,
        compiler_params=limits,
    )(own)
    shapes += [(features, 3 * features), (features, features)]
    projection, output, pool, fine_projection, fine_output = pl.pallas_call(
        functools.partial(other_sums_kernel, scaling=scaling),
        out_shape=[pltpu.HBM(shape, F32) for shape in shapes],
        in_specs=[VMEM] * 2 + [HBM] * 3,
        out_specs=[HBM] * 5,
        scratch_shapes=stages
        + [
            pltpu.VMEM((features, 3 * features), F32),
            pltpu.VMEM((features, features), F32),
            pltpu.SemaphoreType.DMA((2,)),
        ],
        input_output_aliases={2: 0, 3: 1, 4: 2},
        compiler_params=limits,
    )(own, other, *firsts)
    return fine_projection, fine_output, pool, projection, output


def fine_backward_kernel(
    arrived,
    receive_slot,
    rotated,
    projected,
    mixture,
    weights,
    projection,
    output,
    tokens,
    kept,
    passed,
    grad_projected,
):
    place = one_hot(receive_slot[...], arrived.shape[0])
    gradient_rows = mm(place, arrived[...], (0, 0)).astype(BF)
    features = rotated.shape[1]
    entering = mm(gradient_rows, output[...], (1, 1)).astype(BF)
    terms = [mm(mixture[...], gradient_rows, (0, 0))]
    balls = rotated.shape[0] // BALL
    heads = features // HD
    query_turned, entering_turned = turned(projected[:, :features]), turned(entering)
    turned_parts = ([], [])
    for ball in range(balls):
        rows = slice(ball * BALL, (ball + 1) * BALL)
        key, value = projected[rows, features : 2 * features], projected[rows, 2 * features :]
        head_weights = [weights[ball * heads + at] for at in range(heads)]
        against = mm(stack_heads(entering[rows], heads), value, (1, 1))
        slopes = slopes_of(jnp.concatenate(head_weights, axis=0), against)
        query_part = unstack_heads(mm(slopes, key), heads) * HD ** (-0.5)
        grad_projected[rows, :features] = query_part.astype(BF)
        pieces = ([], [])
        for at in range(heads):
            band = slice(at * HD, (at + 1) * HD)
            own = slopes[at * BALL : (at + 1) * BALL]
            pieces[0].append(mm(query_turned[band, rows], own) * HD ** (-0.5))
            pieces[1].append(mm(entering_turned[band, rows], head_weights[at]))
        for at in range(2):
            turned_parts[at].append(jnp.concatenate(pieces[at], axis=0))
    for at in range(2):
        whole = jnp.concatenate(turned_parts[at], axis=1).T.astype(BF)
        grad_projected[:, (at + 1) * features : (at + 2) * features] = whole
    normed, inverse = normalize(rotated[...])
    unit_rows = normed.astype(BF)
    for at in range(3):
        columns = slice(at * features, (at + 1) * features)
        terms.insert(at, mm(unit_rows, grad_projected[:, columns], (0, 0)))
    low = jnp.concatenate(terms[:2], axis=1)
    high = jnp.concatenate(terms[2:], axis=1)
    upper = lax.axis_index("grp") == 1
    kept[...] = jnp.where(upper, high, low)
    passed[...] = jnp.where(upper, low, high).astype(BF)
    back = mm(grad_projected[...], projection[...], (1, 1))
    result = gradient_rows.astype(F32) + norm_backward(back, normed, inverse)
    tokens[...] = mm(place, result.astype(BF)).reshape(tokens.shape).astype(BF)


def coarse_part_kernel(
    kept, got_first, got_second, own_pack, other_pack, own_gradient, other_gradient, coarse
):
    width = got_first.shape[3]
    for at, got in enumerate((got_first, got_second)):
        lanes = slice(at * width, (at + 1) * width)
        mine = kept[:, :, :, lanes].astype(F32)
        coarse[:, :, :, lanes] = (mine + got[...].astype(F32)).astype(BF)
    part = own_gradient.shape[1] // 2
    first = pl.multiple_of(lax.axis_index("grp") * part, part)
    pool_term = mm(own_pack[:, pl.ds(first, part)], own_gradient[...], (0, 0))
    pool_term = pool_term + mm(other_pack[:, pl.ds(first, part)], other_gradient[...], (0, 0))
    put_quarters(coarse, 2 * width, pool_term)


def assemble_kernel(tokens, fine_kept, fine_got, coarse, send):
    start = tokens.shape[3]
    send[:, :, :, :start] = tokens[...]
    put_quarters(send, start, fine_kept[...] + fine_got[...].astype(F32))
    send[:, :, :, send.shape[3] - coarse.shape[3] :] = coarse[...]


def take_kernel(arrived, slots, rows_out):
    place = one_hot(slots[...], slots.shape[1] * 2)
    rows = arrived[...].reshape(place.shape[0], arrived.shape[-1])
    rows_out[...] = mm(place, rows, (0, 0)).astype(BF)


VMEM = pl.BlockSpec(memory_space=pltpu.VMEM)
HBM = pl.BlockSpec(memory_space=pltpu.HBM)


class Far(NamedTuple):
    value: jax.Array


class Near(NamedTuple):
    shape: tuple
    dtype: jnp.dtype = BF
    far: bool = False


class Fetched:
    def __init__(self, source, buffer, semaphore):
        self.buffer, self.shape, self.waited = buffer, buffer.shape, False
        self.copy = pltpu.make_async_copy(source, buffer, semaphore)
        self.copy.start()

    def wait(self):
        if not self.waited:
            self.copy.wait()
            self.waited = True

    def __getitem__(self, index):
        self.wait()
        return self.buffer[index]


class Stored:
    def __init__(self, target, buffer, semaphore):
        self.buffer, self.shape, self.dtype, self.started = buffer, buffer.shape, buffer.dtype, False
        self.copy = pltpu.make_async_copy(buffer, target, semaphore)

    def __setitem__(self, index, values):
        self.buffer[index] = values

    def __getitem__(self, index):
        return self.buffer[index]

    def flush(self):
        if not self.started:
            self.copy.start()
            self.started = True


def call(kernel, inputs, outputs, scratch=(), mebibytes=16):
    in_specs, arrays, buffers = [], [], []
    for value in inputs:
        far = isinstance(value, Far)
        in_specs.append(HBM if far else VMEM)
        arrays.append(
            pltpu.with_memory_space_constraint(value.value, pltpu.HBM) if far else value
        )
        if far:
            buffers.append(pltpu.VMEM(value.value.shape, value.value.dtype))
    buffers.extend(pltpu.VMEM(out.shape, out.dtype) for out in outputs if out.far)
    flags = [isinstance(value, Far) for value in inputs] + [out.far for out in outputs]
    sizes = len(inputs), len(flags), len(flags) + len(buffers)

    def body(*refs):
        semaphores = refs[sizes[2]] if buffers else None
        given, views = 0, []
        for at, far in enumerate(flags):
            if far:
                kind = Fetched if at < sizes[0] else Stored
                views.append(kind(refs[at], refs[sizes[1] + given], semaphores.at[given]))
                given += 1
            else:
                views.append(refs[at])
        kernel(*views, *refs[sizes[2] + (1 if buffers else 0) :])
        for view in views:
            if isinstance(view, Stored):
                view.flush()
        for view in views:
            if isinstance(view, Fetched):
                view.wait()
            if isinstance(view, Stored):
                view.copy.wait()

    own = [pltpu.SemaphoreType.DMA((len(buffers),))] if buffers else []
    return pl.pallas_call(
        body,
        out_shape=[
            (pltpu.HBM if out.far else jax.ShapeDtypeStruct)(out.shape, out.dtype)
            for out in outputs
        ],
        in_specs=in_specs,
        out_specs=[HBM if out.far else VMEM for out in outputs],
        scratch_shapes=buffers + own + list(scratch),
        compiler_params=pltpu.CompilerParams(vmem_limit_bytes=mebibytes * 1024 * 1024),
    )(*arrays)


def exchange(values):
    return lax.ppermute(values, "grp", [(0, 1), (1, 0)])


def spread_blocks(values, axes):
    return lax.all_to_all(values, axes, split_axis=0, concat_axis=0, tiled=True)


def neighbours(owners, stride):
    pairs = []
    for chip in range(owners):
        place = chip // stride % 4
        for core in range(2):
            partner = ((place + core ^ 1) - core) % 4
            pairs.append((2 * chip + core, 2 * (chip + (partner - place) * stride) + core))
    return pairs


def route(values, devices):
    rows, features = values.shape
    blocks = values.reshape(devices, rows // devices, features)
    return spread_blocks(blocks, ("pts", "grp")).reshape(rows, features)


def on_device(
    points,
    rotated_place,
    rotated_source,
    ball_counts,
    fine_projection,
    fine_output,
    pool_weight,
    coarse_projection,
    coarse_output,
    coarse_cotangent,
):
    count, features = points.shape
    devices = lax.axis_size(("pts", "grp"))
    slots = 2 * count
    scaling = 1.0 / math.sqrt(count * devices)
    owners = lax.axis_size("pts")
    run, step = owners // 4, owners // 16
    wide = 2 * features
    half_rows = count // 2

    send, send_slot, pair_slot, receive_slot, live = call(
        route_kernel,
        (
            Far(rotated_place.reshape(1, count)),
            Far(rotated_source.reshape(1, count)),
            Far(ball_counts.reshape(1, -1)),
            Far(points),
        ),
        (
            Near((slots, features)),
            Near((1, count), jnp.int32),
            Near((1, count), jnp.int32),
            Near((1, count), jnp.int32),
            Near((1, count), F32),
        ),
    )
    arrived = route(send, devices)
    heads = features // HD * (count // BALL)
    send, rotated, projected, mixture, weights = call(
        fine_forward_kernel,
        (arrived, receive_slot, live, fine_projection, Far(fine_output)),
        (
            Near((slots, features)),
            Near((count, features)),
            Near((count, 3 * features)),
            Near((count, features)),
            Near((heads, BALL, BALL)),
        ),
    )
    arrived = route(send, devices)
    (own_pack,) = call(
        join_kernel, (arrived, pair_slot, coarse_cotangent), (Near((half_rows, 2 * wide)),)
    )
    other_pack = exchange(own_pack)
    coarse, keep, give, unit = call(
        coarse_kernel,
        (own_pack, other_pack, pool_weight, coarse_projection, Far(coarse_output)),
        (
            Near((half_rows, wide)),
            Near((half_rows, 2 * wide)),
            Near((half_rows, 2 * wide)),
            Near((count, wide)),
        ),
    )
    got = exchange(give)
    blocks = (owners, 2, slots // devices)
    kept, first_half, second_half = call(
        functools.partial(coarse_weights_kernel, strides=(run, step)),
        (unit, keep, give, own_pack, other_pack),
        (
            Near((*blocks, wide // 2)),
            Near((*blocks, wide // 4)),
            Near((*blocks, wide // 4)),
        ),
    )
    got, kept, first_half, second_half = lax.optimization_barrier(
        (got, kept, first_half, second_half)
    )
    coarse_result, coarse_gradient, send = call(
        coarse_finish_kernel,
        (
            coarse,
            keep,
            got,
            coarse_cotangent,
            pool_weight,
            coarse_projection,
            coarse_output,
            pair_slot,
        ),
        (
            Near((half_rows, wide), far=True),
            Near((half_rows, wide)),
            Near((slots, features)),
        ),
    )
    arrived = route(send, devices)
    arrived, first_half, second_half, coarse_gradient = lax.optimization_barrier(
        (arrived, first_half, second_half, coarse_gradient)
    )
    got_first = lax.ppermute(first_half, ("pts", "grp"), neighbours(owners, run))
    got_second = lax.ppermute(second_half, ("pts", "grp"), neighbours(owners, step))
    other_gradient = exchange(coarse_gradient)
    tokens, fine_kept, fine_passed = call(
        fine_backward_kernel,
        (
            arrived,
            receive_slot,
            rotated,
            projected,
            mixture,
            weights,
            fine_projection,
            fine_output,
        ),
        (
            Near((*blocks, features)),
            Near((features, 2 * features), F32),
            Near((features, 2 * features)),
        ),
        scratch=(pltpu.VMEM((count, 3 * features), BF),),
    )
    fine_got = exchange(fine_passed)
    (coarse_part,) = call(
        coarse_part_kernel,
        (
            kept,
            got_first,
            got_second,
            own_pack,
            other_pack,
            coarse_gradient,
            other_gradient,
        ),
        (Near((*blocks, 3 * wide // 4)),),
    )
    across = features + wide
    (send,) = call(
        assemble_kernel,
        (tokens, fine_kept, fine_got, coarse_part),
        (Near((*blocks, across)),),
    )
    arrived = spread_blocks(send.reshape(devices, slots // devices, across), ("pts", "grp"))
    (spread,) = call(
        functools.partial(sum_kernel, tokens=features, run=run, step=step),
        (arrived.reshape(send.shape),),
        (Near((owners, slots // devices, features + 5 * wide // 2)),),
    )
    own_sums = spread_blocks(spread, "pts")
    (points_gradient,) = call(
        take_kernel, (arrived[:, :, :features], send_slot), (Near((count, features)),)
    )
    other_sums = exchange(own_sums)
    sums = write_sums(own_sums, other_sums, features, wide, scaling)
    return (coarse_result, points_gradient, *sums)


def solution(mesh):
    tokens = P(("pts", "grp"), None)
    in_specs = (
        tokens,
        P(("pts", "grp")),
        P(("pts", "grp")),
        P(),
        P(),
        P(),
        P(),
        P(),
        P(),
        tokens,
    )
    out_specs = (tokens, tokens, P(), P(), P(), P(), P())
    return jax.shard_map(
        on_device, mesh=mesh, in_specs=in_specs, out_specs=out_specs, check_vma=False
    )
```

```python
import functools
import math
from typing import NamedTuple

import jax
import jax.numpy as jnp
from jax import lax
from jax.experimental import pallas as pl
from jax.experimental.pallas import tpu as pltpu
from jax.sharding import PartitionSpec as P

HD = 64
BALL = 256
PAIR = 2 * HD
EPSILON = 1e-05
BF = jnp.bfloat16
F32 = jnp.float32


def mm(a, b, contract=(1, 0)):
    return lax.dot_general(
        a, b, (((contract[0],), (contract[1],)), ((), ())), preferred_element_type=F32
    )


def normalize(values):
    floats = values.astype(F32)
    center = floats - jnp.mean(floats, axis=-1, keepdims=True)
    inverse = lax.rsqrt(jnp.mean(center * center, axis=-1, keepdims=True) + EPSILON)
    return center * inverse, inverse


def norm_backward(incoming, normed, inverse):
    first_mean = jnp.mean(incoming, axis=-1, keepdims=True)
    second_mean = jnp.mean(incoming * normed, axis=-1, keepdims=True)
    return inverse * (incoming - first_mean - normed * second_mean)


def one_hot(slots, total):
    shape = (total, slots.shape[1])
    return (lax.broadcasted_iota(jnp.int32, shape, 0) == slots).astype(BF)


def softmax_rows(scores):
    raised = jnp.exp(scores - jnp.max(scores, axis=-1, keepdims=True))
    return (raised * (1.0 / jnp.sum(raised, axis=-1, keepdims=True))).astype(BF)


def slopes_of(weights, against):
    wide = weights.astype(F32)
    diagonal = jnp.sum(wide * against, axis=-1, keepdims=True)
    return (wide * (against - diagonal)).astype(BF)


def stack_heads(rows, heads):
    lanes = lax.broadcasted_iota(jnp.int32, rows.shape, 1) // HD
    none = jnp.zeros_like(rows)
    return jnp.concatenate([jnp.where(lanes == at, rows, none) for at in range(heads)], axis=0)


def unstack_heads(rows, heads):
    count = rows.shape[0] // heads
    merged = rows[:count]
    lanes = lax.broadcasted_iota(jnp.int32, merged.shape, 1) // HD
    for at in range(1, heads):
        merged = jnp.where(lanes == at, rows[at * count : (at + 1) * count], merged)
    return merged


def turned(rows):
    return rows.astype(F32).T.astype(BF)


def column_of(row):
    count = row.shape[1]
    turned = jnp.broadcast_to(row.astype(F32), (128, count)).T
    return jnp.concatenate([turned] * (count // 128), axis=1)


def route_kernel(
    place, source, counts, points, send, send_slot, pair_slot, receive_slot, live
):
    count = place.shape[1]
    shift = count.bit_length() - 1
    capacity = send.shape[0] * count // (counts.shape[1] * BALL)
    to_row = place[...] >> shift
    rows = lax.broadcasted_iota(jnp.int32, (count, count), 0)
    columns = lax.broadcasted_iota(jnp.int32, (count, count), 1)
    earlier = (column_of(to_row) == to_row.astype(F32)) & (rows < columns)
    rank = jnp.sum(jnp.where(earlier, 1.0, 0.0), axis=0, keepdims=True)
    slot = to_row * capacity + rank.astype(jnp.int32)
    send_slot[...] = slot
    even_first = jnp.where(columns < count // 2, 2 * columns, 2 * columns + 1 - count)
    digits = jnp.concatenate([slot >> 5, slot & 31] + [jnp.zeros_like(slot)] * 6, axis=0)
    moved = mm(digits.astype(F32).astype(BF), (rows == even_first).astype(BF)).astype(jnp.int32)
    pair_slot[...] = moved[0:1] * 32 + moved[1:2]
    source_row = source[...]
    from_row = source_row >> shift
    earlier = (column_of(from_row) == from_row.astype(F32)) & (
        column_of(source_row) < source_row.astype(F32)
    )
    rank = jnp.sum(jnp.where(earlier, 1.0, 0.0), axis=0, keepdims=True)
    receive_slot[...] = from_row * capacity + rank.astype(jnp.int32)
    balls = counts.shape[1]
    own_ball = one_hot(source_row >> (BALL.bit_length() - 1), balls)
    filled = mm(jnp.broadcast_to(counts[...].astype(F32), (8, balls)).astype(BF), own_ball)
    inside = (source_row & (BALL - 1)).astype(F32)
    live[...] = jnp.where(inside < filled[:1], 1.0, 0.0)
    send[...] = mm(one_hot(slot, send.shape[0]), points[...]).astype(BF)


def fine_forward_kernel(
    arrived, receive_slot, live, projection, output, send, rotated, projected, mixture, weights
):
    place = one_hot(receive_slot[...], arrived.shape[0])
    rows_in = mm(place, arrived[...], (0, 0))
    rotated[...] = rows_in.astype(BF)
    features = rows_in.shape[1]
    normed, _ = normalize(rows_in)
    projected[...] = mm(normed.astype(BF), projection[...]).astype(BF)
    balls = rows_in.shape[0] // BALL
    for ball in range(balls):
        rows = slice(ball * BALL, (ball + 1) * BALL)
        alive = live[:, rows] > 0.5
        for pair in range(features // PAIR):
            lanes = slice(pair * PAIR, (pair + 1) * PAIR)
            query = projected[rows, lanes] * jnp.asarray(HD ** (-0.5), BF)
            key = projected[rows, features + pair * PAIR : features + (pair + 1) * PAIR]
            value = projected[rows, 2 * features + pair * PAIR : 2 * features + (pair + 1) * PAIR]
            scores = mm(stack_heads(query, 2), key, (1, 1))
            both = softmax_rows(jnp.where(alive, scores, -1e30))
            first = (ball * features + pair * PAIR) // HD
            weights[first : first + 2] = both.reshape(2, BALL, BALL)
            mixture[rows, lanes] = unstack_heads(mm(both, value), 2).astype(BF)
    result = (rows_in + mm(mixture[...], output[...])).astype(BF)
    send[...] = mm(place, result).astype(BF)


def join_kernel(arrived, pair_slot, cotangent, pack):
    half_rows, wide = cotangent.shape
    place = one_hot(pair_slot[...], arrived.shape[0])
    rows = mm(place, arrived[...], (0, 0)).astype(BF)
    pack[:, : wide // 2] = rows[:half_rows]
    pack[:, wide // 2 : wide] = rows[half_rows:]
    pack[:, wide:] = cotangent[...]


def coarse_kernel(
    own_pack, other_pack, pool, projection, output, coarse, keep, give, unit
):
    half_rows, wide = coarse.shape
    part = wide // 2
    first = pl.multiple_of(lax.axis_index("grp") * part, part)
    joined = jnp.concatenate([own_pack[:, :wide], other_pack[:, :wide]], axis=0)
    tokens = mm(joined, pool[...]).astype(BF)
    coarse[...] = tokens[:half_rows]
    normed, _ = normalize(tokens)
    unit_rows = normed.astype(BF)
    unit[...] = unit_rows
    queries = mm(unit_rows, projection[:, pl.ds(first, part)]).astype(BF)
    keys = mm(unit_rows, projection[:, pl.ds(wide + first, part)]).astype(BF)
    values = mm(unit_rows, projection[:, pl.ds(2 * wide + first, part)]).astype(BF)
    cotangent = jnp.concatenate([own_pack[:, wide:], other_pack[:, wide:]], axis=0)
    incoming = mm(cotangent, output[pl.ds(first, part), :], (1, 1)).astype(BF)
    queries_turned, incoming_turned = turned(queries), turned(incoming)
    key_parts, value_parts = [], []

    def put(at, rows):
        target = slice(at, at + rows.shape[1])
        keep[:, target] = rows[:half_rows]
        give[:, target] = rows[half_rows:]

    for pair in range(part // PAIR):
        lanes = slice(pair * PAIR, (pair + 1) * PAIR)
        key, value = keys[:, lanes], values[:, lanes]
        query = queries[:, lanes] * jnp.asarray(HD ** (-0.5), BF)
        head_weights = softmax_rows(mm(stack_heads(query, 2), key, (1, 1)))
        against = mm(stack_heads(incoming[:, lanes], 2), value, (1, 1))
        slopes = slopes_of(head_weights, against)
        put(pair * PAIR, unstack_heads(mm(head_weights, value), 2).astype(BF))
        query_part = unstack_heads(mm(slopes, key), 2) * HD ** (-0.5)
        put(part + pair * PAIR, query_part.astype(BF))
        for half in range(2):
            band = slice(pair * PAIR + half * HD, pair * PAIR + (half + 1) * HD)
            rows = slice(half * 2 * half_rows, (half + 1) * 2 * half_rows)
            key_parts.append(mm(queries_turned[band], slopes[rows]) * HD ** (-0.5))
            value_parts.append(mm(incoming_turned[band], head_weights[rows]))
    put(2 * part, jnp.concatenate(key_parts, axis=0).T.astype(BF))
    put(3 * part, jnp.concatenate(value_parts, axis=0).T.astype(BF))


def coarse_finish_kernel(
    coarse,
    keep,
    got,
    cotangent,
    pool,
    projection,
    output,
    pair_slot,
    result,
    gradient,
    send,
):
    half_rows, wide = coarse.shape
    part = wide // 2
    mixed = coarse[...].astype(F32)
    back = jnp.zeros((half_rows, wide), F32)
    for source, index in ((keep, lax.axis_index("grp")), (got, 1 - lax.axis_index("grp"))):
        first = pl.multiple_of(index * part, part)
        mixed = mixed + mm(source[:, :part], output[pl.ds(first, part), :])
        for at in range(3):
            back = back + mm(
                source[:, (at + 1) * part : (at + 2) * part],
                projection[:, pl.ds(at * wide + first, part)],
                (1, 1),
            )
    result[...] = mixed.astype(BF)
    result.flush()
    normed, inverse = normalize(coarse[...])
    gradient_rows = (
        cotangent[...].astype(F32) + norm_backward(back, normed, inverse)
    ).astype(BF)
    gradient[...] = gradient_rows
    fine = mm(gradient_rows, pool[...], (1, 1)).astype(BF)
    features = send.shape[1]
    stacked = jnp.concatenate([fine[:, :features], fine[:, features:]], axis=0)
    send[...] = mm(one_hot(pair_slot[...], send.shape[0]), stacked).astype(BF)


def coarse_weights_kernel(
    unit, keep, give, own_pack, other_pack, kept, across_x, across_y, across_both, *, strides
):
    chip, core = lax.axis_index("pts"), lax.axis_index("grp")
    roles = [(chip // stride + core) % 2 == 1 for stride in strides]
    wide = unit.shape[1]
    part = wide // 2
    stacked = jnp.concatenate([keep[...], give[...]], axis=0)
    cotangent = jnp.concatenate([own_pack[:, wide:], other_pack[:, wide:]], axis=0)
    projection_term = mm(unit[...], stacked[:, part:], (0, 0))
    output_term = mm(stacked[:, :part], cotangent, (0, 0))
    across = projection_term.shape[1] // 2
    width = wide // 4
    for side in range(2):
        stack = [output_term[:, (2 * side + k) * width : (2 * side + k + 1) * width] for k in range(2)]
        first = side * across
        tiles = [projection_term[:, first + k * width : first + (k + 1) * width] for k in range(3)]
        tiles.append(jnp.concatenate(stack, axis=0))
        same = [jnp.where(roles[0], tiles[2 + k], tiles[k]) for k in range(2)]
        other = [jnp.where(roles[0], tiles[k], tiles[2 + k]) for k in range(2)]
        put_blocks(kept, side, 0, jnp.where(roles[1], same[1], same[0]))
        put_blocks(across_y, side, 0, jnp.where(roles[1], same[0], same[1]))
        put_blocks(across_x, side, 0, jnp.where(roles[1], other[1], other[0]))
        put_blocks(across_both, side, 0, jnp.where(roles[1], other[0], other[1]))


def put_quarters(blocks, lane, term):
    width = term.shape[1] // 4
    for side in range(2):
        stack = [term[:, (2 * side + k) * width : (2 * side + k + 1) * width] for k in range(2)]
        put_blocks(blocks, side, lane, jnp.concatenate(stack, axis=0))


def put_blocks(blocks, side, lane, rows):
    owners, width = blocks.shape[0], rows.shape[1]
    pieces = rows.reshape(owners, rows.shape[0] // owners, width)
    blocks[:, side, :, lane : lane + width] = pieces.astype(BF)


def sum_kernel(arrived, spread, *, tokens, run, step):
    senders, _, rows, across = arrived.shape
    width = (across - tokens) // 3

    def pieces(side, at):
        start = tokens + at * width
        return arrived[:, side, :, start : start + width].astype(F32)

    total = [jnp.sum(pieces(side, 0), axis=0) for side in range(2)]
    for side in range(2):
        shape = (senders // (2 * run), 2, run // (2 * step), 2, step, rows, width)
        split = jnp.sum(jnp.sum(pieces(side, 1).reshape(shape), axis=4), axis=2)
        split = jnp.sum(split, axis=0)
        total.extend(split[(x + side) % 2, (y + side) % 2] for x in range(2) for y in range(2))
        total.append(jnp.sum(pieces(side, 2), axis=0))
    total = jnp.concatenate(total, axis=1).astype(BF)
    spread[...] = jnp.broadcast_to(total[None], spread.shape)


def write_half(terms, side, refs, stages, semaphores, scaling):
    projection, output, pool = refs
    tall, square = stages
    wide = pool.shape[0]
    part, width = wide // 2, wide // 4
    across = 3 * part // 2
    copies = []

    def lanes(start, count):
        values = terms[:, :, start : start + count].astype(F32) * scaling
        return values.reshape(terms.shape[0] * terms.shape[1], count)

    def send(stage, target):
        copies.append(pltpu.make_async_copy(stage, target, semaphores.at[len(copies)]))
        copies[-1].start()

    for heads in range(2):
        start = 2 * width + heads * (across + 2 * width)
        for k in range(3):
            columns = [half * across + k * width for half in range(2)]
            places = [column // part * wide + heads * part + column % part for column in columns]
            target = pl.multiple_of(jnp.where(side == 0, places[0], places[1]), width)
            stage = tall.at[3 * heads + k]
            stage[...] = lanes(start + k * width, width)
            send(stage, projection.at[:, pl.ds(target, width)])
        for at, ref in enumerate((output, pool)):
            block = lanes(start + across + at * width, width)
            stage = square.at[2 * heads + at]
            stage[:, :width] = block[:part]
            stage[:, width:] = block[part:]
            target = pl.multiple_of(side * part, part)
            send(stage, ref.at[heads * part : (heads + 1) * part, pl.ds(target, part)])
    return copies


def own_sums_kernel(own, projection, output, pool, tall, square, semaphores, *, scaling):
    side = lax.axis_index("grp")
    refs = (projection, output, pool)
    for copy in write_half(own, side, refs, (tall, square), semaphores, scaling):
        copy.wait()


def other_sums_kernel(
    own,
    other,
    projection_in,
    output_in,
    pool_in,
    projection,
    output,
    pool,
    fine_projection,
    fine_output,
    tall,
    square,
    semaphores,
    fine,
    fine_square,
    fine_semaphores,
    *,
    scaling,
):
    side = 1 - lax.axis_index("grp")
    refs = (projection, output, pool)
    copies = write_half(other, side, refs, (tall, square), semaphores, scaling)
    features = fine_output.shape[0]
    width = features // 2
    for heads in range(2):
        start = heads * width
        here, there = own[:, :, start : start + width], other[:, :, start : start + width]
        for half in range(2):
            values = jnp.where(side == half, there, here).astype(F32) * scaling
            block = values.reshape(own.shape[0] * own.shape[1], width)
            column = (2 * heads + half) * features
            for k in range(2):
                piece = block[k * features : (k + 1) * features]
                if column < 3 * features:
                    fine[:, column + k * width : column + (k + 1) * width] = piece
                else:
                    fine_square[:, k * width : (k + 1) * width] = piece
    copies.append(pltpu.make_async_copy(fine, fine_projection, fine_semaphores.at[0]))
    copies.append(pltpu.make_async_copy(fine_square, fine_output, fine_semaphores.at[1]))
    for copy in copies[-2:]:
        copy.start()
    for copy in copies:
        copy.wait()


def write_sums(own, other, features, wide, scaling):
    part, width = wide // 2, wide // 4
    shapes = [(wide, 3 * wide), (wide, wide), (wide, wide)]
    stages = [
        pltpu.VMEM((6, wide, width), F32),
        pltpu.VMEM((4, part, part), F32),
        pltpu.SemaphoreType.DMA((10,)),
    ]
    limits = pltpu.CompilerParams(vmem_limit_bytes=16 * 1024 * 1024)
    firsts = pl.pallas_call(
        functools.partial(own_sums_kernel, scaling=scaling),
        out_shape=[pltpu.HBM(shape, F32) for shape in shapes],
        in_specs=[VMEM],
        out_specs=[HBM] * 3,
        scratch_shapes=stages,
        compiler_params=limits,
    )(own)
    shapes += [(features, 3 * features), (features, features)]
    projection, output, pool, fine_projection, fine_output = pl.pallas_call(
        functools.partial(other_sums_kernel, scaling=scaling),
        out_shape=[pltpu.HBM(shape, F32) for shape in shapes],
        in_specs=[VMEM] * 2 + [HBM] * 3,
        out_specs=[HBM] * 5,
        scratch_shapes=stages
        + [
            pltpu.VMEM((features, 3 * features), F32),
            pltpu.VMEM((features, features), F32),
            pltpu.SemaphoreType.DMA((2,)),
        ],
        input_output_aliases={2: 0, 3: 1, 4: 2},
        compiler_params=limits,
    )(own, other, *firsts)
    return fine_projection, fine_output, pool, projection, output


def fine_backward_kernel(
    arrived,
    receive_slot,
    rotated,
    projected,
    mixture,
    weights,
    projection,
    output,
    tokens,
    kept,
    passed,
    grad_projected,
):
    place = one_hot(receive_slot[...], arrived.shape[0])
    gradient_rows = mm(place, arrived[...], (0, 0)).astype(BF)
    features = rotated.shape[1]
    entering = mm(gradient_rows, output[...], (1, 1)).astype(BF)
    terms = [mm(mixture[...], gradient_rows, (0, 0))]
    balls = rotated.shape[0] // BALL
    heads = features // HD
    query_turned, entering_turned = turned(projected[:, :features]), turned(entering)
    turned_parts = ([], [])
    for ball in range(balls):
        rows = slice(ball * BALL, (ball + 1) * BALL)
        key, value = projected[rows, features : 2 * features], projected[rows, 2 * features :]
        head_weights = [weights[ball * heads + at] for at in range(heads)]
        against = mm(stack_heads(entering[rows], heads), value, (1, 1))
        slopes = slopes_of(jnp.concatenate(head_weights, axis=0), against)
        query_part = unstack_heads(mm(slopes, key), heads) * HD ** (-0.5)
        grad_projected[rows, :features] = query_part.astype(BF)
        pieces = ([], [])
        for at in range(heads):
            band = slice(at * HD, (at + 1) * HD)
            own = slopes[at * BALL : (at + 1) * BALL]
            pieces[0].append(mm(query_turned[band, rows], own) * HD ** (-0.5))
            pieces[1].append(mm(entering_turned[band, rows], head_weights[at]))
        for at in range(2):
            turned_parts[at].append(jnp.concatenate(pieces[at], axis=0))
    for at in range(2):
        whole = jnp.concatenate(turned_parts[at], axis=1).T.astype(BF)
        grad_projected[:, (at + 1) * features : (at + 2) * features] = whole
    normed, inverse = normalize(rotated[...])
    unit_rows = normed.astype(BF)
    for at in range(3):
        columns = slice(at * features, (at + 1) * features)
        terms.insert(at, mm(unit_rows, grad_projected[:, columns], (0, 0)))
    low = jnp.concatenate(terms[:2], axis=1)
    high = jnp.concatenate(terms[2:], axis=1)
    upper = lax.axis_index("grp") == 1
    kept[...] = jnp.where(upper, high, low)
    passed[...] = jnp.where(upper, low, high).astype(BF)
    back = mm(grad_projected[...], projection[...], (1, 1))
    result = gradient_rows.astype(F32) + norm_backward(back, normed, inverse)
    tokens[...] = mm(place, result.astype(BF)).reshape(tokens.shape).astype(BF)


def coarse_part_kernel(
    kept, got_x, got_y, got_both, own_pack, other_pack, own_gradient, other_gradient, coarse
):
    width = kept.shape[3]
    pairs = kept[...].astype(F32) + got_x[...].astype(F32)
    pairs = pairs + (got_y[...].astype(F32) + got_both[...].astype(F32))
    coarse[:, :, :, :width] = pairs.astype(BF)
    part = own_gradient.shape[1] // 2
    first = pl.multiple_of(lax.axis_index("grp") * part, part)
    pool_term = mm(own_pack[:, pl.ds(first, part)], own_gradient[...], (0, 0))
    pool_term = pool_term + mm(other_pack[:, pl.ds(first, part)], other_gradient[...], (0, 0))
    put_quarters(coarse, width, pool_term)


def assemble_kernel(tokens, fine_kept, fine_got, coarse, send):
    start = tokens.shape[3]
    send[:, :, :, :start] = tokens[...]
    put_quarters(send, start, fine_kept[...] + fine_got[...].astype(F32))
    send[:, :, :, send.shape[3] - coarse.shape[3] :] = coarse[...]


def take_kernel(arrived, slots, rows_out):
    place = one_hot(slots[...], slots.shape[1] * 2)
    rows = arrived[...].reshape(place.shape[0], arrived.shape[-1])
    rows_out[...] = mm(place, rows, (0, 0)).astype(BF)


VMEM = pl.BlockSpec(memory_space=pltpu.VMEM)
HBM = pl.BlockSpec(memory_space=pltpu.HBM)


class Far(NamedTuple):
    value: jax.Array


class Near(NamedTuple):
    shape: tuple
    dtype: jnp.dtype = BF
    far: bool = False


class Fetched:
    def __init__(self, source, buffer, semaphore):
        self.buffer, self.shape, self.waited = buffer, buffer.shape, False
        self.copy = pltpu.make_async_copy(source, buffer, semaphore)
        self.copy.start()

    def wait(self):
        if not self.waited:
            self.copy.wait()
            self.waited = True

    def __getitem__(self, index):
        self.wait()
        return self.buffer[index]


class Stored:
    def __init__(self, target, buffer, semaphore):
        self.buffer, self.shape, self.dtype, self.started = buffer, buffer.shape, buffer.dtype, False
        self.copy = pltpu.make_async_copy(buffer, target, semaphore)

    def __setitem__(self, index, values):
        self.buffer[index] = values

    def __getitem__(self, index):
        return self.buffer[index]

    def flush(self):
        if not self.started:
            self.copy.start()
            self.started = True


def call(kernel, inputs, outputs, scratch=(), mebibytes=16):
    in_specs, arrays, buffers = [], [], []
    for value in inputs:
        far = isinstance(value, Far)
        in_specs.append(HBM if far else VMEM)
        arrays.append(
            pltpu.with_memory_space_constraint(value.value, pltpu.HBM) if far else value
        )
        if far:
            buffers.append(pltpu.VMEM(value.value.shape, value.value.dtype))
    buffers.extend(pltpu.VMEM(out.shape, out.dtype) for out in outputs if out.far)
    flags = [isinstance(value, Far) for value in inputs] + [out.far for out in outputs]
    sizes = len(inputs), len(flags), len(flags) + len(buffers)

    def body(*refs):
        semaphores = refs[sizes[2]] if buffers else None
        given, views = 0, []
        for at, far in enumerate(flags):
            if far:
                kind = Fetched if at < sizes[0] else Stored
                views.append(kind(refs[at], refs[sizes[1] + given], semaphores.at[given]))
                given += 1
            else:
                views.append(refs[at])
        kernel(*views, *refs[sizes[2] + (1 if buffers else 0) :])
        for view in views:
            if isinstance(view, Stored):
                view.flush()
        for view in views:
            if isinstance(view, Fetched):
                view.wait()
            if isinstance(view, Stored):
                view.copy.wait()

    own = [pltpu.SemaphoreType.DMA((len(buffers),))] if buffers else []
    return pl.pallas_call(
        body,
        out_shape=[
            (pltpu.HBM if out.far else jax.ShapeDtypeStruct)(out.shape, out.dtype)
            for out in outputs
        ],
        in_specs=in_specs,
        out_specs=[HBM if out.far else VMEM for out in outputs],
        scratch_shapes=buffers + own + list(scratch),
        compiler_params=pltpu.CompilerParams(vmem_limit_bytes=mebibytes * 1024 * 1024),
    )(*arrays)


def exchange(values):
    return lax.ppermute(values, "grp", [(0, 1), (1, 0)])


def spread_blocks(values, axes):
    return lax.all_to_all(values, axes, split_axis=0, concat_axis=0, tiled=True)


def neighbours(owners, stride):
    pairs = []
    for chip in range(owners):
        place = chip // stride % 4
        for core in range(2):
            partner = ((place + core ^ 1) - core) % 4
            pairs.append((2 * chip + core, 2 * (chip + (partner - place) * stride) + core))
    return pairs


def route(values, devices):
    rows, features = values.shape
    blocks = values.reshape(devices, rows // devices, features)
    return spread_blocks(blocks, ("pts", "grp")).reshape(rows, features)


def on_device(
    points,
    rotated_place,
    rotated_source,
    ball_counts,
    fine_projection,
    fine_output,
    pool_weight,
    coarse_projection,
    coarse_output,
    coarse_cotangent,
):
    count, features = points.shape
    devices = lax.axis_size(("pts", "grp"))
    slots = 2 * count
    scaling = 1.0 / math.sqrt(count * devices)
    owners = lax.axis_size("pts")
    run, step = owners // 4, owners // 16
    wide = 2 * features
    half_rows = count // 2

    send, send_slot, pair_slot, receive_slot, live = call(
        route_kernel,
        (
            Far(rotated_place.reshape(1, count)),
            Far(rotated_source.reshape(1, count)),
            Far(ball_counts.reshape(1, -1)),
            Far(points),
        ),
        (
            Near((slots, features)),
            Near((1, count), jnp.int32),
            Near((1, count), jnp.int32),
            Near((1, count), jnp.int32),
            Near((1, count), F32),
        ),
    )
    arrived = route(send, devices)
    heads = features // HD * (count // BALL)
    send, rotated, projected, mixture, weights = call(
        fine_forward_kernel,
        (arrived, receive_slot, live, fine_projection, Far(fine_output)),
        (
            Near((slots, features)),
            Near((count, features)),
            Near((count, 3 * features)),
            Near((count, features)),
            Near((heads, BALL, BALL)),
        ),
    )
    arrived = route(send, devices)
    (own_pack,) = call(
        join_kernel, (arrived, pair_slot, coarse_cotangent), (Near((half_rows, 2 * wide)),)
    )
    other_pack = exchange(own_pack)
    coarse, keep, give, unit = call(
        coarse_kernel,
        (own_pack, other_pack, pool_weight, coarse_projection, Far(coarse_output)),
        (
            Near((half_rows, wide)),
            Near((half_rows, 2 * wide)),
            Near((half_rows, 2 * wide)),
            Near((count, wide)),
        ),
    )
    got = exchange(give)
    blocks = (owners, 2, slots // devices)
    kept, *passed = call(
        functools.partial(coarse_weights_kernel, strides=(run, step)),
        (unit, keep, give, own_pack, other_pack),
        (Near((*blocks, wide // 4)),) * 4,
    )
    got, kept, passed = lax.optimization_barrier((got, kept, passed))
    coarse_result, coarse_gradient, send = call(
        coarse_finish_kernel,
        (
            coarse,
            keep,
            got,
            coarse_cotangent,
            pool_weight,
            coarse_projection,
            coarse_output,
            pair_slot,
        ),
        (
            Near((half_rows, wide), far=True),
            Near((half_rows, wide)),
            Near((slots, features)),
        ),
    )
    arrived = route(send, devices)
    arrived, passed, coarse_gradient = lax.optimization_barrier(
        (arrived, passed, coarse_gradient)
    )
    to_x, to_y = neighbours(owners, run), neighbours(owners, step)
    to_both = [(source, dict(to_y)[target]) for source, target in to_x]
    received = [
        lax.ppermute(tile, ("pts", "grp"), pairs)
        for tile, pairs in zip(passed, (to_x, to_y, to_both))
    ]
    other_gradient = exchange(coarse_gradient)
    tokens, fine_kept, fine_passed = call(
        fine_backward_kernel,
        (
            arrived,
            receive_slot,
            rotated,
            projected,
            mixture,
            weights,
            fine_projection,
            fine_output,
        ),
        (
            Near((*blocks, features)),
            Near((features, 2 * features), F32),
            Near((features, 2 * features)),
        ),
        scratch=(pltpu.VMEM((count, 3 * features), BF),),
    )
    fine_got = exchange(fine_passed)
    (coarse_part,) = call(
        coarse_part_kernel,
        (
            kept,
            *received,
            own_pack,
            other_pack,
            coarse_gradient,
            other_gradient,
        ),
        (Near((*blocks, wide // 2)),),
    )
    across = features + 3 * wide // 4
    (send,) = call(
        assemble_kernel,
        (tokens, fine_kept, fine_got, coarse_part),
        (Near((*blocks, across)),),
    )
    arrived = spread_blocks(send.reshape(devices, slots // devices, across), ("pts", "grp"))
    (spread,) = call(
        functools.partial(sum_kernel, tokens=features, run=run, step=step),
        (arrived.reshape(send.shape),),
        (Near((owners, slots // devices, features + 5 * wide // 2)),),
    )
    own_sums = spread_blocks(spread, "pts")
    (points_gradient,) = call(
        take_kernel, (arrived[:, :, :features], send_slot), (Near((count, features)),)
    )
    other_sums = exchange(own_sums)
    sums = write_sums(own_sums, other_sums, features, wide, scaling)
    return (coarse_result, points_gradient, *sums)


def solution(mesh):
    tokens = P(("pts", "grp"), None)
    in_specs = (
        tokens,
        P(("pts", "grp")),
        P(("pts", "grp")),
        P(),
        P(),
        P(),
        P(),
        P(),
        P(),
        tokens,
    )
    out_specs = (tokens, tokens, P(), P(), P(), P(), P())
    return jax.shard_map(
        on_device, mesh=mesh, in_specs=in_specs, out_specs=out_specs, check_vma=False
    )
```

```python
import functools
import math
from typing import NamedTuple

import jax
import jax.numpy as jnp
from jax import lax
from jax.experimental import pallas as pl
from jax.experimental.pallas import tpu as pltpu
from jax.sharding import PartitionSpec as P

HD = 64
BALL = 256
PAIR = 2 * HD
EPSILON = 1e-05
BF = jnp.bfloat16
F32 = jnp.float32


def mm(a, b, contract=(1, 0)):
    return lax.dot_general(
        a, b, (((contract[0],), (contract[1],)), ((), ())), preferred_element_type=F32
    )


def normalize(values):
    floats = values.astype(F32)
    center = floats - jnp.mean(floats, axis=-1, keepdims=True)
    inverse = lax.rsqrt(jnp.mean(center * center, axis=-1, keepdims=True) + EPSILON)
    return center * inverse, inverse


def norm_backward(incoming, normed, inverse):
    first_mean = jnp.mean(incoming, axis=-1, keepdims=True)
    second_mean = jnp.mean(incoming * normed, axis=-1, keepdims=True)
    return inverse * (incoming - first_mean - normed * second_mean)


def one_hot(slots, total):
    shape = (total, slots.shape[1])
    return (lax.broadcasted_iota(jnp.int32, shape, 0) == slots).astype(BF)


def softmax_rows(scores):
    raised = jnp.exp(scores - jnp.max(scores, axis=-1, keepdims=True))
    return (raised * (1.0 / jnp.sum(raised, axis=-1, keepdims=True))).astype(BF)


def slopes_of(weights, against):
    wide = weights.astype(F32)
    diagonal = jnp.sum(wide * against, axis=-1, keepdims=True)
    return (wide * (against - diagonal)).astype(BF)


def stack_heads(rows, heads):
    lanes = lax.broadcasted_iota(jnp.int32, rows.shape, 1) // HD
    none = jnp.zeros_like(rows)
    return jnp.concatenate([jnp.where(lanes == at, rows, none) for at in range(heads)], axis=0)


def unstack_heads(rows, heads):
    count = rows.shape[0] // heads
    merged = rows[:count]
    lanes = lax.broadcasted_iota(jnp.int32, merged.shape, 1) // HD
    for at in range(1, heads):
        merged = jnp.where(lanes == at, rows[at * count : (at + 1) * count], merged)
    return merged


def turned(rows):
    return rows.astype(F32).T.astype(BF)


def column_of(row):
    count = row.shape[1]
    turned = jnp.broadcast_to(row.astype(F32), (128, count)).T
    return jnp.concatenate([turned] * (count // 128), axis=1)


def route_kernel(
    place, source, counts, points, send, send_slot, pair_slot, receive_slot, live
):
    count = place.shape[1]
    shift = count.bit_length() - 1
    capacity = send.shape[0] * count // (counts.shape[1] * BALL)
    to_row = place[...] >> shift
    rows = lax.broadcasted_iota(jnp.int32, (count, count), 0)
    columns = lax.broadcasted_iota(jnp.int32, (count, count), 1)
    earlier = (column_of(to_row) == to_row.astype(F32)) & (rows < columns)
    rank = jnp.sum(jnp.where(earlier, 1.0, 0.0), axis=0, keepdims=True)
    slot = to_row * capacity + rank.astype(jnp.int32)
    send_slot[...] = slot
    even_first = jnp.where(columns < count // 2, 2 * columns, 2 * columns + 1 - count)
    digits = jnp.concatenate([slot >> 5, slot & 31] + [jnp.zeros_like(slot)] * 6, axis=0)
    moved = mm(digits.astype(F32).astype(BF), (rows == even_first).astype(BF)).astype(jnp.int32)
    pair_slot[...] = moved[0:1] * 32 + moved[1:2]
    source_row = source[...]
    from_row = source_row >> shift
    earlier = (column_of(from_row) == from_row.astype(F32)) & (
        column_of(source_row) < source_row.astype(F32)
    )
    rank = jnp.sum(jnp.where(earlier, 1.0, 0.0), axis=0, keepdims=True)
    receive_slot[...] = from_row * capacity + rank.astype(jnp.int32)
    balls = counts.shape[1]
    own_ball = one_hot(source_row >> (BALL.bit_length() - 1), balls)
    filled = mm(jnp.broadcast_to(counts[...].astype(F32), (8, balls)).astype(BF), own_ball)
    inside = (source_row & (BALL - 1)).astype(F32)
    live[...] = jnp.where(inside < filled[:1], 1.0, 0.0)
    send[...] = mm(one_hot(slot, send.shape[0]), points[...]).astype(BF)


def fine_forward_kernel(
    arrived, receive_slot, live, projection, output, send, rotated, projected, mixture, weights
):
    place = one_hot(receive_slot[...], arrived.shape[0])
    rows_in = mm(place, arrived[...], (0, 0))
    rotated[...] = rows_in.astype(BF)
    features = rows_in.shape[1]
    normed, _ = normalize(rows_in)
    projected[...] = mm(normed.astype(BF), projection[...]).astype(BF)
    balls = rows_in.shape[0] // BALL
    for ball in range(balls):
        rows = slice(ball * BALL, (ball + 1) * BALL)
        alive = live[:, rows] > 0.5
        for pair in range(features // PAIR):
            lanes = slice(pair * PAIR, (pair + 1) * PAIR)
            query = projected[rows, lanes] * jnp.asarray(HD ** (-0.5), BF)
            key = projected[rows, features + pair * PAIR : features + (pair + 1) * PAIR]
            value = projected[rows, 2 * features + pair * PAIR : 2 * features + (pair + 1) * PAIR]
            scores = mm(stack_heads(query, 2), key, (1, 1))
            both = softmax_rows(jnp.where(alive, scores, -1e30))
            first = (ball * features + pair * PAIR) // HD
            weights[first : first + 2] = both.reshape(2, BALL, BALL)
            mixture[rows, lanes] = unstack_heads(mm(both, value), 2).astype(BF)
    result = (rows_in + mm(mixture[...], output[...])).astype(BF)
    send[...] = mm(place, result).astype(BF)


def join_kernel(arrived, pair_slot, cotangent, pack):
    half_rows, wide = cotangent.shape
    place = one_hot(pair_slot[...], arrived.shape[0])
    rows = mm(place, arrived[...], (0, 0)).astype(BF)
    pack[:, : wide // 2] = rows[:half_rows]
    pack[:, wide // 2 : wide] = rows[half_rows:]
    pack[:, wide:] = cotangent[...]


def coarse_kernel(
    own_pack, other_pack, pool, projection, output, coarse, keep, give, unit
):
    half_rows, wide = coarse.shape
    part = wide // 2
    first = pl.multiple_of(lax.axis_index("grp") * part, part)
    joined = jnp.concatenate([own_pack[:, :wide], other_pack[:, :wide]], axis=0)
    tokens = mm(joined, pool[...]).astype(BF)
    coarse[...] = tokens[:half_rows]
    normed, _ = normalize(tokens)
    unit_rows = normed.astype(BF)
    unit[...] = unit_rows
    queries = mm(unit_rows, projection[:, pl.ds(first, part)]).astype(BF)
    keys = mm(unit_rows, projection[:, pl.ds(wide + first, part)]).astype(BF)
    values = mm(unit_rows, projection[:, pl.ds(2 * wide + first, part)]).astype(BF)
    cotangent = jnp.concatenate([own_pack[:, wide:], other_pack[:, wide:]], axis=0)
    incoming = mm(cotangent, output[pl.ds(first, part), :], (1, 1)).astype(BF)
    queries_turned, incoming_turned = turned(queries), turned(incoming)
    key_parts, value_parts = [], []

    def put(at, rows):
        target = slice(at, at + rows.shape[1])
        keep[:, target] = rows[:half_rows]
        give[:, target] = rows[half_rows:]

    for pair in range(part // PAIR):
        lanes = slice(pair * PAIR, (pair + 1) * PAIR)
        key, value = keys[:, lanes], values[:, lanes]
        query = queries[:, lanes] * jnp.asarray(HD ** (-0.5), BF)
        head_weights = softmax_rows(mm(stack_heads(query, 2), key, (1, 1)))
        against = mm(stack_heads(incoming[:, lanes], 2), value, (1, 1))
        slopes = slopes_of(head_weights, against)
        put(pair * PAIR, unstack_heads(mm(head_weights, value), 2).astype(BF))
        query_part = unstack_heads(mm(slopes, key), 2) * HD ** (-0.5)
        put(part + pair * PAIR, query_part.astype(BF))
        for half in range(2):
            band = slice(pair * PAIR + half * HD, pair * PAIR + (half + 1) * HD)
            rows = slice(half * 2 * half_rows, (half + 1) * 2 * half_rows)
            key_parts.append(mm(queries_turned[band], slopes[rows]) * HD ** (-0.5))
            value_parts.append(mm(incoming_turned[band], head_weights[rows]))
    put(2 * part, jnp.concatenate(key_parts, axis=0).T.astype(BF))
    put(3 * part, jnp.concatenate(value_parts, axis=0).T.astype(BF))


def heads_back(grads, index, projection, output):
    wide = output.shape[1]
    part = wide // 2
    first = pl.multiple_of(index * part, part)
    mixed = mm(grads[:, :part], output[pl.ds(first, part), :])
    back = jnp.zeros_like(mixed)
    for at in range(3):
        back = back + mm(
            grads[:, (at + 1) * part : (at + 2) * part],
            projection[:, pl.ds(at * wide + first, part)],
            (1, 1),
        )
    return mixed, back


def coarse_own_kernel(coarse, keep, projection, output, mixed, back):
    own_mixed, own_back = heads_back(keep, lax.axis_index("grp"), projection, output)
    mixed[...] = coarse[...].astype(F32) + own_mixed
    back[...] = own_back


def coarse_finish_kernel(
    coarse,
    mixed,
    back,
    got,
    cotangent,
    pool,
    projection,
    output,
    pair_slot,
    result,
    gradient,
    send,
):
    other_mixed, other_back = heads_back(got, 1 - lax.axis_index("grp"), projection, output)
    result[...] = (mixed[...] + other_mixed).astype(BF)
    result.flush()
    normed, inverse = normalize(coarse[...])
    gradient_rows = (
        cotangent[...].astype(F32) + norm_backward(back[...] + other_back, normed, inverse)
    ).astype(BF)
    gradient[...] = gradient_rows
    fine = mm(gradient_rows, pool[...], (1, 1)).astype(BF)
    features = send.shape[1]
    stacked = jnp.concatenate([fine[:, :features], fine[:, features:]], axis=0)
    send[...] = mm(one_hot(pair_slot[...], send.shape[0]), stacked).astype(BF)


def coarse_weights_kernel(
    unit, keep, give, own_pack, other_pack, kept, first_half, second_half, *, strides
):
    chip, core = lax.axis_index("pts"), lax.axis_index("grp")
    wide = unit.shape[1]
    part = wide // 2
    stacked = jnp.concatenate([keep[...], give[...]], axis=0)
    cotangent = jnp.concatenate([own_pack[:, wide:], other_pack[:, wide:]], axis=0)
    projection_term = mm(unit[...], stacked[:, part:], (0, 0))
    output_term = mm(stacked[:, :part], cotangent, (0, 0))
    across = projection_term.shape[1] // 2
    width = wide // 4
    for side in range(2):
        stack = [output_term[:, (2 * side + k) * width : (2 * side + k + 1) * width] for k in range(2)]
        columns = projection_term[:, side * across : (side + 1) * across]
        terms = jnp.concatenate([columns, jnp.concatenate(stack, axis=0)], axis=1)
        for at, passed in enumerate((first_half, second_half)):
            low = terms[:, 2 * at * width : (2 * at + 1) * width]
            high = terms[:, (2 * at + 1) * width : (2 * at + 2) * width]
            upper = (chip // strides[at] + core) % 2 == 1
            put_blocks(kept, side, at * width, jnp.where(upper, high, low))
            put_blocks(passed, side, 0, jnp.where(upper, low, high))


def put_quarters(blocks, lane, term):
    width = term.shape[1] // 4
    for side in range(2):
        stack = [term[:, (2 * side + k) * width : (2 * side + k + 1) * width] for k in range(2)]
        put_blocks(blocks, side, lane, jnp.concatenate(stack, axis=0))


def put_blocks(blocks, side, lane, rows):
    owners, width = blocks.shape[0], rows.shape[1]
    pieces = rows.reshape(owners, rows.shape[0] // owners, width)
    blocks[:, side, :, lane : lane + width] = pieces.astype(BF)


def sum_kernel(arrived, spread, *, tokens, run, step):
    senders, _, rows, across = arrived.shape
    width = (across - tokens) // 4

    def pieces(side, at):
        start = tokens + at * width
        return arrived[:, side, :, start : start + width].astype(F32)

    total = [jnp.sum(pieces(side, 0), axis=0) for side in range(2)]
    for side in range(2):
        for at, block in enumerate((run, step)):
            split = pieces(side, 1 + at).reshape(senders // (2 * block), 2, block, rows, width)
            halves = jnp.sum(jnp.sum(split, axis=2), axis=0)
            total.extend([halves[side], halves[1 - side]])
        total.append(jnp.sum(pieces(side, 3), axis=0))
    total = jnp.concatenate(total, axis=1).astype(BF)
    spread[...] = jnp.broadcast_to(total[None], spread.shape)


def write_half(terms, side, refs, stages, semaphores, scaling):
    projection, output, pool = refs
    tall, square = stages
    wide = pool.shape[0]
    part, width = wide // 2, wide // 4
    across = 3 * part // 2
    copies = []

    def lanes(start, count):
        values = terms[:, :, start : start + count].astype(F32) * scaling
        return values.reshape(terms.shape[0] * terms.shape[1], count)

    def send(stage, target):
        copies.append(pltpu.make_async_copy(stage, target, semaphores.at[len(copies)]))
        copies[-1].start()

    for heads in range(2):
        start = 2 * width + heads * (across + 2 * width)
        for k in range(3):
            columns = [half * across + k * width for half in range(2)]
            places = [column // part * wide + heads * part + column % part for column in columns]
            target = pl.multiple_of(jnp.where(side == 0, places[0], places[1]), width)
            stage = tall.at[3 * heads + k]
            stage[...] = lanes(start + k * width, width)
            send(stage, projection.at[:, pl.ds(target, width)])
        for at, ref in enumerate((output, pool)):
            block = lanes(start + across + at * width, width)
            stage = square.at[2 * heads + at]
            stage[:, :width] = block[:part]
            stage[:, width:] = block[part:]
            target = pl.multiple_of(side * part, part)
            send(stage, ref.at[heads * part : (heads + 1) * part, pl.ds(target, part)])
    return copies


def own_sums_kernel(own, projection, output, pool, tall, square, semaphores, *, scaling):
    side = lax.axis_index("grp")
    refs = (projection, output, pool)
    for copy in write_half(own, side, refs, (tall, square), semaphores, scaling):
        copy.wait()


def other_sums_kernel(
    own,
    other,
    projection_in,
    output_in,
    pool_in,
    projection,
    output,
    pool,
    fine_projection,
    fine_output,
    tall,
    square,
    semaphores,
    fine,
    fine_square,
    fine_semaphores,
    *,
    scaling,
):
    side = 1 - lax.axis_index("grp")
    refs = (projection, output, pool)
    copies = write_half(other, side, refs, (tall, square), semaphores, scaling)
    features = fine_output.shape[0]
    width = features // 2
    for heads in range(2):
        start = heads * width
        here, there = own[:, :, start : start + width], other[:, :, start : start + width]
        for half in range(2):
            values = jnp.where(side == half, there, here).astype(F32) * scaling
            block = values.reshape(own.shape[0] * own.shape[1], width)
            column = (2 * heads + half) * features
            for k in range(2):
                piece = block[k * features : (k + 1) * features]
                if column < 3 * features:
                    fine[:, column + k * width : column + (k + 1) * width] = piece
                else:
                    fine_square[:, k * width : (k + 1) * width] = piece
    copies.append(pltpu.make_async_copy(fine, fine_projection, fine_semaphores.at[0]))
    copies.append(pltpu.make_async_copy(fine_square, fine_output, fine_semaphores.at[1]))
    for copy in copies[-2:]:
        copy.start()
    for copy in copies:
        copy.wait()


def write_sums(own, other, features, wide, scaling):
    part, width = wide // 2, wide // 4
    shapes = [(wide, 3 * wide), (wide, wide), (wide, wide)]
    stages = [
        pltpu.VMEM((6, wide, width), F32),
        pltpu.VMEM((4, part, part), F32),
        pltpu.SemaphoreType.DMA((10,)),
    ]
    limits = pltpu.CompilerParams(vmem_limit_bytes=16 * 1024 * 1024)
    firsts = pl.pallas_call(
        functools.partial(own_sums_kernel, scaling=scaling),
        out_shape=[pltpu.HBM(shape, F32) for shape in shapes],
        in_specs=[VMEM],
        out_specs=[HBM] * 3,
        scratch_shapes=stages,
        compiler_params=limits,
    )(own)
    shapes += [(features, 3 * features), (features, features)]
    projection, output, pool, fine_projection, fine_output = pl.pallas_call(
        functools.partial(other_sums_kernel, scaling=scaling),
        out_shape=[pltpu.HBM(shape, F32) for shape in shapes],
        in_specs=[VMEM] * 2 + [HBM] * 3,
        out_specs=[HBM] * 5,
        scratch_shapes=stages
        + [
            pltpu.VMEM((features, 3 * features), F32),
            pltpu.VMEM((features, features), F32),
            pltpu.SemaphoreType.DMA((2,)),
        ],
        input_output_aliases={2: 0, 3: 1, 4: 2},
        compiler_params=limits,
    )(own, other, *firsts)
    return fine_projection, fine_output, pool, projection, output


def fine_backward_kernel(
    arrived,
    receive_slot,
    rotated,
    projected,
    mixture,
    weights,
    projection,
    output,
    tokens,
    kept,
    passed,
    grad_projected,
):
    place = one_hot(receive_slot[...], arrived.shape[0])
    gradient_rows = mm(place, arrived[...], (0, 0)).astype(BF)
    features = rotated.shape[1]
    entering = mm(gradient_rows, output[...], (1, 1)).astype(BF)
    terms = [mm(mixture[...], gradient_rows, (0, 0))]
    balls = rotated.shape[0] // BALL
    heads = features // HD
    query_turned, entering_turned = turned(projected[:, :features]), turned(entering)
    turned_parts = ([], [])
    for ball in range(balls):
        rows = slice(ball * BALL, (ball + 1) * BALL)
        key, value = projected[rows, features : 2 * features], projected[rows, 2 * features :]
        head_weights = [weights[ball * heads + at] for at in range(heads)]
        against = mm(stack_heads(entering[rows], heads), value, (1, 1))
        slopes = slopes_of(jnp.concatenate(head_weights, axis=0), against)
        query_part = unstack_heads(mm(slopes, key), heads) * HD ** (-0.5)
        grad_projected[rows, :features] = query_part.astype(BF)
        pieces = ([], [])
        for at in range(heads):
            band = slice(at * HD, (at + 1) * HD)
            own = slopes[at * BALL : (at + 1) * BALL]
            pieces[0].append(mm(query_turned[band, rows], own) * HD ** (-0.5))
            pieces[1].append(mm(entering_turned[band, rows], head_weights[at]))
        for at in range(2):
            turned_parts[at].append(jnp.concatenate(pieces[at], axis=0))
    for at in range(2):
        whole = jnp.concatenate(turned_parts[at], axis=1).T.astype(BF)
        grad_projected[:, (at + 1) * features : (at + 2) * features] = whole
    normed, inverse = normalize(rotated[...])
    unit_rows = normed.astype(BF)
    for at in range(3):
        columns = slice(at * features, (at + 1) * features)
        terms.insert(at, mm(unit_rows, grad_projected[:, columns], (0, 0)))
    low = jnp.concatenate(terms[:2], axis=1)
    high = jnp.concatenate(terms[2:], axis=1)
    upper = lax.axis_index("grp") == 1
    kept[...] = jnp.where(upper, high, low)
    passed[...] = jnp.where(upper, low, high).astype(BF)
    back = mm(grad_projected[...], projection[...], (1, 1))
    result = gradient_rows.astype(F32) + norm_backward(back, normed, inverse)
    tokens[...] = mm(place, result.astype(BF)).reshape(tokens.shape).astype(BF)


def coarse_part_kernel(
    kept, got_first, got_second, own_pack, other_pack, own_gradient, other_gradient, coarse
):
    width = got_first.shape[3]
    for at, got in enumerate((got_first, got_second)):
        lanes = slice(at * width, (at + 1) * width)
        mine = kept[:, :, :, lanes].astype(F32)
        coarse[:, :, :, lanes] = (mine + got[...].astype(F32)).astype(BF)
    part = own_gradient.shape[1] // 2
    first = pl.multiple_of(lax.axis_index("grp") * part, part)
    pool_term = mm(own_pack[:, pl.ds(first, part)], own_gradient[...], (0, 0))
    pool_term = pool_term + mm(other_pack[:, pl.ds(first, part)], other_gradient[...], (0, 0))
    put_quarters(coarse, 2 * width, pool_term)


def assemble_kernel(tokens, fine_kept, fine_got, coarse, send):
    start = tokens.shape[3]
    send[:, :, :, :start] = tokens[...]
    put_quarters(send, start, fine_kept[...] + fine_got[...].astype(F32))
    send[:, :, :, send.shape[3] - coarse.shape[3] :] = coarse[...]


def take_kernel(arrived, slots, rows_out):
    place = one_hot(slots[...], slots.shape[1] * 2)
    rows = arrived[...].reshape(place.shape[0], arrived.shape[-1])
    rows_out[...] = mm(place, rows, (0, 0)).astype(BF)


VMEM = pl.BlockSpec(memory_space=pltpu.VMEM)
HBM = pl.BlockSpec(memory_space=pltpu.HBM)


class Far(NamedTuple):
    value: jax.Array


class Near(NamedTuple):
    shape: tuple
    dtype: jnp.dtype = BF
    far: bool = False


class Fetched:
    def __init__(self, source, buffer, semaphore):
        self.buffer, self.shape, self.waited = buffer, buffer.shape, False
        self.copy = pltpu.make_async_copy(source, buffer, semaphore)
        self.copy.start()

    def wait(self):
        if not self.waited:
            self.copy.wait()
            self.waited = True

    def __getitem__(self, index):
        self.wait()
        return self.buffer[index]


class Stored:
    def __init__(self, target, buffer, semaphore):
        self.buffer, self.shape, self.dtype, self.started = buffer, buffer.shape, buffer.dtype, False
        self.copy = pltpu.make_async_copy(buffer, target, semaphore)

    def __setitem__(self, index, values):
        self.buffer[index] = values

    def __getitem__(self, index):
        return self.buffer[index]

    def flush(self):
        if not self.started:
            self.copy.start()
            self.started = True


def call(kernel, inputs, outputs, scratch=(), mebibytes=16):
    in_specs, arrays, buffers = [], [], []
    for value in inputs:
        far = isinstance(value, Far)
        in_specs.append(HBM if far else VMEM)
        arrays.append(
            pltpu.with_memory_space_constraint(value.value, pltpu.HBM) if far else value
        )
        if far:
            buffers.append(pltpu.VMEM(value.value.shape, value.value.dtype))
    buffers.extend(pltpu.VMEM(out.shape, out.dtype) for out in outputs if out.far)
    flags = [isinstance(value, Far) for value in inputs] + [out.far for out in outputs]
    sizes = len(inputs), len(flags), len(flags) + len(buffers)

    def body(*refs):
        semaphores = refs[sizes[2]] if buffers else None
        given, views = 0, []
        for at, far in enumerate(flags):
            if far:
                kind = Fetched if at < sizes[0] else Stored
                views.append(kind(refs[at], refs[sizes[1] + given], semaphores.at[given]))
                given += 1
            else:
                views.append(refs[at])
        kernel(*views, *refs[sizes[2] + (1 if buffers else 0) :])
        for view in views:
            if isinstance(view, Stored):
                view.flush()
        for view in views:
            if isinstance(view, Fetched):
                view.wait()
            if isinstance(view, Stored):
                view.copy.wait()

    own = [pltpu.SemaphoreType.DMA((len(buffers),))] if buffers else []
    return pl.pallas_call(
        body,
        out_shape=[
            (pltpu.HBM if out.far else jax.ShapeDtypeStruct)(out.shape, out.dtype)
            for out in outputs
        ],
        in_specs=in_specs,
        out_specs=[HBM if out.far else VMEM for out in outputs],
        scratch_shapes=buffers + own + list(scratch),
        compiler_params=pltpu.CompilerParams(vmem_limit_bytes=mebibytes * 1024 * 1024),
    )(*arrays)


def exchange(values):
    return lax.ppermute(values, "grp", [(0, 1), (1, 0)])


def spread_blocks(values, axes):
    return lax.all_to_all(values, axes, split_axis=0, concat_axis=0, tiled=True)


def neighbours(owners, stride):
    pairs = []
    for chip in range(owners):
        place = chip // stride % 4
        for core in range(2):
            partner = ((place + core ^ 1) - core) % 4
            pairs.append((2 * chip + core, 2 * (chip + (partner - place) * stride) + core))
    return pairs


def route(values, devices):
    rows, features = values.shape
    blocks = values.reshape(devices, rows // devices, features)
    return spread_blocks(blocks, ("pts", "grp")).reshape(rows, features)


def on_device(
    points,
    rotated_place,
    rotated_source,
    ball_counts,
    fine_projection,
    fine_output,
    pool_weight,
    coarse_projection,
    coarse_output,
    coarse_cotangent,
):
    count, features = points.shape
    devices = lax.axis_size(("pts", "grp"))
    slots = 2 * count
    scaling = 1.0 / math.sqrt(count * devices)
    owners = lax.axis_size("pts")
    run, step = owners // 4, owners // 16
    wide = 2 * features
    half_rows = count // 2

    send, send_slot, pair_slot, receive_slot, live = call(
        route_kernel,
        (
            Far(rotated_place.reshape(1, count)),
            Far(rotated_source.reshape(1, count)),
            Far(ball_counts.reshape(1, -1)),
            Far(points),
        ),
        (
            Near((slots, features)),
            Near((1, count), jnp.int32),
            Near((1, count), jnp.int32),
            Near((1, count), jnp.int32),
            Near((1, count), F32),
        ),
    )
    arrived = route(send, devices)
    heads = features // HD * (count // BALL)
    send, rotated, projected, mixture, weights = call(
        fine_forward_kernel,
        (arrived, receive_slot, live, fine_projection, Far(fine_output)),
        (
            Near((slots, features)),
            Near((count, features)),
            Near((count, 3 * features)),
            Near((count, features)),
            Near((heads, BALL, BALL)),
        ),
    )
    arrived = route(send, devices)
    (own_pack,) = call(
        join_kernel, (arrived, pair_slot, coarse_cotangent), (Near((half_rows, 2 * wide)),)
    )
    other_pack = exchange(own_pack)
    coarse, keep, give, unit = call(
        coarse_kernel,
        (own_pack, other_pack, pool_weight, coarse_projection, Far(coarse_output)),
        (
            Near((half_rows, wide)),
            Near((half_rows, 2 * wide)),
            Near((half_rows, 2 * wide)),
            Near((count, wide)),
        ),
    )
    got = exchange(give)
    blocks = (owners, 2, slots // devices)
    kept, first_half, second_half = call(
        functools.partial(coarse_weights_kernel, strides=(run, step)),
        (unit, keep, give, own_pack, other_pack),
        (
            Near((*blocks, wide // 2)),
            Near((*blocks, wide // 4)),
            Near((*blocks, wide // 4)),
        ),
    )
    mixed, back = call(
        coarse_own_kernel,
        (coarse, keep, coarse_projection, coarse_output),
        (Near((half_rows, wide), F32), Near((half_rows, wide), F32)),
    )
    got, kept, first_half, second_half = lax.optimization_barrier(
        (got, kept, first_half, second_half)
    )
    coarse_result, coarse_gradient, send = call(
        coarse_finish_kernel,
        (
            coarse,
            mixed,
            back,
            got,
            coarse_cotangent,
            pool_weight,
            coarse_projection,
            coarse_output,
            pair_slot,
        ),
        (
            Near((half_rows, wide), far=True),
            Near((half_rows, wide)),
            Near((slots, features)),
        ),
    )
    arrived = route(send, devices)
    arrived, first_half, second_half, coarse_gradient = lax.optimization_barrier(
        (arrived, first_half, second_half, coarse_gradient)
    )
    got_first = lax.ppermute(first_half, ("pts", "grp"), neighbours(owners, run))
    got_second = lax.ppermute(second_half, ("pts", "grp"), neighbours(owners, step))
    other_gradient = exchange(coarse_gradient)
    tokens, fine_kept, fine_passed = call(
        fine_backward_kernel,
        (
            arrived,
            receive_slot,
            rotated,
            projected,
            mixture,
            weights,
            fine_projection,
            fine_output,
        ),
        (
            Near((*blocks, features)),
            Near((features, 2 * features), F32),
            Near((features, 2 * features)),
        ),
        scratch=(pltpu.VMEM((count, 3 * features), BF),),
    )
    fine_got = exchange(fine_passed)
    (coarse_part,) = call(
        coarse_part_kernel,
        (
            kept,
            got_first,
            got_second,
            own_pack,
            other_pack,
            coarse_gradient,
            other_gradient,
        ),
        (Near((*blocks, 3 * wide // 4)),),
    )
    across = features + wide
    (send,) = call(
        assemble_kernel,
        (tokens, fine_kept, fine_got, coarse_part),
        (Near((*blocks, across)),),
    )
    arrived = spread_blocks(send.reshape(devices, slots // devices, across), ("pts", "grp"))
    (spread,) = call(
        functools.partial(sum_kernel, tokens=features, run=run, step=step),
        (arrived.reshape(send.shape),),
        (Near((owners, slots // devices, features + 5 * wide // 2)),),
    )
    own_sums = spread_blocks(spread, "pts")
    (points_gradient,) = call(
        take_kernel, (arrived[:, :, :features], send_slot), (Near((count, features)),)
    )
    other_sums = exchange(own_sums)
    sums = write_sums(own_sums, other_sums, features, wide, scaling)
    return (coarse_result, points_gradient, *sums)


def solution(mesh):
    tokens = P(("pts", "grp"), None)
    in_specs = (
        tokens,
        P(("pts", "grp")),
        P(("pts", "grp")),
        P(),
        P(),
        P(),
        P(),
        P(),
        P(),
        tokens,
    )
    out_specs = (tokens, tokens, P(), P(), P(), P(), P())
    return jax.shard_map(
        on_device, mesh=mesh, in_specs=in_specs, out_specs=out_specs, check_vma=False
    )
```

```python
import functools
import math
from typing import NamedTuple

import jax
import jax.numpy as jnp
from jax import lax
from jax.experimental import pallas as pl
from jax.experimental.pallas import tpu as pltpu
from jax.sharding import PartitionSpec as P

HD = 64
BALL = 256
PAIR = 2 * HD
EPSILON = 1e-05
BF = jnp.bfloat16
F32 = jnp.float32


def mm(a, b, contract=(1, 0)):
    return lax.dot_general(
        a, b, (((contract[0],), (contract[1],)), ((), ())), preferred_element_type=F32
    )


def normalize(values):
    floats = values.astype(F32)
    center = floats - jnp.mean(floats, axis=-1, keepdims=True)
    inverse = lax.rsqrt(jnp.mean(center * center, axis=-1, keepdims=True) + EPSILON)
    return center * inverse, inverse


def norm_backward(incoming, normed, inverse):
    first_mean = jnp.mean(incoming, axis=-1, keepdims=True)
    second_mean = jnp.mean(incoming * normed, axis=-1, keepdims=True)
    return inverse * (incoming - first_mean - normed * second_mean)


def one_hot(slots, total):
    shape = (total, slots.shape[1])
    return (lax.broadcasted_iota(jnp.int32, shape, 0) == slots).astype(BF)


def softmax_rows(scores):
    raised = jnp.exp(scores - jnp.max(scores, axis=-1, keepdims=True))
    return (raised * (1.0 / jnp.sum(raised, axis=-1, keepdims=True))).astype(BF)


def slopes_of(weights, against):
    wide = weights.astype(F32)
    diagonal = jnp.sum(wide * against, axis=-1, keepdims=True)
    return (wide * (against - diagonal)).astype(BF)


def stack_heads(rows, heads):
    lanes = lax.broadcasted_iota(jnp.int32, rows.shape, 1) // HD
    none = jnp.zeros_like(rows)
    return jnp.concatenate([jnp.where(lanes == at, rows, none) for at in range(heads)], axis=0)


def unstack_heads(rows, heads):
    count = rows.shape[0] // heads
    merged = rows[:count]
    lanes = lax.broadcasted_iota(jnp.int32, merged.shape, 1) // HD
    for at in range(1, heads):
        merged = jnp.where(lanes == at, rows[at * count : (at + 1) * count], merged)
    return merged


def turned(rows):
    return rows.astype(F32).T.astype(BF)


def column_of(row):
    count = row.shape[1]
    turned = jnp.broadcast_to(row.astype(F32), (128, count)).T
    return jnp.concatenate([turned] * (count // 128), axis=1)


def route_kernel(
    place, source, counts, points, send, send_slot, pair_slot, receive_slot, live
):
    count = place.shape[1]
    shift = count.bit_length() - 1
    capacity = send.shape[0] * count // (counts.shape[1] * BALL)
    to_row = place[...] >> shift
    rows = lax.broadcasted_iota(jnp.int32, (count, count), 0)
    columns = lax.broadcasted_iota(jnp.int32, (count, count), 1)
    earlier = (column_of(to_row) == to_row.astype(F32)) & (rows < columns)
    rank = jnp.sum(jnp.where(earlier, 1.0, 0.0), axis=0, keepdims=True)
    slot = to_row * capacity + rank.astype(jnp.int32)
    send_slot[...] = slot
    even_first = jnp.where(columns < count // 2, 2 * columns, 2 * columns + 1 - count)
    digits = jnp.concatenate([slot >> 5, slot & 31] + [jnp.zeros_like(slot)] * 6, axis=0)
    moved = mm(digits.astype(F32).astype(BF), (rows == even_first).astype(BF)).astype(jnp.int32)
    pair_slot[...] = moved[0:1] * 32 + moved[1:2]
    source_row = source[...]
    from_row = source_row >> shift
    earlier = (column_of(from_row) == from_row.astype(F32)) & (
        column_of(source_row) < source_row.astype(F32)
    )
    rank = jnp.sum(jnp.where(earlier, 1.0, 0.0), axis=0, keepdims=True)
    receive_slot[...] = from_row * capacity + rank.astype(jnp.int32)
    balls = counts.shape[1]
    own_ball = one_hot(source_row >> (BALL.bit_length() - 1), balls)
    filled = mm(jnp.broadcast_to(counts[...].astype(F32), (8, balls)).astype(BF), own_ball)
    inside = (source_row & (BALL - 1)).astype(F32)
    live[...] = jnp.where(inside < filled[:1], 1.0, 0.0)
    send[...] = mm(one_hot(slot, send.shape[0]), points[...]).astype(BF)


def fine_forward_kernel(
    arrived, receive_slot, live, projection, output, send, rotated, projected, mixture, weights
):
    place = one_hot(receive_slot[...], arrived.shape[0])
    rows_in = mm(place, arrived[...], (0, 0))
    rotated[...] = rows_in.astype(BF)
    features = rows_in.shape[1]
    normed, _ = normalize(rows_in)
    projected[...] = mm(normed.astype(BF), projection[...]).astype(BF)
    balls = rows_in.shape[0] // BALL
    for ball in range(balls):
        rows = slice(ball * BALL, (ball + 1) * BALL)
        alive = live[:, rows] > 0.5
        for pair in range(features // PAIR):
            lanes = slice(pair * PAIR, (pair + 1) * PAIR)
            query = projected[rows, lanes] * jnp.asarray(HD ** (-0.5), BF)
            key = projected[rows, features + pair * PAIR : features + (pair + 1) * PAIR]
            value = projected[rows, 2 * features + pair * PAIR : 2 * features + (pair + 1) * PAIR]
            scores = mm(stack_heads(query, 2), key, (1, 1))
            both = softmax_rows(jnp.where(alive, scores, -1e30))
            first = (ball * features + pair * PAIR) // HD
            weights[first : first + 2] = both.reshape(2, BALL, BALL)
            mixture[rows, lanes] = unstack_heads(mm(both, value), 2).astype(BF)
    result = (rows_in + mm(mixture[...], output[...])).astype(BF)
    send[...] = mm(place, result).astype(BF)


def join_kernel(arrived, pair_slot, cotangent, pack):
    half_rows, wide = cotangent.shape
    place = one_hot(pair_slot[...], arrived.shape[0])
    rows = mm(place, arrived[...], (0, 0)).astype(BF)
    pack[:, : wide // 2] = rows[:half_rows]
    pack[:, wide // 2 : wide] = rows[half_rows:]
    pack[:, wide:] = cotangent[...]


def coarse_kernel(
    own_pack, other_pack, pool, projection, output, coarse, keep, give, unit
):
    half_rows, wide = coarse.shape
    part = wide // 2
    first = pl.multiple_of(lax.axis_index("grp") * part, part)
    joined = jnp.concatenate([own_pack[:, :wide], other_pack[:, :wide]], axis=0)
    tokens = mm(joined, pool[...]).astype(BF)
    coarse[...] = tokens[:half_rows]
    normed, _ = normalize(tokens)
    unit_rows = normed.astype(BF)
    unit[...] = unit_rows
    queries = mm(unit_rows, projection[:, pl.ds(first, part)]).astype(BF)
    keys = mm(unit_rows, projection[:, pl.ds(wide + first, part)]).astype(BF)
    values = mm(unit_rows, projection[:, pl.ds(2 * wide + first, part)]).astype(BF)
    cotangent = jnp.concatenate([own_pack[:, wide:], other_pack[:, wide:]], axis=0)
    incoming = mm(cotangent, output[pl.ds(first, part), :], (1, 1)).astype(BF)
    queries_turned, incoming_turned = turned(queries), turned(incoming)
    key_parts, value_parts = [], []

    def put(at, rows):
        target = slice(at, at + rows.shape[1])
        keep[:, target] = rows[:half_rows]
        give[:, target] = rows[half_rows:]

    for pair in range(part // PAIR):
        lanes = slice(pair * PAIR, (pair + 1) * PAIR)
        key, value = keys[:, lanes], values[:, lanes]
        query = queries[:, lanes] * jnp.asarray(HD ** (-0.5), BF)
        head_weights = softmax_rows(mm(stack_heads(query, 2), key, (1, 1)))
        against = mm(stack_heads(incoming[:, lanes], 2), value, (1, 1))
        slopes = slopes_of(head_weights, against)
        put(pair * PAIR, unstack_heads(mm(head_weights, value), 2).astype(BF))
        query_part = unstack_heads(mm(slopes, key), 2) * HD ** (-0.5)
        put(part + pair * PAIR, query_part.astype(BF))
        for half in range(2):
            band = slice(pair * PAIR + half * HD, pair * PAIR + (half + 1) * HD)
            rows = slice(half * 2 * half_rows, (half + 1) * 2 * half_rows)
            key_parts.append(mm(queries_turned[band], slopes[rows]) * HD ** (-0.5))
            value_parts.append(mm(incoming_turned[band], head_weights[rows]))
    put(2 * part, jnp.concatenate(key_parts, axis=0).T.astype(BF))
    put(3 * part, jnp.concatenate(value_parts, axis=0).T.astype(BF))


def heads_back(grads, index, projection, output):
    wide = output.shape[1]
    part = wide // 2
    first = pl.multiple_of(index * part, part)
    mixed = mm(grads[:, :part], output[pl.ds(first, part), :])
    back = jnp.zeros_like(mixed)
    for at in range(3):
        back = back + mm(
            grads[:, (at + 1) * part : (at + 2) * part],
            projection[:, pl.ds(at * wide + first, part)],
            (1, 1),
        )
    return mixed, back


def coarse_own_kernel(coarse, keep, projection, output, mixed, back):
    own_mixed, own_back = heads_back(keep, lax.axis_index("grp"), projection, output)
    mixed[...] = coarse[...].astype(F32) + own_mixed
    back[...] = own_back


def coarse_finish_kernel(
    coarse,
    mixed,
    back,
    got,
    cotangent,
    pool,
    projection,
    output,
    pair_slot,
    result,
    gradient,
    send,
):
    other_mixed, other_back = heads_back(got, 1 - lax.axis_index("grp"), projection, output)
    result[...] = (mixed[...] + other_mixed).astype(BF)
    result.flush()
    normed, inverse = normalize(coarse[...])
    gradient_rows = (
        cotangent[...].astype(F32) + norm_backward(back[...] + other_back, normed, inverse)
    ).astype(BF)
    gradient[...] = gradient_rows
    fine = mm(gradient_rows, pool[...], (1, 1)).astype(BF)
    features = send.shape[1]
    stacked = jnp.concatenate([fine[:, :features], fine[:, features:]], axis=0)
    send[...] = mm(one_hot(pair_slot[...], send.shape[0]), stacked).astype(BF)


def coarse_weights_kernel(
    unit, keep, give, own_pack, other_pack, kept, first_half, second_half, *, strides
):
    chip, core = lax.axis_index("pts"), lax.axis_index("grp")
    wide = unit.shape[1]
    part = wide // 2
    stacked = jnp.concatenate([keep[...], give[...]], axis=0)
    cotangent = jnp.concatenate([own_pack[:, wide:], other_pack[:, wide:]], axis=0)
    projection_term = mm(unit[...], stacked[:, part:], (0, 0))
    output_term = mm(stacked[:, :part], cotangent, (0, 0))
    across = projection_term.shape[1] // 2
    width = wide // 4
    for side in range(2):
        stack = [output_term[:, (2 * side + k) * width : (2 * side + k + 1) * width] for k in range(2)]
        columns = projection_term[:, side * across : (side + 1) * across]
        terms = jnp.concatenate([columns, jnp.concatenate(stack, axis=0)], axis=1)
        for at, passed in enumerate((first_half, second_half)):
            low = terms[:, 2 * at * width : (2 * at + 1) * width]
            high = terms[:, (2 * at + 1) * width : (2 * at + 2) * width]
            upper = (chip // strides[at] + core) % 2 == 1
            put_blocks(kept, side, at * width, jnp.where(upper, high, low))
            put_blocks(passed, side, 0, jnp.where(upper, low, high))


def put_quarters(blocks, lane, term):
    width = term.shape[1] // 4
    for side in range(2):
        stack = [term[:, (2 * side + k) * width : (2 * side + k + 1) * width] for k in range(2)]
        put_blocks(blocks, side, lane, jnp.concatenate(stack, axis=0))


def put_blocks(blocks, side, lane, rows):
    owners, width = blocks.shape[0], rows.shape[1]
    pieces = rows.reshape(owners, rows.shape[0] // owners, width)
    blocks[:, side, :, lane : lane + width] = pieces.astype(BF)


def sum_kernel(arrived, spread, own_tokens, passed_tokens, *, tokens, run, step):
    senders, sides, rows, across = arrived.shape
    width = (across - tokens) // 4
    upper = lax.axis_index("grp") == 1
    low_tokens, high_tokens = arrived[:, 0, :, :tokens], arrived[:, 1, :, :tokens]
    own_tokens[...] = jnp.where(upper, high_tokens, low_tokens)
    passed_tokens[...] = jnp.where(upper, low_tokens, high_tokens)

    def pieces(side, at):
        start = tokens + at * width
        return arrived[:, side, :, start : start + width].astype(F32)

    for side in range(sides):
        total = [jnp.sum(pieces(side, 0), axis=0)]
        for at, block in enumerate((run, step)):
            split = pieces(side, 1 + at).reshape(senders // (2 * block), 2, block, rows, width)
            even, odd = jnp.sum(jnp.sum(split, axis=2), axis=0)
            total.extend([jnp.where(upper, odd, even), jnp.where(upper, even, odd)])
        total.append(jnp.sum(pieces(side, 3), axis=0))
        total = jnp.concatenate(total, axis=1).astype(BF)
        spread[:, side] = jnp.broadcast_to(total[None], (senders, rows, total.shape[1]))


def write_heads(terms, heads, refs, stages, semaphores, scaling):
    projection, output, pool = refs
    tall, square = stages
    wide = pool.shape[0]
    part, width = wide // 2, wide // 4
    across = 3 * part // 2
    copies = []

    def lanes(side, start, count):
        values = terms[:, side, :, start : start + count].astype(F32) * scaling
        return values.reshape(wide, count)

    def send(stage, target):
        copies.append(pltpu.make_async_copy(stage, target, semaphores.at[len(copies)]))
        copies[-1].start()

    for side in range(2):
        for k in range(3):
            column = side * across + k * width
            place = column // part * wide + column % part
            target = pl.multiple_of(place + heads * part, width)
            stage = tall.at[3 * side + k]
            stage[...] = lanes(side, width + k * width, width)
            send(stage, projection.at[:, pl.ds(target, width)])
    for at, ref in enumerate((output, pool)):
        stage = square.at[at]
        for side in range(2):
            block = lanes(side, width + across + at * width, width)
            for k in range(2):
                first = (2 * side + k) * width
                stage[:, first : first + width] = block[k * part : (k + 1) * part]
        send(stage, ref.at[pl.ds(pl.multiple_of(heads * part, part), part), :])
    return copies


def own_sums_kernel(own, projection, output, pool, tall, square, semaphores, *, scaling):
    refs = (projection, output, pool)
    heads = lax.axis_index("grp")
    for copy in write_heads(own, heads, refs, (tall, square), semaphores, scaling):
        copy.wait()


def other_sums_kernel(
    own,
    other,
    projection_in,
    output_in,
    pool_in,
    projection,
    output,
    pool,
    fine_projection,
    fine_output,
    tall,
    square,
    semaphores,
    fine,
    fine_square,
    fine_semaphores,
    *,
    scaling,
):
    heads = 1 - lax.axis_index("grp")
    refs = (projection, output, pool)
    copies = write_heads(other, heads, refs, (tall, square), semaphores, scaling)
    features = fine_output.shape[0]
    width = features // 2
    for at in range(2):
        for side in range(2):
            here, there = own[:, side, :, :width], other[:, side, :, :width]
            values = jnp.where(heads == at, there, here).astype(F32) * scaling
            block = values.reshape(2 * features, width)
            column = (2 * at + side) * features
            for k in range(2):
                piece = block[k * features : (k + 1) * features]
                if column < 3 * features:
                    fine[:, column + k * width : column + (k + 1) * width] = piece
                else:
                    fine_square[:, k * width : (k + 1) * width] = piece
    copies.append(pltpu.make_async_copy(fine, fine_projection, fine_semaphores.at[0]))
    copies.append(pltpu.make_async_copy(fine_square, fine_output, fine_semaphores.at[1]))
    for copy in copies[-2:]:
        copy.start()
    for copy in copies:
        copy.wait()


def write_sums(own, other, features, wide, scaling):
    part, width = wide // 2, wide // 4
    shapes = [(wide, 3 * wide), (wide, wide), (wide, wide)]
    stages = [
        pltpu.VMEM((6, wide, width), F32),
        pltpu.VMEM((2, part, wide), F32),
        pltpu.SemaphoreType.DMA((8,)),
    ]
    limits = pltpu.CompilerParams(vmem_limit_bytes=16 * 1024 * 1024)
    firsts = pl.pallas_call(
        functools.partial(own_sums_kernel, scaling=scaling),
        out_shape=[pltpu.HBM(shape, F32) for shape in shapes],
        in_specs=[VMEM],
        out_specs=[HBM] * 3,
        scratch_shapes=stages,
        compiler_params=limits,
    )(own)
    shapes += [(features, 3 * features), (features, features)]
    projection, output, pool, fine_projection, fine_output = pl.pallas_call(
        functools.partial(other_sums_kernel, scaling=scaling),
        out_shape=[pltpu.HBM(shape, F32) for shape in shapes],
        in_specs=[VMEM] * 2 + [HBM] * 3,
        out_specs=[HBM] * 5,
        scratch_shapes=stages
        + [
            pltpu.VMEM((features, 3 * features), F32),
            pltpu.VMEM((features, features), F32),
            pltpu.SemaphoreType.DMA((2,)),
        ],
        input_output_aliases={2: 0, 3: 1, 4: 2},
        compiler_params=limits,
    )(own, other, *firsts)
    return fine_projection, fine_output, pool, projection, output


def fine_backward_kernel(
    arrived,
    receive_slot,
    rotated,
    projected,
    mixture,
    weights,
    projection,
    output,
    tokens,
    kept,
    passed,
    grad_projected,
):
    place = one_hot(receive_slot[...], arrived.shape[0])
    gradient_rows = mm(place, arrived[...], (0, 0)).astype(BF)
    features = rotated.shape[1]
    entering = mm(gradient_rows, output[...], (1, 1)).astype(BF)
    terms = [mm(mixture[...], gradient_rows, (0, 0))]
    balls = rotated.shape[0] // BALL
    heads = features // HD
    query_turned, entering_turned = turned(projected[:, :features]), turned(entering)
    turned_parts = ([], [])
    for ball in range(balls):
        rows = slice(ball * BALL, (ball + 1) * BALL)
        key, value = projected[rows, features : 2 * features], projected[rows, 2 * features :]
        head_weights = [weights[ball * heads + at] for at in range(heads)]
        against = mm(stack_heads(entering[rows], heads), value, (1, 1))
        slopes = slopes_of(jnp.concatenate(head_weights, axis=0), against)
        query_part = unstack_heads(mm(slopes, key), heads) * HD ** (-0.5)
        grad_projected[rows, :features] = query_part.astype(BF)
        pieces = ([], [])
        for at in range(heads):
            band = slice(at * HD, (at + 1) * HD)
            own = slopes[at * BALL : (at + 1) * BALL]
            pieces[0].append(mm(query_turned[band, rows], own) * HD ** (-0.5))
            pieces[1].append(mm(entering_turned[band, rows], head_weights[at]))
        for at in range(2):
            turned_parts[at].append(jnp.concatenate(pieces[at], axis=0))
    for at in range(2):
        whole = jnp.concatenate(turned_parts[at], axis=1).T.astype(BF)
        grad_projected[:, (at + 1) * features : (at + 2) * features] = whole
    normed, inverse = normalize(rotated[...])
    unit_rows = normed.astype(BF)
    for at in range(3):
        columns = slice(at * features, (at + 1) * features)
        terms.insert(at, mm(unit_rows, grad_projected[:, columns], (0, 0)))
    low = jnp.concatenate(terms[:2], axis=1)
    high = jnp.concatenate(terms[2:], axis=1)
    upper = lax.axis_index("grp") == 1
    kept[...] = jnp.where(upper, high, low)
    passed[...] = jnp.where(upper, low, high).astype(BF)
    back = mm(grad_projected[...], projection[...], (1, 1))
    result = gradient_rows.astype(F32) + norm_backward(back, normed, inverse)
    tokens[...] = mm(place, result.astype(BF)).reshape(tokens.shape).astype(BF)


def coarse_part_kernel(
    kept, got_first, got_second, own_pack, other_pack, own_gradient, other_gradient, coarse
):
    width = got_first.shape[3]
    for at, got in enumerate((got_first, got_second)):
        lanes = slice(at * width, (at + 1) * width)
        mine = kept[:, :, :, lanes].astype(F32)
        coarse[:, :, :, lanes] = (mine + got[...].astype(F32)).astype(BF)
    part = own_gradient.shape[1] // 2
    first = pl.multiple_of(lax.axis_index("grp") * part, part)
    pool_term = mm(own_pack[:, pl.ds(first, part)], own_gradient[...], (0, 0))
    pool_term = pool_term + mm(other_pack[:, pl.ds(first, part)], other_gradient[...], (0, 0))
    put_quarters(coarse, 2 * width, pool_term)


def assemble_kernel(tokens, fine_kept, fine_got, coarse, send):
    start = tokens.shape[3]
    send[:, :, :, :start] = tokens[...]
    put_quarters(send, start, fine_kept[...] + fine_got[...].astype(F32))
    send[:, :, :, send.shape[3] - coarse.shape[3] :] = coarse[...]


def take_parts_kernel(own, got, slots, rows_out):
    upper = lax.axis_index("grp") == 1
    senders, rows, features = own.shape
    shape = (senders, 1, rows, features)
    first = jnp.where(upper, got[...], own[...]).astype(F32).reshape(shape)
    second = jnp.where(upper, own[...], got[...]).astype(F32).reshape(shape)
    both = jnp.concatenate([first, second], axis=1).reshape(2 * senders * rows, features)
    place = one_hot(slots[...], both.shape[0])
    rows_out[...] = mm(place, both.astype(BF), (0, 0)).astype(BF)


VMEM = pl.BlockSpec(memory_space=pltpu.VMEM)
HBM = pl.BlockSpec(memory_space=pltpu.HBM)


class Far(NamedTuple):
    value: jax.Array


class Near(NamedTuple):
    shape: tuple
    dtype: jnp.dtype = BF
    far: bool = False


class Fetched:
    def __init__(self, source, buffer, semaphore):
        self.buffer, self.shape, self.waited = buffer, buffer.shape, False
        self.copy = pltpu.make_async_copy(source, buffer, semaphore)
        self.copy.start()

    def wait(self):
        if not self.waited:
            self.copy.wait()
            self.waited = True

    def __getitem__(self, index):
        self.wait()
        return self.buffer[index]


class Stored:
    def __init__(self, target, buffer, semaphore):
        self.buffer, self.shape, self.dtype, self.started = buffer, buffer.shape, buffer.dtype, False
        self.copy = pltpu.make_async_copy(buffer, target, semaphore)

    def __setitem__(self, index, values):
        self.buffer[index] = values

    def __getitem__(self, index):
        return self.buffer[index]

    def flush(self):
        if not self.started:
            self.copy.start()
            self.started = True


def call(kernel, inputs, outputs, scratch=(), mebibytes=16):
    in_specs, arrays, buffers = [], [], []
    for value in inputs:
        far = isinstance(value, Far)
        in_specs.append(HBM if far else VMEM)
        arrays.append(
            pltpu.with_memory_space_constraint(value.value, pltpu.HBM) if far else value
        )
        if far:
            buffers.append(pltpu.VMEM(value.value.shape, value.value.dtype))
    buffers.extend(pltpu.VMEM(out.shape, out.dtype) for out in outputs if out.far)
    flags = [isinstance(value, Far) for value in inputs] + [out.far for out in outputs]
    sizes = len(inputs), len(flags), len(flags) + len(buffers)

    def body(*refs):
        semaphores = refs[sizes[2]] if buffers else None
        given, views = 0, []
        for at, far in enumerate(flags):
            if far:
                kind = Fetched if at < sizes[0] else Stored
                views.append(kind(refs[at], refs[sizes[1] + given], semaphores.at[given]))
                given += 1
            else:
                views.append(refs[at])
        kernel(*views, *refs[sizes[2] + (1 if buffers else 0) :])
        for view in views:
            if isinstance(view, Stored):
                view.flush()
        for view in views:
            if isinstance(view, Fetched):
                view.wait()
            if isinstance(view, Stored):
                view.copy.wait()

    own = [pltpu.SemaphoreType.DMA((len(buffers),))] if buffers else []
    return pl.pallas_call(
        body,
        out_shape=[
            (pltpu.HBM if out.far else jax.ShapeDtypeStruct)(out.shape, out.dtype)
            for out in outputs
        ],
        in_specs=in_specs,
        out_specs=[HBM if out.far else VMEM for out in outputs],
        scratch_shapes=buffers + own + list(scratch),
        compiler_params=pltpu.CompilerParams(vmem_limit_bytes=mebibytes * 1024 * 1024),
    )(*arrays)


def exchange(values):
    return lax.ppermute(values, "grp", [(0, 1), (1, 0)])


def spread_blocks(values, axes):
    return lax.all_to_all(values, axes, split_axis=0, concat_axis=0, tiled=True)


def neighbours(owners, stride):
    pairs = []
    for chip in range(owners):
        place = chip // stride % 4
        for core in range(2):
            partner = ((place + core ^ 1) - core) % 4
            pairs.append((2 * chip + core, 2 * (chip + (partner - place) * stride) + core))
    return pairs


def route(values, devices):
    rows, features = values.shape
    blocks = values.reshape(devices, rows // devices, features)
    return spread_blocks(blocks, ("pts", "grp")).reshape(rows, features)


def on_device(
    points,
    rotated_place,
    rotated_source,
    ball_counts,
    fine_projection,
    fine_output,
    pool_weight,
    coarse_projection,
    coarse_output,
    coarse_cotangent,
):
    count, features = points.shape
    devices = lax.axis_size(("pts", "grp"))
    slots = 2 * count
    scaling = 1.0 / math.sqrt(count * devices)
    owners = lax.axis_size("pts")
    run, step = owners // 4, owners // 16
    wide = 2 * features
    half_rows = count // 2

    send, send_slot, pair_slot, receive_slot, live = call(
        route_kernel,
        (
            Far(rotated_place.reshape(1, count)),
            Far(rotated_source.reshape(1, count)),
            Far(ball_counts.reshape(1, -1)),
            Far(points),
        ),
        (
            Near((slots, features)),
            Near((1, count), jnp.int32),
            Near((1, count), jnp.int32),
            Near((1, count), jnp.int32),
            Near((1, count), F32),
        ),
    )
    arrived = route(send, devices)
    heads = features // HD * (count // BALL)
    send, rotated, projected, mixture, weights = call(
        fine_forward_kernel,
        (arrived, receive_slot, live, fine_projection, Far(fine_output)),
        (
            Near((slots, features)),
            Near((count, features)),
            Near((count, 3 * features)),
            Near((count, features)),
            Near((heads, BALL, BALL)),
        ),
    )
    arrived = route(send, devices)
    (own_pack,) = call(
        join_kernel, (arrived, pair_slot, coarse_cotangent), (Near((half_rows, 2 * wide)),)
    )
    other_pack = exchange(own_pack)
    coarse, keep, give, unit = call(
        coarse_kernel,
        (own_pack, other_pack, pool_weight, coarse_projection, Far(coarse_output)),
        (
            Near((half_rows, wide)),
            Near((half_rows, 2 * wide)),
            Near((half_rows, 2 * wide)),
            Near((count, wide)),
        ),
    )
    got = exchange(give)
    blocks = (owners, 2, slots // devices)
    kept, first_half, second_half = call(
        functools.partial(coarse_weights_kernel, strides=(run, step)),
        (unit, keep, give, own_pack, other_pack),
        (
            Near((*blocks, wide // 2)),
            Near((*blocks, wide // 4)),
            Near((*blocks, wide // 4)),
        ),
    )
    mixed, back = call(
        coarse_own_kernel,
        (coarse, keep, coarse_projection, coarse_output),
        (Near((half_rows, wide), F32), Near((half_rows, wide), F32)),
    )
    got, kept, first_half, second_half = lax.optimization_barrier(
        (got, kept, first_half, second_half)
    )
    coarse_result, coarse_gradient, send = call(
        coarse_finish_kernel,
        (
            coarse,
            mixed,
            back,
            got,
            coarse_cotangent,
            pool_weight,
            coarse_projection,
            coarse_output,
            pair_slot,
        ),
        (
            Near((half_rows, wide), far=True),
            Near((half_rows, wide)),
            Near((slots, features)),
        ),
    )
    arrived = route(send, devices)
    arrived, first_half, second_half, coarse_gradient = lax.optimization_barrier(
        (arrived, first_half, second_half, coarse_gradient)
    )
    got_first = lax.ppermute(first_half, ("pts", "grp"), neighbours(owners, run))
    got_second = lax.ppermute(second_half, ("pts", "grp"), neighbours(owners, step))
    other_gradient = exchange(coarse_gradient)
    tokens, fine_kept, fine_passed = call(
        fine_backward_kernel,
        (
            arrived,
            receive_slot,
            rotated,
            projected,
            mixture,
            weights,
            fine_projection,
            fine_output,
        ),
        (
            Near((*blocks, features)),
            Near((features, 2 * features), F32),
            Near((features, 2 * features)),
        ),
        scratch=(pltpu.VMEM((count, 3 * features), BF),),
    )
    fine_got = exchange(fine_passed)
    (coarse_part,) = call(
        coarse_part_kernel,
        (
            kept,
            got_first,
            got_second,
            own_pack,
            other_pack,
            coarse_gradient,
            other_gradient,
        ),
        (Near((*blocks, 3 * wide // 4)),),
    )
    across = features + wide
    (send,) = call(
        assemble_kernel,
        (tokens, fine_kept, fine_got, coarse_part),
        (Near((*blocks, across)),),
    )
    arrived = spread_blocks(send, "pts")
    spread, own_tokens, passed_tokens = call(
        functools.partial(sum_kernel, tokens=features, run=run, step=step),
        (arrived,),
        (
            Near((*blocks, 3 * wide // 2)),
            Near((owners, slots // devices, features)),
            Near((owners, slots // devices, features)),
        ),
    )
    own_sums = spread_blocks(spread, "pts")
    own_sums, own_tokens, passed_tokens = lax.optimization_barrier(
        (own_sums, own_tokens, passed_tokens)
    )
    other_sums = exchange(own_sums)
    got_tokens = exchange(passed_tokens)
    (points_gradient,) = call(
        take_parts_kernel, (own_tokens, got_tokens, send_slot), (Near((count, features)),)
    )
    sums = write_sums(own_sums, other_sums, features, wide, scaling)
    return (coarse_result, points_gradient, *sums)


def solution(mesh):
    tokens = P(("pts", "grp"), None)
    in_specs = (
        tokens,
        P(("pts", "grp")),
        P(("pts", "grp")),
        P(),
        P(),
        P(),
        P(),
        P(),
        P(),
        tokens,
    )
    out_specs = (tokens, tokens, P(), P(), P(), P(), P())
    return jax.shard_map(
        on_device, mesh=mesh, in_specs=in_specs, out_specs=out_specs, check_vma=False
    )
```

```python
import functools
import math
from typing import NamedTuple

import jax
import jax.numpy as jnp
from jax import lax
from jax.experimental import pallas as pl
from jax.experimental.pallas import tpu as pltpu
from jax.sharding import PartitionSpec as P

HD = 64
BALL = 256
PAIR = 2 * HD
EPSILON = 1e-05
BF = jnp.bfloat16
F32 = jnp.float32


def mm(a, b, contract=(1, 0)):
    return lax.dot_general(
        a, b, (((contract[0],), (contract[1],)), ((), ())), preferred_element_type=F32
    )


def normalize(values):
    floats = values.astype(F32)
    center = floats - jnp.mean(floats, axis=-1, keepdims=True)
    inverse = lax.rsqrt(jnp.mean(center * center, axis=-1, keepdims=True) + EPSILON)
    return center * inverse, inverse


def norm_backward(incoming, normed, inverse):
    first_mean = jnp.mean(incoming, axis=-1, keepdims=True)
    second_mean = jnp.mean(incoming * normed, axis=-1, keepdims=True)
    return inverse * (incoming - first_mean - normed * second_mean)


def one_hot(slots, total):
    shape = (total, slots.shape[1])
    return (lax.broadcasted_iota(jnp.int32, shape, 0) == slots).astype(BF)


def softmax_rows(scores):
    raised = jnp.exp(scores - jnp.max(scores, axis=-1, keepdims=True))
    return (raised * (1.0 / jnp.sum(raised, axis=-1, keepdims=True))).astype(BF)


def slopes_of(weights, against):
    wide = weights.astype(F32)
    diagonal = jnp.sum(wide * against, axis=-1, keepdims=True)
    return (wide * (against - diagonal)).astype(BF)


def stack_heads(rows, heads):
    lanes = lax.broadcasted_iota(jnp.int32, rows.shape, 1) // HD
    none = jnp.zeros_like(rows)
    return jnp.concatenate([jnp.where(lanes == at, rows, none) for at in range(heads)], axis=0)


def unstack_heads(rows, heads):
    count = rows.shape[0] // heads
    merged = rows[:count]
    lanes = lax.broadcasted_iota(jnp.int32, merged.shape, 1) // HD
    for at in range(1, heads):
        merged = jnp.where(lanes == at, rows[at * count : (at + 1) * count], merged)
    return merged


def turned(rows):
    return rows.astype(F32).T.astype(BF)


def column_of(row):
    count = row.shape[1]
    turned = jnp.broadcast_to(row.astype(F32), (128, count)).T
    return jnp.concatenate([turned] * (count // 128), axis=1)


def route_kernel(
    place, source, counts, points, send, send_slot, pair_slot, receive_slot, live
):
    count = place.shape[1]
    shift = count.bit_length() - 1
    capacity = send.shape[0] * count // (counts.shape[1] * BALL)
    to_row = place[...] >> shift
    rows = lax.broadcasted_iota(jnp.int32, (count, count), 0)
    columns = lax.broadcasted_iota(jnp.int32, (count, count), 1)
    earlier = (column_of(to_row) == to_row.astype(F32)) & (rows < columns)
    rank = jnp.sum(jnp.where(earlier, 1.0, 0.0), axis=0, keepdims=True)
    slot = to_row * capacity + rank.astype(jnp.int32)
    send_slot[...] = slot
    even_first = jnp.where(columns < count // 2, 2 * columns, 2 * columns + 1 - count)
    digits = jnp.concatenate([slot >> 5, slot & 31] + [jnp.zeros_like(slot)] * 6, axis=0)
    moved = mm(digits.astype(F32).astype(BF), (rows == even_first).astype(BF)).astype(jnp.int32)
    pair_slot[...] = moved[0:1] * 32 + moved[1:2]
    source_row = source[...]
    from_row = source_row >> shift
    earlier = (column_of(from_row) == from_row.astype(F32)) & (
        column_of(source_row) < source_row.astype(F32)
    )
    rank = jnp.sum(jnp.where(earlier, 1.0, 0.0), axis=0, keepdims=True)
    receive_slot[...] = from_row * capacity + rank.astype(jnp.int32)
    balls = counts.shape[1]
    own_ball = one_hot(source_row >> (BALL.bit_length() - 1), balls)
    filled = mm(jnp.broadcast_to(counts[...].astype(F32), (8, balls)).astype(BF), own_ball)
    inside = (source_row & (BALL - 1)).astype(F32)
    live[...] = jnp.where(inside < filled[:1], 1.0, 0.0)
    send[...] = mm(one_hot(slot, send.shape[0]), points[...]).astype(BF)


def fine_forward_kernel(
    arrived, receive_slot, live, projection, output, send, rotated, projected, mixture, weights
):
    place = one_hot(receive_slot[...], arrived.shape[0])
    rows_in = mm(place, arrived[...], (0, 0))
    rotated[...] = rows_in.astype(BF)
    features = rows_in.shape[1]
    normed, _ = normalize(rows_in)
    projected[...] = mm(normed.astype(BF), projection[...]).astype(BF)
    balls = rows_in.shape[0] // BALL
    for ball in range(balls):
        rows = slice(ball * BALL, (ball + 1) * BALL)
        alive = live[:, rows] > 0.5
        for pair in range(features // PAIR):
            lanes = slice(pair * PAIR, (pair + 1) * PAIR)
            query = projected[rows, lanes] * jnp.asarray(HD ** (-0.5), BF)
            key = projected[rows, features + pair * PAIR : features + (pair + 1) * PAIR]
            value = projected[rows, 2 * features + pair * PAIR : 2 * features + (pair + 1) * PAIR]
            scores = mm(stack_heads(query, 2), key, (1, 1))
            both = softmax_rows(jnp.where(alive, scores, -1e30))
            first = (ball * features + pair * PAIR) // HD
            weights[first : first + 2] = both.reshape(2, BALL, BALL)
            mixture[rows, lanes] = unstack_heads(mm(both, value), 2).astype(BF)
    result = (rows_in + mm(mixture[...], output[...])).astype(BF)
    send[...] = mm(place, result).astype(BF)


def join_kernel(arrived, pair_slot, cotangent, pack):
    half_rows, wide = cotangent.shape
    place = one_hot(pair_slot[...], arrived.shape[0])
    rows = mm(place, arrived[...], (0, 0)).astype(BF)
    pack[:, : wide // 2] = rows[:half_rows]
    pack[:, wide // 2 : wide] = rows[half_rows:]
    pack[:, wide:] = cotangent[...]


def project_rows(joined, cotangent, pool, projection, output):
    wide = pool.shape[1]
    part = wide // 2
    first = pl.multiple_of(lax.axis_index("grp") * part, part)
    tokens = mm(joined, pool[...]).astype(BF)
    normed, _ = normalize(tokens)
    unit = normed.astype(BF)
    rows = [
        mm(unit, projection[:, pl.ds(at * wide + first, part)]).astype(BF) for at in range(3)
    ]
    rows.append(mm(cotangent, output[pl.ds(first, part), :], (1, 1)).astype(BF))
    return tokens, unit, rows


def coarse_own_rows_kernel(own_pack, pool, projection, output, coarse, unit, rows_out):
    wide = pool.shape[1]
    tokens, unit_rows, rows = project_rows(
        own_pack[:, :wide], own_pack[:, wide:], pool, projection, output
    )
    coarse[...] = tokens
    unit[...] = unit_rows
    for at, values in enumerate(rows):
        rows_out[:, at * wide // 2 : (at + 1) * wide // 2] = values


def coarse_kernel(other_pack, own_rows, pool, projection, output, keep, give, unit):
    wide = pool.shape[1]
    part = wide // 2
    half_rows = own_rows.shape[0]
    _, unit_rows, rows = project_rows(
        other_pack[:, :wide], other_pack[:, wide:], pool, projection, output
    )
    unit[...] = unit_rows
    queries, keys, values, incoming = [
        jnp.concatenate([own_rows[:, at * part : (at + 1) * part], rows[at]], axis=0)
        for at in range(4)
    ]
    queries_turned, incoming_turned = turned(queries), turned(incoming)
    key_parts, value_parts = [], []

    def put(at, rows):
        target = slice(at, at + rows.shape[1])
        keep[:, target] = rows[:half_rows]
        give[:, target] = rows[half_rows:]

    for pair in range(part // PAIR):
        lanes = slice(pair * PAIR, (pair + 1) * PAIR)
        key, value = keys[:, lanes], values[:, lanes]
        query = queries[:, lanes] * jnp.asarray(HD ** (-0.5), BF)
        head_weights = softmax_rows(mm(stack_heads(query, 2), key, (1, 1)))
        against = mm(stack_heads(incoming[:, lanes], 2), value, (1, 1))
        slopes = slopes_of(head_weights, against)
        put(pair * PAIR, unstack_heads(mm(head_weights, value), 2).astype(BF))
        query_part = unstack_heads(mm(slopes, key), 2) * HD ** (-0.5)
        put(part + pair * PAIR, query_part.astype(BF))
        for half in range(2):
            band = slice(pair * PAIR + half * HD, pair * PAIR + (half + 1) * HD)
            rows = slice(half * 2 * half_rows, (half + 1) * 2 * half_rows)
            key_parts.append(mm(queries_turned[band], slopes[rows]) * HD ** (-0.5))
            value_parts.append(mm(incoming_turned[band], head_weights[rows]))
    put(2 * part, jnp.concatenate(key_parts, axis=0).T.astype(BF))
    put(3 * part, jnp.concatenate(value_parts, axis=0).T.astype(BF))


def heads_back(grads, index, projection, output):
    wide = output.shape[1]
    part = wide // 2
    first = pl.multiple_of(index * part, part)
    mixed = mm(grads[:, :part], output[pl.ds(first, part), :])
    back = jnp.zeros_like(mixed)
    for at in range(3):
        back = back + mm(
            grads[:, (at + 1) * part : (at + 2) * part],
            projection[:, pl.ds(at * wide + first, part)],
            (1, 1),
        )
    return mixed, back


def coarse_own_kernel(coarse, keep, projection, output, mixed, back):
    own_mixed, own_back = heads_back(keep, lax.axis_index("grp"), projection, output)
    mixed[...] = coarse[...].astype(F32) + own_mixed
    back[...] = own_back


def coarse_finish_kernel(
    coarse,
    mixed,
    back,
    got,
    cotangent,
    pool,
    projection,
    output,
    pair_slot,
    result,
    gradient,
    send,
):
    other_mixed, other_back = heads_back(got, 1 - lax.axis_index("grp"), projection, output)
    result[...] = (mixed[...] + other_mixed).astype(BF)
    result.flush()
    normed, inverse = normalize(coarse[...])
    gradient_rows = (
        cotangent[...].astype(F32) + norm_backward(back[...] + other_back, normed, inverse)
    ).astype(BF)
    gradient[...] = gradient_rows
    fine = mm(gradient_rows, pool[...], (1, 1)).astype(BF)
    features = send.shape[1]
    stacked = jnp.concatenate([fine[:, :features], fine[:, features:]], axis=0)
    send[...] = mm(one_hot(pair_slot[...], send.shape[0]), stacked).astype(BF)


def coarse_weights_kernel(
    own_unit,
    other_unit,
    keep,
    give,
    own_pack,
    other_pack,
    kept,
    first_half,
    second_half,
    *,
    strides,
):
    chip, core = lax.axis_index("pts"), lax.axis_index("grp")
    wide = own_unit.shape[1]
    part = wide // 2
    unit = jnp.concatenate([own_unit[...], other_unit[...]], axis=0)
    stacked = jnp.concatenate([keep[...], give[...]], axis=0)
    cotangent = jnp.concatenate([own_pack[:, wide:], other_pack[:, wide:]], axis=0)
    projection_term = mm(unit, stacked[:, part:], (0, 0))
    output_term = mm(stacked[:, :part], cotangent, (0, 0))
    across = projection_term.shape[1] // 2
    width = wide // 4
    for side in range(2):
        stack = [output_term[:, (2 * side + k) * width : (2 * side + k + 1) * width] for k in range(2)]
        columns = projection_term[:, side * across : (side + 1) * across]
        terms = jnp.concatenate([columns, jnp.concatenate(stack, axis=0)], axis=1)
        for at, passed in enumerate((first_half, second_half)):
            low = terms[:, 2 * at * width : (2 * at + 1) * width]
            high = terms[:, (2 * at + 1) * width : (2 * at + 2) * width]
            upper = (chip // strides[at] + core) % 2 == 1
            put_blocks(kept, side, at * width, jnp.where(upper, high, low))
            put_blocks(passed, side, 0, jnp.where(upper, low, high))


def put_quarters(blocks, lane, term):
    width = term.shape[1] // 4
    for side in range(2):
        stack = [term[:, (2 * side + k) * width : (2 * side + k + 1) * width] for k in range(2)]
        put_blocks(blocks, side, lane, jnp.concatenate(stack, axis=0))


def put_blocks(blocks, side, lane, rows):
    owners, width = blocks.shape[0], rows.shape[1]
    pieces = rows.reshape(owners, rows.shape[0] // owners, width)
    blocks[:, side, :, lane : lane + width] = pieces.astype(BF)


def sum_kernel(arrived, spread, *, tokens, run, step):
    senders, _, rows, across = arrived.shape
    width = (across - tokens) // 4

    def pieces(side, at):
        start = tokens + at * width
        return arrived[:, side, :, start : start + width].astype(F32)

    total = [jnp.sum(pieces(side, 0), axis=0) for side in range(2)]
    for side in range(2):
        for at, block in enumerate((run, step)):
            split = pieces(side, 1 + at).reshape(senders // (2 * block), 2, block, rows, width)
            halves = jnp.sum(jnp.sum(split, axis=2), axis=0)
            total.extend([halves[side], halves[1 - side]])
        total.append(jnp.sum(pieces(side, 3), axis=0))
    total = jnp.concatenate(total, axis=1).astype(BF)
    spread[...] = jnp.broadcast_to(total[None], spread.shape)


def write_half(terms, side, refs, stages, semaphores, scaling):
    projection, output, pool = refs
    tall, square = stages
    wide = pool.shape[0]
    part, width = wide // 2, wide // 4
    across = 3 * part // 2
    copies = []

    def lanes(start, count):
        values = terms[:, :, start : start + count].astype(F32) * scaling
        return values.reshape(terms.shape[0] * terms.shape[1], count)

    def send(stage, target):
        copies.append(pltpu.make_async_copy(stage, target, semaphores.at[len(copies)]))
        copies[-1].start()

    for heads in range(2):
        start = 2 * width + heads * (across + 2 * width)
        for k in range(3):
            columns = [half * across + k * width for half in range(2)]
            places = [column // part * wide + heads * part + column % part for column in columns]
            target = pl.multiple_of(jnp.where(side == 0, places[0], places[1]), width)
            stage = tall.at[3 * heads + k]
            stage[...] = lanes(start + k * width, width)
            send(stage, projection.at[:, pl.ds(target, width)])
        for at, ref in enumerate((output, pool)):
            block = lanes(start + across + at * width, width)
            stage = square.at[2 * heads + at]
            stage[:, :width] = block[:part]
            stage[:, width:] = block[part:]
            target = pl.multiple_of(side * part, part)
            send(stage, ref.at[heads * part : (heads + 1) * part, pl.ds(target, part)])
    return copies


def own_sums_kernel(own, projection, output, pool, tall, square, semaphores, *, scaling):
    side = lax.axis_index("grp")
    refs = (projection, output, pool)
    for copy in write_half(own, side, refs, (tall, square), semaphores, scaling):
        copy.wait()


def other_sums_kernel(
    own,
    other,
    projection_in,
    output_in,
    pool_in,
    projection,
    output,
    pool,
    fine_projection,
    fine_output,
    tall,
    square,
    semaphores,
    fine,
    fine_square,
    fine_semaphores,
    *,
    scaling,
):
    side = 1 - lax.axis_index("grp")
    refs = (projection, output, pool)
    copies = write_half(other, side, refs, (tall, square), semaphores, scaling)
    features = fine_output.shape[0]
    width = features // 2
    for heads in range(2):
        start = heads * width
        here, there = own[:, :, start : start + width], other[:, :, start : start + width]
        for half in range(2):
            values = jnp.where(side == half, there, here).astype(F32) * scaling
            block = values.reshape(own.shape[0] * own.shape[1], width)
            column = (2 * heads + half) * features
            for k in range(2):
                piece = block[k * features : (k + 1) * features]
                if column < 3 * features:
                    fine[:, column + k * width : column + (k + 1) * width] = piece
                else:
                    fine_square[:, k * width : (k + 1) * width] = piece
    copies.append(pltpu.make_async_copy(fine, fine_projection, fine_semaphores.at[0]))
    copies.append(pltpu.make_async_copy(fine_square, fine_output, fine_semaphores.at[1]))
    for copy in copies[-2:]:
        copy.start()
    for copy in copies:
        copy.wait()


def write_sums(own, other, features, wide, scaling):
    part, width = wide // 2, wide // 4
    shapes = [(wide, 3 * wide), (wide, wide), (wide, wide)]
    stages = [
        pltpu.VMEM((6, wide, width), F32),
        pltpu.VMEM((4, part, part), F32),
        pltpu.SemaphoreType.DMA((10,)),
    ]
    limits = pltpu.CompilerParams(vmem_limit_bytes=16 * 1024 * 1024)
    firsts = pl.pallas_call(
        functools.partial(own_sums_kernel, scaling=scaling),
        out_shape=[pltpu.HBM(shape, F32) for shape in shapes],
        in_specs=[VMEM],
        out_specs=[HBM] * 3,
        scratch_shapes=stages,
        compiler_params=limits,
    )(own)
    shapes += [(features, 3 * features), (features, features)]
    projection, output, pool, fine_projection, fine_output = pl.pallas_call(
        functools.partial(other_sums_kernel, scaling=scaling),
        out_shape=[pltpu.HBM(shape, F32) for shape in shapes],
        in_specs=[VMEM] * 2 + [HBM] * 3,
        out_specs=[HBM] * 5,
        scratch_shapes=stages
        + [
            pltpu.VMEM((features, 3 * features), F32),
            pltpu.VMEM((features, features), F32),
            pltpu.SemaphoreType.DMA((2,)),
        ],
        input_output_aliases={2: 0, 3: 1, 4: 2},
        compiler_params=limits,
    )(own, other, *firsts)
    return fine_projection, fine_output, pool, projection, output


def fine_backward_kernel(
    arrived,
    receive_slot,
    rotated,
    projected,
    mixture,
    weights,
    projection,
    output,
    tokens,
    kept,
    passed,
    grad_projected,
):
    place = one_hot(receive_slot[...], arrived.shape[0])
    gradient_rows = mm(place, arrived[...], (0, 0)).astype(BF)
    features = rotated.shape[1]
    entering = mm(gradient_rows, output[...], (1, 1)).astype(BF)
    terms = [mm(mixture[...], gradient_rows, (0, 0))]
    balls = rotated.shape[0] // BALL
    heads = features // HD
    query_turned, entering_turned = turned(projected[:, :features]), turned(entering)
    turned_parts = ([], [])
    for ball in range(balls):
        rows = slice(ball * BALL, (ball + 1) * BALL)
        key, value = projected[rows, features : 2 * features], projected[rows, 2 * features :]
        head_weights = [weights[ball * heads + at] for at in range(heads)]
        against = mm(stack_heads(entering[rows], heads), value, (1, 1))
        slopes = slopes_of(jnp.concatenate(head_weights, axis=0), against)
        query_part = unstack_heads(mm(slopes, key), heads) * HD ** (-0.5)
        grad_projected[rows, :features] = query_part.astype(BF)
        pieces = ([], [])
        for at in range(heads):
            band = slice(at * HD, (at + 1) * HD)
            own = slopes[at * BALL : (at + 1) * BALL]
            pieces[0].append(mm(query_turned[band, rows], own) * HD ** (-0.5))
            pieces[1].append(mm(entering_turned[band, rows], head_weights[at]))
        for at in range(2):
            turned_parts[at].append(jnp.concatenate(pieces[at], axis=0))
    for at in range(2):
        whole = jnp.concatenate(turned_parts[at], axis=1).T.astype(BF)
        grad_projected[:, (at + 1) * features : (at + 2) * features] = whole
    normed, inverse = normalize(rotated[...])
    unit_rows = normed.astype(BF)
    for at in range(3):
        columns = slice(at * features, (at + 1) * features)
        terms.insert(at, mm(unit_rows, grad_projected[:, columns], (0, 0)))
    low = jnp.concatenate(terms[:2], axis=1)
    high = jnp.concatenate(terms[2:], axis=1)
    upper = lax.axis_index("grp") == 1
    kept[...] = jnp.where(upper, high, low)
    passed[...] = jnp.where(upper, low, high).astype(BF)
    back = mm(grad_projected[...], projection[...], (1, 1))
    result = gradient_rows.astype(F32) + norm_backward(back, normed, inverse)
    tokens[...] = mm(place, result.astype(BF)).reshape(tokens.shape).astype(BF)


def pool_kernel(own_pack, other_pack, own_gradient, other_gradient, blocks):
    part = own_gradient.shape[1] // 2
    first = pl.multiple_of(lax.axis_index("grp") * part, part)
    term = mm(own_pack[:, pl.ds(first, part)], own_gradient[...], (0, 0))
    term = term + mm(other_pack[:, pl.ds(first, part)], other_gradient[...], (0, 0))
    put_quarters(blocks, 0, term)


def coarse_part_kernel(kept, got_first, got_second, pool, coarse):
    width = got_first.shape[3]
    for at, got in enumerate((got_first, got_second)):
        lanes = slice(at * width, (at + 1) * width)
        mine = kept[:, :, :, lanes].astype(F32)
        coarse[:, :, :, lanes] = (mine + got[...].astype(F32)).astype(BF)
    coarse[:, :, :, 2 * width :] = pool[...]


def assemble_kernel(tokens, fine_kept, fine_got, coarse, send):
    start = tokens.shape[3]
    send[:, :, :, :start] = tokens[...]
    put_quarters(send, start, fine_kept[...] + fine_got[...].astype(F32))
    send[:, :, :, send.shape[3] - coarse.shape[3] :] = coarse[...]


def take_kernel(arrived, slots, rows_out):
    place = one_hot(slots[...], slots.shape[1] * 2)
    rows = arrived[...].reshape(place.shape[0], arrived.shape[-1])
    rows_out[...] = mm(place, rows, (0, 0)).astype(BF)


VMEM = pl.BlockSpec(memory_space=pltpu.VMEM)
HBM = pl.BlockSpec(memory_space=pltpu.HBM)


class Far(NamedTuple):
    value: jax.Array


class Near(NamedTuple):
    shape: tuple
    dtype: jnp.dtype = BF
    far: bool = False


class Fetched:
    def __init__(self, source, buffer, semaphore):
        self.buffer, self.shape, self.waited = buffer, buffer.shape, False
        self.copy = pltpu.make_async_copy(source, buffer, semaphore)
        self.copy.start()

    def wait(self):
        if not self.waited:
            self.copy.wait()
            self.waited = True

    def __getitem__(self, index):
        self.wait()
        return self.buffer[index]


class Stored:
    def __init__(self, target, buffer, semaphore):
        self.buffer, self.shape, self.dtype, self.started = buffer, buffer.shape, buffer.dtype, False
        self.copy = pltpu.make_async_copy(buffer, target, semaphore)

    def __setitem__(self, index, values):
        self.buffer[index] = values

    def __getitem__(self, index):
        return self.buffer[index]

    def flush(self):
        if not self.started:
            self.copy.start()
            self.started = True


def call(kernel, inputs, outputs, scratch=(), mebibytes=16):
    in_specs, arrays, buffers = [], [], []
    for value in inputs:
        far = isinstance(value, Far)
        in_specs.append(HBM if far else VMEM)
        arrays.append(
            pltpu.with_memory_space_constraint(value.value, pltpu.HBM) if far else value
        )
        if far:
            buffers.append(pltpu.VMEM(value.value.shape, value.value.dtype))
    buffers.extend(pltpu.VMEM(out.shape, out.dtype) for out in outputs if out.far)
    flags = [isinstance(value, Far) for value in inputs] + [out.far for out in outputs]
    sizes = len(inputs), len(flags), len(flags) + len(buffers)

    def body(*refs):
        semaphores = refs[sizes[2]] if buffers else None
        given, views = 0, []
        for at, far in enumerate(flags):
            if far:
                kind = Fetched if at < sizes[0] else Stored
                views.append(kind(refs[at], refs[sizes[1] + given], semaphores.at[given]))
                given += 1
            else:
                views.append(refs[at])
        kernel(*views, *refs[sizes[2] + (1 if buffers else 0) :])
        for view in views:
            if isinstance(view, Stored):
                view.flush()
        for view in views:
            if isinstance(view, Fetched):
                view.wait()
            if isinstance(view, Stored):
                view.copy.wait()

    own = [pltpu.SemaphoreType.DMA((len(buffers),))] if buffers else []
    return pl.pallas_call(
        body,
        out_shape=[
            (pltpu.HBM if out.far else jax.ShapeDtypeStruct)(out.shape, out.dtype)
            for out in outputs
        ],
        in_specs=in_specs,
        out_specs=[HBM if out.far else VMEM for out in outputs],
        scratch_shapes=buffers + own + list(scratch),
        compiler_params=pltpu.CompilerParams(vmem_limit_bytes=mebibytes * 1024 * 1024),
    )(*arrays)


def exchange(values):
    return lax.ppermute(values, "grp", [(0, 1), (1, 0)])


def spread_blocks(values, axes):
    return lax.all_to_all(values, axes, split_axis=0, concat_axis=0, tiled=True)


def neighbours(owners, stride):
    pairs = []
    for chip in range(owners):
        place = chip // stride % 4
        for core in range(2):
            partner = ((place + core ^ 1) - core) % 4
            pairs.append((2 * chip + core, 2 * (chip + (partner - place) * stride) + core))
    return pairs


def route(values, devices):
    rows, features = values.shape
    blocks = values.reshape(devices, rows // devices, features)
    return spread_blocks(blocks, ("pts", "grp")).reshape(rows, features)


def on_device(
    points,
    rotated_place,
    rotated_source,
    ball_counts,
    fine_projection,
    fine_output,
    pool_weight,
    coarse_projection,
    coarse_output,
    coarse_cotangent,
):
    count, features = points.shape
    devices = lax.axis_size(("pts", "grp"))
    slots = 2 * count
    scaling = 1.0 / math.sqrt(count * devices)
    owners = lax.axis_size("pts")
    run, step = owners // 4, owners // 16
    wide = 2 * features
    half_rows = count // 2

    send, send_slot, pair_slot, receive_slot, live = call(
        route_kernel,
        (
            Far(rotated_place.reshape(1, count)),
            Far(rotated_source.reshape(1, count)),
            Far(ball_counts.reshape(1, -1)),
            Far(points),
        ),
        (
            Near((slots, features)),
            Near((1, count), jnp.int32),
            Near((1, count), jnp.int32),
            Near((1, count), jnp.int32),
            Near((1, count), F32),
        ),
    )
    arrived = route(send, devices)
    heads = features // HD * (count // BALL)
    send, rotated, projected, mixture, weights = call(
        fine_forward_kernel,
        (arrived, receive_slot, live, fine_projection, Far(fine_output)),
        (
            Near((slots, features)),
            Near((count, features)),
            Near((count, 3 * features)),
            Near((count, features)),
            Near((heads, BALL, BALL)),
        ),
    )
    arrived = route(send, devices)
    (own_pack,) = call(
        join_kernel, (arrived, pair_slot, coarse_cotangent), (Near((half_rows, 2 * wide)),)
    )
    other_pack = exchange(own_pack)
    coarse, own_unit, own_rows = call(
        coarse_own_rows_kernel,
        (own_pack, pool_weight, coarse_projection, Far(coarse_output)),
        (
            Near((half_rows, wide)),
            Near((half_rows, wide)),
            Near((half_rows, 2 * wide)),
        ),
    )
    keep, give, other_unit = call(
        coarse_kernel,
        (other_pack, own_rows, pool_weight, coarse_projection, coarse_output),
        (
            Near((half_rows, 2 * wide)),
            Near((half_rows, 2 * wide)),
            Near((half_rows, wide)),
        ),
    )
    got = exchange(give)
    blocks = (owners, 2, slots // devices)
    kept, first_half, second_half = call(
        functools.partial(coarse_weights_kernel, strides=(run, step)),
        (own_unit, other_unit, keep, give, own_pack, other_pack),
        (
            Near((*blocks, wide // 2)),
            Near((*blocks, wide // 4)),
            Near((*blocks, wide // 4)),
        ),
    )
    mixed, back = call(
        coarse_own_kernel,
        (coarse, keep, coarse_projection, coarse_output),
        (Near((half_rows, wide), F32), Near((half_rows, wide), F32)),
    )
    got, kept, first_half, second_half = lax.optimization_barrier(
        (got, kept, first_half, second_half)
    )
    coarse_result, coarse_gradient, send = call(
        coarse_finish_kernel,
        (
            coarse,
            mixed,
            back,
            got,
            coarse_cotangent,
            pool_weight,
            coarse_projection,
            coarse_output,
            pair_slot,
        ),
        (
            Near((half_rows, wide), far=True),
            Near((half_rows, wide)),
            Near((slots, features)),
        ),
    )
    arrived = route(send, devices)
    arrived, first_half, second_half, coarse_gradient = lax.optimization_barrier(
        (arrived, first_half, second_half, coarse_gradient)
    )
    got_first = lax.ppermute(first_half, ("pts", "grp"), neighbours(owners, run))
    got_second = lax.ppermute(second_half, ("pts", "grp"), neighbours(owners, step))
    other_gradient = exchange(coarse_gradient)
    tokens, fine_kept, fine_passed = call(
        fine_backward_kernel,
        (
            arrived,
            receive_slot,
            rotated,
            projected,
            mixture,
            weights,
            fine_projection,
            fine_output,
        ),
        (
            Near((*blocks, features)),
            Near((features, 2 * features), F32),
            Near((features, 2 * features)),
        ),
        scratch=(pltpu.VMEM((count, 3 * features), BF),),
    )
    fine_got = exchange(fine_passed)
    (pool_part,) = call(
        pool_kernel,
        (own_pack, other_pack, coarse_gradient, other_gradient),
        (Near((*blocks, wide // 4)),),
    )
    (coarse_part,) = call(
        coarse_part_kernel,
        (kept, got_first, got_second, pool_part),
        (Near((*blocks, 3 * wide // 4)),),
    )
    across = features + wide
    (send,) = call(
        assemble_kernel,
        (tokens, fine_kept, fine_got, coarse_part),
        (Near((*blocks, across)),),
    )
    arrived = spread_blocks(send.reshape(devices, slots // devices, across), ("pts", "grp"))
    (spread,) = call(
        functools.partial(sum_kernel, tokens=features, run=run, step=step),
        (arrived.reshape(send.shape),),
        (Near((owners, slots // devices, features + 5 * wide // 2)),),
    )
    own_sums = spread_blocks(spread, "pts")
    (points_gradient,) = call(
        take_kernel, (arrived[:, :, :features], send_slot), (Near((count, features)),)
    )
    other_sums = exchange(own_sums)
    sums = write_sums(own_sums, other_sums, features, wide, scaling)
    return (coarse_result, points_gradient, *sums)


def solution(mesh):
    tokens = P(("pts", "grp"), None)
    in_specs = (
        tokens,
        P(("pts", "grp")),
        P(("pts", "grp")),
        P(),
        P(),
        P(),
        P(),
        P(),
        P(),
        tokens,
    )
    out_specs = (tokens, tokens, P(), P(), P(), P(), P())
    return jax.shard_map(
        on_device, mesh=mesh, in_specs=in_specs, out_specs=out_specs, check_vma=False
    )
```

```python
import functools
import math
from typing import NamedTuple

import jax
import jax.numpy as jnp
from jax import lax
from jax.experimental import pallas as pl
from jax.experimental.pallas import tpu as pltpu
from jax.sharding import PartitionSpec as P

HD = 64
BALL = 256
PAIR = 2 * HD
EPSILON = 1e-05
BF = jnp.bfloat16
F32 = jnp.float32


def mm(a, b, contract=(1, 0)):
    return lax.dot_general(
        a, b, (((contract[0],), (contract[1],)), ((), ())), preferred_element_type=F32
    )


def normalize(values):
    floats = values.astype(F32)
    center = floats - jnp.mean(floats, axis=-1, keepdims=True)
    inverse = lax.rsqrt(jnp.mean(center * center, axis=-1, keepdims=True) + EPSILON)
    return center * inverse, inverse


def norm_backward(incoming, normed, inverse):
    first_mean = jnp.mean(incoming, axis=-1, keepdims=True)
    second_mean = jnp.mean(incoming * normed, axis=-1, keepdims=True)
    return inverse * (incoming - first_mean - normed * second_mean)


def one_hot(slots, total):
    shape = (total, slots.shape[1])
    return (lax.broadcasted_iota(jnp.int32, shape, 0) == slots).astype(BF)


def softmax_rows(scores):
    raised = jnp.exp(scores - jnp.max(scores, axis=-1, keepdims=True))
    return (raised * (1.0 / jnp.sum(raised, axis=-1, keepdims=True))).astype(BF)


def slopes_of(weights, against):
    wide = weights.astype(F32)
    diagonal = jnp.sum(wide * against, axis=-1, keepdims=True)
    return (wide * (against - diagonal)).astype(BF)


def stack_heads(rows, heads):
    lanes = lax.broadcasted_iota(jnp.int32, rows.shape, 1) // HD
    none = jnp.zeros_like(rows)
    return jnp.concatenate([jnp.where(lanes == at, rows, none) for at in range(heads)], axis=0)


def unstack_heads(rows, heads):
    count = rows.shape[0] // heads
    merged = rows[:count]
    lanes = lax.broadcasted_iota(jnp.int32, merged.shape, 1) // HD
    for at in range(1, heads):
        merged = jnp.where(lanes == at, rows[at * count : (at + 1) * count], merged)
    return merged


def turned(rows):
    return rows.astype(F32).T.astype(BF)


def column_of(row):
    count = row.shape[1]
    turned = jnp.broadcast_to(row.astype(F32), (128, count)).T
    return jnp.concatenate([turned] * (count // 128), axis=1)


def route_kernel(
    place, source, counts, points, send, send_slot, pair_slot, receive_slot, live
):
    count = place.shape[1]
    shift = count.bit_length() - 1
    capacity = send.shape[0] * count // (counts.shape[1] * BALL)
    to_row = place[...] >> shift
    rows = lax.broadcasted_iota(jnp.int32, (count, count), 0)
    columns = lax.broadcasted_iota(jnp.int32, (count, count), 1)
    earlier = (column_of(to_row) == to_row.astype(F32)) & (rows < columns)
    rank = jnp.sum(jnp.where(earlier, 1.0, 0.0), axis=0, keepdims=True)
    slot = to_row * capacity + rank.astype(jnp.int32)
    send_slot[...] = slot
    even_first = jnp.where(columns < count // 2, 2 * columns, 2 * columns + 1 - count)
    digits = jnp.concatenate([slot >> 5, slot & 31] + [jnp.zeros_like(slot)] * 6, axis=0)
    moved = mm(digits.astype(F32).astype(BF), (rows == even_first).astype(BF)).astype(jnp.int32)
    pair_slot[...] = moved[0:1] * 32 + moved[1:2]
    source_row = source[...]
    from_row = source_row >> shift
    earlier = (column_of(from_row) == from_row.astype(F32)) & (
        column_of(source_row) < source_row.astype(F32)
    )
    rank = jnp.sum(jnp.where(earlier, 1.0, 0.0), axis=0, keepdims=True)
    receive_slot[...] = from_row * capacity + rank.astype(jnp.int32)
    balls = counts.shape[1]
    own_ball = one_hot(source_row >> (BALL.bit_length() - 1), balls)
    filled = mm(jnp.broadcast_to(counts[...].astype(F32), (8, balls)).astype(BF), own_ball)
    inside = (source_row & (BALL - 1)).astype(F32)
    live[...] = jnp.where(inside < filled[:1], 1.0, 0.0)
    send[...] = mm(one_hot(slot, send.shape[0]), points[...]).astype(BF)


def fine_forward_kernel(
    arrived, receive_slot, live, projection, output, send, rotated, projected, mixture, weights
):
    place = one_hot(receive_slot[...], arrived.shape[0])
    rows_in = mm(place, arrived[...], (0, 0))
    rotated[...] = rows_in.astype(BF)
    features = rows_in.shape[1]
    normed, _ = normalize(rows_in)
    projected[...] = mm(normed.astype(BF), projection[...]).astype(BF)
    balls = rows_in.shape[0] // BALL
    for ball in range(balls):
        rows = slice(ball * BALL, (ball + 1) * BALL)
        alive = live[:, rows] > 0.5
        for pair in range(features // PAIR):
            lanes = slice(pair * PAIR, (pair + 1) * PAIR)
            query = projected[rows, lanes] * jnp.asarray(HD ** (-0.5), BF)
            key = projected[rows, features + pair * PAIR : features + (pair + 1) * PAIR]
            value = projected[rows, 2 * features + pair * PAIR : 2 * features + (pair + 1) * PAIR]
            scores = mm(stack_heads(query, 2), key, (1, 1))
            both = softmax_rows(jnp.where(alive, scores, -1e30))
            first = (ball * features + pair * PAIR) // HD
            weights[first : first + 2] = both.reshape(2, BALL, BALL)
            mixture[rows, lanes] = unstack_heads(mm(both, value), 2).astype(BF)
    result = (rows_in + mm(mixture[...], output[...])).astype(BF)
    send[...] = mm(place, result).astype(BF)


def join_kernel(arrived, pair_slot, cotangent, pack):
    half_rows, wide = cotangent.shape
    place = one_hot(pair_slot[...], arrived.shape[0])
    rows = mm(place, arrived[...], (0, 0)).astype(BF)
    pack[:, : wide // 2] = rows[:half_rows]
    pack[:, wide // 2 : wide] = rows[half_rows:]
    pack[:, wide:] = cotangent[...]


def project_rows(joined, cotangent, pool, projection, output):
    wide = pool.shape[1]
    part = wide // 2
    first = pl.multiple_of(lax.axis_index("grp") * part, part)
    tokens = mm(joined, pool[...]).astype(BF)
    normed, _ = normalize(tokens)
    unit = normed.astype(BF)
    rows = [
        mm(unit, projection[:, pl.ds(at * wide + first, part)]).astype(BF) for at in range(3)
    ]
    rows.append(mm(cotangent, output[pl.ds(first, part), :], (1, 1)).astype(BF))
    return tokens, unit, rows


def coarse_own_rows_kernel(own_pack, pool, projection, output, coarse, unit, rows_out):
    wide = pool.shape[1]
    tokens, unit_rows, rows = project_rows(
        own_pack[:, :wide], own_pack[:, wide:], pool, projection, output
    )
    coarse[...] = tokens
    unit[...] = unit_rows
    for at, values in enumerate(rows):
        rows_out[:, at * wide // 2 : (at + 1) * wide // 2] = values


def coarse_kernel(other_pack, own_rows, pool, projection, output, keep, give, unit):
    wide = pool.shape[1]
    part = wide // 2
    half_rows = own_rows.shape[0]
    _, unit_rows, rows = project_rows(
        other_pack[:, :wide], other_pack[:, wide:], pool, projection, output
    )
    unit[...] = unit_rows
    queries, keys, values, incoming = [
        jnp.concatenate([own_rows[:, at * part : (at + 1) * part], rows[at]], axis=0)
        for at in range(4)
    ]
    queries_turned, incoming_turned = turned(queries), turned(incoming)
    key_parts, value_parts = [], []

    def put(at, rows):
        target = slice(at, at + rows.shape[1])
        keep[:, target] = rows[:half_rows]
        give[:, target] = rows[half_rows:]

    for pair in range(part // PAIR):
        lanes = slice(pair * PAIR, (pair + 1) * PAIR)
        key, value = keys[:, lanes], values[:, lanes]
        query = queries[:, lanes] * jnp.asarray(HD ** (-0.5), BF)
        head_weights = softmax_rows(mm(stack_heads(query, 2), key, (1, 1)))
        entering = stack_heads(incoming[:, lanes], 2)
        mixed = mm(head_weights, value)
        put(pair * PAIR, unstack_heads(mixed, 2).astype(BF))
        diagonal = jnp.sum(entering.astype(F32) * mixed, axis=-1, keepdims=True)
        against = mm(entering, value, (1, 1))
        slopes = (head_weights.astype(F32) * (against - diagonal)).astype(BF)
        query_part = unstack_heads(mm(slopes, key), 2) * HD ** (-0.5)
        put(part + pair * PAIR, query_part.astype(BF))
        for half in range(2):
            band = slice(pair * PAIR + half * HD, pair * PAIR + (half + 1) * HD)
            rows = slice(half * 2 * half_rows, (half + 1) * 2 * half_rows)
            key_parts.append(mm(queries_turned[band], slopes[rows]) * HD ** (-0.5))
            value_parts.append(mm(incoming_turned[band], head_weights[rows]))
    put(2 * part, jnp.concatenate(key_parts, axis=0).T.astype(BF))
    put(3 * part, jnp.concatenate(value_parts, axis=0).T.astype(BF))


def heads_back(grads, index, projection, output):
    wide = output.shape[1]
    part = wide // 2
    first = pl.multiple_of(index * part, part)
    mixed = mm(grads[:, :part], output[pl.ds(first, part), :])
    back = jnp.zeros_like(mixed)
    for at in range(3):
        back = back + mm(
            grads[:, (at + 1) * part : (at + 2) * part],
            projection[:, pl.ds(at * wide + first, part)],
            (1, 1),
        )
    return mixed, back


def coarse_own_kernel(coarse, keep, projection, output, mixed, back):
    own_mixed, own_back = heads_back(keep, lax.axis_index("grp"), projection, output)
    mixed[...] = coarse[...].astype(F32) + own_mixed
    back[...] = own_back


def coarse_finish_kernel(
    coarse,
    mixed,
    back,
    got,
    cotangent,
    pool,
    projection,
    output,
    pair_slot,
    result,
    gradient,
    send,
):
    other_mixed, other_back = heads_back(got, 1 - lax.axis_index("grp"), projection, output)
    result[...] = (mixed[...] + other_mixed).astype(BF)
    result.flush()
    normed, inverse = normalize(coarse[...])
    gradient_rows = (
        cotangent[...].astype(F32) + norm_backward(back[...] + other_back, normed, inverse)
    ).astype(BF)
    gradient[...] = gradient_rows
    fine = mm(gradient_rows, pool[...], (1, 1)).astype(BF)
    features = send.shape[1]
    stacked = jnp.concatenate([fine[:, :features], fine[:, features:]], axis=0)
    send[...] = mm(one_hot(pair_slot[...], send.shape[0]), stacked).astype(BF)


def coarse_weights_kernel(
    own_unit,
    other_unit,
    keep,
    give,
    own_pack,
    other_pack,
    kept,
    first_half,
    second_half,
    *,
    strides,
):
    chip, core = lax.axis_index("pts"), lax.axis_index("grp")
    wide = own_unit.shape[1]
    part = wide // 2
    unit = jnp.concatenate([own_unit[...], other_unit[...]], axis=0)
    stacked = jnp.concatenate([keep[...], give[...]], axis=0)
    cotangent = jnp.concatenate([own_pack[:, wide:], other_pack[:, wide:]], axis=0)
    projection_term = mm(unit, stacked[:, part:], (0, 0))
    output_term = mm(stacked[:, :part], cotangent, (0, 0))
    across = projection_term.shape[1] // 2
    width = wide // 4
    for side in range(2):
        stack = [output_term[:, (2 * side + k) * width : (2 * side + k + 1) * width] for k in range(2)]
        columns = projection_term[:, side * across : (side + 1) * across]
        terms = jnp.concatenate([columns, jnp.concatenate(stack, axis=0)], axis=1)
        for at, passed in enumerate((first_half, second_half)):
            low = terms[:, 2 * at * width : (2 * at + 1) * width]
            high = terms[:, (2 * at + 1) * width : (2 * at + 2) * width]
            upper = (chip // strides[at] + core) % 2 == 1
            put_blocks(kept, side, at * width, jnp.where(upper, high, low))
            put_blocks(passed, side, 0, jnp.where(upper, low, high))


def put_quarters(blocks, lane, term):
    width = term.shape[1] // 4
    for side in range(2):
        stack = [term[:, (2 * side + k) * width : (2 * side + k + 1) * width] for k in range(2)]
        put_blocks(blocks, side, lane, jnp.concatenate(stack, axis=0))


def put_blocks(blocks, side, lane, rows):
    owners, width = blocks.shape[0], rows.shape[1]
    pieces = rows.reshape(owners, rows.shape[0] // owners, width)
    blocks[:, side, :, lane : lane + width] = pieces.astype(BF)


def sum_kernel(arrived, spread, *, tokens, run, step):
    senders, _, rows, across = arrived.shape
    width = (across - tokens) // 4

    def pieces(side, at):
        start = tokens + at * width
        return arrived[:, side, :, start : start + width].astype(F32)

    total = [jnp.sum(pieces(side, 0), axis=0) for side in range(2)]
    for side in range(2):
        for at, block in enumerate((run, step)):
            split = pieces(side, 1 + at).reshape(senders // (2 * block), 2, block, rows, width)
            halves = jnp.sum(jnp.sum(split, axis=2), axis=0)
            total.extend([halves[side], halves[1 - side]])
        total.append(jnp.sum(pieces(side, 3), axis=0))
    total = jnp.concatenate(total, axis=1).astype(BF)
    spread[...] = jnp.broadcast_to(total[None], spread.shape)


def write_half(terms, side, refs, stages, semaphores, scaling):
    projection, output, pool = refs
    tall, square = stages
    wide = pool.shape[0]
    part, width = wide // 2, wide // 4
    across = 3 * part // 2
    copies = []

    def lanes(start, count):
        values = terms[:, :, start : start + count].astype(F32) * scaling
        return values.reshape(terms.shape[0] * terms.shape[1], count)

    def send(stage, target):
        copies.append(pltpu.make_async_copy(stage, target, semaphores.at[len(copies)]))
        copies[-1].start()

    for heads in range(2):
        start = 2 * width + heads * (across + 2 * width)
        for k in range(3):
            columns = [half * across + k * width for half in range(2)]
            places = [column // part * wide + heads * part + column % part for column in columns]
            target = pl.multiple_of(jnp.where(side == 0, places[0], places[1]), width)
            stage = tall.at[3 * heads + k]
            stage[...] = lanes(start + k * width, width)
            send(stage, projection.at[:, pl.ds(target, width)])
        for at, ref in enumerate((output, pool)):
            block = lanes(start + across + at * width, width)
            stage = square.at[2 * heads + at]
            stage[:, :width] = block[:part]
            stage[:, width:] = block[part:]
            target = pl.multiple_of(side * part, part)
            send(stage, ref.at[heads * part : (heads + 1) * part, pl.ds(target, part)])
    return copies


def own_sums_kernel(own, projection, output, pool, tall, square, semaphores, *, scaling):
    side = lax.axis_index("grp")
    refs = (projection, output, pool)
    for copy in write_half(own, side, refs, (tall, square), semaphores, scaling):
        copy.wait()


def other_sums_kernel(
    own,
    other,
    projection_in,
    output_in,
    pool_in,
    projection,
    output,
    pool,
    fine_projection,
    fine_output,
    tall,
    square,
    semaphores,
    fine,
    fine_square,
    fine_semaphores,
    *,
    scaling,
):
    side = 1 - lax.axis_index("grp")
    refs = (projection, output, pool)
    copies = write_half(other, side, refs, (tall, square), semaphores, scaling)
    features = fine_output.shape[0]
    width = features // 2
    for heads in range(2):
        start = heads * width
        here, there = own[:, :, start : start + width], other[:, :, start : start + width]
        for half in range(2):
            values = jnp.where(side == half, there, here).astype(F32) * scaling
            block = values.reshape(own.shape[0] * own.shape[1], width)
            column = (2 * heads + half) * features
            for k in range(2):
                piece = block[k * features : (k + 1) * features]
                if column < 3 * features:
                    fine[:, column + k * width : column + (k + 1) * width] = piece
                else:
                    fine_square[:, k * width : (k + 1) * width] = piece
    copies.append(pltpu.make_async_copy(fine, fine_projection, fine_semaphores.at[0]))
    copies.append(pltpu.make_async_copy(fine_square, fine_output, fine_semaphores.at[1]))
    for copy in copies[-2:]:
        copy.start()
    for copy in copies:
        copy.wait()


def write_sums(own, other, features, wide, scaling):
    part, width = wide // 2, wide // 4
    shapes = [(wide, 3 * wide), (wide, wide), (wide, wide)]
    stages = [
        pltpu.VMEM((6, wide, width), F32),
        pltpu.VMEM((4, part, part), F32),
        pltpu.SemaphoreType.DMA((10,)),
    ]
    limits = pltpu.CompilerParams(vmem_limit_bytes=16 * 1024 * 1024)
    firsts = pl.pallas_call(
        functools.partial(own_sums_kernel, scaling=scaling),
        out_shape=[pltpu.HBM(shape, F32) for shape in shapes],
        in_specs=[VMEM],
        out_specs=[HBM] * 3,
        scratch_shapes=stages,
        compiler_params=limits,
    )(own)
    shapes += [(features, 3 * features), (features, features)]
    projection, output, pool, fine_projection, fine_output = pl.pallas_call(
        functools.partial(other_sums_kernel, scaling=scaling),
        out_shape=[pltpu.HBM(shape, F32) for shape in shapes],
        in_specs=[VMEM] * 2 + [HBM] * 3,
        out_specs=[HBM] * 5,
        scratch_shapes=stages
        + [
            pltpu.VMEM((features, 3 * features), F32),
            pltpu.VMEM((features, features), F32),
            pltpu.SemaphoreType.DMA((2,)),
        ],
        input_output_aliases={2: 0, 3: 1, 4: 2},
        compiler_params=limits,
    )(own, other, *firsts)
    return fine_projection, fine_output, pool, projection, output


def fine_backward_kernel(
    arrived,
    receive_slot,
    rotated,
    projected,
    mixture,
    weights,
    projection,
    output,
    tokens,
    kept,
    passed,
    grad_projected,
):
    place = one_hot(receive_slot[...], arrived.shape[0])
    gradient_rows = mm(place, arrived[...], (0, 0)).astype(BF)
    features = rotated.shape[1]
    entering = mm(gradient_rows, output[...], (1, 1)).astype(BF)
    terms = [mm(mixture[...], gradient_rows, (0, 0))]
    balls = rotated.shape[0] // BALL
    heads = features // HD
    query_turned, entering_turned = turned(projected[:, :features]), turned(entering)
    turned_parts = ([], [])
    for ball in range(balls):
        rows = slice(ball * BALL, (ball + 1) * BALL)
        key, value = projected[rows, features : 2 * features], projected[rows, 2 * features :]
        head_weights = [weights[ball * heads + at] for at in range(heads)]
        against = mm(stack_heads(entering[rows], heads), value, (1, 1))
        slopes = slopes_of(jnp.concatenate(head_weights, axis=0), against)
        query_part = unstack_heads(mm(slopes, key), heads) * HD ** (-0.5)
        grad_projected[rows, :features] = query_part.astype(BF)
        pieces = ([], [])
        for at in range(heads):
            band = slice(at * HD, (at + 1) * HD)
            own = slopes[at * BALL : (at + 1) * BALL]
            pieces[0].append(mm(query_turned[band, rows], own) * HD ** (-0.5))
            pieces[1].append(mm(entering_turned[band, rows], head_weights[at]))
        for at in range(2):
            turned_parts[at].append(jnp.concatenate(pieces[at], axis=0))
    for at in range(2):
        whole = jnp.concatenate(turned_parts[at], axis=1).T.astype(BF)
        grad_projected[:, (at + 1) * features : (at + 2) * features] = whole
    normed, inverse = normalize(rotated[...])
    unit_rows = normed.astype(BF)
    for at in range(3):
        columns = slice(at * features, (at + 1) * features)
        terms.insert(at, mm(unit_rows, grad_projected[:, columns], (0, 0)))
    low = jnp.concatenate(terms[:2], axis=1)
    high = jnp.concatenate(terms[2:], axis=1)
    upper = lax.axis_index("grp") == 1
    kept[...] = jnp.where(upper, high, low)
    passed[...] = jnp.where(upper, low, high).astype(BF)
    back = mm(grad_projected[...], projection[...], (1, 1))
    result = gradient_rows.astype(F32) + norm_backward(back, normed, inverse)
    tokens[...] = mm(place, result.astype(BF)).reshape(tokens.shape).astype(BF)


def pool_kernel(own_pack, other_pack, own_gradient, other_gradient, blocks):
    part = own_gradient.shape[1] // 2
    first = pl.multiple_of(lax.axis_index("grp") * part, part)
    term = mm(own_pack[:, pl.ds(first, part)], own_gradient[...], (0, 0))
    term = term + mm(other_pack[:, pl.ds(first, part)], other_gradient[...], (0, 0))
    put_quarters(blocks, 0, term)


def coarse_part_kernel(kept, got_first, got_second, pool, coarse):
    width = got_first.shape[3]
    for at, got in enumerate((got_first, got_second)):
        lanes = slice(at * width, (at + 1) * width)
        mine = kept[:, :, :, lanes].astype(F32)
        coarse[:, :, :, lanes] = (mine + got[...].astype(F32)).astype(BF)
    coarse[:, :, :, 2 * width :] = pool[...]


def assemble_kernel(tokens, fine_kept, fine_got, coarse, send):
    start = tokens.shape[3]
    send[:, :, :, :start] = tokens[...]
    put_quarters(send, start, fine_kept[...] + fine_got[...].astype(F32))
    send[:, :, :, send.shape[3] - coarse.shape[3] :] = coarse[...]


def take_kernel(arrived, slots, rows_out):
    place = one_hot(slots[...], slots.shape[1] * 2)
    rows = arrived[...].reshape(place.shape[0], arrived.shape[-1])
    rows_out[...] = mm(place, rows, (0, 0)).astype(BF)


VMEM = pl.BlockSpec(memory_space=pltpu.VMEM)
HBM = pl.BlockSpec(memory_space=pltpu.HBM)


class Far(NamedTuple):
    value: jax.Array


class Near(NamedTuple):
    shape: tuple
    dtype: jnp.dtype = BF
    far: bool = False


class Fetched:
    def __init__(self, source, buffer, semaphore):
        self.buffer, self.shape, self.waited = buffer, buffer.shape, False
        self.copy = pltpu.make_async_copy(source, buffer, semaphore)
        self.copy.start()

    def wait(self):
        if not self.waited:
            self.copy.wait()
            self.waited = True

    def __getitem__(self, index):
        self.wait()
        return self.buffer[index]


class Stored:
    def __init__(self, target, buffer, semaphore):
        self.buffer, self.shape, self.dtype, self.started = buffer, buffer.shape, buffer.dtype, False
        self.copy = pltpu.make_async_copy(buffer, target, semaphore)

    def __setitem__(self, index, values):
        self.buffer[index] = values

    def __getitem__(self, index):
        return self.buffer[index]

    def flush(self):
        if not self.started:
            self.copy.start()
            self.started = True


def call(kernel, inputs, outputs, scratch=(), mebibytes=16):
    in_specs, arrays, buffers = [], [], []
    for value in inputs:
        far = isinstance(value, Far)
        in_specs.append(HBM if far else VMEM)
        arrays.append(
            pltpu.with_memory_space_constraint(value.value, pltpu.HBM) if far else value
        )
        if far:
            buffers.append(pltpu.VMEM(value.value.shape, value.value.dtype))
    buffers.extend(pltpu.VMEM(out.shape, out.dtype) for out in outputs if out.far)
    flags = [isinstance(value, Far) for value in inputs] + [out.far for out in outputs]
    sizes = len(inputs), len(flags), len(flags) + len(buffers)

    def body(*refs):
        semaphores = refs[sizes[2]] if buffers else None
        given, views = 0, []
        for at, far in enumerate(flags):
            if far:
                kind = Fetched if at < sizes[0] else Stored
                views.append(kind(refs[at], refs[sizes[1] + given], semaphores.at[given]))
                given += 1
            else:
                views.append(refs[at])
        kernel(*views, *refs[sizes[2] + (1 if buffers else 0) :])
        for view in views:
            if isinstance(view, Stored):
                view.flush()
        for view in views:
            if isinstance(view, Fetched):
                view.wait()
            if isinstance(view, Stored):
                view.copy.wait()

    own = [pltpu.SemaphoreType.DMA((len(buffers),))] if buffers else []
    return pl.pallas_call(
        body,
        out_shape=[
            (pltpu.HBM if out.far else jax.ShapeDtypeStruct)(out.shape, out.dtype)
            for out in outputs
        ],
        in_specs=in_specs,
        out_specs=[HBM if out.far else VMEM for out in outputs],
        scratch_shapes=buffers + own + list(scratch),
        compiler_params=pltpu.CompilerParams(vmem_limit_bytes=mebibytes * 1024 * 1024),
    )(*arrays)


def exchange(values):
    return lax.ppermute(values, "grp", [(0, 1), (1, 0)])


def spread_blocks(values, axes):
    return lax.all_to_all(values, axes, split_axis=0, concat_axis=0, tiled=True)


def neighbours(owners, stride):
    pairs = []
    for chip in range(owners):
        place = chip // stride % 4
        for core in range(2):
            partner = ((place + core ^ 1) - core) % 4
            pairs.append((2 * chip + core, 2 * (chip + (partner - place) * stride) + core))
    return pairs


def route(values, devices):
    rows, features = values.shape
    blocks = values.reshape(devices, rows // devices, features)
    return spread_blocks(blocks, ("pts", "grp")).reshape(rows, features)


def on_device(
    points,
    rotated_place,
    rotated_source,
    ball_counts,
    fine_projection,
    fine_output,
    pool_weight,
    coarse_projection,
    coarse_output,
    coarse_cotangent,
):
    count, features = points.shape
    devices = lax.axis_size(("pts", "grp"))
    slots = 2 * count
    scaling = 1.0 / math.sqrt(count * devices)
    owners = lax.axis_size("pts")
    run, step = owners // 4, owners // 16
    wide = 2 * features
    half_rows = count // 2

    send, send_slot, pair_slot, receive_slot, live = call(
        route_kernel,
        (
            Far(rotated_place.reshape(1, count)),
            Far(rotated_source.reshape(1, count)),
            Far(ball_counts.reshape(1, -1)),
            Far(points),
        ),
        (
            Near((slots, features)),
            Near((1, count), jnp.int32),
            Near((1, count), jnp.int32),
            Near((1, count), jnp.int32),
            Near((1, count), F32),
        ),
    )
    arrived = route(send, devices)
    heads = features // HD * (count // BALL)
    send, rotated, projected, mixture, weights = call(
        fine_forward_kernel,
        (arrived, receive_slot, live, fine_projection, Far(fine_output)),
        (
            Near((slots, features)),
            Near((count, features)),
            Near((count, 3 * features)),
            Near((count, features)),
            Near((heads, BALL, BALL)),
        ),
    )
    arrived = route(send, devices)
    (own_pack,) = call(
        join_kernel, (arrived, pair_slot, coarse_cotangent), (Near((half_rows, 2 * wide)),)
    )
    other_pack = exchange(own_pack)
    coarse, own_unit, own_rows = call(
        coarse_own_rows_kernel,
        (own_pack, pool_weight, coarse_projection, Far(coarse_output)),
        (
            Near((half_rows, wide)),
            Near((half_rows, wide)),
            Near((half_rows, 2 * wide)),
        ),
    )
    keep, give, other_unit = call(
        coarse_kernel,
        (other_pack, own_rows, pool_weight, coarse_projection, coarse_output),
        (
            Near((half_rows, 2 * wide)),
            Near((half_rows, 2 * wide)),
            Near((half_rows, wide)),
        ),
    )
    got = exchange(give)
    blocks = (owners, 2, slots // devices)
    kept, first_half, second_half = call(
        functools.partial(coarse_weights_kernel, strides=(run, step)),
        (own_unit, other_unit, keep, give, own_pack, other_pack),
        (
            Near((*blocks, wide // 2)),
            Near((*blocks, wide // 4)),
            Near((*blocks, wide // 4)),
        ),
    )
    mixed, back = call(
        coarse_own_kernel,
        (coarse, keep, coarse_projection, coarse_output),
        (Near((half_rows, wide), F32), Near((half_rows, wide), F32)),
    )
    got, kept, first_half, second_half = lax.optimization_barrier(
        (got, kept, first_half, second_half)
    )
    coarse_result, coarse_gradient, send = call(
        coarse_finish_kernel,
        (
            coarse,
            mixed,
            back,
            got,
            coarse_cotangent,
            pool_weight,
            coarse_projection,
            coarse_output,
            pair_slot,
        ),
        (
            Near((half_rows, wide), far=True),
            Near((half_rows, wide)),
            Near((slots, features)),
        ),
    )
    arrived = route(send, devices)
    arrived, first_half, second_half, coarse_gradient = lax.optimization_barrier(
        (arrived, first_half, second_half, coarse_gradient)
    )
    got_first = lax.ppermute(first_half, ("pts", "grp"), neighbours(owners, run))
    got_second = lax.ppermute(second_half, ("pts", "grp"), neighbours(owners, step))
    other_gradient = exchange(coarse_gradient)
    tokens, fine_kept, fine_passed = call(
        fine_backward_kernel,
        (
            arrived,
            receive_slot,
            rotated,
            projected,
            mixture,
            weights,
            fine_projection,
            fine_output,
        ),
        (
            Near((*blocks, features)),
            Near((features, 2 * features), F32),
            Near((features, 2 * features)),
        ),
        scratch=(pltpu.VMEM((count, 3 * features), BF),),
    )
    fine_got = exchange(fine_passed)
    (pool_part,) = call(
        pool_kernel,
        (own_pack, other_pack, coarse_gradient, other_gradient),
        (Near((*blocks, wide // 4)),),
    )
    (coarse_part,) = call(
        coarse_part_kernel,
        (kept, got_first, got_second, pool_part),
        (Near((*blocks, 3 * wide // 4)),),
    )
    across = features + wide
    (send,) = call(
        assemble_kernel,
        (tokens, fine_kept, fine_got, coarse_part),
        (Near((*blocks, across)),),
    )
    arrived = spread_blocks(send.reshape(devices, slots // devices, across), ("pts", "grp"))
    (spread,) = call(
        functools.partial(sum_kernel, tokens=features, run=run, step=step),
        (arrived.reshape(send.shape),),
        (Near((owners, slots // devices, features + 5 * wide // 2)),),
    )
    own_sums = spread_blocks(spread, "pts")
    (points_gradient,) = call(
        take_kernel, (arrived[:, :, :features], send_slot), (Near((count, features)),)
    )
    other_sums = exchange(own_sums)
    sums = write_sums(own_sums, other_sums, features, wide, scaling)
    return (coarse_result, points_gradient, *sums)


def solution(mesh):
    tokens = P(("pts", "grp"), None)
    in_specs = (
        tokens,
        P(("pts", "grp")),
        P(("pts", "grp")),
        P(),
        P(),
        P(),
        P(),
        P(),
        P(),
        tokens,
    )
    out_specs = (tokens, tokens, P(), P(), P(), P(), P())
    return jax.shard_map(
        on_device, mesh=mesh, in_specs=in_specs, out_specs=out_specs, check_vma=False
    )
```

```python
import functools
import math
from typing import NamedTuple

import jax
import jax.numpy as jnp
from jax import lax
from jax.experimental import pallas as pl
from jax.experimental.pallas import tpu as pltpu
from jax.sharding import PartitionSpec as P

HD = 64
BALL = 256
PAIR = 2 * HD
EPSILON = 1e-05
BF = jnp.bfloat16
F32 = jnp.float32


def mm(a, b, contract=(1, 0)):
    return lax.dot_general(
        a, b, (((contract[0],), (contract[1],)), ((), ())), preferred_element_type=F32
    )


def normalize(values):
    floats = values.astype(F32)
    center = floats - jnp.mean(floats, axis=-1, keepdims=True)
    inverse = lax.rsqrt(jnp.mean(center * center, axis=-1, keepdims=True) + EPSILON)
    return center * inverse, inverse


def norm_backward(incoming, normed, inverse):
    first_mean = jnp.mean(incoming, axis=-1, keepdims=True)
    second_mean = jnp.mean(incoming * normed, axis=-1, keepdims=True)
    return inverse * (incoming - first_mean - normed * second_mean)


def one_hot(slots, total):
    shape = (total, slots.shape[1])
    return (lax.broadcasted_iota(jnp.int32, shape, 0) == slots).astype(BF)


def softmax_rows(scores):
    raised = jnp.exp(scores - jnp.max(scores, axis=-1, keepdims=True))
    return (raised * (1.0 / jnp.sum(raised, axis=-1, keepdims=True))).astype(BF)


def slopes_of(weights, against):
    wide = weights.astype(F32)
    diagonal = jnp.sum(wide * against, axis=-1, keepdims=True)
    return (wide * (against - diagonal)).astype(BF)


def stack_heads(rows, heads):
    lanes = lax.broadcasted_iota(jnp.int32, rows.shape, 1) // HD
    none = jnp.zeros_like(rows)
    return jnp.concatenate([jnp.where(lanes == at, rows, none) for at in range(heads)], axis=0)


def unstack_heads(rows, heads):
    count = rows.shape[0] // heads
    merged = rows[:count]
    lanes = lax.broadcasted_iota(jnp.int32, merged.shape, 1) // HD
    for at in range(1, heads):
        merged = jnp.where(lanes == at, rows[at * count : (at + 1) * count], merged)
    return merged


def turned(rows):
    return rows.astype(F32).T.astype(BF)


def column_of(row):
    count = row.shape[1]
    turned = jnp.broadcast_to(row.astype(F32), (128, count)).T
    return jnp.concatenate([turned] * (count // 128), axis=1)


def route_kernel(
    place, source, counts, points, send, send_slot, pair_slot, receive_slot, live
):
    count = place.shape[1]
    shift = count.bit_length() - 1
    capacity = send.shape[0] * count // (counts.shape[1] * BALL)
    to_row = place[...] >> shift
    rows = lax.broadcasted_iota(jnp.int32, (count, count), 0)
    columns = lax.broadcasted_iota(jnp.int32, (count, count), 1)
    earlier = (column_of(to_row) == to_row.astype(F32)) & (rows < columns)
    rank = jnp.sum(jnp.where(earlier, 1.0, 0.0), axis=0, keepdims=True)
    slot = to_row * capacity + rank.astype(jnp.int32)
    send_slot[...] = slot
    even_first = jnp.where(columns < count // 2, 2 * columns, 2 * columns + 1 - count)
    digits = jnp.concatenate([slot >> 5, slot & 31] + [jnp.zeros_like(slot)] * 6, axis=0)
    moved = mm(digits.astype(F32).astype(BF), (rows == even_first).astype(BF)).astype(jnp.int32)
    pair_slot[...] = moved[0:1] * 32 + moved[1:2]
    source_row = source[...]
    from_row = source_row >> shift
    earlier = (column_of(from_row) == from_row.astype(F32)) & (
        column_of(source_row) < source_row.astype(F32)
    )
    rank = jnp.sum(jnp.where(earlier, 1.0, 0.0), axis=0, keepdims=True)
    receive_slot[...] = from_row * capacity + rank.astype(jnp.int32)
    balls = counts.shape[1]
    own_ball = one_hot(source_row >> (BALL.bit_length() - 1), balls)
    filled = mm(jnp.broadcast_to(counts[...].astype(F32), (8, balls)).astype(BF), own_ball)
    inside = (source_row & (BALL - 1)).astype(F32)
    live[...] = jnp.where(inside < filled[:1], 1.0, 0.0)
    send[...] = mm(one_hot(slot, send.shape[0]), points[...]).astype(BF)


def fine_forward_kernel(
    arrived, receive_slot, live, projection, output, send, rotated, projected, mixture, weights
):
    place = one_hot(receive_slot[...], arrived.shape[0])
    rows_in = mm(place, arrived[...], (0, 0))
    rotated[...] = rows_in.astype(BF)
    features = rows_in.shape[1]
    normed, _ = normalize(rows_in)
    projected[...] = mm(normed.astype(BF), projection[...]).astype(BF)
    balls = rows_in.shape[0] // BALL
    for ball in range(balls):
        rows = slice(ball * BALL, (ball + 1) * BALL)
        alive = live[:, rows] > 0.5
        for pair in range(features // PAIR):
            lanes = slice(pair * PAIR, (pair + 1) * PAIR)
            query = projected[rows, lanes] * jnp.asarray(HD ** (-0.5), BF)
            key = projected[rows, features + pair * PAIR : features + (pair + 1) * PAIR]
            value = projected[rows, 2 * features + pair * PAIR : 2 * features + (pair + 1) * PAIR]
            scores = mm(stack_heads(query, 2), key, (1, 1))
            both = softmax_rows(jnp.where(alive, scores, -1e30))
            first = (ball * features + pair * PAIR) // HD
            weights[first : first + 2] = both.reshape(2, BALL, BALL)
            mixture[rows, lanes] = unstack_heads(mm(both, value), 2).astype(BF)
    result = (rows_in + mm(mixture[...], output[...])).astype(BF)
    send[...] = mm(place, result).astype(BF)


def join_kernel(arrived, pair_slot, cotangent, pack):
    half_rows, wide = cotangent.shape
    place = one_hot(pair_slot[...], arrived.shape[0])
    rows = mm(place, arrived[...], (0, 0)).astype(BF)
    pack[:, : wide // 2] = rows[:half_rows]
    pack[:, wide // 2 : wide] = rows[half_rows:]
    pack[:, wide:] = cotangent[...]


def project_rows(joined, cotangent, pool, projection, output):
    wide = pool.shape[1]
    part = wide // 2
    first = pl.multiple_of(lax.axis_index("grp") * part, part)
    tokens = mm(joined, pool[...]).astype(BF)
    normed, _ = normalize(tokens)
    unit = normed.astype(BF)
    rows = [
        mm(unit, projection[:, pl.ds(at * wide + first, part)]).astype(BF) for at in range(3)
    ]
    rows.append(mm(cotangent, output[pl.ds(first, part), :], (1, 1)).astype(BF))
    return tokens, unit, rows


def coarse_own_rows_kernel(own_pack, pool, projection, output, coarse, unit, rows_out):
    wide = pool.shape[1]
    tokens, unit_rows, rows = project_rows(
        own_pack[:, :wide], own_pack[:, wide:], pool, projection, output
    )
    coarse[...] = tokens
    unit[...] = unit_rows
    for at, values in enumerate(rows):
        rows_out[:, at * wide // 2 : (at + 1) * wide // 2] = values


def coarse_kernel(other_pack, own_rows, pool, projection, output, keep, give, unit):
    wide = pool.shape[1]
    part = wide // 2
    half_rows = own_rows.shape[0]
    _, unit_rows, rows = project_rows(
        other_pack[:, :wide], other_pack[:, wide:], pool, projection, output
    )
    unit[...] = unit_rows
    queries, keys, values, incoming = [
        jnp.concatenate([own_rows[:, at * part : (at + 1) * part], rows[at]], axis=0)
        for at in range(4)
    ]
    queries_turned, incoming_turned = turned(queries), turned(incoming)
    key_parts, value_parts = [], []

    def put(at, rows):
        target = slice(at, at + rows.shape[1])
        keep[:, target] = rows[:half_rows]
        give[:, target] = rows[half_rows:]

    for pair in range(part // PAIR):
        lanes = slice(pair * PAIR, (pair + 1) * PAIR)
        key, value = keys[:, lanes], values[:, lanes]
        query = queries[:, lanes] * jnp.asarray(HD ** (-0.5), BF)
        head_weights = softmax_rows(mm(stack_heads(query, 2), key, (1, 1)))
        against = mm(stack_heads(incoming[:, lanes], 2), value, (1, 1))
        slopes = slopes_of(head_weights, against)
        put(pair * PAIR, unstack_heads(mm(head_weights, value), 2).astype(BF))
        query_part = unstack_heads(mm(slopes, key), 2) * HD ** (-0.5)
        put(part + pair * PAIR, query_part.astype(BF))
        for half in range(2):
            band = slice(pair * PAIR + half * HD, pair * PAIR + (half + 1) * HD)
            rows = slice(half * 2 * half_rows, (half + 1) * 2 * half_rows)
            key_parts.append(mm(queries_turned[band], slopes[rows]) * HD ** (-0.5))
            value_parts.append(mm(incoming_turned[band], head_weights[rows]))
    put(2 * part, jnp.concatenate(key_parts, axis=0).T.astype(BF))
    put(3 * part, jnp.concatenate(value_parts, axis=0).T.astype(BF))


def heads_back(grads, index, projection, output):
    wide = output.shape[1]
    part = wide // 2
    first = pl.multiple_of(index * part, part)
    mixed = mm(grads[:, :part], output[pl.ds(first, part), :])
    back = jnp.zeros_like(mixed)
    for at in range(3):
        back = back + mm(
            grads[:, (at + 1) * part : (at + 2) * part],
            projection[:, pl.ds(at * wide + first, part)],
            (1, 1),
        )
    return mixed, back


def coarse_own_kernel(coarse, keep, projection, output, mixed, back):
    own_mixed, own_back = heads_back(keep, lax.axis_index("grp"), projection, output)
    mixed[...] = coarse[...].astype(F32) + own_mixed
    back[...] = own_back


def coarse_finish_kernel(
    coarse,
    mixed,
    back,
    got,
    cotangent,
    pool,
    projection,
    output,
    pair_slot,
    result,
    gradient,
    send,
):
    other_mixed, other_back = heads_back(got, 1 - lax.axis_index("grp"), projection, output)
    result[...] = (mixed[...] + other_mixed).astype(BF)
    result.flush()
    normed, inverse = normalize(coarse[...])
    gradient_rows = (
        cotangent[...].astype(F32) + norm_backward(back[...] + other_back, normed, inverse)
    ).astype(BF)
    gradient[...] = gradient_rows
    fine = mm(gradient_rows, pool[...], (1, 1)).astype(BF)
    features = send.shape[1]
    stacked = jnp.concatenate([fine[:, :features], fine[:, features:]], axis=0)
    send[...] = mm(one_hot(pair_slot[...], send.shape[0]), stacked).astype(BF)


def coarse_weights_kernel(
    own_unit,
    other_unit,
    keep,
    give,
    own_pack,
    other_pack,
    kept,
    first_half,
    second_half,
    *,
    strides,
):
    chip, core = lax.axis_index("pts"), lax.axis_index("grp")
    wide = own_unit.shape[1]
    part = wide // 2
    unit = jnp.concatenate([own_unit[...], other_unit[...]], axis=0)
    stacked = jnp.concatenate([keep[...], give[...]], axis=0)
    cotangent = jnp.concatenate([own_pack[:, wide:], other_pack[:, wide:]], axis=0)
    projection_term = mm(unit, stacked[:, part:], (0, 0))
    output_term = mm(stacked[:, :part], cotangent, (0, 0))
    across = projection_term.shape[1] // 2
    width = wide // 4
    for side in range(2):
        stack = [output_term[:, (2 * side + k) * width : (2 * side + k + 1) * width] for k in range(2)]
        columns = projection_term[:, side * across : (side + 1) * across]
        terms = jnp.concatenate([columns, jnp.concatenate(stack, axis=0)], axis=1)
        for at, passed in enumerate((first_half, second_half)):
            low = terms[:, 2 * at * width : (2 * at + 1) * width]
            high = terms[:, (2 * at + 1) * width : (2 * at + 2) * width]
            upper = (chip // strides[at] + core) % 2 == 1
            put_blocks(kept, side, at * width, jnp.where(upper, high, low))
            put_blocks(passed, side, 0, jnp.where(upper, low, high))


def put_quarters(blocks, lane, term):
    width = term.shape[1] // 4
    for side in range(2):
        stack = [term[:, (2 * side + k) * width : (2 * side + k + 1) * width] for k in range(2)]
        put_blocks(blocks, side, lane, jnp.concatenate(stack, axis=0))


def put_blocks(blocks, side, lane, rows):
    owners, width = blocks.shape[0], rows.shape[1]
    pieces = rows.reshape(owners, rows.shape[0] // owners, width)
    blocks[:, side, :, lane : lane + width] = pieces.astype(BF)


def sum_kernel(arrived, spread, *, tokens, run, step):
    senders, _, rows, across = arrived.shape
    width = (across - tokens) // 4

    def pieces(side, at):
        start = tokens + at * width
        return arrived[:, side, :, start : start + width].astype(F32)

    total = [jnp.sum(pieces(side, 0), axis=0) for side in range(2)]
    for side in range(2):
        for at, block in enumerate((run, step)):
            split = pieces(side, 1 + at).reshape(senders // (2 * block), 2, block, rows, width)
            halves = jnp.sum(jnp.sum(split, axis=2), axis=0)
            total.extend([halves[side], halves[1 - side]])
        total.append(jnp.sum(pieces(side, 3), axis=0))
    total = jnp.concatenate(total, axis=1).astype(BF)
    spread[...] = jnp.broadcast_to(total[None], spread.shape)


def write_half(terms, side, refs, stages, semaphores, scaling):
    projection, output, pool, fine_projection, fine_output = refs
    tall, square = stages
    wide = pool.shape[0]
    part, width = wide // 2, wide // 4
    across = 3 * part // 2
    copies = []

    def lanes(start, count):
        values = terms[:, :, start : start + count].astype(F32) * scaling
        return values.reshape(terms.shape[0] * terms.shape[1], count)

    def prepare(stage, target):
        copies.append(pltpu.make_async_copy(stage, target, semaphores.at[len(copies)]))
        return copies[-1]

    def fill(stage, start):
        block = lanes(start, width)
        stage[:, :width] = block[:part]
        stage[:, width:] = block[part:]

    place = pl.multiple_of(side * part, part)
    for heads in range(2):
        start = 2 * width + heads * (across + 2 * width)
        for k in range(3):
            columns = [half * across + k * width for half in range(2)]
            places = [column // part * wide + heads * part + column % part for column in columns]
            target = pl.multiple_of(jnp.where(side == 0, places[0], places[1]), width)
            stage = tall.at[3 * heads + k]
            stage[...] = lanes(start + k * width, width)
            prepare(stage, projection.at[:, pl.ds(target, width)]).start()
        for at, ref in enumerate((output, pool)):
            stage = square.at[2 * heads + at]
            fill(stage, start + across + at * width)
            target = ref.at[heads * part : (heads + 1) * part, pl.ds(place, part)]
            prepare(stage, target).start()
    fill(square.at[4], 0)
    prepare(square.at[4], fine_projection.at[:, pl.ds(place, part)]).start()
    fill(square.at[5], width)
    last = semaphores.at[len(copies)]
    to_projection = pltpu.make_async_copy(
        square.at[5], fine_projection.at[:, 2 * part : 3 * part], last
    )
    to_output = pltpu.make_async_copy(square.at[5], fine_output, last)

    @pl.when(side == 0)
    def _():
        to_projection.start()
        to_projection.wait()

    @pl.when(side != 0)
    def _():
        to_output.start()
        to_output.wait()

    for copy in copies:
        copy.wait()


def own_sums_kernel(terms, *refs, scaling):
    write_half(terms, lax.axis_index("grp"), refs[:5], refs[5:7], refs[7], scaling)


def other_sums_kernel(terms, *refs, scaling):
    write_half(terms, 1 - lax.axis_index("grp"), refs[5:10], refs[10:12], refs[12], scaling)


def write_sums(own, other, features, wide, scaling):
    part, width = wide // 2, wide // 4
    shapes = [(wide, 3 * wide), (wide, wide), (wide, wide)]
    shapes += [(features, 3 * features), (features, features)]
    stages = [
        pltpu.VMEM((6, wide, width), F32),
        pltpu.VMEM((6, part, part), F32),
        pltpu.SemaphoreType.DMA((12,)),
    ]
    limits = pltpu.CompilerParams(vmem_limit_bytes=16 * 1024 * 1024)
    outputs = [pltpu.HBM(shape, F32) for shape in shapes]
    firsts = pl.pallas_call(
        functools.partial(own_sums_kernel, scaling=scaling),
        out_shape=outputs,
        in_specs=[VMEM],
        out_specs=[HBM] * 5,
        scratch_shapes=stages,
        compiler_params=limits,
    )(own)
    projection, output, pool, fine_projection, fine_output = pl.pallas_call(
        functools.partial(other_sums_kernel, scaling=scaling),
        out_shape=outputs,
        in_specs=[VMEM] + [HBM] * 5,
        out_specs=[HBM] * 5,
        scratch_shapes=stages,
        input_output_aliases={at + 1: at for at in range(5)},
        compiler_params=limits,
    )(other, *firsts)
    return fine_projection, fine_output, pool, projection, output


def fine_backward_kernel(
    arrived,
    receive_slot,
    rotated,
    projected,
    mixture,
    weights,
    projection,
    output,
    tokens,
    kept,
    passed,
    grad_projected,
):
    place = one_hot(receive_slot[...], arrived.shape[0])
    gradient_rows = mm(place, arrived[...], (0, 0)).astype(BF)
    features = rotated.shape[1]
    entering = mm(gradient_rows, output[...], (1, 1)).astype(BF)
    terms = [mm(mixture[...], gradient_rows, (0, 0))]
    balls = rotated.shape[0] // BALL
    heads = features // HD
    query_turned, entering_turned = turned(projected[:, :features]), turned(entering)
    turned_parts = ([], [])
    for ball in range(balls):
        rows = slice(ball * BALL, (ball + 1) * BALL)
        key, value = projected[rows, features : 2 * features], projected[rows, 2 * features :]
        head_weights = [weights[ball * heads + at] for at in range(heads)]
        against = mm(stack_heads(entering[rows], heads), value, (1, 1))
        slopes = slopes_of(jnp.concatenate(head_weights, axis=0), against)
        query_part = unstack_heads(mm(slopes, key), heads) * HD ** (-0.5)
        grad_projected[rows, :features] = query_part.astype(BF)
        pieces = ([], [])
        for at in range(heads):
            band = slice(at * HD, (at + 1) * HD)
            own = slopes[at * BALL : (at + 1) * BALL]
            pieces[0].append(mm(query_turned[band, rows], own) * HD ** (-0.5))
            pieces[1].append(mm(entering_turned[band, rows], head_weights[at]))
        for at in range(2):
            turned_parts[at].append(jnp.concatenate(pieces[at], axis=0))
    for at in range(2):
        whole = jnp.concatenate(turned_parts[at], axis=1).T.astype(BF)
        grad_projected[:, (at + 1) * features : (at + 2) * features] = whole
    normed, inverse = normalize(rotated[...])
    unit_rows = normed.astype(BF)
    for at in range(3):
        columns = slice(at * features, (at + 1) * features)
        terms.insert(at, mm(unit_rows, grad_projected[:, columns], (0, 0)))
    low = jnp.concatenate(terms[:2], axis=1)
    high = jnp.concatenate(terms[2:], axis=1)
    upper = lax.axis_index("grp") == 1
    kept[...] = jnp.where(upper, high, low)
    passed[...] = jnp.where(upper, low, high).astype(BF)
    back = mm(grad_projected[...], projection[...], (1, 1))
    result = gradient_rows.astype(F32) + norm_backward(back, normed, inverse)
    tokens[...] = mm(place, result.astype(BF)).reshape(tokens.shape).astype(BF)


def pool_kernel(own_pack, other_pack, own_gradient, other_gradient, blocks):
    part = own_gradient.shape[1] // 2
    first = pl.multiple_of(lax.axis_index("grp") * part, part)
    term = mm(own_pack[:, pl.ds(first, part)], own_gradient[...], (0, 0))
    term = term + mm(other_pack[:, pl.ds(first, part)], other_gradient[...], (0, 0))
    put_quarters(blocks, 0, term)


def coarse_part_kernel(kept, got_first, got_second, pool, coarse):
    width = got_first.shape[3]
    for at, got in enumerate((got_first, got_second)):
        lanes = slice(at * width, (at + 1) * width)
        mine = kept[:, :, :, lanes].astype(F32)
        coarse[:, :, :, lanes] = (mine + got[...].astype(F32)).astype(BF)
    coarse[:, :, :, 2 * width :] = pool[...]


def assemble_kernel(tokens, fine_kept, fine_got, coarse, send):
    start = tokens.shape[3]
    send[:, :, :, :start] = tokens[...]
    put_quarters(send, start, fine_kept[...] + fine_got[...].astype(F32))
    send[:, :, :, send.shape[3] - coarse.shape[3] :] = coarse[...]


def take_kernel(arrived, slots, rows_out):
    place = one_hot(slots[...], slots.shape[1] * 2)
    rows = arrived[...].reshape(place.shape[0], arrived.shape[-1])
    rows_out[...] = mm(place, rows, (0, 0)).astype(BF)


VMEM = pl.BlockSpec(memory_space=pltpu.VMEM)
HBM = pl.BlockSpec(memory_space=pltpu.HBM)


class Far(NamedTuple):
    value: jax.Array


class Near(NamedTuple):
    shape: tuple
    dtype: jnp.dtype = BF
    far: bool = False


class Fetched:
    def __init__(self, source, buffer, semaphore):
        self.buffer, self.shape, self.waited = buffer, buffer.shape, False
        self.copy = pltpu.make_async_copy(source, buffer, semaphore)
        self.copy.start()

    def wait(self):
        if not self.waited:
            self.copy.wait()
            self.waited = True

    def __getitem__(self, index):
        self.wait()
        return self.buffer[index]


class Stored:
    def __init__(self, target, buffer, semaphore):
        self.buffer, self.shape, self.dtype, self.started = buffer, buffer.shape, buffer.dtype, False
        self.copy = pltpu.make_async_copy(buffer, target, semaphore)

    def __setitem__(self, index, values):
        self.buffer[index] = values

    def __getitem__(self, index):
        return self.buffer[index]

    def flush(self):
        if not self.started:
            self.copy.start()
            self.started = True


def call(kernel, inputs, outputs, scratch=(), mebibytes=16):
    in_specs, arrays, buffers = [], [], []
    for value in inputs:
        far = isinstance(value, Far)
        in_specs.append(HBM if far else VMEM)
        arrays.append(
            pltpu.with_memory_space_constraint(value.value, pltpu.HBM) if far else value
        )
        if far:
            buffers.append(pltpu.VMEM(value.value.shape, value.value.dtype))
    buffers.extend(pltpu.VMEM(out.shape, out.dtype) for out in outputs if out.far)
    flags = [isinstance(value, Far) for value in inputs] + [out.far for out in outputs]
    sizes = len(inputs), len(flags), len(flags) + len(buffers)

    def body(*refs):
        semaphores = refs[sizes[2]] if buffers else None
        given, views = 0, []
        for at, far in enumerate(flags):
            if far:
                kind = Fetched if at < sizes[0] else Stored
                views.append(kind(refs[at], refs[sizes[1] + given], semaphores.at[given]))
                given += 1
            else:
                views.append(refs[at])
        kernel(*views, *refs[sizes[2] + (1 if buffers else 0) :])
        for view in views:
            if isinstance(view, Stored):
                view.flush()
        for view in views:
            if isinstance(view, Fetched):
                view.wait()
            if isinstance(view, Stored):
                view.copy.wait()

    own = [pltpu.SemaphoreType.DMA((len(buffers),))] if buffers else []
    return pl.pallas_call(
        body,
        out_shape=[
            (pltpu.HBM if out.far else jax.ShapeDtypeStruct)(out.shape, out.dtype)
            for out in outputs
        ],
        in_specs=in_specs,
        out_specs=[HBM if out.far else VMEM for out in outputs],
        scratch_shapes=buffers + own + list(scratch),
        compiler_params=pltpu.CompilerParams(vmem_limit_bytes=mebibytes * 1024 * 1024),
    )(*arrays)


def exchange(values):
    return lax.ppermute(values, "grp", [(0, 1), (1, 0)])


def spread_blocks(values, axes):
    return lax.all_to_all(values, axes, split_axis=0, concat_axis=0, tiled=True)


def neighbours(owners, stride):
    pairs = []
    for chip in range(owners):
        place = chip // stride % 4
        for core in range(2):
            partner = ((place + core ^ 1) - core) % 4
            pairs.append((2 * chip + core, 2 * (chip + (partner - place) * stride) + core))
    return pairs


def route(values, devices):
    rows, features = values.shape
    blocks = values.reshape(devices, rows // devices, features)
    return spread_blocks(blocks, ("pts", "grp")).reshape(rows, features)


def on_device(
    points,
    rotated_place,
    rotated_source,
    ball_counts,
    fine_projection,
    fine_output,
    pool_weight,
    coarse_projection,
    coarse_output,
    coarse_cotangent,
):
    count, features = points.shape
    devices = lax.axis_size(("pts", "grp"))
    slots = 2 * count
    scaling = 1.0 / math.sqrt(count * devices)
    owners = lax.axis_size("pts")
    run, step = owners // 4, owners // 16
    wide = 2 * features
    half_rows = count // 2

    send, send_slot, pair_slot, receive_slot, live = call(
        route_kernel,
        (
            Far(rotated_place.reshape(1, count)),
            Far(rotated_source.reshape(1, count)),
            Far(ball_counts.reshape(1, -1)),
            Far(points),
        ),
        (
            Near((slots, features)),
            Near((1, count), jnp.int32),
            Near((1, count), jnp.int32),
            Near((1, count), jnp.int32),
            Near((1, count), F32),
        ),
    )
    arrived = route(send, devices)
    heads = features // HD * (count // BALL)
    send, rotated, projected, mixture, weights = call(
        fine_forward_kernel,
        (arrived, receive_slot, live, fine_projection, Far(fine_output)),
        (
            Near((slots, features)),
            Near((count, features)),
            Near((count, 3 * features)),
            Near((count, features)),
            Near((heads, BALL, BALL)),
        ),
    )
    arrived = route(send, devices)
    (own_pack,) = call(
        join_kernel, (arrived, pair_slot, coarse_cotangent), (Near((half_rows, 2 * wide)),)
    )
    other_pack = exchange(own_pack)
    coarse, own_unit, own_rows = call(
        coarse_own_rows_kernel,
        (own_pack, pool_weight, coarse_projection, Far(coarse_output)),
        (
            Near((half_rows, wide)),
            Near((half_rows, wide)),
            Near((half_rows, 2 * wide)),
        ),
    )
    keep, give, other_unit = call(
        coarse_kernel,
        (other_pack, own_rows, pool_weight, coarse_projection, coarse_output),
        (
            Near((half_rows, 2 * wide)),
            Near((half_rows, 2 * wide)),
            Near((half_rows, wide)),
        ),
    )
    got = exchange(give)
    blocks = (owners, 2, slots // devices)
    kept, first_half, second_half = call(
        functools.partial(coarse_weights_kernel, strides=(run, step)),
        (own_unit, other_unit, keep, give, own_pack, other_pack),
        (
            Near((*blocks, wide // 2)),
            Near((*blocks, wide // 4)),
            Near((*blocks, wide // 4)),
        ),
    )
    mixed, back = call(
        coarse_own_kernel,
        (coarse, keep, coarse_projection, coarse_output),
        (Near((half_rows, wide), F32), Near((half_rows, wide), F32)),
    )
    got, kept, first_half, second_half = lax.optimization_barrier(
        (got, kept, first_half, second_half)
    )
    coarse_result, coarse_gradient, send = call(
        coarse_finish_kernel,
        (
            coarse,
            mixed,
            back,
            got,
            coarse_cotangent,
            pool_weight,
            coarse_projection,
            coarse_output,
            pair_slot,
        ),
        (
            Near((half_rows, wide), far=True),
            Near((half_rows, wide)),
            Near((slots, features)),
        ),
    )
    arrived = route(send, devices)
    arrived, first_half, second_half, coarse_gradient = lax.optimization_barrier(
        (arrived, first_half, second_half, coarse_gradient)
    )
    got_first = lax.ppermute(first_half, ("pts", "grp"), neighbours(owners, run))
    got_second = lax.ppermute(second_half, ("pts", "grp"), neighbours(owners, step))
    other_gradient = exchange(coarse_gradient)
    tokens, fine_kept, fine_passed = call(
        fine_backward_kernel,
        (
            arrived,
            receive_slot,
            rotated,
            projected,
            mixture,
            weights,
            fine_projection,
            fine_output,
        ),
        (
            Near((*blocks, features)),
            Near((features, 2 * features), F32),
            Near((features, 2 * features)),
        ),
        scratch=(pltpu.VMEM((count, 3 * features), BF),),
    )
    fine_got = exchange(fine_passed)
    (pool_part,) = call(
        pool_kernel,
        (own_pack, other_pack, coarse_gradient, other_gradient),
        (Near((*blocks, wide // 4)),),
    )
    (coarse_part,) = call(
        coarse_part_kernel,
        (kept, got_first, got_second, pool_part),
        (Near((*blocks, 3 * wide // 4)),),
    )
    across = features + wide
    (send,) = call(
        assemble_kernel,
        (tokens, fine_kept, fine_got, coarse_part),
        (Near((*blocks, across)),),
    )
    arrived = spread_blocks(send.reshape(devices, slots // devices, across), ("pts", "grp"))
    (spread,) = call(
        functools.partial(sum_kernel, tokens=features, run=run, step=step),
        (arrived.reshape(send.shape),),
        (Near((owners, slots // devices, features + 5 * wide // 2)),),
    )
    own_sums = spread_blocks(spread, "pts")
    (points_gradient,) = call(
        take_kernel, (arrived[:, :, :features], send_slot), (Near((count, features)),)
    )
    other_sums = exchange(own_sums)
    sums = write_sums(own_sums, other_sums, features, wide, scaling)
    return (coarse_result, points_gradient, *sums)


def solution(mesh):
    tokens = P(("pts", "grp"), None)
    in_specs = (
        tokens,
        P(("pts", "grp")),
        P(("pts", "grp")),
        P(),
        P(),
        P(),
        P(),
        P(),
        P(),
        tokens,
    )
    out_specs = (tokens, tokens, P(), P(), P(), P(), P())
    return jax.shard_map(
        on_device, mesh=mesh, in_specs=in_specs, out_specs=out_specs, check_vma=False
    )
```

```python
import functools
import math
from typing import NamedTuple

import jax
import jax.numpy as jnp
from jax import lax
from jax.experimental import pallas as pl
from jax.experimental.pallas import tpu as pltpu
from jax.sharding import PartitionSpec as P

HD = 64
BALL = 256
PAIR = 2 * HD
EPSILON = 1e-05
BF = jnp.bfloat16
F32 = jnp.float32


def mm(a, b, contract=(1, 0)):
    return lax.dot_general(
        a, b, (((contract[0],), (contract[1],)), ((), ())), preferred_element_type=F32
    )


def normalize(values):
    floats = values.astype(F32)
    center = floats - jnp.mean(floats, axis=-1, keepdims=True)
    inverse = lax.rsqrt(jnp.mean(center * center, axis=-1, keepdims=True) + EPSILON)
    return center * inverse, inverse


def norm_backward(incoming, normed, inverse):
    first_mean = jnp.mean(incoming, axis=-1, keepdims=True)
    second_mean = jnp.mean(incoming * normed, axis=-1, keepdims=True)
    return inverse * (incoming - first_mean - normed * second_mean)


def one_hot(slots, total):
    shape = (total, slots.shape[1])
    return (lax.broadcasted_iota(jnp.int32, shape, 0) == slots).astype(BF)


def softmax_rows(scores):
    raised = jnp.exp(scores - jnp.max(scores, axis=-1, keepdims=True))
    return (raised * (1.0 / jnp.sum(raised, axis=-1, keepdims=True))).astype(BF)


def slopes_of(weights, against):
    wide = weights.astype(F32)
    diagonal = jnp.sum(wide * against, axis=-1, keepdims=True)
    return (wide * (against - diagonal)).astype(BF)


def stack_heads(rows, heads):
    lanes = lax.broadcasted_iota(jnp.int32, rows.shape, 1) // HD
    none = jnp.zeros_like(rows)
    return jnp.concatenate([jnp.where(lanes == at, rows, none) for at in range(heads)], axis=0)


def unstack_heads(rows, heads):
    count = rows.shape[0] // heads
    merged = rows[:count]
    lanes = lax.broadcasted_iota(jnp.int32, merged.shape, 1) // HD
    for at in range(1, heads):
        merged = jnp.where(lanes == at, rows[at * count : (at + 1) * count], merged)
    return merged


def turned(rows):
    return rows.astype(F32).T.astype(BF)


def column_of(row):
    count = row.shape[1]
    turned = jnp.broadcast_to(row.astype(F32), (128, count)).T
    return jnp.concatenate([turned] * (count // 128), axis=1)


def route_kernel(
    place, source, counts, points, send, send_slot, pair_slot, receive_slot, live
):
    count = place.shape[1]
    shift = count.bit_length() - 1
    capacity = send.shape[0] * count // (counts.shape[1] * BALL)
    to_row = place[...] >> shift
    rows = lax.broadcasted_iota(jnp.int32, (count, count), 0)
    columns = lax.broadcasted_iota(jnp.int32, (count, count), 1)
    earlier = (column_of(to_row) == to_row.astype(F32)) & (rows < columns)
    rank = jnp.sum(jnp.where(earlier, 1.0, 0.0), axis=0, keepdims=True)
    slot = to_row * capacity + rank.astype(jnp.int32)
    send_slot[...] = slot
    even_first = jnp.where(columns < count // 2, 2 * columns, 2 * columns + 1 - count)
    digits = jnp.concatenate([slot >> 5, slot & 31] + [jnp.zeros_like(slot)] * 6, axis=0)
    moved = mm(digits.astype(F32).astype(BF), (rows == even_first).astype(BF)).astype(jnp.int32)
    pair_slot[...] = moved[0:1] * 32 + moved[1:2]
    source_row = source[...]
    from_row = source_row >> shift
    earlier = (column_of(from_row) == from_row.astype(F32)) & (
        column_of(source_row) < source_row.astype(F32)
    )
    rank = jnp.sum(jnp.where(earlier, 1.0, 0.0), axis=0, keepdims=True)
    receive_slot[...] = from_row * capacity + rank.astype(jnp.int32)
    balls = counts.shape[1]
    own_ball = one_hot(source_row >> (BALL.bit_length() - 1), balls)
    filled = mm(jnp.broadcast_to(counts[...].astype(F32), (8, balls)).astype(BF), own_ball)
    inside = (source_row & (BALL - 1)).astype(F32)
    live[...] = jnp.where(inside < filled[:1], 1.0, 0.0)
    send[...] = mm(one_hot(slot, send.shape[0]), points[...]).astype(BF)


def fine_forward_kernel(
    arrived, receive_slot, live, projection, output, send, rotated, projected, mixture, weights
):
    place = one_hot(receive_slot[...], arrived.shape[0])
    rows_in = mm(place, arrived[...], (0, 0))
    rotated[...] = rows_in.astype(BF)
    features = rows_in.shape[1]
    normed, _ = normalize(rows_in)
    projected[...] = mm(normed.astype(BF), projection[...]).astype(BF)
    balls = rows_in.shape[0] // BALL
    for ball in range(balls):
        rows = slice(ball * BALL, (ball + 1) * BALL)
        alive = live[:, rows] > 0.5
        for pair in range(features // PAIR):
            lanes = slice(pair * PAIR, (pair + 1) * PAIR)
            query = projected[rows, lanes] * jnp.asarray(HD ** (-0.5), BF)
            key = projected[rows, features + pair * PAIR : features + (pair + 1) * PAIR]
            value = projected[rows, 2 * features + pair * PAIR : 2 * features + (pair + 1) * PAIR]
            scores = mm(stack_heads(query, 2), key, (1, 1))
            both = softmax_rows(jnp.where(alive, scores, -1e30))
            first = (ball * features + pair * PAIR) // HD
            weights[first : first + 2] = both.reshape(2, BALL, BALL)
            mixture[rows, lanes] = unstack_heads(mm(both, value), 2).astype(BF)
    result = (rows_in + mm(mixture[...], output[...])).astype(BF)
    send[...] = mm(place, result).astype(BF)


def join_kernel(arrived, pair_slot, cotangent, pack):
    half_rows, wide = cotangent.shape
    place = one_hot(pair_slot[...], arrived.shape[0])
    rows = mm(place, arrived[...], (0, 0)).astype(BF)
    pack[:, : wide // 2] = rows[:half_rows]
    pack[:, wide // 2 : wide] = rows[half_rows:]
    pack[:, wide:] = cotangent[...]


def project_rows(joined, cotangent, pool, projection, output):
    wide = pool.shape[1]
    part = wide // 2
    first = pl.multiple_of(lax.axis_index("grp") * part, part)
    tokens = mm(joined, pool[...]).astype(BF)
    normed, _ = normalize(tokens)
    unit = normed.astype(BF)
    rows = [
        mm(unit, projection[:, pl.ds(at * wide + first, part)]).astype(BF) for at in range(3)
    ]
    rows.append(mm(cotangent, output[pl.ds(first, part), :], (1, 1)).astype(BF))
    return tokens, unit, rows


def coarse_own_rows_kernel(own_pack, pool, projection, output, coarse, unit, rows_out):
    wide = pool.shape[1]
    tokens, unit_rows, rows = project_rows(
        own_pack[:, :wide], own_pack[:, wide:], pool, projection, output
    )
    coarse[...] = tokens
    unit[...] = unit_rows
    for at, values in enumerate(rows):
        rows_out[:, at * wide // 2 : (at + 1) * wide // 2] = values


def coarse_kernel(
    other_pack, own_rows, pool, projection, output, keep, give, give_mixed, unit
):
    wide = pool.shape[1]
    part = wide // 2
    half_rows = own_rows.shape[0]
    _, unit_rows, rows = project_rows(
        other_pack[:, :wide], other_pack[:, wide:], pool, projection, output
    )
    unit[...] = unit_rows
    queries, keys, values, incoming = [
        jnp.concatenate([own_rows[:, at * part : (at + 1) * part], rows[at]], axis=0)
        for at in range(4)
    ]
    queries_turned, incoming_turned = turned(queries), turned(incoming)
    key_parts, value_parts = [], []

    def put(at, rows):
        target = slice(at, at + rows.shape[1])
        keep[:, target] = rows[:half_rows]
        if at < part:
            give_mixed[:, target] = rows[half_rows:]
        else:
            give[:, at - part : at - part + rows.shape[1]] = rows[half_rows:]

    for pair in range(part // PAIR):
        lanes = slice(pair * PAIR, (pair + 1) * PAIR)
        key, value = keys[:, lanes], values[:, lanes]
        query = queries[:, lanes] * jnp.asarray(HD ** (-0.5), BF)
        head_weights = softmax_rows(mm(stack_heads(query, 2), key, (1, 1)))
        against = mm(stack_heads(incoming[:, lanes], 2), value, (1, 1))
        slopes = slopes_of(head_weights, against)
        put(pair * PAIR, unstack_heads(mm(head_weights, value), 2).astype(BF))
        query_part = unstack_heads(mm(slopes, key), 2) * HD ** (-0.5)
        put(part + pair * PAIR, query_part.astype(BF))
        for half in range(2):
            band = slice(pair * PAIR + half * HD, pair * PAIR + (half + 1) * HD)
            rows = slice(half * 2 * half_rows, (half + 1) * 2 * half_rows)
            key_parts.append(mm(queries_turned[band], slopes[rows]) * HD ** (-0.5))
            value_parts.append(mm(incoming_turned[band], head_weights[rows]))
    put(2 * part, jnp.concatenate(key_parts, axis=0).T.astype(BF))
    put(3 * part, jnp.concatenate(value_parts, axis=0).T.astype(BF))


def heads_back(grads, start, index, projection):
    wide = projection.shape[0]
    part = wide // 2
    first = pl.multiple_of(index * part, part)
    back = jnp.zeros((grads.shape[0], wide), F32)
    for at in range(3):
        back = back + mm(
            grads[:, start + at * part : start + (at + 1) * part],
            projection[:, pl.ds(at * wide + first, part)],
            (1, 1),
        )
    return back


def coarse_own_kernel(keep, projection, back):
    part = projection.shape[0] // 2
    back[...] = heads_back(keep, part, lax.axis_index("grp"), projection)


def coarse_finish_kernel(
    coarse, back, got, cotangent, pool, projection, pair_slot, give_mixed, pack, send
):
    other_back = heads_back(got, 0, 1 - lax.axis_index("grp"), projection)
    normed, inverse = normalize(coarse[...])
    gradient_rows = (
        cotangent[...].astype(F32) + norm_backward(back[...] + other_back, normed, inverse)
    ).astype(BF)
    wide = pool.shape[1]
    pack[:, :wide] = gradient_rows
    pack[:, wide:] = give_mixed[...]
    fine = mm(gradient_rows, pool[...], (1, 1)).astype(BF)
    features = send.shape[1]
    stacked = jnp.concatenate([fine[:, :features], fine[:, features:]], axis=0)
    send[...] = mm(one_hot(pair_slot[...], send.shape[0]), stacked).astype(BF)


def coarse_weights_kernel(
    own_unit,
    other_unit,
    keep,
    give,
    give_mixed,
    own_pack,
    other_pack,
    kept,
    first_half,
    second_half,
    *,
    strides,
):
    chip, core = lax.axis_index("pts"), lax.axis_index("grp")
    wide = own_unit.shape[1]
    part = wide // 2
    unit = jnp.concatenate([own_unit[...], other_unit[...]], axis=0)
    given = jnp.concatenate([give_mixed[...], give[...]], axis=1)
    stacked = jnp.concatenate([keep[...], given], axis=0)
    cotangent = jnp.concatenate([own_pack[:, wide:], other_pack[:, wide:]], axis=0)
    projection_term = mm(unit, stacked[:, part:], (0, 0))
    output_term = mm(stacked[:, :part], cotangent, (0, 0))
    across = projection_term.shape[1] // 2
    width = wide // 4
    for side in range(2):
        stack = [output_term[:, (2 * side + k) * width : (2 * side + k + 1) * width] for k in range(2)]
        columns = projection_term[:, side * across : (side + 1) * across]
        terms = jnp.concatenate([columns, jnp.concatenate(stack, axis=0)], axis=1)
        for at, passed in enumerate((first_half, second_half)):
            low = terms[:, 2 * at * width : (2 * at + 1) * width]
            high = terms[:, (2 * at + 1) * width : (2 * at + 2) * width]
            upper = (chip // strides[at] + core) % 2 == 1
            put_blocks(kept, side, at * width, jnp.where(upper, high, low))
            put_blocks(passed, side, 0, jnp.where(upper, low, high))


def put_quarters(blocks, lane, term):
    width = term.shape[1] // 4
    for side in range(2):
        stack = [term[:, (2 * side + k) * width : (2 * side + k + 1) * width] for k in range(2)]
        put_blocks(blocks, side, lane, jnp.concatenate(stack, axis=0))


def put_blocks(blocks, side, lane, rows):
    owners, width = blocks.shape[0], rows.shape[1]
    pieces = rows.reshape(owners, rows.shape[0] // owners, width)
    blocks[:, side, :, lane : lane + width] = pieces.astype(BF)


def sum_kernel(arrived, spread, *, tokens, run, step):
    senders, _, rows, across = arrived.shape
    width = (across - tokens) // 4

    def pieces(side, at):
        start = tokens + at * width
        return arrived[:, side, :, start : start + width].astype(F32)

    total = [jnp.sum(pieces(side, 0), axis=0) for side in range(2)]
    for side in range(2):
        for at, block in enumerate((run, step)):
            split = pieces(side, 1 + at).reshape(senders // (2 * block), 2, block, rows, width)
            halves = jnp.sum(jnp.sum(split, axis=2), axis=0)
            total.extend([halves[side], halves[1 - side]])
        total.append(jnp.sum(pieces(side, 3), axis=0))
    total = jnp.concatenate(total, axis=1).astype(BF)
    spread[...] = jnp.broadcast_to(total[None], spread.shape)


def write_half(terms, side, refs, stages, semaphores, scaling):
    projection, output, pool = refs
    tall, square = stages
    wide = pool.shape[0]
    part, width = wide // 2, wide // 4
    across = 3 * part // 2
    copies = []

    def lanes(start, count):
        values = terms[:, :, start : start + count].astype(F32) * scaling
        return values.reshape(terms.shape[0] * terms.shape[1], count)

    def send(stage, target):
        copies.append(pltpu.make_async_copy(stage, target, semaphores.at[len(copies)]))
        copies[-1].start()

    for heads in range(2):
        start = 2 * width + heads * (across + 2 * width)
        for k in range(3):
            columns = [half * across + k * width for half in range(2)]
            places = [column // part * wide + heads * part + column % part for column in columns]
            target = pl.multiple_of(jnp.where(side == 0, places[0], places[1]), width)
            stage = tall.at[3 * heads + k]
            stage[...] = lanes(start + k * width, width)
            send(stage, projection.at[:, pl.ds(target, width)])
        for at, ref in enumerate((output, pool)):
            block = lanes(start + across + at * width, width)
            stage = square.at[2 * heads + at]
            stage[:, :width] = block[:part]
            stage[:, width:] = block[part:]
            target = pl.multiple_of(side * part, part)
            send(stage, ref.at[heads * part : (heads + 1) * part, pl.ds(target, part)])
    return copies


def own_sums_kernel(own, projection, output, pool, tall, square, semaphores, *, scaling):
    side = lax.axis_index("grp")
    refs = (projection, output, pool)
    for copy in write_half(own, side, refs, (tall, square), semaphores, scaling):
        copy.wait()


def other_sums_kernel(
    own,
    other,
    projection_in,
    output_in,
    pool_in,
    projection,
    output,
    pool,
    fine_projection,
    fine_output,
    tall,
    square,
    semaphores,
    fine,
    fine_square,
    fine_semaphores,
    *,
    scaling,
):
    side = 1 - lax.axis_index("grp")
    refs = (projection, output, pool)
    copies = write_half(other, side, refs, (tall, square), semaphores, scaling)
    features = fine_output.shape[0]
    width = features // 2
    for heads in range(2):
        start = heads * width
        here, there = own[:, :, start : start + width], other[:, :, start : start + width]
        for half in range(2):
            values = jnp.where(side == half, there, here).astype(F32) * scaling
            block = values.reshape(own.shape[0] * own.shape[1], width)
            column = (2 * heads + half) * features
            for k in range(2):
                piece = block[k * features : (k + 1) * features]
                if column < 3 * features:
                    fine[:, column + k * width : column + (k + 1) * width] = piece
                else:
                    fine_square[:, k * width : (k + 1) * width] = piece
    copies.append(pltpu.make_async_copy(fine, fine_projection, fine_semaphores.at[0]))
    copies.append(pltpu.make_async_copy(fine_square, fine_output, fine_semaphores.at[1]))
    for copy in copies[-2:]:
        copy.start()
    for copy in copies:
        copy.wait()


def write_sums(own, other, features, wide, scaling):
    part, width = wide // 2, wide // 4
    shapes = [(wide, 3 * wide), (wide, wide), (wide, wide)]
    stages = [
        pltpu.VMEM((6, wide, width), F32),
        pltpu.VMEM((4, part, part), F32),
        pltpu.SemaphoreType.DMA((10,)),
    ]
    limits = pltpu.CompilerParams(vmem_limit_bytes=16 * 1024 * 1024)
    firsts = pl.pallas_call(
        functools.partial(own_sums_kernel, scaling=scaling),
        out_shape=[pltpu.HBM(shape, F32) for shape in shapes],
        in_specs=[VMEM],
        out_specs=[HBM] * 3,
        scratch_shapes=stages,
        compiler_params=limits,
    )(own)
    shapes += [(features, 3 * features), (features, features)]
    projection, output, pool, fine_projection, fine_output = pl.pallas_call(
        functools.partial(other_sums_kernel, scaling=scaling),
        out_shape=[pltpu.HBM(shape, F32) for shape in shapes],
        in_specs=[VMEM] * 2 + [HBM] * 3,
        out_specs=[HBM] * 5,
        scratch_shapes=stages
        + [
            pltpu.VMEM((features, 3 * features), F32),
            pltpu.VMEM((features, features), F32),
            pltpu.SemaphoreType.DMA((2,)),
        ],
        input_output_aliases={2: 0, 3: 1, 4: 2},
        compiler_params=limits,
    )(own, other, *firsts)
    return fine_projection, fine_output, pool, projection, output


def fine_backward_kernel(
    arrived,
    receive_slot,
    rotated,
    projected,
    mixture,
    weights,
    projection,
    output,
    tokens,
    kept,
    passed,
    grad_projected,
):
    place = one_hot(receive_slot[...], arrived.shape[0])
    gradient_rows = mm(place, arrived[...], (0, 0)).astype(BF)
    features = rotated.shape[1]
    entering = mm(gradient_rows, output[...], (1, 1)).astype(BF)
    terms = [mm(mixture[...], gradient_rows, (0, 0))]
    balls = rotated.shape[0] // BALL
    heads = features // HD
    query_turned, entering_turned = turned(projected[:, :features]), turned(entering)
    turned_parts = ([], [])
    for ball in range(balls):
        rows = slice(ball * BALL, (ball + 1) * BALL)
        key, value = projected[rows, features : 2 * features], projected[rows, 2 * features :]
        head_weights = [weights[ball * heads + at] for at in range(heads)]
        against = mm(stack_heads(entering[rows], heads), value, (1, 1))
        slopes = slopes_of(jnp.concatenate(head_weights, axis=0), against)
        query_part = unstack_heads(mm(slopes, key), heads) * HD ** (-0.5)
        grad_projected[rows, :features] = query_part.astype(BF)
        pieces = ([], [])
        for at in range(heads):
            band = slice(at * HD, (at + 1) * HD)
            own = slopes[at * BALL : (at + 1) * BALL]
            pieces[0].append(mm(query_turned[band, rows], own) * HD ** (-0.5))
            pieces[1].append(mm(entering_turned[band, rows], head_weights[at]))
        for at in range(2):
            turned_parts[at].append(jnp.concatenate(pieces[at], axis=0))
    for at in range(2):
        whole = jnp.concatenate(turned_parts[at], axis=1).T.astype(BF)
        grad_projected[:, (at + 1) * features : (at + 2) * features] = whole
    normed, inverse = normalize(rotated[...])
    unit_rows = normed.astype(BF)
    for at in range(3):
        columns = slice(at * features, (at + 1) * features)
        terms.insert(at, mm(unit_rows, grad_projected[:, columns], (0, 0)))
    low = jnp.concatenate(terms[:2], axis=1)
    high = jnp.concatenate(terms[2:], axis=1)
    upper = lax.axis_index("grp") == 1
    kept[...] = jnp.where(upper, high, low)
    passed[...] = jnp.where(upper, low, high).astype(BF)
    back = mm(grad_projected[...], projection[...], (1, 1))
    result = gradient_rows.astype(F32) + norm_backward(back, normed, inverse)
    tokens[...] = mm(place, result.astype(BF)).reshape(tokens.shape).astype(BF)


def pool_kernel(
    own_pack, other_pack, own_gradient, other_gradient, coarse, keep, output, blocks, result
):
    wide = coarse.shape[1]
    part = wide // 2
    core = lax.axis_index("grp")
    first = pl.multiple_of(core * part, part)
    second = pl.multiple_of((1 - core) * part, part)
    mixed = mm(keep[:, :part], output[pl.ds(first, part), :])
    mixed = mixed + mm(other_gradient[:, wide:], output[pl.ds(second, part), :])
    result[...] = (coarse[...].astype(F32) + mixed).astype(BF)
    result.flush()
    term = mm(own_pack[:, pl.ds(first, part)], own_gradient[:, :wide], (0, 0))
    term = term + mm(other_pack[:, pl.ds(first, part)], other_gradient[:, :wide], (0, 0))
    put_quarters(blocks, 0, term)


def coarse_part_kernel(kept, got_first, got_second, pool, coarse):
    width = got_first.shape[3]
    for at, got in enumerate((got_first, got_second)):
        lanes = slice(at * width, (at + 1) * width)
        mine = kept[:, :, :, lanes].astype(F32)
        coarse[:, :, :, lanes] = (mine + got[...].astype(F32)).astype(BF)
    coarse[:, :, :, 2 * width :] = pool[...]


def assemble_kernel(tokens, fine_kept, fine_got, coarse, send):
    start = tokens.shape[3]
    send[:, :, :, :start] = tokens[...]
    put_quarters(send, start, fine_kept[...] + fine_got[...].astype(F32))
    send[:, :, :, send.shape[3] - coarse.shape[3] :] = coarse[...]


def take_kernel(arrived, slots, rows_out):
    place = one_hot(slots[...], slots.shape[1] * 2)
    rows = arrived[...].reshape(place.shape[0], arrived.shape[-1])
    rows_out[...] = mm(place, rows, (0, 0)).astype(BF)


VMEM = pl.BlockSpec(memory_space=pltpu.VMEM)
HBM = pl.BlockSpec(memory_space=pltpu.HBM)


class Far(NamedTuple):
    value: jax.Array


class Near(NamedTuple):
    shape: tuple
    dtype: jnp.dtype = BF
    far: bool = False


class Fetched:
    def __init__(self, source, buffer, semaphore):
        self.buffer, self.shape, self.waited = buffer, buffer.shape, False
        self.copy = pltpu.make_async_copy(source, buffer, semaphore)
        self.copy.start()

    def wait(self):
        if not self.waited:
            self.copy.wait()
            self.waited = True

    def __getitem__(self, index):
        self.wait()
        return self.buffer[index]


class Stored:
    def __init__(self, target, buffer, semaphore):
        self.buffer, self.shape, self.dtype, self.started = buffer, buffer.shape, buffer.dtype, False
        self.copy = pltpu.make_async_copy(buffer, target, semaphore)

    def __setitem__(self, index, values):
        self.buffer[index] = values

    def __getitem__(self, index):
        return self.buffer[index]

    def flush(self):
        if not self.started:
            self.copy.start()
            self.started = True


def call(kernel, inputs, outputs, scratch=(), mebibytes=16):
    in_specs, arrays, buffers = [], [], []
    for value in inputs:
        far = isinstance(value, Far)
        in_specs.append(HBM if far else VMEM)
        arrays.append(
            pltpu.with_memory_space_constraint(value.value, pltpu.HBM) if far else value
        )
        if far:
            buffers.append(pltpu.VMEM(value.value.shape, value.value.dtype))
    buffers.extend(pltpu.VMEM(out.shape, out.dtype) for out in outputs if out.far)
    flags = [isinstance(value, Far) for value in inputs] + [out.far for out in outputs]
    sizes = len(inputs), len(flags), len(flags) + len(buffers)

    def body(*refs):
        semaphores = refs[sizes[2]] if buffers else None
        given, views = 0, []
        for at, far in enumerate(flags):
            if far:
                kind = Fetched if at < sizes[0] else Stored
                views.append(kind(refs[at], refs[sizes[1] + given], semaphores.at[given]))
                given += 1
            else:
                views.append(refs[at])
        kernel(*views, *refs[sizes[2] + (1 if buffers else 0) :])
        for view in views:
            if isinstance(view, Stored):
                view.flush()
        for view in views:
            if isinstance(view, Fetched):
                view.wait()
            if isinstance(view, Stored):
                view.copy.wait()

    own = [pltpu.SemaphoreType.DMA((len(buffers),))] if buffers else []
    return pl.pallas_call(
        body,
        out_shape=[
            (pltpu.HBM if out.far else jax.ShapeDtypeStruct)(out.shape, out.dtype)
            for out in outputs
        ],
        in_specs=in_specs,
        out_specs=[HBM if out.far else VMEM for out in outputs],
        scratch_shapes=buffers + own + list(scratch),
        compiler_params=pltpu.CompilerParams(vmem_limit_bytes=mebibytes * 1024 * 1024),
    )(*arrays)


def exchange(values):
    return lax.ppermute(values, "grp", [(0, 1), (1, 0)])


def spread_blocks(values, axes):
    return lax.all_to_all(values, axes, split_axis=0, concat_axis=0, tiled=True)


def neighbours(owners, stride):
    pairs = []
    for chip in range(owners):
        place = chip // stride % 4
        for core in range(2):
            partner = ((place + core ^ 1) - core) % 4
            pairs.append((2 * chip + core, 2 * (chip + (partner - place) * stride) + core))
    return pairs


def route(values, devices):
    rows, features = values.shape
    blocks = values.reshape(devices, rows // devices, features)
    return spread_blocks(blocks, ("pts", "grp")).reshape(rows, features)


def on_device(
    points,
    rotated_place,
    rotated_source,
    ball_counts,
    fine_projection,
    fine_output,
    pool_weight,
    coarse_projection,
    coarse_output,
    coarse_cotangent,
):
    count, features = points.shape
    devices = lax.axis_size(("pts", "grp"))
    slots = 2 * count
    scaling = 1.0 / math.sqrt(count * devices)
    owners = lax.axis_size("pts")
    run, step = owners // 4, owners // 16
    wide = 2 * features
    half_rows = count // 2

    send, send_slot, pair_slot, receive_slot, live = call(
        route_kernel,
        (
            Far(rotated_place.reshape(1, count)),
            Far(rotated_source.reshape(1, count)),
            Far(ball_counts.reshape(1, -1)),
            Far(points),
        ),
        (
            Near((slots, features)),
            Near((1, count), jnp.int32),
            Near((1, count), jnp.int32),
            Near((1, count), jnp.int32),
            Near((1, count), F32),
        ),
    )
    arrived = route(send, devices)
    heads = features // HD * (count // BALL)
    send, rotated, projected, mixture, weights = call(
        fine_forward_kernel,
        (arrived, receive_slot, live, fine_projection, Far(fine_output)),
        (
            Near((slots, features)),
            Near((count, features)),
            Near((count, 3 * features)),
            Near((count, features)),
            Near((heads, BALL, BALL)),
        ),
    )
    arrived = route(send, devices)
    (own_pack,) = call(
        join_kernel, (arrived, pair_slot, coarse_cotangent), (Near((half_rows, 2 * wide)),)
    )
    other_pack = exchange(own_pack)
    coarse, own_unit, own_rows = call(
        coarse_own_rows_kernel,
        (own_pack, pool_weight, coarse_projection, Far(coarse_output)),
        (
            Near((half_rows, wide)),
            Near((half_rows, wide)),
            Near((half_rows, 2 * wide)),
        ),
    )
    keep, give, give_mixed, other_unit = call(
        coarse_kernel,
        (other_pack, own_rows, pool_weight, coarse_projection, coarse_output),
        (
            Near((half_rows, 2 * wide)),
            Near((half_rows, 3 * wide // 2)),
            Near((half_rows, wide // 2)),
            Near((half_rows, wide)),
        ),
    )
    got = exchange(give)
    blocks = (owners, 2, slots // devices)
    kept, first_half, second_half = call(
        functools.partial(coarse_weights_kernel, strides=(run, step)),
        (own_unit, other_unit, keep, give, give_mixed, own_pack, other_pack),
        (
            Near((*blocks, wide // 2)),
            Near((*blocks, wide // 4)),
            Near((*blocks, wide // 4)),
        ),
    )
    (back,) = call(coarse_own_kernel, (keep, coarse_projection), (Near((half_rows, wide), F32),))
    got, kept, first_half, second_half = lax.optimization_barrier(
        (got, kept, first_half, second_half)
    )
    coarse_gradient, send = call(
        coarse_finish_kernel,
        (
            coarse,
            back,
            got,
            coarse_cotangent,
            pool_weight,
            coarse_projection,
            pair_slot,
            give_mixed,
        ),
        (Near((half_rows, 3 * wide // 2)), Near((slots, features))),
    )
    arrived = route(send, devices)
    arrived, first_half, second_half, coarse_gradient = lax.optimization_barrier(
        (arrived, first_half, second_half, coarse_gradient)
    )
    got_first = lax.ppermute(first_half, ("pts", "grp"), neighbours(owners, run))
    got_second = lax.ppermute(second_half, ("pts", "grp"), neighbours(owners, step))
    other_gradient = exchange(coarse_gradient)
    tokens, fine_kept, fine_passed = call(
        fine_backward_kernel,
        (
            arrived,
            receive_slot,
            rotated,
            projected,
            mixture,
            weights,
            fine_projection,
            fine_output,
        ),
        (
            Near((*blocks, features)),
            Near((features, 2 * features), F32),
            Near((features, 2 * features)),
        ),
        scratch=(pltpu.VMEM((count, 3 * features), BF),),
    )
    fine_got = exchange(fine_passed)
    pool_part, coarse_result = call(
        pool_kernel,
        (
            own_pack,
            other_pack,
            coarse_gradient,
            other_gradient,
            coarse,
            keep,
            coarse_output,
        ),
        (Near((*blocks, wide // 4)), Near((half_rows, wide), far=True)),
    )
    (coarse_part,) = call(
        coarse_part_kernel,
        (kept, got_first, got_second, pool_part),
        (Near((*blocks, 3 * wide // 4)),),
    )
    across = features + wide
    (send,) = call(
        assemble_kernel,
        (tokens, fine_kept, fine_got, coarse_part),
        (Near((*blocks, across)),),
    )
    arrived = spread_blocks(send.reshape(devices, slots // devices, across), ("pts", "grp"))
    (spread,) = call(
        functools.partial(sum_kernel, tokens=features, run=run, step=step),
        (arrived.reshape(send.shape),),
        (Near((owners, slots // devices, features + 5 * wide // 2)),),
    )
    own_sums = spread_blocks(spread, "pts")
    (points_gradient,) = call(
        take_kernel, (arrived[:, :, :features], send_slot), (Near((count, features)),)
    )
    other_sums = exchange(own_sums)
    sums = write_sums(own_sums, other_sums, features, wide, scaling)
    return (coarse_result, points_gradient, *sums)


def solution(mesh):
    tokens = P(("pts", "grp"), None)
    in_specs = (
        tokens,
        P(("pts", "grp")),
        P(("pts", "grp")),
        P(),
        P(),
        P(),
        P(),
        P(),
        P(),
        tokens,
    )
    out_specs = (tokens, tokens, P(), P(), P(), P(), P())
    return jax.shard_map(
        on_device, mesh=mesh, in_specs=in_specs, out_specs=out_specs, check_vma=False
    )
```

```python
import functools
import math
from typing import NamedTuple

import jax
import jax.numpy as jnp
from jax import lax
from jax.experimental import pallas as pl
from jax.experimental.pallas import tpu as pltpu
from jax.sharding import PartitionSpec as P

HD = 64
BALL = 256
PAIR = 2 * HD
EPSILON = 1e-05
BF = jnp.bfloat16
F32 = jnp.float32


def mm(a, b, contract=(1, 0)):
    return lax.dot_general(
        a, b, (((contract[0],), (contract[1],)), ((), ())), preferred_element_type=F32
    )


def normalize(values):
    floats = values.astype(F32)
    center = floats - jnp.mean(floats, axis=-1, keepdims=True)
    inverse = lax.rsqrt(jnp.mean(center * center, axis=-1, keepdims=True) + EPSILON)
    return center * inverse, inverse


def norm_backward(incoming, normed, inverse):
    first_mean = jnp.mean(incoming, axis=-1, keepdims=True)
    second_mean = jnp.mean(incoming * normed, axis=-1, keepdims=True)
    return inverse * (incoming - first_mean - normed * second_mean)


def one_hot(slots, total):
    shape = (total, slots.shape[1])
    return (lax.broadcasted_iota(jnp.int32, shape, 0) == slots).astype(BF)


def softmax_rows(scores):
    raised = jnp.exp(scores - jnp.max(scores, axis=-1, keepdims=True))
    return (raised * (1.0 / jnp.sum(raised, axis=-1, keepdims=True))).astype(BF)


def slopes_of(weights, against):
    wide = weights.astype(F32)
    diagonal = jnp.sum(wide * against, axis=-1, keepdims=True)
    return (wide * (against - diagonal)).astype(BF)


def stack_heads(rows, heads):
    lanes = lax.broadcasted_iota(jnp.int32, rows.shape, 1) // HD
    none = jnp.zeros_like(rows)
    return jnp.concatenate([jnp.where(lanes == at, rows, none) for at in range(heads)], axis=0)


def unstack_heads(rows, heads):
    count = rows.shape[0] // heads
    merged = rows[:count]
    lanes = lax.broadcasted_iota(jnp.int32, merged.shape, 1) // HD
    for at in range(1, heads):
        merged = jnp.where(lanes == at, rows[at * count : (at + 1) * count], merged)
    return merged


def turned(rows):
    return rows.astype(F32).T.astype(BF)


def column_of(row):
    count = row.shape[1]
    turned = jnp.broadcast_to(row.astype(F32), (128, count)).T
    return jnp.concatenate([turned] * (count // 128), axis=1)


def route_kernel(
    place, source, counts, points, send, send_slot, pair_slot, receive_slot, live
):
    count = place.shape[1]
    shift = count.bit_length() - 1
    capacity = send.shape[0] * count // (counts.shape[1] * BALL)
    to_row = place[...] >> shift
    rows = lax.broadcasted_iota(jnp.int32, (count, count), 0)
    columns = lax.broadcasted_iota(jnp.int32, (count, count), 1)
    earlier = (column_of(to_row) == to_row.astype(F32)) & (rows < columns)
    rank = jnp.sum(jnp.where(earlier, 1.0, 0.0), axis=0, keepdims=True)
    slot = to_row * capacity + rank.astype(jnp.int32)
    send_slot[...] = slot
    even_first = jnp.where(columns < count // 2, 2 * columns, 2 * columns + 1 - count)
    digits = jnp.concatenate([slot >> 5, slot & 31] + [jnp.zeros_like(slot)] * 6, axis=0)
    moved = mm(digits.astype(F32).astype(BF), (rows == even_first).astype(BF)).astype(jnp.int32)
    pair_slot[...] = moved[0:1] * 32 + moved[1:2]
    source_row = source[...]
    from_row = source_row >> shift
    earlier = (column_of(from_row) == from_row.astype(F32)) & (
        column_of(source_row) < source_row.astype(F32)
    )
    rank = jnp.sum(jnp.where(earlier, 1.0, 0.0), axis=0, keepdims=True)
    receive_slot[...] = from_row * capacity + rank.astype(jnp.int32)
    balls = counts.shape[1]
    own_ball = one_hot(source_row >> (BALL.bit_length() - 1), balls)
    filled = mm(jnp.broadcast_to(counts[...].astype(F32), (8, balls)).astype(BF), own_ball)
    inside = (source_row & (BALL - 1)).astype(F32)
    live[...] = jnp.where(inside < filled[:1], 1.0, 0.0)
    send[...] = mm(one_hot(slot, send.shape[0]), points[...]).astype(BF)


def fine_forward_kernel(
    arrived, receive_slot, live, projection, output, send, rotated, projected, mixture, weights
):
    place = one_hot(receive_slot[...], arrived.shape[0])
    rows_in = mm(place, arrived[...], (0, 0))
    rotated[...] = rows_in.astype(BF)
    features = rows_in.shape[1]
    normed, _ = normalize(rows_in)
    projected[...] = mm(normed.astype(BF), projection[...]).astype(BF)
    balls = rows_in.shape[0] // BALL
    for ball in range(balls):
        rows = slice(ball * BALL, (ball + 1) * BALL)
        alive = live[:, rows] > 0.5
        for pair in range(features // PAIR):
            lanes = slice(pair * PAIR, (pair + 1) * PAIR)
            query = projected[rows, lanes] * jnp.asarray(HD ** (-0.5), BF)
            key = projected[rows, features + pair * PAIR : features + (pair + 1) * PAIR]
            value = projected[rows, 2 * features + pair * PAIR : 2 * features + (pair + 1) * PAIR]
            scores = mm(stack_heads(query, 2), key, (1, 1))
            both = softmax_rows(jnp.where(alive, scores, -1e30))
            first = (ball * features + pair * PAIR) // HD
            weights[first : first + 2] = both.reshape(2, BALL, BALL)
            mixture[rows, lanes] = unstack_heads(mm(both, value), 2).astype(BF)
    result = (rows_in + mm(mixture[...], output[...])).astype(BF)
    send[...] = mm(place, result).astype(BF)


def join_kernel(arrived, pair_slot, cotangent, pack):
    half_rows, wide = cotangent.shape
    place = one_hot(pair_slot[...], arrived.shape[0])
    rows = mm(place, arrived[...], (0, 0)).astype(BF)
    pack[:, : wide // 2] = rows[:half_rows]
    pack[:, wide // 2 : wide] = rows[half_rows:]
    pack[:, wide:] = cotangent[...]


def project_rows(joined, cotangent, pool, projection, output):
    wide = pool.shape[1]
    part = wide // 2
    first = pl.multiple_of(lax.axis_index("grp") * part, part)
    tokens = mm(joined, pool[...]).astype(BF)
    normed, _ = normalize(tokens)
    unit = normed.astype(BF)
    rows = [
        mm(unit, projection[:, pl.ds(at * wide + first, part)]).astype(BF) for at in range(3)
    ]
    rows.append(mm(cotangent, output[pl.ds(first, part), :], (1, 1)).astype(BF))
    return tokens, unit, rows


def coarse_own_rows_kernel(own_pack, pool, projection, output, coarse, unit, rows_out):
    wide = pool.shape[1]
    tokens, unit_rows, rows = project_rows(
        own_pack[:, :wide], own_pack[:, wide:], pool, projection, output
    )
    coarse[...] = tokens
    unit[...] = unit_rows
    for at, values in enumerate(rows):
        rows_out[:, at * wide // 2 : (at + 1) * wide // 2] = values


def coarse_kernel(
    other_pack, own_rows, pool, projection, output, keep, give, give_mixed, unit
):
    wide = pool.shape[1]
    part = wide // 2
    half_rows = own_rows.shape[0]
    _, unit_rows, rows = project_rows(
        other_pack[:, :wide], other_pack[:, wide:], pool, projection, output
    )
    unit[...] = unit_rows
    queries, keys, values, incoming = [
        jnp.concatenate([own_rows[:, at * part : (at + 1) * part], rows[at]], axis=0)
        for at in range(4)
    ]
    queries_turned, incoming_turned = turned(queries), turned(incoming)
    key_parts, value_parts = [], []

    def put(at, rows):
        target = slice(at, at + rows.shape[1])
        keep[:, target] = rows[:half_rows]
        if at < part:
            give_mixed[:, target] = rows[half_rows:]
        else:
            give[:, at - part : at - part + rows.shape[1]] = rows[half_rows:]

    for pair in range(part // PAIR):
        lanes = slice(pair * PAIR, (pair + 1) * PAIR)
        key, value = keys[:, lanes], values[:, lanes]
        query = queries[:, lanes] * jnp.asarray(HD ** (-0.5), BF)
        head_weights = softmax_rows(mm(stack_heads(query, 2), key, (1, 1)))
        against = mm(stack_heads(incoming[:, lanes], 2), value, (1, 1))
        slopes = slopes_of(head_weights, against)
        put(pair * PAIR, unstack_heads(mm(head_weights, value), 2).astype(BF))
        query_part = unstack_heads(mm(slopes, key), 2) * HD ** (-0.5)
        put(part + pair * PAIR, query_part.astype(BF))
        for half in range(2):
            band = slice(pair * PAIR + half * HD, pair * PAIR + (half + 1) * HD)
            rows = slice(half * 2 * half_rows, (half + 1) * 2 * half_rows)
            key_parts.append(mm(queries_turned[band], slopes[rows]) * HD ** (-0.5))
            value_parts.append(mm(incoming_turned[band], head_weights[rows]))
    put(2 * part, jnp.concatenate(key_parts, axis=0).T.astype(BF))
    put(3 * part, jnp.concatenate(value_parts, axis=0).T.astype(BF))


def heads_back(grads, start, index, projection):
    wide = projection.shape[0]
    part = wide // 2
    first = pl.multiple_of(index * part, part)
    back = jnp.zeros((grads.shape[0], wide), F32)
    for at in range(3):
        back = back + mm(
            grads[:, start + at * part : start + (at + 1) * part],
            projection[:, pl.ds(at * wide + first, part)],
            (1, 1),
        )
    return back


def coarse_own_kernel(keep, projection, back):
    part = projection.shape[0] // 2
    back[...] = heads_back(keep, part, lax.axis_index("grp"), projection)


def coarse_finish_kernel(
    coarse, back, got, cotangent, pool, projection, pair_slot, give_mixed, pack, send
):
    other_back = heads_back(got, 0, 1 - lax.axis_index("grp"), projection)
    normed, inverse = normalize(coarse[...])
    gradient_rows = (
        cotangent[...].astype(F32) + norm_backward(back[...] + other_back, normed, inverse)
    ).astype(BF)
    wide = pool.shape[1]
    pack[:, :wide] = gradient_rows
    pack[:, wide:] = give_mixed[...]
    fine = mm(gradient_rows, pool[...], (1, 1)).astype(BF)
    features = send.shape[1]
    stacked = jnp.concatenate([fine[:, :features], fine[:, features:]], axis=0)
    send[...] = mm(one_hot(pair_slot[...], send.shape[0]), stacked).astype(BF)


def coarse_weights_kernel(
    own_unit,
    other_unit,
    keep,
    give,
    give_mixed,
    own_pack,
    other_pack,
    kept,
    first_half,
    second_half,
    *,
    strides,
):
    chip, core = lax.axis_index("pts"), lax.axis_index("grp")
    wide = own_unit.shape[1]
    part = wide // 2
    unit = jnp.concatenate([own_unit[...], other_unit[...]], axis=0)
    given = jnp.concatenate([give_mixed[...], give[...]], axis=1)
    stacked = jnp.concatenate([keep[...], given], axis=0)
    cotangent = jnp.concatenate([own_pack[:, wide:], other_pack[:, wide:]], axis=0)
    projection_term = mm(unit, stacked[:, part:], (0, 0))
    output_term = mm(stacked[:, :part], cotangent, (0, 0))
    across = projection_term.shape[1] // 2
    width = wide // 4
    for side in range(2):
        stack = [output_term[:, (2 * side + k) * width : (2 * side + k + 1) * width] for k in range(2)]
        columns = projection_term[:, side * across : (side + 1) * across]
        terms = jnp.concatenate([columns, jnp.concatenate(stack, axis=0)], axis=1)
        for at, passed in enumerate((first_half, second_half)):
            low = terms[:, 2 * at * width : (2 * at + 1) * width]
            high = terms[:, (2 * at + 1) * width : (2 * at + 2) * width]
            upper = (chip // strides[at] + core) % 2 == 1
            put_blocks(kept, side, at * width, jnp.where(upper, high, low))
            put_blocks(passed, side, 0, jnp.where(upper, low, high))


def put_quarters(blocks, lane, term):
    width = term.shape[1] // 4
    for side in range(2):
        stack = [term[:, (2 * side + k) * width : (2 * side + k + 1) * width] for k in range(2)]
        put_blocks(blocks, side, lane, jnp.concatenate(stack, axis=0))


def put_blocks(blocks, side, lane, rows):
    owners, width = blocks.shape[0], rows.shape[1]
    pieces = rows.reshape(owners, rows.shape[0] // owners, width)
    blocks[:, side, :, lane : lane + width] = pieces.astype(BF)


def sum_kernel(arrived, spread, *, tokens, run, step):
    senders, _, rows, across = arrived.shape
    width = (across - tokens) // 4

    def pieces(side, at):
        start = tokens + at * width
        return arrived[:, side, :, start : start + width].astype(F32)

    total = [jnp.sum(pieces(side, 0), axis=0) for side in range(2)]
    for side in range(2):
        for at, block in enumerate((run, step)):
            split = pieces(side, 1 + at).reshape(senders // (2 * block), 2, block, rows, width)
            halves = jnp.sum(jnp.sum(split, axis=2), axis=0)
            total.extend([halves[side], halves[1 - side]])
        total.append(jnp.sum(pieces(side, 3), axis=0))
    total = jnp.concatenate(total, axis=1).astype(BF)
    spread[...] = jnp.broadcast_to(total[None], spread.shape)


def write_half(terms, side, refs, stages, semaphores, scaling):
    projection, output, pool, fine_projection, fine_output = refs
    tall, square = stages
    wide = pool.shape[0]
    part, width = wide // 2, wide // 4
    across = 3 * part // 2
    copies = []

    def lanes(start, count):
        values = terms[:, :, start : start + count].astype(F32) * scaling
        return values.reshape(terms.shape[0] * terms.shape[1], count)

    def prepare(stage, target):
        copies.append(pltpu.make_async_copy(stage, target, semaphores.at[len(copies)]))
        return copies[-1]

    def fill(stage, start):
        block = lanes(start, width)
        stage[:, :width] = block[:part]
        stage[:, width:] = block[part:]

    place = pl.multiple_of(side * part, part)
    for heads in range(2):
        start = 2 * width + heads * (across + 2 * width)
        for k in range(3):
            columns = [half * across + k * width for half in range(2)]
            places = [column // part * wide + heads * part + column % part for column in columns]
            target = pl.multiple_of(jnp.where(side == 0, places[0], places[1]), width)
            stage = tall.at[3 * heads + k]
            stage[...] = lanes(start + k * width, width)
            prepare(stage, projection.at[:, pl.ds(target, width)]).start()
        for at, ref in enumerate((output, pool)):
            stage = square.at[2 * heads + at]
            fill(stage, start + across + at * width)
            target = ref.at[heads * part : (heads + 1) * part, pl.ds(place, part)]
            prepare(stage, target).start()
    fill(square.at[4], 0)
    prepare(square.at[4], fine_projection.at[:, pl.ds(place, part)]).start()
    fill(square.at[5], width)
    last = semaphores.at[len(copies)]
    to_projection = pltpu.make_async_copy(
        square.at[5], fine_projection.at[:, 2 * part : 3 * part], last
    )
    to_output = pltpu.make_async_copy(square.at[5], fine_output, last)

    @pl.when(side == 0)
    def _():
        to_projection.start()
        to_projection.wait()

    @pl.when(side != 0)
    def _():
        to_output.start()
        to_output.wait()

    for copy in copies:
        copy.wait()


def own_sums_kernel(terms, *refs, scaling):
    write_half(terms, lax.axis_index("grp"), refs[:5], refs[5:7], refs[7], scaling)


def other_sums_kernel(terms, *refs, scaling):
    write_half(terms, 1 - lax.axis_index("grp"), refs[5:10], refs[10:12], refs[12], scaling)


def write_sums(own, other, features, wide, scaling):
    part, width = wide // 2, wide // 4
    shapes = [(wide, 3 * wide), (wide, wide), (wide, wide)]
    shapes += [(features, 3 * features), (features, features)]
    stages = [
        pltpu.VMEM((6, wide, width), F32),
        pltpu.VMEM((6, part, part), F32),
        pltpu.SemaphoreType.DMA((12,)),
    ]
    limits = pltpu.CompilerParams(vmem_limit_bytes=16 * 1024 * 1024)
    outputs = [pltpu.HBM(shape, F32) for shape in shapes]
    firsts = pl.pallas_call(
        functools.partial(own_sums_kernel, scaling=scaling),
        out_shape=outputs,
        in_specs=[VMEM],
        out_specs=[HBM] * 5,
        scratch_shapes=stages,
        compiler_params=limits,
    )(own)
    projection, output, pool, fine_projection, fine_output = pl.pallas_call(
        functools.partial(other_sums_kernel, scaling=scaling),
        out_shape=outputs,
        in_specs=[VMEM] + [HBM] * 5,
        out_specs=[HBM] * 5,
        scratch_shapes=stages,
        input_output_aliases={at + 1: at for at in range(5)},
        compiler_params=limits,
    )(other, *firsts)
    return fine_projection, fine_output, pool, projection, output


def fine_backward_kernel(
    arrived,
    receive_slot,
    rotated,
    projected,
    mixture,
    weights,
    projection,
    output,
    tokens,
    kept,
    passed,
    grad_projected,
):
    place = one_hot(receive_slot[...], arrived.shape[0])
    gradient_rows = mm(place, arrived[...], (0, 0)).astype(BF)
    features = rotated.shape[1]
    entering = mm(gradient_rows, output[...], (1, 1)).astype(BF)
    terms = [mm(mixture[...], gradient_rows, (0, 0))]
    balls = rotated.shape[0] // BALL
    heads = features // HD
    query_turned, entering_turned = turned(projected[:, :features]), turned(entering)
    turned_parts = ([], [])
    for ball in range(balls):
        rows = slice(ball * BALL, (ball + 1) * BALL)
        key, value = projected[rows, features : 2 * features], projected[rows, 2 * features :]
        head_weights = [weights[ball * heads + at] for at in range(heads)]
        against = mm(stack_heads(entering[rows], heads), value, (1, 1))
        slopes = slopes_of(jnp.concatenate(head_weights, axis=0), against)
        query_part = unstack_heads(mm(slopes, key), heads) * HD ** (-0.5)
        grad_projected[rows, :features] = query_part.astype(BF)
        pieces = ([], [])
        for at in range(heads):
            band = slice(at * HD, (at + 1) * HD)
            own = slopes[at * BALL : (at + 1) * BALL]
            pieces[0].append(mm(query_turned[band, rows], own) * HD ** (-0.5))
            pieces[1].append(mm(entering_turned[band, rows], head_weights[at]))
        for at in range(2):
            turned_parts[at].append(jnp.concatenate(pieces[at], axis=0))
    for at in range(2):
        whole = jnp.concatenate(turned_parts[at], axis=1).T.astype(BF)
        grad_projected[:, (at + 1) * features : (at + 2) * features] = whole
    normed, inverse = normalize(rotated[...])
    unit_rows = normed.astype(BF)
    for at in range(3):
        columns = slice(at * features, (at + 1) * features)
        terms.insert(at, mm(unit_rows, grad_projected[:, columns], (0, 0)))
    low = jnp.concatenate(terms[:2], axis=1)
    high = jnp.concatenate(terms[2:], axis=1)
    upper = lax.axis_index("grp") == 1
    kept[...] = jnp.where(upper, high, low)
    passed[...] = jnp.where(upper, low, high).astype(BF)
    back = mm(grad_projected[...], projection[...], (1, 1))
    result = gradient_rows.astype(F32) + norm_backward(back, normed, inverse)
    tokens[...] = mm(place, result.astype(BF)).reshape(tokens.shape).astype(BF)


def pool_kernel(
    own_pack, other_pack, own_gradient, other_gradient, coarse, keep, output, blocks, result
):
    wide = coarse.shape[1]
    part = wide // 2
    core = lax.axis_index("grp")
    first = pl.multiple_of(core * part, part)
    second = pl.multiple_of((1 - core) * part, part)
    mixed = mm(keep[:, :part], output[pl.ds(first, part), :])
    mixed = mixed + mm(other_gradient[:, wide:], output[pl.ds(second, part), :])
    result[...] = (coarse[...].astype(F32) + mixed).astype(BF)
    result.flush()
    term = mm(own_pack[:, pl.ds(first, part)], own_gradient[:, :wide], (0, 0))
    term = term + mm(other_pack[:, pl.ds(first, part)], other_gradient[:, :wide], (0, 0))
    put_quarters(blocks, 0, term)


def coarse_part_kernel(kept, got_first, got_second, pool, coarse):
    width = got_first.shape[3]
    for at, got in enumerate((got_first, got_second)):
        lanes = slice(at * width, (at + 1) * width)
        mine = kept[:, :, :, lanes].astype(F32)
        coarse[:, :, :, lanes] = (mine + got[...].astype(F32)).astype(BF)
    coarse[:, :, :, 2 * width :] = pool[...]


def assemble_kernel(tokens, fine_kept, fine_got, coarse, send):
    start = tokens.shape[3]
    send[:, :, :, :start] = tokens[...]
    put_quarters(send, start, fine_kept[...] + fine_got[...].astype(F32))
    send[:, :, :, send.shape[3] - coarse.shape[3] :] = coarse[...]


def take_kernel(arrived, slots, rows_out):
    place = one_hot(slots[...], slots.shape[1] * 2)
    rows = arrived[...].reshape(place.shape[0], arrived.shape[-1])
    rows_out[...] = mm(place, rows, (0, 0)).astype(BF)


VMEM = pl.BlockSpec(memory_space=pltpu.VMEM)
HBM = pl.BlockSpec(memory_space=pltpu.HBM)


class Far(NamedTuple):
    value: jax.Array


class Near(NamedTuple):
    shape: tuple
    dtype: jnp.dtype = BF
    far: bool = False


class Fetched:
    def __init__(self, source, buffer, semaphore):
        self.buffer, self.shape, self.waited = buffer, buffer.shape, False
        self.copy = pltpu.make_async_copy(source, buffer, semaphore)
        self.copy.start()

    def wait(self):
        if not self.waited:
            self.copy.wait()
            self.waited = True

    def __getitem__(self, index):
        self.wait()
        return self.buffer[index]


class Stored:
    def __init__(self, target, buffer, semaphore):
        self.buffer, self.shape, self.dtype, self.started = buffer, buffer.shape, buffer.dtype, False
        self.copy = pltpu.make_async_copy(buffer, target, semaphore)

    def __setitem__(self, index, values):
        self.buffer[index] = values

    def __getitem__(self, index):
        return self.buffer[index]

    def flush(self):
        if not self.started:
            self.copy.start()
            self.started = True


def call(kernel, inputs, outputs, scratch=(), mebibytes=16):
    in_specs, arrays, buffers = [], [], []
    for value in inputs:
        far = isinstance(value, Far)
        in_specs.append(HBM if far else VMEM)
        arrays.append(
            pltpu.with_memory_space_constraint(value.value, pltpu.HBM) if far else value
        )
        if far:
            buffers.append(pltpu.VMEM(value.value.shape, value.value.dtype))
    buffers.extend(pltpu.VMEM(out.shape, out.dtype) for out in outputs if out.far)
    flags = [isinstance(value, Far) for value in inputs] + [out.far for out in outputs]
    sizes = len(inputs), len(flags), len(flags) + len(buffers)

    def body(*refs):
        semaphores = refs[sizes[2]] if buffers else None
        given, views = 0, []
        for at, far in enumerate(flags):
            if far:
                kind = Fetched if at < sizes[0] else Stored
                views.append(kind(refs[at], refs[sizes[1] + given], semaphores.at[given]))
                given += 1
            else:
                views.append(refs[at])
        kernel(*views, *refs[sizes[2] + (1 if buffers else 0) :])
        for view in views:
            if isinstance(view, Stored):
                view.flush()
        for view in views:
            if isinstance(view, Fetched):
                view.wait()
            if isinstance(view, Stored):
                view.copy.wait()

    own = [pltpu.SemaphoreType.DMA((len(buffers),))] if buffers else []
    return pl.pallas_call(
        body,
        out_shape=[
            (pltpu.HBM if out.far else jax.ShapeDtypeStruct)(out.shape, out.dtype)
            for out in outputs
        ],
        in_specs=in_specs,
        out_specs=[HBM if out.far else VMEM for out in outputs],
        scratch_shapes=buffers + own + list(scratch),
        compiler_params=pltpu.CompilerParams(vmem_limit_bytes=mebibytes * 1024 * 1024),
    )(*arrays)


def exchange(values):
    return lax.ppermute(values, "grp", [(0, 1), (1, 0)])


def spread_blocks(values, axes):
    return lax.all_to_all(values, axes, split_axis=0, concat_axis=0, tiled=True)


def neighbours(owners, stride):
    pairs = []
    for chip in range(owners):
        place = chip // stride % 4
        for core in range(2):
            partner = ((place + core ^ 1) - core) % 4
            pairs.append((2 * chip + core, 2 * (chip + (partner - place) * stride) + core))
    return pairs


def route(values, devices):
    rows, features = values.shape
    blocks = values.reshape(devices, rows // devices, features)
    return spread_blocks(blocks, ("pts", "grp")).reshape(rows, features)


def on_device(
    points,
    rotated_place,
    rotated_source,
    ball_counts,
    fine_projection,
    fine_output,
    pool_weight,
    coarse_projection,
    coarse_output,
    coarse_cotangent,
):
    count, features = points.shape
    devices = lax.axis_size(("pts", "grp"))
    slots = 2 * count
    scaling = 1.0 / math.sqrt(count * devices)
    owners = lax.axis_size("pts")
    run, step = owners // 4, owners // 16
    wide = 2 * features
    half_rows = count // 2

    send, send_slot, pair_slot, receive_slot, live = call(
        route_kernel,
        (
            Far(rotated_place.reshape(1, count)),
            Far(rotated_source.reshape(1, count)),
            Far(ball_counts.reshape(1, -1)),
            Far(points),
        ),
        (
            Near((slots, features)),
            Near((1, count), jnp.int32),
            Near((1, count), jnp.int32),
            Near((1, count), jnp.int32),
            Near((1, count), F32),
        ),
    )
    arrived = route(send, devices)
    heads = features // HD * (count // BALL)
    send, rotated, projected, mixture, weights = call(
        fine_forward_kernel,
        (arrived, receive_slot, live, fine_projection, Far(fine_output)),
        (
            Near((slots, features)),
            Near((count, features)),
            Near((count, 3 * features)),
            Near((count, features)),
            Near((heads, BALL, BALL)),
        ),
    )
    arrived = route(send, devices)
    (own_pack,) = call(
        join_kernel, (arrived, pair_slot, coarse_cotangent), (Near((half_rows, 2 * wide)),)
    )
    other_pack = exchange(own_pack)
    coarse, own_unit, own_rows = call(
        coarse_own_rows_kernel,
        (own_pack, pool_weight, coarse_projection, Far(coarse_output)),
        (
            Near((half_rows, wide)),
            Near((half_rows, wide)),
            Near((half_rows, 2 * wide)),
        ),
    )
    keep, give, give_mixed, other_unit = call(
        coarse_kernel,
        (other_pack, own_rows, pool_weight, coarse_projection, coarse_output),
        (
            Near((half_rows, 2 * wide)),
            Near((half_rows, 3 * wide // 2)),
            Near((half_rows, wide // 2)),
            Near((half_rows, wide)),
        ),
    )
    got = exchange(give)
    blocks = (owners, 2, slots // devices)
    kept, first_half, second_half = call(
        functools.partial(coarse_weights_kernel, strides=(run, step)),
        (own_unit, other_unit, keep, give, give_mixed, own_pack, other_pack),
        (
            Near((*blocks, wide // 2)),
            Near((*blocks, wide // 4)),
            Near((*blocks, wide // 4)),
        ),
    )
    (back,) = call(coarse_own_kernel, (keep, coarse_projection), (Near((half_rows, wide), F32),))
    got, kept, first_half, second_half = lax.optimization_barrier(
        (got, kept, first_half, second_half)
    )
    coarse_gradient, send = call(
        coarse_finish_kernel,
        (
            coarse,
            back,
            got,
            coarse_cotangent,
            pool_weight,
            coarse_projection,
            pair_slot,
            give_mixed,
        ),
        (Near((half_rows, 3 * wide // 2)), Near((slots, features))),
    )
    arrived = route(send, devices)
    arrived, first_half, second_half, coarse_gradient = lax.optimization_barrier(
        (arrived, first_half, second_half, coarse_gradient)
    )
    got_first = lax.ppermute(first_half, ("pts", "grp"), neighbours(owners, run))
    got_second = lax.ppermute(second_half, ("pts", "grp"), neighbours(owners, step))
    other_gradient = exchange(coarse_gradient)
    tokens, fine_kept, fine_passed = call(
        fine_backward_kernel,
        (
            arrived,
            receive_slot,
            rotated,
            projected,
            mixture,
            weights,
            fine_projection,
            fine_output,
        ),
        (
            Near((*blocks, features)),
            Near((features, 2 * features), F32),
            Near((features, 2 * features)),
        ),
        scratch=(pltpu.VMEM((count, 3 * features), BF),),
    )
    fine_got = exchange(fine_passed)
    pool_part, coarse_result = call(
        pool_kernel,
        (
            own_pack,
            other_pack,
            coarse_gradient,
            other_gradient,
            coarse,
            keep,
            coarse_output,
        ),
        (Near((*blocks, wide // 4)), Near((half_rows, wide), far=True)),
    )
    (coarse_part,) = call(
        coarse_part_kernel,
        (kept, got_first, got_second, pool_part),
        (Near((*blocks, 3 * wide // 4)),),
    )
    across = features + wide
    (send,) = call(
        assemble_kernel,
        (tokens, fine_kept, fine_got, coarse_part),
        (Near((*blocks, across)),),
    )
    arrived = spread_blocks(send.reshape(devices, slots // devices, across), ("pts", "grp"))
    (spread,) = call(
        functools.partial(sum_kernel, tokens=features, run=run, step=step),
        (arrived.reshape(send.shape),),
        (Near((owners, slots // devices, features + 5 * wide // 2)),),
    )
    own_sums = spread_blocks(spread, "pts")
    (points_gradient,) = call(
        take_kernel, (arrived[:, :, :features], send_slot), (Near((count, features)),)
    )
    other_sums = exchange(own_sums)
    sums = write_sums(own_sums, other_sums, features, wide, scaling)
    return (coarse_result, points_gradient, *sums)


def solution(mesh):
    tokens = P(("pts", "grp"), None)
    in_specs = (
        tokens,
        P(("pts", "grp")),
        P(("pts", "grp")),
        P(),
        P(),
        P(),
        P(),
        P(),
        P(),
        tokens,
    )
    out_specs = (tokens, tokens, P(), P(), P(), P(), P())
    return jax.shard_map(
        on_device, mesh=mesh, in_specs=in_specs, out_specs=out_specs, check_vma=False
    )
```
